32 devices in a mesh: seq: 16 (over z, y, core), tp: 2 (over x).
Axes of the slice: x: 2, y: 2, z: 4, core: 2. Of those that a mesh axis runs over, the one named last changes fastest.
Arguments:
- q_pre: bfloat16 [4096, 7168], P('seq', 'tp')
- k_cache: bfloat16 [4096, 1024], P('seq', 'tp')
- v_cache: bfloat16 [4096, 1024], P('seq', 'tp'), may hold values from -6 to 6
- prompt_lengths: int32 [3], replicated, may hold values from 1 to 3072, 4096 in all
- q_dec: bfloat16 [64, 4, 7168], P(None, None, 'tp')
- k_new: bfloat16 [64, 4, 1024], P(None, None, 'tp')
- v_new: bfloat16 [64, 4, 1024], P(None, None, 'tp'), may hold values from -6 to 6
- block_table: int32 [64, 32], replicated, may hold values from 0 to 63, as said below
- w_out: bfloat16 [7168, 7168], P('tp', 'seq'), may hold values from -0.0625 to 0.0625
Outputs:
- pre_out: bfloat16 [4096, 7168], P('seq', 'tp')
- dec_out: bfloat16 [64, 4, 7168], P('tp', None, 'seq')
The draws below stay inside these ranges and needn't reach their ends.
Inputs may be any that keep to these rules, and one draw needn't show every extreme that they name: `block_table`: each row names 32 different cache blocks.
All inputs are finite; a program needn't handle non-finite values.
Results may differ from the reference program's by a relative error of at most 0.022.
Values may be sent and summed in bfloat16 or wider, within the bound.
No kernel may reach another device: no remote copies, remote signals or barrier semaphores. Data moves between devices by JAX's collectives and lax.ppermute only.
A program may use at most 128 MiB of HBM per device.

```python
import math
import jax
import jax.numpy as jnp
import numpy as np
from jax import lax

D = 7168
H = 56
KVH = 8
HD = 128
R = 64
STEPS = 4
PROMPTS = 3
BLK = 64
L = 4096
NB = 64
NPAGE = 32


def prompt_keys(key):
    return jax.random.normal(jax.random.fold_in(key, 11), (L, KVH * HD), jnp.float32)


def fresh_keys(key):
    return jax.random.normal(jax.random.fold_in(key, 13), (R, STEPS, KVH * HD), jnp.float32)


def block_choice(key):
    row_keys = jax.random.split(jax.random.fold_in(key, 17), R)
    picks = jax.vmap(lambda one: jax.random.permutation(one, NB)[:NPAGE])(row_keys)
    return picks.astype(jnp.int32)


def draw_k_cache(key, part):
    base = prompt_keys(key)
    return base.astype(jnp.bfloat16)


def draw_k_new(key, part):
    base = fresh_keys(key)
    return base.astype(jnp.bfloat16)


def draw_q_pre(key, part):
    key = jax.random.fold_in(key, 5)
    noise = jax.random.normal(key, (L, H * HD), jnp.float32)
    return noise.astype(jnp.bfloat16)


def draw_q_dec(key, part):
    key = jax.random.fold_in(key, 6)
    noise = jax.random.normal(key, (R, STEPS, H * HD), jnp.float32)
    return noise.astype(jnp.bfloat16)


def draw_block_table(key, part):
    picks = block_choice(key)
    return picks


def block_levels(rng, extent, cuts, least, top_value):
    loudness = 1.0
    for position, shards_of in cuts:
        heights = jax.random.uniform(jax.random.fold_in(jax.random.fold_in(rng, 6), position), (shards_of,), jnp.float32, least / len(cuts), top_value / len(cuts))
        loudness = loudness * jnp.repeat(jnp.exp(heights), extent[position] // shards_of).reshape((-1,) + (1,) * (len(extent) - 1 - position))
    return loudness


def length_profile(number_of, total, most, lean):
    portions = [(1 << 20) // math.isqrt(standing ** lean) + 1 for standing in range(2, number_of + 1)]
    surplus, counts = total - most - (number_of - 1), [1] * (number_of - 1)
    while surplus > 0:
        movable = [i for i in range(number_of - 1) if counts[i] < most]
        mass, remaining = sum([portions[i] for i in movable]), surplus
        for i in movable:
            extra = min(most - counts[i], max(1, remaining * portions[i] // mass), surplus)
            counts[i] = counts[i] + extra
            surplus = surplus - extra
    return np.array([most] + counts)


def ragged_sizes(own_key, amount, total, bound, lean):
    if amount == 2:
        one = jax.random.randint(own_key, (), max(1, total - bound), min(bound, total - 1) + 1)
        return jnp.stack([one, total - one])
    sizes = jnp.asarray(length_profile(amount, total, bound, lean), jnp.int32)
    couples = (amount - 1) // 2
    giver, sink = sizes[1:1 + 2 * couples:2], sizes[2:2 + 2 * couples:2]
    slack = jnp.minimum(giver - 1, bound - sink)
    passed = jax.random.randint(jax.random.fold_in(own_key, 1), (couples,), 0, 1 << 20) % (slack + 1)
    sizes = sizes.at[1:1 + 2 * couples:2].set(giver - passed).at[2:2 + 2 * couples:2].set(sink + passed)
    return sizes[jax.random.permutation(jax.random.fold_in(own_key, 2), amount)]


def bell_draw(key, extent, deviation, bound, pieces=(), kind=jnp.bfloat16):
    factor_of = block_levels(key, extent, pieces, -0.22, 0.18) if pieces else 1.0
    entries = jax.random.normal(key, extent, jnp.float32) * deviation * factor_of
    return jnp.minimum(jnp.maximum(entries, -bound), bound).astype(kind)


def setup_inputs(seed: int = 0) -> dict:
    streams_of = jax.random.split(jax.random.key(seed), 10)
    q_pre = draw_q_pre(jax.random.fold_in(streams_of[9], 71), 0)
    k_cache = draw_k_cache(jax.random.fold_in(streams_of[9], 71), 0)
    v_cache = bell_draw(streams_of[2], (L, KVH * HD), 1.0, 6.0, ((0, 16), (1, 2)))
    prompt_lengths = ragged_sizes(streams_of[3], PROMPTS, L, L * 3 // 4, 2).astype(jnp.int32)
    q_dec = draw_q_dec(jax.random.fold_in(streams_of[9], 71), 0)
    k_new = draw_k_new(jax.random.fold_in(streams_of[9], 71), 0)
    v_new = bell_draw(streams_of[6], (R, STEPS, KVH * HD), 1.0, 6.0, ((2, 2),))
    block_table = draw_block_table(jax.random.fold_in(streams_of[9], 71), 0)
    w_out = bell_draw(streams_of[8], (H * HD, D), (H * HD) ** -0.5, 0.0625, ((0, 2), (1, 16)))
    return dict(q_pre=q_pre, k_cache=k_cache, v_cache=v_cache, prompt_lengths=prompt_lengths, q_dec=q_dec, k_new=k_new, v_new=v_new, block_table=block_table, w_out=w_out)


def segment_of(positions, ends):
    return lax.optimization_barrier(jnp.sum((positions[:, None] >= ends[None, :]).astype(jnp.int32), axis=1))

def reference(q_pre, k_cache, v_cache, prompt_lengths, q_dec, k_new, v_new, block_table, w_out):
    total_len = q_pre.shape[0]
    group = H // KVH
    scale = 1.0 / math.sqrt(HD)
    ends = jnp.cumsum(prompt_lengths).astype(jnp.int32)
    positions = jnp.arange(total_len, dtype=jnp.int32)
    segment = segment_of(positions, ends)
    qblock = min(512, total_len)
    nblocks = total_len // qblock
    queries = q_pre.reshape(nblocks, qblock, KVH, group, HD)
    keys = k_cache.reshape(total_len, KVH, HD)
    values = v_cache.reshape(total_len, KVH, HD)

    def one_block(bidx):
        qpos = bidx * qblock + jnp.arange(qblock, dtype=jnp.int32)
        allowed = (positions[None, :] <= qpos[:, None]) & (segment[None, :] == segment_of(qpos, ends)[:, None])
        block_q = queries[bidx]

        def one_head(hidx):
            qh = block_q[:, hidx].astype(jnp.float32)
            scores = jnp.einsum('trd,nd->trn', qh, keys[:, hidx].astype(jnp.float32)) * scale
            scores = jnp.where(allowed[:, None, :], scores, -1e+30)
            top = lax.optimization_barrier(jnp.max(scores, axis=-1, keepdims=True))
            weights = jnp.where(allowed[:, None, :], jnp.exp(scores - top), 0.0)
            total = lax.optimization_barrier(jnp.sum(weights, axis=-1))
            rounded = weights.astype(jnp.bfloat16).astype(jnp.float32)
            summed = jnp.einsum('trn,nd->trd', rounded, values[:, hidx].astype(jnp.float32))
            return summed / total[..., None]
        heads_out = lax.map(one_head, jnp.arange(KVH, dtype=jnp.int32))
        return jnp.transpose(heads_out, (1, 0, 2, 3))
    pre = lax.map(one_block, jnp.arange(nblocks, dtype=jnp.int32))
    pre_out = pre.reshape(total_len, H * HD).astype(jnp.bfloat16)
    rows = q_dec.shape[0]
    steps = q_dec.shape[1]
    nblk = total_len // BLK
    member = jnp.zeros((rows, nblk), jnp.float32).at[jnp.arange(rows)[:, None], block_table].set(1.0)
    keymask = jnp.repeat(member, BLK, axis=1) > 0.5
    newmask = jnp.arange(steps)[None, :] <= jnp.arange(steps)[:, None]
    qd = q_dec.reshape(rows, steps, KVH, group, HD)
    kn = k_new.reshape(rows, steps, KVH, HD)
    vn = v_new.reshape(rows, steps, KVH, HD)

    def dec_head(hidx):
        qh = qd[:, :, hidx].astype(jnp.float32)
        scores = jnp.einsum('rsqd,td->rsqt', qh, keys[:, hidx].astype(jnp.float32)) * scale
        scores = jnp.where(keymask[:, None, None, :], scores, -1e+30)
        fresh = jnp.einsum('rsqd,rjd->rsqj', qh, kn[:, :, hidx].astype(jnp.float32)) * scale
        fresh = jnp.where(newmask[None, :, None, :], fresh, -1e+30)
        top = jnp.maximum(lax.optimization_barrier(jnp.max(scores, axis=-1)), lax.optimization_barrier(jnp.max(fresh, axis=-1)))[..., None]
        weights = jnp.where(keymask[:, None, None, :], jnp.exp(scores - top), 0.0)
        fweights = jnp.where(newmask[None, :, None, :], jnp.exp(fresh - top), 0.0)
        total = lax.optimization_barrier(jnp.sum(weights, axis=-1)) + lax.optimization_barrier(jnp.sum(fweights, axis=-1))
        summed = jnp.einsum('rsqt,td->rsqd', weights.astype(jnp.bfloat16).astype(jnp.float32), values[:, hidx].astype(jnp.float32))
        summed = summed + jnp.einsum('rsqj,rjd->rsqd', fweights.astype(jnp.bfloat16).astype(jnp.float32), vn[:, :, hidx].astype(jnp.float32))
        return summed / total[..., None]
    dec = lax.map(dec_head, jnp.arange(KVH, dtype=jnp.int32))
    attn = jnp.transpose(dec, (1, 2, 0, 3, 4)).reshape(rows * steps, H * HD).astype(jnp.bfloat16)
    dec_out = jnp.dot(attn, w_out, preferred_element_type=jnp.float32).reshape(rows, steps, -1).astype(jnp.bfloat16)
    return (pre_out, dec_out)
```

```python
import functools
import math

import jax
import jax.numpy as jnp
from jax import lax
from jax.experimental import pallas as pl
from jax.experimental.pallas import tpu as pltpu
from jax.sharding import PartitionSpec as P

H = 56
KVH = 8
HD = 128
BLK = 64
SPAN = 512
NEG = -1e30
FACTOR = math.log2(math.e) / math.sqrt(HD)
ROOM = 60 * 1024 * 1024


def dot_nt(a, b):
    return lax.dot_general(a, b, (((1,), (1,)), ((), ())), preferred_element_type=jnp.float32)


def dot_nn(a, b):
    return lax.dot_general(a, b, (((1,), (0,)), ((), ())), preferred_element_type=jnp.float32)


def fold(x, op):
    out = x[:, :HD]
    for i in range(1, x.shape[1] // HD):
        out = op(out, x[:, i * HD : (i + 1) * HD])
    return out


def start_of(position, lengths):
    end = jnp.int32(0)
    out = jnp.zeros_like(position)
    for i in range(lengths.shape[0]):
        end = end + lengths[i]
        out = jnp.where(position >= end, end, out)
    return out


def fetches(parts, starts, full, sems, base, offset):
    return [
        pltpu.make_async_copy(
            part,
            full.at[pl.ds(pl.multiple_of(starts[offset + i], BLK), part.shape[0])],
            sems.at[base + i],
        )
        for i, part in enumerate(parts)
    ]


def prefill_kernel(nk, nv, tok, heads, first_group, starts, lengths, place, q, *refs):
    kparts, vparts = refs[:nk], refs[nk : nk + nv]
    out, kfull, vfull, sems, qs, scores, peak, total, acc = refs[-9:]
    step = pl.program_id(0)
    group = step + first_group
    kcopies = fetches(kparts, starts, kfull, sems, 0, 0)
    vcopies = fetches(vparts, starts, vfull, sems, nk, nk)

    @pl.when(step == 0)
    def _():
        for copy in kcopies + vcopies:
            copy.start()

    for j in range(heads):
        qs[j * tok : (j + 1) * tok] = q[:, j * HD : (j + 1) * HD]

    @pl.when(step == 0)
    def _():
        for copy in kcopies:
            copy.wait()

    begin = place[0] * tok
    finish = begin + tok
    low = start_of(begin, lengths)
    high = start_of(finish - 1, lengths)
    blocks = lax.div(finish - low + SPAN - 1, SPAN)
    clear = lax.div(finish - high, SPAN)
    columns = pl.ds(pl.multiple_of(group * HD, HD), HD)

    def rows_of(k):
        return pl.ds(pl.multiple_of(jnp.maximum(finish - (k + 1) * SPAN, 0), BLK), SPAN)

    def slot(k):
        return pl.ds(pl.multiple_of(k * SPAN, SPAN), SPAN)

    peak[...] = jnp.full_like(peak, NEG)

    def score_block(k, masked):
        keys = kfull[rows_of(k), columns]
        s = dot_nt(qs[...], keys) * FACTOR
        if masked:
            t = begin + lax.broadcasted_iota(jnp.int32, (tok, 1), 0)
            u = jnp.maximum(finish - (k + 1) * SPAN, 0) + lax.broadcasted_iota(
                jnp.int32, (tok, SPAN), 1
            )
            last = jnp.minimum(t, finish - k * SPAN - 1)
            allowed = (u <= last) & (u >= start_of(t, lengths))
            s = jnp.where(allowed[None], s.reshape(heads, tok, SPAN), NEG).reshape(s.shape)
        scores[:, slot(k)] = s
        peak[...] = jnp.maximum(peak[...], fold(s, jnp.maximum))

    score_block(0, True)

    @pl.loop(1, jnp.maximum(clear, 1))
    def _(k):
        score_block(k, False)

    @pl.loop(jnp.maximum(clear, 1), blocks)
    def _(k):
        score_block(k, True)

    peak[...] = jnp.broadcast_to(jnp.max(peak[...], axis=1, keepdims=True), peak.shape)
    total[...] = jnp.zeros_like(total)
    acc[...] = jnp.zeros_like(acc)

    @pl.when(step == 0)
    def _():
        for copy in vcopies:
            copy.wait()

    @pl.loop(0, blocks)
    def _(k):
        s = scores[:, slot(k)]
        p = jnp.exp2(s - jnp.concatenate([peak[...]] * (SPAN // HD), axis=1))
        total[...] += fold(p, jnp.add)
        acc[...] += dot_nn(p.astype(jnp.bfloat16), vfull[rows_of(k), columns])

    whole = jnp.sum(total[...], axis=1, keepdims=True)
    result = (acc[...] / whole).astype(out.dtype)
    for j in range(heads):
        out[:, j * HD : (j + 1) * HD] = result[j * tok : (j + 1) * tok]


def prefill(q, kparts, vparts, starts, lengths, place, first_group, groups, before=None):
    tok = q.shape[0]
    count = sum(part.shape[0] for part in kparts)
    total_groups = kparts[0].shape[1] // HD
    heads = q.shape[1] // HD // total_groups
    rows = heads * tok
    longest = min(count * 3 // 4 + tok, count)
    slots = pl.cdiv(longest, SPAN)
    nk, nv = len(kparts), len(vparts)
    anywhere = pl.BlockSpec(memory_space=pl.ANY)
    block = pl.BlockSpec((tok, heads * HD), lambda g, *_: (0, g + first_group))
    extra = [] if before is None else [before]
    pairs = rows * longest * groups
    return pl.pallas_call(
        functools.partial(prefill_kernel, nk, nv, tok, heads, first_group),
        out_shape=jax.ShapeDtypeStruct(q.shape, jnp.bfloat16),
        grid_spec=pltpu.PrefetchScalarGridSpec(
            num_scalar_prefetch=3,
            grid=(groups,),
            in_specs=[block] + [anywhere] * (nk + nv + len(extra)),
            out_specs=block,
            scratch_shapes=[
                pltpu.VMEM((count, kparts[0].shape[1]), jnp.bfloat16),
                pltpu.VMEM((count, vparts[0].shape[1]), jnp.bfloat16),
                pltpu.SemaphoreType.DMA((nk + nv,)),
                pltpu.VMEM((rows, HD), jnp.bfloat16),
                pltpu.VMEM((rows, slots * SPAN), jnp.float32),
                pltpu.VMEM((rows, HD), jnp.float32),
                pltpu.VMEM((rows, HD), jnp.float32),
                pltpu.VMEM((rows, HD), jnp.float32),
            ],
        ),
        compiler_params=pltpu.CompilerParams(vmem_limit_bytes=ROOM),
        cost_estimate=pl.CostEstimate(
            flops=pairs * HD * 4, bytes_accessed=count * HD * 8 * groups, transcendentals=pairs
        ),
        input_output_aliases={} if before is None else {4 + nk + nv: 0},
        name="prefill",
    )(starts, lengths, place, q, *kparts, *vparts, *extra)


def decode_kernel(nk, nv, steps, starts, q, mask, newk, newv, *refs):
    kparts, vparts = refs[:nk], refs[nk : nk + nv]
    out, kfull, vfull, sems, scores = refs[-5:]
    kcopies = fetches(kparts, starts, kfull, sems, 0, 0)
    vcopies = fetches(vparts, starts, vfull, sems, nk, nk)
    for copy in kcopies + vcopies:
        copy.start()
    groups, rows, unused = q.shape
    count = kfull.shape[0]
    own = newk.shape[0]
    copies = rows // own
    row = lax.broadcasted_iota(jnp.int32, (own, own), 0)
    col = lax.broadcasted_iota(jnp.int32, (own, own), 1)
    fresh_ok = (lax.div(row, steps) == lax.div(col, steps)) & (col <= row)
    for copy in kcopies:
        copy.wait()
    for g in range(groups):
        columns = slice(g * HD, (g + 1) * HD)
        fresh = dot_nt(q[g], newk[:, columns]) * FACTOR
        fresh = jnp.where(fresh_ok[None], fresh.reshape(copies, own, own), NEG).reshape(rows, own)
        peak = jnp.full((rows, HD), NEG, jnp.float32)
        for k in range(0, count, SPAN):
            s = dot_nt(q[g], kfull[k : k + SPAN, columns]) * FACTOR
            s = s.reshape(copies, own, SPAN)
            s = jnp.where(mask[:, k : k + SPAN][None] > 0, s, NEG).reshape(rows, SPAN)
            scores[g, :, k : k + SPAN] = s
            peak = jnp.maximum(peak, fold(s, jnp.maximum))
        top = jnp.maximum(
            jnp.max(peak, axis=1, keepdims=True), jnp.max(fresh, axis=1, keepdims=True)
        )
        if g == 0:
            for copy in vcopies:
                copy.wait()
        weights = jnp.exp2(fresh - top)
        whole = jnp.sum(weights, axis=1, keepdims=True)
        acc = dot_nn(weights.astype(jnp.bfloat16), newv[:, columns])
        total = jnp.zeros((rows, HD), jnp.float32)
        for k in range(0, count, SPAN):
            p = jnp.exp2(scores[g, :, k : k + SPAN] - top)
            total = total + fold(p, jnp.add)
            acc = acc + dot_nn(p.astype(jnp.bfloat16), vfull[k : k + SPAN, columns])
        whole = whole + jnp.sum(total, axis=1, keepdims=True)
        out[g] = (acc / whole).astype(out.dtype)


def decode(q, mask, newk, newv, kparts, vparts, starts, steps):
    groups, rows, unused = q.shape
    count = sum(part.shape[0] for part in kparts)
    nk, nv = len(kparts), len(vparts)
    anywhere = pl.BlockSpec(memory_space=pl.ANY)
    vmem = pl.BlockSpec(memory_space=pltpu.VMEM)
    pairs = groups * rows * count
    return pl.pallas_call(
        functools.partial(decode_kernel, nk, nv, steps),
        out_shape=jax.ShapeDtypeStruct(q.shape, jnp.bfloat16),
        grid_spec=pltpu.PrefetchScalarGridSpec(
            num_scalar_prefetch=1,
            grid=(),
            in_specs=[vmem] * 4 + [anywhere] * (nk + nv),
            out_specs=vmem,
            scratch_shapes=[
                pltpu.VMEM((count, groups * HD), jnp.bfloat16),
                pltpu.VMEM((count, groups * HD), jnp.bfloat16),
                pltpu.SemaphoreType.DMA((nk + nv,)),
                pltpu.VMEM((groups, rows, count), jnp.float32),
            ],
        ),
        compiler_params=pltpu.CompilerParams(vmem_limit_bytes=32 * 1024 * 1024),
        cost_estimate=pl.CostEstimate(
            flops=pairs * HD * 4, bytes_accessed=count * groups * HD * 4, transcendentals=pairs
        ),
        name="decode",
    )(starts, q, mask, newk, newv, *kparts, *vparts)


def spread(x, n):
    place = lax.axis_index("seq")
    deep = n // 4

    def index(z, y, c):
        return (z * 2 + y) * 2 + c

    everyone = [(z, y, c) for z in range(deep) for y in range(2) for c in range(2)]
    z, y, c = place // 4, (place // 2) % 2, place % 2
    held = [(x, z, y, c)]
    for d in range(1, deep):
        perm = [(index(*p), index((p[0] - d) % deep, p[1], p[2])) for p in everyone]
        held.append((lax.ppermute(x, "seq", perm), lax.rem(z + d, deep), y, c))
    perm = [(index(*p), index(p[0], 1 - p[1], p[2])) for p in everyone]
    held += [(lax.ppermute(b, "seq", perm), bz, 1 - by, bc) for b, bz, by, bc in held]
    perm = [(index(*p), index(p[0], p[1], 1 - p[2])) for p in everyone]
    held += [(lax.ppermute(b, "seq", perm), bz, by, 1 - bc) for b, bz, by, bc in held]
    return [b for b, *_ in held], jnp.stack([index(bz, by, bc) for _, bz, by, bc in held])


def per_device(n, tp, q_pre, k_cache, v_cache, prompt_lengths, q_dec, k_new, v_new, block_table, w_out):
    tok = q_pre.shape[0]
    groups = k_cache.shape[1] // HD
    heads = H // KVH
    place = lax.axis_index("seq").astype(jnp.int32)
    rows, steps = q_dec.shape[0], q_dec.shape[1]
    own = rows // n

    vparts, sources = spread(v_cache, n)
    kparts = [lax.all_gather(k_cache, "seq", axis=0, tiled=True)]
    starts = jnp.concatenate([jnp.zeros((1,), jnp.int32), sources.astype(jnp.int32) * tok])
    lengths = prompt_lengths.astype(jnp.int32)

    def mine(x):
        return lax.dynamic_slice_in_dim(x, place * own, own, 0)

    table = mine(block_table)
    number = lax.broadcasted_iota(jnp.int32, (own, table.shape[1], n * tok), 2) // BLK
    mask = jnp.any(table[:, :, None] == number, axis=1).astype(jnp.float32)
    mask = jnp.repeat(mask, steps, axis=0)
    qd = mine(q_dec).reshape(own * steps, groups, heads, HD)
    qd = qd.transpose(1, 2, 0, 3).reshape(groups, heads * own * steps, HD)
    newk = mine(k_new).reshape(own * steps, -1)
    newv = mine(v_new).reshape(own * steps, -1)
    attn_own = decode(qd, mask, newk, newv, kparts, vparts, starts, steps)
    attn_own = attn_own.reshape(groups, heads, own * steps, HD).transpose(2, 0, 1, 3)
    attn = lax.all_gather(attn_own.reshape(own * steps, -1), "seq", axis=0, tiled=True)

    half = max(groups // 2, 1)
    pre_out = prefill(q_pre, kparts, vparts, starts, lengths, place[None], 0, half)
    flat = jnp.dot(attn, w_out, preferred_element_type=jnp.float32).astype(jnp.bfloat16)
    dec_out = lax.psum_scatter(
        flat.reshape(rows, steps, -1), "tp", scatter_dimension=0, tiled=True
    )
    if half < groups:
        pre_out = prefill(
            q_pre, kparts, vparts, starts, lengths, place[None], half, groups - half, pre_out
        )
    return (pre_out, dec_out)


def solution(mesh):
    placed = (
        P("seq", "tp"),
        P("seq", "tp"),
        P("seq", "tp"),
        P(),
        P(None, None, "tp"),
        P(None, None, "tp"),
        P(None, None, "tp"),
        P(),
        P("tp", "seq"),
    )
    return jax.shard_map(
        functools.partial(per_device, mesh.shape["seq"], mesh.shape["tp"]),
        mesh=mesh,
        in_specs=placed,
        out_specs=(P("seq", "tp"), P("tp", None, "seq")),
        check_vma=False,
    )
```

```python
import functools
import math

import jax
import jax.numpy as jnp
from jax import lax
from jax.experimental import pallas as pl
from jax.experimental.pallas import tpu as pltpu
from jax.sharding import PartitionSpec as P

H = 56
KVH = 8
HD = 128
BLK = 64
SPAN = 512
PAIR = 2
NEG = -1e30
LEAST, MOST = 2.0**-60, 2.0**100
FACTOR = math.log2(math.e) / math.sqrt(HD)
ROOM = 32 * 1024 * 1024
HBM = pl.BlockSpec(memory_space=pltpu.HBM)
VMEM = pl.BlockSpec(memory_space=pltpu.VMEM)


def dot_nt(a, b):
    return lax.dot_general(a, b, (((1,), (1,)), ((), ())), preferred_element_type=jnp.float32)


def dot_nn(a, b):
    return lax.dot_general(a, b, (((1,), (0,)), ((), ())), preferred_element_type=jnp.float32)


def fold(x, op):
    out = x[:, :HD]
    for i in range(1, x.shape[1] // HD):
        out = op(out, x[:, i * HD : (i + 1) * HD])
    return out


def start_of(position, lengths):
    end = jnp.int32(0)
    out = jnp.zeros_like(position)
    for i in range(lengths.shape[0]):
        end = end + lengths[i]
        out = jnp.where(position >= end, end, out)
    return out


def sound(total):
    return (jnp.min(total) >= LEAST) & (jnp.max(total) <= MOST)


def prefill_kernel(parts, tok, heads, groups, meta, lengths, q, *refs):
    kparts, vparts = refs[:parts], refs[parts : 2 * parts]
    out, kfull, vfull, sems, qs, peak, total, acc = refs[2 * parts :]
    step = pl.program_id(0)

    def copies(group):
        columns = pl.ds(pl.multiple_of(group * HD, HD), HD)
        both = []
        for i in range(parts):
            rows = pl.ds(pl.multiple_of(meta[3 + i], BLK), kparts[i].shape[0])
            for part, full, sem in ((kparts[i], kfull, 2 * i), (vparts[i], vfull, 2 * i + 1)):
                both.append(
                    pltpu.make_async_copy(
                        part.at[:, columns], full.at[rows, columns], sems.at[group, sem]
                    )
                )
        return both

    @pl.when(step == 0)
    def _():
        for group in range(groups):
            for copy in copies(group):
                copy.start()

    for j in range(heads):
        qs[j * tok : (j + 1) * tok] = q[:, j * HD : (j + 1) * HD]
    total[...] = jnp.zeros_like(total)
    acc[...] = jnp.zeros_like(acc)

    begin = meta[0]
    finish = begin + tok
    low = start_of(begin, lengths)
    high = start_of(finish - 1, lengths)
    blocks = lax.div(finish - low + SPAN - 1, SPAN)
    clear = lax.div(finish - high, SPAN)
    columns = pl.ds(pl.multiple_of(step * HD, HD), HD)

    def first_of(k):
        return jnp.maximum(finish - (k + 1) * SPAN, 0)

    def allowed_in(k):
        t = begin + lax.broadcasted_iota(jnp.int32, (tok, 1), 0)
        u = first_of(k) + lax.broadcasted_iota(jnp.int32, (tok, SPAN), 1)
        last = jnp.minimum(t, finish - k * SPAN - 1)
        return (u <= last) & (u >= start_of(t, lengths))

    def keep(allowed, x, other):
        some = x.shape[0] // tok
        return jnp.where(allowed[None], x.reshape(some, tok, SPAN), other).reshape(x.shape)

    def block(k, masked):
        rows = pl.ds(pl.multiple_of(first_of(k), BLK), SPAN)
        keys, values = kfull[rows, columns], vfull[rows, columns]
        allowed = allowed_in(k) if masked else None
        for j in range(0, heads, PAIR):
            here = slice(j * tok, min(j + PAIR, heads) * tok)
            p = jnp.exp2(dot_nt(qs[here], keys) * FACTOR)
            if masked:
                p = keep(allowed, p, 0.0)
            total[here] += fold(p, jnp.add)
            acc[here] += dot_nn(p.astype(jnp.bfloat16), values)

    for copy in copies(step):
        copy.wait()

    block(0, True)

    @pl.loop(1, jnp.maximum(clear, 1))
    def _(k):
        block(k, False)

    @pl.loop(jnp.maximum(clear, 1), blocks)
    def _(k):
        block(k, True)

    def write():
        whole = jnp.sum(total[...], axis=1, keepdims=True)
        result = (acc[...] / whole).astype(out.dtype)
        for j in range(heads):
            out[:, j * HD : (j + 1) * HD] = result[j * tok : (j + 1) * tok]
        return whole

    fine = sound(write())

    @pl.when(jnp.logical_not(fine))
    def _():
        peak[...] = jnp.full_like(peak, NEG)
        total[...] = jnp.zeros_like(total)
        acc[...] = jnp.zeros_like(acc)

        @pl.loop(0, blocks)
        def _(k):
            rows = pl.ds(pl.multiple_of(first_of(k), BLK), SPAN)
            keys, values = kfull[rows, columns], vfull[rows, columns]
            allowed = allowed_in(k)

            @pl.loop(0, heads)
            def _(j):
                here = pl.ds(pl.multiple_of(j * tok, tok), tok)
                s = jnp.where(allowed, dot_nt(qs[here], keys) * FACTOR, NEG)
                top = jnp.maximum(peak[here], jnp.max(s, axis=1, keepdims=True))
                p = jnp.where(allowed, jnp.exp2(s - top[:, :1]), 0.0)
                shrink = jnp.exp2(peak[here] - top)
                total[here] = total[here] * shrink + fold(p, jnp.add)
                acc[here] = acc[here] * shrink + dot_nn(p.astype(jnp.bfloat16), values)
                peak[here] = top

        write()


def prefill(q, kparts, vparts, meta, lengths, columns, name):
    tok = q.shape[0]
    parts = len(kparts)
    count = sum(part.shape[0] for part in kparts)
    groups = kparts[0].shape[1] // HD
    heads = H // KVH
    rows = heads * tok
    pairs = rows * count // 2 * groups
    return pl.pallas_call(
        functools.partial(prefill_kernel, parts, tok, heads, groups),
        out_shape=jax.ShapeDtypeStruct((tok, columns), jnp.bfloat16),
        grid_spec=pltpu.PrefetchScalarGridSpec(
            num_scalar_prefetch=2,
            grid=(groups,),
            in_specs=[pl.BlockSpec((tok, heads * HD), lambda g, meta, lengths: (0, meta[1] + g))]
            + [HBM] * (2 * parts),
            out_specs=pl.BlockSpec((tok, heads * HD), lambda g, meta, lengths: (0, meta[2] + g)),
            scratch_shapes=[
                pltpu.VMEM((count, groups * HD), jnp.bfloat16),
                pltpu.VMEM((count, groups * HD), jnp.bfloat16),
                pltpu.SemaphoreType.DMA((groups, 2 * parts)),
                pltpu.VMEM((rows, HD), jnp.bfloat16),
                pltpu.VMEM((rows, HD), jnp.float32),
                pltpu.VMEM((rows, HD), jnp.float32),
                pltpu.VMEM((rows, HD), jnp.float32),
            ],
        ),
        compiler_params=pltpu.CompilerParams(vmem_limit_bytes=ROOM),
        cost_estimate=pl.CostEstimate(
            flops=pairs * HD * 8, bytes_accessed=count * HD * 4 * groups, transcendentals=pairs
        ),
        name=name,
    )(meta, lengths, q, *kparts, *vparts)


def decode_kernel(parts, steps, heads, groups, starts, q, mask, newk, newv, *refs):
    kparts, vparts = refs[:parts], refs[parts : 2 * parts]
    out, kheld, vheld, sems, scores = refs[2 * parts :]
    kcopies = [
        pltpu.make_async_copy(kparts[i], kheld.at[i], sems.at[2 * i]) for i in range(parts)
    ]
    vcopies = [
        pltpu.make_async_copy(vparts[i], vheld.at[i], sems.at[2 * i + 1]) for i in range(parts)
    ]
    for i in range(parts):
        kcopies[i].start()
        vcopies[i].start()
    own = q.shape[0]
    rows = heads * own
    length = kheld.shape[1]
    row = lax.broadcasted_iota(jnp.int32, (own, own), 0)
    col = lax.broadcasted_iota(jnp.int32, (own, own), 1)
    fresh_ok = (lax.div(row, steps) == lax.div(col, steps)) & (col <= row)

    def columns(g):
        return slice(g * HD, (g + 1) * HD)

    def stacked(g):
        first = g * heads
        slices = [q[:, (first + j) * HD : (first + j + 1) * HD] for j in range(heads)]
        return jnp.concatenate([x.astype(jnp.float32) for x in slices], 0).astype(jnp.bfloat16)

    def keep(allowed, x, other):
        y = x.reshape(heads, own, x.shape[1])
        return jnp.where(allowed[None], y, other).reshape(x.shape)

    def open_to(i):
        return mask[:, pl.ds(pl.multiple_of(starts[i], HD), length)] > 0

    def write(g, acc, whole):
        result = acc / whole
        for j in range(heads):
            out[:, (g * heads + j) * HD : (g * heads + j + 1) * HD] = result[
                j * own : (j + 1) * own
            ].astype(out.dtype)

    queries = [stacked(g) for g in range(groups)]
    totals, sums, wholes = [], [], []
    for g in range(groups):
        p = keep(fresh_ok, jnp.exp2(dot_nt(queries[g], newk[:, columns(g)]) * FACTOR), 0.0)
        wholes.append(jnp.sum(p, axis=1, keepdims=True))
        totals.append(jnp.zeros((rows, HD), jnp.float32))
        sums.append(dot_nn(p.astype(jnp.bfloat16), newv[:, columns(g)]))
    for i in range(parts):
        kcopies[i].wait()
        vcopies[i].wait()
        for g in range(groups):
            s = dot_nt(queries[g], kheld[i, :, columns(g)])
            p = keep(open_to(i), jnp.exp2(s * FACTOR), 0.0)
            totals[g] = totals[g] + fold(p, jnp.add)
            sums[g] = sums[g] + dot_nn(p.astype(jnp.bfloat16), vheld[i, :, columns(g)])
    fine = None
    for g in range(groups):
        whole = wholes[g] + jnp.sum(totals[g], axis=1, keepdims=True)
        write(g, sums[g], whole)
        fine = sound(whole) if fine is None else fine & sound(whole)

    @pl.when(jnp.logical_not(fine))
    def _():
        for g in range(groups):
            query = stacked(g)
            fresh = keep(fresh_ok, dot_nt(query, newk[:, columns(g)]) * FACTOR, NEG)
            top = jnp.max(fresh, axis=1, keepdims=True)
            for i in range(parts):
                s = keep(open_to(i), dot_nt(query, kheld[i, :, columns(g)]) * FACTOR, NEG)
                scores[:, i * length : (i + 1) * length] = s
                top = jnp.maximum(top, jnp.max(s, axis=1, keepdims=True))
            p = jnp.exp2(fresh - top)
            whole = jnp.sum(p, axis=1, keepdims=True)
            acc = dot_nn(p.astype(jnp.bfloat16), newv[:, columns(g)])
            for i in range(parts):
                p = jnp.exp2(scores[:, i * length : (i + 1) * length] - top)
                whole = whole + jnp.sum(p, axis=1, keepdims=True)
                acc = acc + dot_nn(p.astype(jnp.bfloat16), vheld[i, :, columns(g)])
            write(g, acc, whole)


def decode(q, mask, newk, newv, kparts, vparts, starts, steps):
    own = q.shape[0]
    parts = len(kparts)
    length, width = kparts[0].shape
    heads = H // KVH
    groups = width // HD
    rows = heads * own
    pairs = groups * rows * parts * length
    return pl.pallas_call(
        functools.partial(decode_kernel, parts, steps, heads, groups),
        out_shape=jax.ShapeDtypeStruct(q.shape, jnp.bfloat16),
        grid_spec=pltpu.PrefetchScalarGridSpec(
            num_scalar_prefetch=1,
            grid=(),
            in_specs=[VMEM] * 4 + [HBM] * (2 * parts),
            out_specs=VMEM,
            scratch_shapes=[
                pltpu.VMEM((parts, length, width), jnp.bfloat16),
                pltpu.VMEM((parts, length, width), jnp.bfloat16),
                pltpu.SemaphoreType.DMA((2 * parts,)),
                pltpu.VMEM((rows, parts * length), jnp.float32),
            ],
        ),
        compiler_params=pltpu.CompilerParams(vmem_limit_bytes=ROOM),
        cost_estimate=pl.CostEstimate(
            flops=pairs * HD * 4, bytes_accessed=parts * length * width * 4, transcendentals=pairs
        ),
        name="decode",
    )(starts, q, mask, newk, newv, *kparts, *vparts)


def project_kernel(parts, meta, *refs):
    pieces, mine, other = refs[:parts], refs[parts], refs[parts + 1]
    kept, beside, across, corner, near, far = refs[parts + 2 :]
    rows = pieces[0].shape[0]
    whole = jnp.concatenate([piece[...] for piece in pieces], axis=0)
    for weights, result in ((mine, near), (other, far)):
        flat = dot_nt(whole, weights[...])
        for i in range(parts):
            where = pl.ds(pl.multiple_of(meta[1 + i], rows), rows)
            result[where] = flat[i * rows : (i + 1) * rows]
    half = kept.shape[0]
    here = pl.ds(pl.multiple_of(meta[0] * half, half), half)
    there = pl.ds(pl.multiple_of((1 - meta[0]) * half, half), half)
    kept[...] = near[here]
    beside[...] = far[here].astype(beside.dtype)
    across[...] = near[there].astype(across.dtype)
    corner[...] = far[there].astype(corner.dtype)


def project(pieces, mine, other, meta):
    parts = len(pieces)
    rows = parts * pieces[0].shape[0]
    width = mine.shape[0]
    block = jax.ShapeDtypeStruct((rows // 2, width), jnp.bfloat16)
    return pl.pallas_call(
        functools.partial(project_kernel, parts),
        out_shape=[jax.ShapeDtypeStruct((rows // 2, width), jnp.float32)] + [block] * 3,
        grid_spec=pltpu.PrefetchScalarGridSpec(
            num_scalar_prefetch=1,
            grid=(),
            in_specs=[VMEM] * (parts + 2),
            out_specs=[VMEM] * 4,
            scratch_shapes=[pltpu.VMEM((rows, width), jnp.float32)] * 2,
        ),
        compiler_params=pltpu.CompilerParams(vmem_limit_bytes=ROOM),
        cost_estimate=pl.CostEstimate(
            flops=rows * width * mine.shape[1] * 4,
            bytes_accessed=width * mine.shape[1] * 4,
            transcendentals=0,
        ),
        name="project",
    )(meta, *pieces, mine, other)


def index(z, y, c):
    return (z * 2 + y) * 2 + c


def on_ring(r, chips):
    return (r, 0) if r < chips // 2 else (chips - 1 - r, 1)


def ring_perm(chips, d):
    return [
        (index(*on_ring(r, chips), c), index(*on_ring((r + d) % chips, chips), c))
        for r in range(chips)
        for c in range(2)
    ]


def ring_place(r, chips):
    r = lax.rem(r + 2 * chips, chips)
    return jnp.where(r < chips // 2, r * 2, (chips - 1 - r) * 2 + 1)


def ring_gather(k, v, chips, r):
    half = chips // 2
    up, down = ring_perm(chips, 1), ring_perm(chips, -1)
    lists = []
    for x, above, below in ((k, half, half - 1), (v, half - 1, half)):
        held = {0: x}
        for d in range(1, half + 1):
            if d <= above:
                held[-d] = lax.ppermute(held[1 - d], "seq", up)
            if d <= below:
                held[d] = lax.ppermute(held[d - 1], "seq", down)
        held.setdefault(half, held.get(-half))
        order = [0] + [o for d in range(1, half) for o in (-d, d)] + [half]
        lists.append([held[o] for o in order])
    return lists[0], lists[1], jnp.stack([ring_place(r + o, chips) for o in order])


def spread(x, n):
    place = lax.axis_index("seq")
    deep = n // 4
    everyone = [(z, y, c) for z in range(deep) for y in range(2) for c in range(2)]
    z, y, c = place // 4, (place // 2) % 2, place % 2
    held = [(x, z, y, c)]
    for d in range(1, deep):
        perm = [(index(*p), index((p[0] - d) % deep, p[1], p[2])) for p in everyone]
        held.append((lax.ppermute(x, "seq", perm), lax.rem(z + d, deep), y, c))
    perm = [(index(*p), index(p[0], 1 - p[1], p[2])) for p in everyone]
    held += [(lax.ppermute(b, "seq", perm), bz, 1 - by, bc) for b, bz, by, bc in held]
    perm = [(index(*p), index(p[0], p[1], 1 - p[2])) for p in everyone]
    held += [(lax.ppermute(b, "seq", perm), bz, by, 1 - bc) for b, bz, by, bc in held]
    return [b for b, *_ in held], jnp.stack([index(bz, by, bc) for _, bz, by, bc in held])


def open_blocks(table, steps, count):
    number = lax.broadcasted_iota(jnp.int32, (*table.shape, count), 2) // BLK
    mask = jnp.any(table[:, :, None] == number, axis=1).astype(jnp.float32)
    return jnp.repeat(mask, steps, axis=0)


def whole_heads(n, q_pre, k_cache, v_cache, lengths, q_dec, k_new, v_new, block_table, w_out):
    tok = q_pre.shape[0]
    place = lax.axis_index("seq").astype(jnp.int32)
    rows, steps = q_dec.shape[0], q_dec.shape[1]
    own = rows // n
    kparts, sources = spread(k_cache, n)
    vparts, _ = spread(v_cache, n)
    starts = sources.astype(jnp.int32) * tok

    def mine(x):
        y = lax.dynamic_slice_in_dim(x, place * own, own, 0)
        return y.reshape(own * steps, -1) if x.ndim == 3 else y

    mask = open_blocks(mine(block_table), steps, n * tok)
    attn_own = decode(mine(q_dec), mask, mine(k_new), mine(v_new), kparts, vparts, starts, steps)
    attn = lax.all_gather(attn_own, "seq", axis=0, tiled=True)
    flat = jnp.dot(attn, w_out, preferred_element_type=jnp.float32).astype(jnp.bfloat16)
    dec_out = lax.psum_scatter(
        flat.reshape(rows, steps, -1), "tp", scatter_dimension=0, tiled=True
    )
    zero = jnp.zeros((), jnp.int32)
    meta = jnp.concatenate([jnp.stack([place * tok, zero, zero]), starts])
    pre_out = prefill(q_pre, kparts, vparts, meta, lengths, q_pre.shape[1], "prefill")
    return (pre_out, dec_out)


def split_heads(n, q_pre, k_cache, v_cache, lengths, q_dec, k_new, v_new, block_table, w_out):
    tok = q_pre.shape[0]
    place = lax.axis_index("seq").astype(jnp.int32)
    across = lax.axis_index("tp").astype(jnp.int32)
    core = lax.rem(place, 2)
    chip = lax.div(place, 2)
    chips = n // 2
    z, y = lax.div(chip, 2), lax.rem(chip, 2)
    r = jnp.where(y == 0, z, chips - 1 - z)
    rows, steps = q_dec.shape[0], q_dec.shape[1]
    own = rows // chips
    sibling = [(i, i ^ 1) for i in range(n)]

    def half(x, which, axis):
        size = x.shape[axis] // 2
        return lax.dynamic_slice_in_dim(x, which * size, size, axis)

    kv = jnp.concatenate([half(k_cache, 1 - core, 1), half(v_cache, 1 - core, 1)], axis=1)
    theirs = lax.ppermute(kv, "seq", sibling)
    ours = jnp.concatenate([half(k_cache, core, 1), half(v_cache, core, 1)], axis=1)
    first = jnp.where(core == 0, ours, theirs)
    second = jnp.where(core == 0, theirs, ours)
    both = jnp.concatenate([first, second], axis=0)
    width = both.shape[1] // 2
    kparts, vparts, numbers = ring_gather(both[:, :width], both[:, width:], chips, r)
    starts = numbers.astype(jnp.int32) * (2 * tok)

    q_near = lax.ppermute(half(q_pre, 1 - core, 1), "seq", sibling)
    weights = w_out.T
    w_near = lax.ppermute(half(weights, 1 - core, 1), "seq", sibling)

    def mine(x):
        y = lax.dynamic_slice_in_dim(x, chip * own, own, 0)
        return half(y, core, 2).reshape(own * steps, -1) if x.ndim == 3 else y

    mask = open_blocks(mine(block_table), steps, n * tok)
    attn_own = decode(mine(q_dec), mask, mine(k_new), mine(v_new), kparts, vparts, starts, steps)
    pieces, firsts = [attn_own], [chip]
    for d in range(1, chips):
        pieces.append(lax.ppermute(attn_own, "seq", ring_perm(chips, d)))
        firsts.append(ring_place(r - d, chips))

    groups = k_cache.shape[1] // HD // 2
    zero = jnp.zeros((), jnp.int32)
    base = core * groups
    meta = jnp.concatenate([jnp.stack([(place + 1 - 2 * core) * tok, zero, zero]), starts])
    out_near = prefill(q_near, kparts, vparts, meta, lengths, q_near.shape[1], "prefill_sibling")
    out_back = lax.ppermute(out_near, "seq", sibling)
    meta = jnp.concatenate([jnp.stack([place * tok, base, base]), starts])
    pre_out = prefill(q_pre, kparts, vparts, meta, lengths, q_pre.shape[1], "prefill_own")
    pre_out = lax.dynamic_update_slice(
        pre_out, out_back, (zero, (1 - core) * out_back.shape[1])
    )

    meta = jnp.stack([across] + [f.astype(jnp.int32) * (own * steps) for f in firsts])
    kept, *sent = project(pieces, half(weights, core, 1), w_near, meta)
    total = kept
    for block, (dc, dx) in zip(sent, ((1, 0), (0, 1), (1, 1))):
        perm = [
            (i * 2 + x, (i ^ dc) * 2 + (x ^ dx)) for i in range(n) for x in range(2)
        ]
        total = total + lax.ppermute(block, ("seq", "tp"), perm).astype(jnp.float32)
    dec_out = total.astype(jnp.bfloat16).reshape(rows // 2, steps, -1)
    return (pre_out, dec_out)


def per_device(n, tp, q_pre, k_cache, v_cache, prompt_lengths, *rest):
    groups = k_cache.shape[1] // HD
    form = split_heads if groups % 2 == 0 and tp == 2 else whole_heads
    return form(n, q_pre, k_cache, v_cache, prompt_lengths.astype(jnp.int32), *rest)


def solution(mesh):
    placed = (
        P("seq", "tp"),
        P("seq", "tp"),
        P("seq", "tp"),
        P(),
        P(None, None, "tp"),
        P(None, None, "tp"),
        P(None, None, "tp"),
        P(),
        P("tp", "seq"),
    )
    return jax.shard_map(
        functools.partial(per_device, mesh.shape["seq"], mesh.shape["tp"]),
        mesh=mesh,
        in_specs=placed,
        out_specs=(P("seq", "tp"), P("tp", None, "seq")),
        check_vma=False,
    )
```

```python
import functools
import math

import jax
import jax.numpy as jnp
from jax import lax
from jax.experimental import pallas as pl
from jax.experimental.pallas import tpu as pltpu
from jax.sharding import PartitionSpec as P

H = 56
KVH = 8
HD = 128
BLK = 64
SPAN = 512
PAIR = 2
NEG = -1e30
LEAST, MOST = 2.0**-60, 2.0**100
FACTOR = math.log2(math.e) / math.sqrt(HD)
ROOM = 32 * 1024 * 1024
HBM = pl.BlockSpec(memory_space=pltpu.HBM)
VMEM = pl.BlockSpec(memory_space=pltpu.VMEM)


def dot_nt(a, b):
    return lax.dot_general(a, b, (((1,), (1,)), ((), ())), preferred_element_type=jnp.float32)


def dot_nn(a, b):
    return lax.dot_general(a, b, (((1,), (0,)), ((), ())), preferred_element_type=jnp.float32)


def fold(x, op):
    out = x[:, :HD]
    for i in range(1, x.shape[1] // HD):
        out = op(out, x[:, i * HD : (i + 1) * HD])
    return out


def start_of(position, lengths):
    end = jnp.int32(0)
    out = jnp.zeros_like(position)
    for i in range(lengths.shape[0]):
        end = end + lengths[i]
        out = jnp.where(position >= end, end, out)
    return out


def sound(total):
    return (jnp.min(total) >= LEAST) & (jnp.max(total) <= MOST)


def prefill_kernel(tok, heads, meta, lengths, q, keys_all, values_all, *refs):
    out, qs, peak, total, acc = refs[-5:]
    for j in range(heads):
        qs[j * tok : (j + 1) * tok] = q[:, j * HD : (j + 1) * HD]
    total[...] = jnp.zeros_like(total)
    acc[...] = jnp.zeros_like(acc)

    begin = meta[0]
    finish = begin + tok
    low = start_of(begin, lengths)
    high = start_of(finish - 1, lengths)
    blocks = lax.div(finish - low + SPAN - 1, SPAN)
    clear = lax.div(finish - high, SPAN)

    def first_of(k):
        return jnp.maximum(finish - (k + 1) * SPAN, 0)

    def load(k):
        here = pl.ds(pl.multiple_of(first_of(k), HD), SPAN)
        return keys_all[:, here], values_all[here, :]

    def allowed_in(k):
        t = begin + lax.broadcasted_iota(jnp.int32, (tok, 1), 0)
        u = first_of(k) + lax.broadcasted_iota(jnp.int32, (tok, SPAN), 1)
        last = jnp.minimum(t, finish - k * SPAN - 1)
        return (u <= last) & (u >= start_of(t, lengths))

    def keep(allowed, x, other):
        some = x.shape[0] // tok
        return jnp.where(allowed[None], x.reshape(some, tok, SPAN), other).reshape(x.shape)

    def block(k, masked):
        keys, values = load(k)
        allowed = allowed_in(k) if masked else None
        for j in range(0, heads, PAIR):
            here = slice(j * tok, min(j + PAIR, heads) * tok)
            p = jnp.exp2(dot_nn(qs[here], keys) * FACTOR)
            if masked:
                p = keep(allowed, p, 0.0)
            total[here] += fold(p, jnp.add)
            acc[here] += dot_nn(p.astype(jnp.bfloat16), values)

    block(0, True)

    @pl.loop(1, jnp.maximum(clear, 1))
    def _(k):
        block(k, False)

    @pl.loop(jnp.maximum(clear, 1), blocks)
    def _(k):
        block(k, True)

    def write():
        whole = jnp.sum(total[...], axis=1, keepdims=True)
        result = (acc[...] / whole).astype(out.dtype)
        for j in range(heads):
            out[:, j * HD : (j + 1) * HD] = result[j * tok : (j + 1) * tok]
        return whole

    fine = sound(write())

    @pl.when(jnp.logical_not(fine))
    def _():
        peak[...] = jnp.full_like(peak, NEG)
        total[...] = jnp.zeros_like(total)
        acc[...] = jnp.zeros_like(acc)

        @pl.loop(0, blocks)
        def _(k):
            keys, values = load(k)
            allowed = allowed_in(k)

            @pl.loop(0, heads)
            def _(j):
                here = pl.ds(pl.multiple_of(j * tok, tok), tok)
                s = jnp.where(allowed, dot_nn(qs[here], keys) * FACTOR, NEG)
                top = jnp.maximum(peak[here], jnp.max(s, axis=1, keepdims=True))
                p = jnp.where(allowed, jnp.exp2(s - top[:, :1]), 0.0)
                shrink = jnp.exp2(peak[here] - top)
                total[here] = total[here] * shrink + fold(p, jnp.add)
                acc[here] = acc[here] * shrink + dot_nn(p.astype(jnp.bfloat16), values)
                peak[here] = top

        write()


def prefill(q, keys, values, meta, lengths, groups, columns, name, before=None):
    tok = q.shape[0]
    count = values.shape[0]
    heads = H // KVH
    rows = heads * tok
    pairs = rows * count // 2 * groups
    extra = [] if before is None else [before]
    return pl.pallas_call(
        functools.partial(prefill_kernel, tok, heads),
        out_shape=jax.ShapeDtypeStruct((tok, columns), jnp.bfloat16),
        grid_spec=pltpu.PrefetchScalarGridSpec(
            num_scalar_prefetch=2,
            grid=(groups,),
            in_specs=[
                pl.BlockSpec((tok, heads * HD), lambda g, meta, lengths: (0, meta[1] + g)),
                pl.BlockSpec((HD, count), lambda g, meta, lengths: (meta[2] + g, 0)),
                pl.BlockSpec((count, HD), lambda g, meta, lengths: (0, meta[2] + g)),
            ]
            + [HBM] * len(extra),
            out_specs=pl.BlockSpec((tok, heads * HD), lambda g, meta, lengths: (0, meta[3] + g)),
            scratch_shapes=[
                pltpu.VMEM((rows, HD), jnp.bfloat16),
                pltpu.VMEM((rows, HD), jnp.float32),
                pltpu.VMEM((rows, HD), jnp.float32),
                pltpu.VMEM((rows, HD), jnp.float32),
            ],
        ),
        compiler_params=pltpu.CompilerParams(vmem_limit_bytes=ROOM),
        cost_estimate=pl.CostEstimate(
            flops=pairs * HD * 8, bytes_accessed=count * HD * 4 * groups, transcendentals=pairs
        ),
        input_output_aliases={} if before is None else {5: 0},
        name=name,
    )(meta, lengths, q, keys, values, *extra)


def settle_kernel(meta, piece, whole, out, sem):
    width = piece.shape[1]
    where = pl.ds(pl.multiple_of(meta[0] * width, width), width)
    copy = pltpu.make_async_copy(piece, out.at[:, where], sem)
    copy.start()
    copy.wait()


def settle(whole, piece, number):
    return pl.pallas_call(
        settle_kernel,
        out_shape=jax.ShapeDtypeStruct(whole.shape, whole.dtype),
        grid_spec=pltpu.PrefetchScalarGridSpec(
            num_scalar_prefetch=1,
            grid=(),
            in_specs=[pl.BlockSpec(memory_space=pl.ANY), HBM],
            out_specs=HBM,
            scratch_shapes=[pltpu.SemaphoreType.DMA],
        ),
        input_output_aliases={2: 0},
        name="settle",
    )(number[None], piece, whole)


def decode_kernel(parts, steps, heads, groups, starts, q, mask, newk, newv, *refs):
    kheld, vheld = refs[:parts], refs[parts : 2 * parts]
    out, kall, vall, sems, scores = refs[2 * parts :]
    own = q.shape[0]
    rows = heads * own
    length = kheld[0].shape[1]
    copies = []
    for i in range(parts):
        where = pl.ds(pl.multiple_of(starts[i], HD), length)
        copies.append(pltpu.make_async_copy(kheld[i], kall.at[:, where], sems.at[2 * i]))
        copies.append(pltpu.make_async_copy(vheld[i], vall.at[where], sems.at[2 * i + 1]))
    for copy in copies:
        copy.start()
    row = lax.broadcasted_iota(jnp.int32, (own, own), 0)
    col = lax.broadcasted_iota(jnp.int32, (own, own), 1)
    fresh_ok = (lax.div(row, steps) == lax.div(col, steps)) & (col <= row)

    def columns(g):
        return slice(g * HD, (g + 1) * HD)

    def stacked(g):
        first = g * heads
        slices = [q[:, (first + j) * HD : (first + j + 1) * HD] for j in range(heads)]
        return jnp.concatenate([x.astype(jnp.float32) for x in slices], 0).astype(jnp.bfloat16)

    def keep(allowed, x, other):
        y = x.reshape(heads, own, x.shape[1])
        return jnp.where(allowed[None], y, other).reshape(x.shape)

    def open_to(i):
        return mask[:, pl.ds(pl.multiple_of(starts[i], HD), length)] > 0

    def write(g, acc, whole):
        result = acc / whole
        for j in range(heads):
            out[:, (g * heads + j) * HD : (g * heads + j + 1) * HD] = result[
                j * own : (j + 1) * own
            ].astype(out.dtype)

    fine = None
    for g in range(groups):
        query = stacked(g)
        p = keep(fresh_ok, jnp.exp2(dot_nt(query, newk[:, columns(g)]) * FACTOR), 0.0)
        whole = jnp.sum(p, axis=1, keepdims=True)
        acc = dot_nn(p.astype(jnp.bfloat16), newv[:, columns(g)])
        total = jnp.zeros((rows, HD), jnp.float32)
        for i in range(parts):
            p = jnp.exp2(dot_nn(query, kheld[i][columns(g)]) * FACTOR)
            p = keep(open_to(i), p, 0.0)
            total = total + fold(p, jnp.add)
            acc = acc + dot_nn(p.astype(jnp.bfloat16), vheld[i][:, columns(g)])
        whole = whole + jnp.sum(total, axis=1, keepdims=True)
        write(g, acc, whole)
        fine = sound(whole) if fine is None else fine & sound(whole)

    @pl.when(jnp.logical_not(fine))
    def _():
        for g in range(groups):
            query = stacked(g)
            fresh = keep(fresh_ok, dot_nt(query, newk[:, columns(g)]) * FACTOR, NEG)
            top = jnp.max(fresh, axis=1, keepdims=True)
            for i in range(parts):
                s = keep(open_to(i), dot_nn(query, kheld[i][columns(g)]) * FACTOR, NEG)
                scores[:, i * length : (i + 1) * length] = s
                top = jnp.maximum(top, jnp.max(s, axis=1, keepdims=True))
            p = jnp.exp2(fresh - top)
            whole = jnp.sum(p, axis=1, keepdims=True)
            acc = dot_nn(p.astype(jnp.bfloat16), newv[:, columns(g)])
            for i in range(parts):
                p = jnp.exp2(scores[:, i * length : (i + 1) * length] - top)
                whole = whole + jnp.sum(p, axis=1, keepdims=True)
                acc = acc + dot_nn(p.astype(jnp.bfloat16), vheld[i][:, columns(g)])
            write(g, acc, whole)

    for copy in copies:
        copy.wait()


def decode(q, mask, newk, newv, kparts, vparts, starts, steps):
    own = q.shape[0]
    parts = len(kparts)
    length, width = vparts[0].shape
    count = parts * length
    heads = H // KVH
    groups = width // HD
    rows = heads * own
    pairs = groups * rows * count
    return pl.pallas_call(
        functools.partial(decode_kernel, parts, steps, heads, groups),
        out_shape=[
            jax.ShapeDtypeStruct(q.shape, jnp.bfloat16),
            jax.ShapeDtypeStruct((width, count), jnp.bfloat16),
            jax.ShapeDtypeStruct((count, width), jnp.bfloat16),
        ],
        grid_spec=pltpu.PrefetchScalarGridSpec(
            num_scalar_prefetch=1,
            grid=(),
            in_specs=[VMEM] * (4 + 2 * parts),
            out_specs=[VMEM, HBM, HBM],
            scratch_shapes=[
                pltpu.SemaphoreType.DMA((2 * parts,)),
                pltpu.VMEM((rows, count), jnp.float32),
            ],
        ),
        compiler_params=pltpu.CompilerParams(vmem_limit_bytes=ROOM),
        cost_estimate=pl.CostEstimate(
            flops=pairs * HD * 4, bytes_accessed=count * width * 4, transcendentals=pairs
        ),
        name="decode",
    )(starts, q, mask, newk, newv, *kparts, *vparts)


def prepare_kernel(meta, k, v, send, own_k, own_v):
    width = own_k.shape[0]
    mine = pl.ds(pl.multiple_of(meta[0] * width, width), width)
    other = pl.ds(pl.multiple_of((1 - meta[0]) * width, width), width)
    send[:width] = k[:, other].astype(jnp.float32).T.astype(send.dtype)
    send[width:] = v[:, other]
    own_k[...] = k[:, mine].astype(jnp.float32).T.astype(own_k.dtype)
    own_v[...] = v[:, mine]


def prepare(k, v, core):
    tok, width = k.shape[0], k.shape[1] // 2
    assert tok == width
    block = jax.ShapeDtypeStruct((tok, width), k.dtype)
    return pl.pallas_call(
        prepare_kernel,
        out_shape=[jax.ShapeDtypeStruct((2 * tok, width), k.dtype), block, block],
        grid_spec=pltpu.PrefetchScalarGridSpec(
            num_scalar_prefetch=1, grid=(), in_specs=[VMEM] * 2, out_specs=[VMEM] * 3
        ),
        name="prepare",
    )(core[None], k, v)


def join_kernel(meta, own_k, own_v, theirs, keys, values):
    tok = own_v.shape[0]
    mine = pl.ds(pl.multiple_of(meta[0] * tok, tok), tok)
    other = pl.ds(pl.multiple_of((1 - meta[0]) * tok, tok), tok)
    keys[:, mine] = own_k[...]
    keys[:, other] = theirs[: own_k.shape[0]]
    values[mine] = own_v[...]
    values[other] = theirs[own_k.shape[0] :]


def join(own_k, own_v, theirs, core):
    tok, width = own_v.shape
    return pl.pallas_call(
        join_kernel,
        out_shape=[
            jax.ShapeDtypeStruct((width, 2 * tok), own_k.dtype),
            jax.ShapeDtypeStruct((2 * tok, width), own_k.dtype),
        ],
        grid_spec=pltpu.PrefetchScalarGridSpec(
            num_scalar_prefetch=1, grid=(), in_specs=[VMEM] * 3, out_specs=[VMEM] * 2
        ),
        name="join",
    )(core[None], own_k, own_v, theirs)


def project_kernel(parts, meta, first, second, mine, other, *refs):
    kept, beside, across, corner, near, far = refs
    rows = 2 * first.shape[0] // parts
    whole = jnp.concatenate([first[...], second[...]], axis=0)
    for weights, result in ((mine, near), (other, far)):
        flat = dot_nt(whole, weights[...])
        for i in range(parts):
            where = pl.ds(pl.multiple_of(meta[1 + i], rows), rows)
            result[where] = flat[i * rows : (i + 1) * rows]
    half = kept.shape[0]
    here = pl.ds(pl.multiple_of(meta[0] * half, half), half)
    there = pl.ds(pl.multiple_of((1 - meta[0]) * half, half), half)
    kept[...] = near[here]
    beside[...] = far[here].astype(beside.dtype)
    across[...] = near[there].astype(across.dtype)
    corner[...] = far[there].astype(corner.dtype)


def project(first, second, mine, other, meta):
    rows = 2 * first.shape[0]
    width = mine.shape[0]
    block = jax.ShapeDtypeStruct((rows // 2, width), jnp.bfloat16)
    return pl.pallas_call(
        functools.partial(project_kernel, meta.shape[0] - 1),
        out_shape=[jax.ShapeDtypeStruct((rows // 2, width), jnp.float32)] + [block] * 3,
        grid_spec=pltpu.PrefetchScalarGridSpec(
            num_scalar_prefetch=1,
            grid=(),
            in_specs=[VMEM] * 4,
            out_specs=[VMEM] * 4,
            scratch_shapes=[pltpu.VMEM((rows, width), jnp.float32)] * 2,
        ),
        compiler_params=pltpu.CompilerParams(vmem_limit_bytes=ROOM),
        cost_estimate=pl.CostEstimate(
            flops=rows * width * mine.shape[1] * 4,
            bytes_accessed=width * mine.shape[1] * 4,
            transcendentals=0,
        ),
        name="project",
    )(meta, first, second, mine, other)


def index(z, y, c):
    return (z * 2 + y) * 2 + c


def on_ring(r, chips):
    return (r, 0) if r < chips // 2 else (chips - 1 - r, 1)


def ring_perm(chips, d):
    return [
        (index(*on_ring(r, chips), c), index(*on_ring((r + d) % chips, chips), c))
        for r in range(chips)
        for c in range(2)
    ]


def ring_place(r, chips):
    r = lax.rem(r + 2 * chips, chips)
    return jnp.where(r < chips // 2, r * 2, (chips - 1 - r) * 2 + 1)


def ring_gather(k, v, chips, r, early):
    half = chips // 2
    up, down = ring_perm(chips, 1), ring_perm(chips, -1)
    keys, values = {0: k}, {0: v}
    for d in range(1, half + 1):
        if d == half - 1:
            values[d - 1], early = lax.optimization_barrier((values[d - 1], early))
        keys[-d] = lax.ppermute(keys[1 - d], "seq", up)
        values[d] = lax.ppermute(values[d - 1], "seq", down)
        if d < half:
            keys[d] = lax.ppermute(keys[d - 1], "seq", down)
            values[-d] = lax.ppermute(values[1 - d], "seq", up)
    keys[half] = keys[-half]
    order = [0] + [o for d in range(1, half) for o in (-d, d)] + [half]
    numbers = jnp.stack([ring_place(r + o, chips) for o in order])
    return [keys[o] for o in order], [values[o] for o in order], numbers, early


def spread(x, n):
    place = lax.axis_index("seq")
    deep = n // 4
    everyone = [(z, y, c) for z in range(deep) for y in range(2) for c in range(2)]
    z, y, c = place // 4, (place // 2) % 2, place % 2
    held = [(x, z, y, c)]
    for d in range(1, deep):
        perm = [(index(*p), index((p[0] - d) % deep, p[1], p[2])) for p in everyone]
        held.append((lax.ppermute(x, "seq", perm), lax.rem(z + d, deep), y, c))
    perm = [(index(*p), index(p[0], 1 - p[1], p[2])) for p in everyone]
    held += [(lax.ppermute(b, "seq", perm), bz, 1 - by, bc) for b, bz, by, bc in held]
    perm = [(index(*p), index(p[0], p[1], 1 - p[2])) for p in everyone]
    held += [(lax.ppermute(b, "seq", perm), bz, by, 1 - bc) for b, bz, by, bc in held]
    return [b for b, *_ in held], jnp.stack([index(bz, by, bc) for _, bz, by, bc in held])


def open_blocks(table, steps, count):
    number = lax.broadcasted_iota(jnp.int32, (*table.shape, count), 2) // BLK
    mask = jnp.any(table[:, :, None] == number, axis=1).astype(jnp.float32)
    return jnp.repeat(mask, steps, axis=0)


def whole_heads(n, q_pre, k_cache, v_cache, lengths, q_dec, k_new, v_new, block_table, w_out):
    tok = q_pre.shape[0]
    place = lax.axis_index("seq").astype(jnp.int32)
    rows, steps = q_dec.shape[0], q_dec.shape[1]
    own = rows // n
    kparts, sources = spread(k_cache.T, n)
    vparts, _ = spread(v_cache, n)
    starts = sources.astype(jnp.int32) * tok

    def mine(x):
        y = lax.dynamic_slice_in_dim(x, place * own, own, 0)
        return y.reshape(own * steps, -1) if x.ndim == 3 else y

    mask = open_blocks(mine(block_table), steps, n * tok)
    attn_own, keys, values = decode(
        mine(q_dec), mask, mine(k_new), mine(v_new), kparts, vparts, starts, steps
    )
    attn = lax.all_gather(attn_own, "seq", axis=0, tiled=True)
    flat = jnp.dot(attn, w_out, preferred_element_type=jnp.float32).astype(jnp.bfloat16)
    dec_out = lax.psum_scatter(
        flat.reshape(rows, steps, -1), "tp", scatter_dimension=0, tiled=True
    )
    zero = jnp.zeros((), jnp.int32)
    meta = jnp.stack([place * tok, zero, zero, zero])
    groups = k_cache.shape[1] // HD
    pre_out = prefill(
        q_pre, keys, values, meta, lengths, groups, q_pre.shape[1], "prefill"
    )
    return (pre_out, dec_out)


def split_heads(n, q_pre, k_cache, v_cache, lengths, q_dec, k_new, v_new, block_table, w_out):
    tok = q_pre.shape[0]
    place = lax.axis_index("seq").astype(jnp.int32)
    across = lax.axis_index("tp").astype(jnp.int32)
    core = lax.rem(place, 2)
    chip = lax.div(place, 2)
    chips = n // 2
    deep = chips // 2
    z, y = lax.div(chip, 2), lax.rem(chip, 2)
    r = jnp.where(y == 0, z, chips - 1 - z)
    rows, steps = q_dec.shape[0], q_dec.shape[1]
    own = rows // chips
    sibling = [(i, i ^ 1) for i in range(n)]

    def half(x, which, axis):
        size = x.shape[axis] // 2
        return lax.dynamic_slice_in_dim(x, which * size, size, axis)

    def mine(x):
        y = lax.dynamic_slice_in_dim(x, chip * own, own, 0)
        return half(y, core, 2).reshape(own * steps, -1) if x.ndim == 3 else y

    send, own_k, own_v = prepare(k_cache, v_cache, core)
    theirs = lax.ppermute(send, "seq", sibling)
    keys, values = join(own_k, own_v, theirs, core)
    keys, values, q_pre, w_out, q_dec, k_new, v_new, block_table = lax.optimization_barrier(
        (keys, values, q_pre, w_out, q_dec, k_new, v_new, block_table)
    )
    q_near = lax.ppermute(half(q_pre, 1 - core, 1), "seq", sibling)
    weights = w_out.T
    w_near = lax.ppermute(half(weights, 1 - core, 1), "seq", sibling)
    early = (
        mine(q_dec),
        open_blocks(mine(block_table), steps, n * tok),
        mine(k_new),
        mine(v_new),
        half(weights, core, 1),
    )
    kparts, vparts, numbers, early = ring_gather(keys, values, chips, r, early)
    *fresh, w_mine = early
    starts = numbers.astype(jnp.int32) * (2 * tok)
    attn_own, keys, values = decode(*fresh, kparts, vparts, starts, steps)

    everyone = [(a, b, c) for a in range(deep) for b in range(2) for c in range(2)]
    pieces, levels = [attn_own], [z]
    for d in range(1, deep):
        perm = [(index(*p), index((p[0] + d) % deep, p[1], p[2])) for p in everyone]
        pieces.append(lax.ppermute(attn_own, "seq", perm))
        levels.append(lax.rem(z + deep - d, deep))
    first = jnp.concatenate(pieces, axis=0)
    perm = [(index(*p), index(p[0], 1 - p[1], p[2])) for p in everyone]
    second = lax.ppermute(first, "seq", perm)
    firsts = [level * 2 + y for level in levels] + [level * 2 + 1 - y for level in levels]

    groups = k_cache.shape[1] // HD // 2
    width = q_near.shape[1] // groups
    zero = jnp.zeros((), jnp.int32)
    back = []
    for g in range(groups):
        one = jnp.int32(g)
        meta = jnp.stack([(place + 1 - 2 * core) * tok, one, one, zero])
        near = prefill(q_near, keys, values, meta, lengths, 1, width, f"prefill_sibling{g}")
        back.append(lax.ppermute(near, "seq", sibling))
    pre_out = None
    for g in range(groups):
        one = jnp.int32(g)
        meta = jnp.stack([place * tok, core * groups + g, one, core * groups + g])
        if g == groups - 1:
            for i, piece in enumerate(back):
                pre_out = settle(pre_out, piece, (1 - core) * groups + i)
        pre_out = prefill(
            q_pre, keys, values, meta, lengths, 1, q_pre.shape[1], f"prefill_own{g}", pre_out
        )

    meta = jnp.stack([across] + [f.astype(jnp.int32) * (own * steps) for f in firsts])
    kept, *sent = project(first, second, w_mine, w_near, meta)
    total = kept
    for block, (dc, dx) in zip(sent, ((1, 0), (0, 1), (1, 1))):
        perm = [
            (i * 2 + x, (i ^ dc) * 2 + (x ^ dx)) for i in range(n) for x in range(2)
        ]
        total = total + lax.ppermute(block, ("seq", "tp"), perm).astype(jnp.float32)
    dec_out = total.astype(jnp.bfloat16).reshape(rows // 2, steps, -1)
    return (pre_out, dec_out)


def per_device(n, tp, q_pre, k_cache, v_cache, prompt_lengths, *rest):
    groups = k_cache.shape[1] // HD
    even = groups % 2 == 0 and groups > 2 and tp == 2
    form = split_heads if even and k_cache.shape[1] == 2 * k_cache.shape[0] else whole_heads
    return form(n, q_pre, k_cache, v_cache, prompt_lengths.astype(jnp.int32), *rest)


def solution(mesh):
    placed = (
        P("seq", "tp"),
        P("seq", "tp"),
        P("seq", "tp"),
        P(),
        P(None, None, "tp"),
        P(None, None, "tp"),
        P(None, None, "tp"),
        P(),
        P("tp", "seq"),
    )
    return jax.shard_map(
        functools.partial(per_device, mesh.shape["seq"], mesh.shape["tp"]),
        mesh=mesh,
        in_specs=placed,
        out_specs=(P("seq", "tp"), P("tp", None, "seq")),
        check_vma=False,
    )
```

```python
import functools
import math

import jax
import jax.numpy as jnp
from jax import lax
from jax.experimental import pallas as pl
from jax.experimental.pallas import tpu as pltpu
from jax.sharding import PartitionSpec as P

H = 56
KVH = 8
HD = 128
BLK = 64
SPAN = 512
PAIR = 2
NEG = -1e30
LEAST, MOST = 2.0**-60, 2.0**100
FACTOR = math.log2(math.e) / math.sqrt(HD)
ROOM = 16 * 1024 * 1024
CORE, CHIP, ACROSS, PARTS = range(4)
HBM = pl.BlockSpec(memory_space=pltpu.HBM)
VMEM = pl.BlockSpec(memory_space=pltpu.VMEM)
SMEM = pl.BlockSpec(memory_space=pltpu.SMEM)


def dot_nt(a, b):
    return lax.dot_general(a, b, (((1,), (1,)), ((), ())), preferred_element_type=jnp.float32)


def dot_nn(a, b):
    return lax.dot_general(a, b, (((1,), (0,)), ((), ())), preferred_element_type=jnp.float32)


def fold(x, op):
    out = x[:, :HD]
    for i in range(1, x.shape[1] // HD):
        out = op(out, x[:, i * HD : (i + 1) * HD])
    return out


def start_of(position, lengths):
    end = jnp.int32(0)
    out = jnp.zeros_like(position)
    for i in range(lengths.shape[0]):
        end = end + lengths[i]
        out = jnp.where(position >= end, end, out)
    return out


def sound(total):
    return (jnp.min(total) >= LEAST) & (jnp.max(total) <= MOST)


def prefill_kernel(tok, heads, meta, lengths, q, keys_all, values_all, *refs):
    out, qs, peak, total, acc = refs[-5:]
    for j in range(heads):
        qs[j * tok : (j + 1) * tok] = q[:, j * HD : (j + 1) * HD]
    total[...] = jnp.zeros_like(total)
    acc[...] = jnp.zeros_like(acc)

    begin = meta[0]
    finish = begin + tok
    low = start_of(begin, lengths)
    high = start_of(finish - 1, lengths)
    blocks = lax.div(finish - low + SPAN - 1, SPAN)
    clear = lax.div(finish - high, SPAN)

    def first_of(k):
        return jnp.maximum(finish - (k + 1) * SPAN, 0)

    def load(k):
        here = pl.ds(pl.multiple_of(first_of(k), HD), SPAN)
        return keys_all[:, here], values_all[here, :]

    def allowed_in(k):
        t = begin + lax.broadcasted_iota(jnp.int32, (tok, 1), 0)
        u = first_of(k) + lax.broadcasted_iota(jnp.int32, (tok, SPAN), 1)
        last = jnp.minimum(t, finish - k * SPAN - 1)
        return (u <= last) & (u >= start_of(t, lengths))

    def keep(allowed, x, other):
        some = x.shape[0] // tok
        return jnp.where(allowed[None], x.reshape(some, tok, SPAN), other).reshape(x.shape)

    def block(k, masked):
        keys, values = load(k)
        allowed = allowed_in(k) if masked else None
        for j in range(0, heads, PAIR):
            here = slice(j * tok, min(j + PAIR, heads) * tok)
            p = jnp.exp2(dot_nn(qs[here], keys) * FACTOR)
            if masked:
                p = keep(allowed, p, 0.0)
            total[here] += fold(p, jnp.add)
            acc[here] += dot_nn(p.astype(jnp.bfloat16), values)

    block(0, True)

    @pl.loop(1, jnp.maximum(clear, 1))
    def _(k):
        block(k, False)

    @pl.loop(jnp.maximum(clear, 1), blocks)
    def _(k):
        block(k, True)

    def write():
        whole = jnp.sum(total[...], axis=1, keepdims=True)
        result = (acc[...] / whole).astype(out.dtype)
        for j in range(heads):
            out[:, j * HD : (j + 1) * HD] = result[j * tok : (j + 1) * tok]
        return whole

    fine = sound(write())

    @pl.when(jnp.logical_not(fine))
    def _():
        peak[...] = jnp.full_like(peak, NEG)
        total[...] = jnp.zeros_like(total)
        acc[...] = jnp.zeros_like(acc)

        @pl.loop(0, blocks)
        def _(k):
            keys, values = load(k)
            allowed = allowed_in(k)

            @pl.loop(0, heads)
            def _(j):
                here = pl.ds(pl.multiple_of(j * tok, tok), tok)
                s = jnp.where(allowed, dot_nn(qs[here], keys) * FACTOR, NEG)
                top = jnp.maximum(peak[here], jnp.max(s, axis=1, keepdims=True))
                p = jnp.where(allowed, jnp.exp2(s - top[:, :1]), 0.0)
                shrink = jnp.exp2(peak[here] - top)
                total[here] = total[here] * shrink + fold(p, jnp.add)
                acc[here] = acc[here] * shrink + dot_nn(p.astype(jnp.bfloat16), values)
                peak[here] = top

        write()


def prefill(q, keys, values, meta, lengths, groups, columns, name, before=None):
    tok = q.shape[0]
    count = values.shape[0]
    heads = H // KVH
    rows = heads * tok
    pairs = rows * count // 2 * groups
    extra = [] if before is None else [before]
    return pl.pallas_call(
        functools.partial(prefill_kernel, tok, heads),
        out_shape=jax.ShapeDtypeStruct((tok, columns), jnp.bfloat16),
        grid_spec=pltpu.PrefetchScalarGridSpec(
            num_scalar_prefetch=2,
            grid=(groups,),
            in_specs=[
                pl.BlockSpec((tok, heads * HD), lambda g, meta, lengths: (0, meta[1] + g)),
                pl.BlockSpec((HD, count), lambda g, meta, lengths: (meta[2] + g, 0)),
                pl.BlockSpec((count, HD), lambda g, meta, lengths: (0, meta[2] + g)),
            ]
            + [HBM] * len(extra),
            out_specs=pl.BlockSpec((tok, heads * HD), lambda g, meta, lengths: (0, meta[3] + g)),
            scratch_shapes=[
                pltpu.VMEM((rows, HD), jnp.bfloat16),
                pltpu.VMEM((rows, HD), jnp.float32),
                pltpu.VMEM((rows, HD), jnp.float32),
                pltpu.VMEM((rows, HD), jnp.float32),
            ],
        ),
        compiler_params=pltpu.CompilerParams(vmem_limit_bytes=ROOM),
        cost_estimate=pl.CostEstimate(
            flops=pairs * HD * 8, bytes_accessed=count * HD * 4 * groups, transcendentals=pairs
        ),
        input_output_aliases={} if before is None else {5: 0},
        name=name,
    )(meta, lengths, q, keys, values, *extra)


def settle_kernel(meta, piece, whole, out, sem):
    width = piece.shape[1]
    where = pl.ds(pl.multiple_of((1 - meta[CORE]) * width, width), width)
    copy = pltpu.make_async_copy(piece, out.at[:, where], sem)
    copy.start()
    copy.wait()


def settle(whole, piece, meta):
    return pl.pallas_call(
        settle_kernel,
        out_shape=jax.ShapeDtypeStruct(whole.shape, whole.dtype),
        in_specs=[SMEM, VMEM, HBM],
        out_specs=HBM,
        scratch_shapes=[pltpu.SemaphoreType.DMA],
        input_output_aliases={2: 0},
        name="settle",
    )(meta, piece, whole)


def allowed_at(first, base, tok, length, lengths):
    t = first + lax.broadcasted_iota(jnp.int32, (tok, 1), 0)
    u = base + lax.broadcasted_iota(jnp.int32, (tok, length), 1)
    return (u <= t) & (u >= start_of(t, lengths))


def add_block(tok, heads, q_at, keys, values, allowed, old, new):
    length = keys.shape[1]
    for j in range(0, heads, PAIR):
        some = min(PAIR, heads - j)
        p = jnp.exp2(dot_nn(q_at(j * tok, some * tok), keys) * FACTOR)
        if allowed is not None:
            p = p.reshape(some, tok, length)
            p = jnp.where(allowed[None], p, 0.0).reshape(some * tok, length)
        more = (fold(p, jnp.add), dot_nn(p.astype(jnp.bfloat16), values))
        new(j * tok, some * tok, more if old is None else
            [x + y for x, y in zip(old(j * tok, some * tok), more)])


def rows_at(refs, g, first):
    def get(at, count):
        return [ref[g, pl.ds(pl.multiple_of(first + at, HD), count)] for ref in refs]

    def put(at, count, values):
        for ref, value in zip(refs, values):
            ref[g, pl.ds(pl.multiple_of(first + at, HD), count)] = value

    return get, put


def group_columns(g):
    return pl.ds(pl.multiple_of(g * HD, HD), HD)


def relation(meta, part, side, tok, lengths):
    first = (meta[CHIP] * 2 + side) * tok
    base = meta[PARTS + part] * 2 * tok
    finish = base + 2 * tok
    relevant = (base < first) & (meta[PARTS + part] != meta[CHIP])
    relevant = relevant & (finish > start_of(first, lengths))
    return relevant, base >= start_of(first + tok - 1, lengths), first, base


def open_kernel(tok, heads, groups, meta, lengths, q, q_near, keys, values, qs, total, acc, q_own, sem):
    core = meta[CORE]
    width = q_near.shape[1]
    rows = heads * tok
    where = pl.ds(pl.multiple_of(core * width, width), width)
    copy = pltpu.make_async_copy(q.at[:, where], q_own, sem)
    copy.start()
    copy.wait()
    for source, side in ((q_own, core), (q_near, 1 - core)):
        for g in range(groups):
            for j in range(heads):
                at = pl.ds(pl.multiple_of(side * rows + j * tok, HD), tok)
                first = (g * heads + j) * HD
                qs[g, at] = source[:, first : first + HD]

    @pl.loop(0, groups)
    def _(g):
        for side in range(2):
            length = (side + 1) * tok
            first = (meta[CHIP] * 2 + side) * tok
            allowed = allowed_at(first, meta[CHIP] * 2 * tok, tok, length, lengths)
            get, put = rows_at((total, acc), g, side * rows)
            q_at = lambda at, count: qs[g, pl.ds(side * rows + at, count)]
            add_block(tok, heads, q_at, keys[group_columns(g), :length],
                      values[:length, group_columns(g)], allowed, None, put)


def open_sums(q, q_near, keys, values, meta, lengths):
    tok = q.shape[0]
    heads = H // KVH
    groups = values.shape[1] // HD
    rows = 2 * heads * tok
    sums = jax.ShapeDtypeStruct((groups, rows, HD), jnp.float32)
    pairs = groups * rows * tok * 2
    return pl.pallas_call(
        functools.partial(open_kernel, tok, heads, groups),
        out_shape=[jax.ShapeDtypeStruct((groups, rows, HD), jnp.bfloat16), sums, sums],
        in_specs=[SMEM, SMEM, HBM, VMEM, VMEM, VMEM],
        out_specs=[VMEM] * 3,
        scratch_shapes=[pltpu.VMEM(q_near.shape, q_near.dtype), pltpu.SemaphoreType.DMA],
        compiler_params=pltpu.CompilerParams(vmem_limit_bytes=ROOM),
        cost_estimate=pl.CostEstimate(
            flops=pairs * HD * 8, bytes_accessed=q.size * 2, transcendentals=pairs
        ),
        name="open",
    )(meta, lengths, q, q_near, keys, values)


def stage_kernel(tok, heads, groups, parts, meta, lengths, qs, total, acc, *refs):
    keys, values = refs[:2], refs[2:4]
    new_total, new_acc = refs[4:]
    rows = heads * tok

    @pl.loop(0, 2 * groups)
    def _(step):
        g, side = lax.div(step, 2), lax.rem(step, 2)
        at = side * rows
        old_get, _ = rows_at((total, acc), g, at)
        new_get, new_put = rows_at((new_total, new_acc), g, at)
        q_at = lambda off, count: qs[g, pl.ds(pl.multiple_of(at + off, HD), count)]
        one, two = [relation(meta, part, side, tok, lengths) for part in parts]

        def add(i, about, old):
            relevant, clear, first, base = about
            k, v = keys[i][group_columns(g), :], values[i][:, group_columns(g)]

            @pl.when(clear)
            def _():
                add_block(tok, heads, q_at, k, v, None, old, new_put)

            @pl.when(jnp.logical_not(clear))
            def _():
                allowed = allowed_at(first, base, tok, k.shape[1], lengths)
                add_block(tok, heads, q_at, k, v, allowed, old, new_put)

        @pl.when(one[0])
        def _():
            add(0, one, old_get)

        @pl.when(jnp.logical_not(one[0]))
        def _():
            @pl.loop(0, heads)
            def _(j):
                new_put(j * tok, tok, old_get(j * tok, tok))

        @pl.when(two[0])
        def _():
            add(1, two, new_get)


def stage(state, keys, values, parts, meta, lengths):
    qs, total, acc = state
    groups, rows, unused = qs.shape
    tok = values[0].shape[0] // 2
    pairs = groups * rows * tok * 2
    new = pl.pallas_call(
        functools.partial(stage_kernel, tok, rows // (2 * tok), groups, parts),
        out_shape=[jax.ShapeDtypeStruct(x.shape, x.dtype) for x in (total, acc)],
        in_specs=[SMEM, SMEM] + [VMEM] * 7,
        out_specs=[VMEM] * 2,
        input_output_aliases={3: 0, 4: 1},
        compiler_params=pltpu.CompilerParams(vmem_limit_bytes=ROOM),
        cost_estimate=pl.CostEstimate(
            flops=pairs * HD * 8, bytes_accessed=tok * HD, transcendentals=pairs
        ),
        name=f"stage{parts[0]}",
    )(meta, lengths, qs, total, acc, *keys, *values)
    return qs, *new


def close_kernel(tok, heads, groups, near, meta, lengths, qs, total, acc, *refs):
    parts = (len(refs) - (4 if near else 6)) // 2
    keys, values = refs[:parts], refs[parts : 2 * parts]
    out, peak, total_now, acc_now = refs[2 * parts : 2 * parts + 4]
    rows = heads * tok
    core = meta[CORE]
    side = 1 - core if near else core
    at = side * rows
    result = out if near else refs[-2]
    first = (meta[CHIP] * 2 + side) * tok
    relevant, clear, _, base = relation(meta, parts - 1, side, tok, lengths)

    def write(g):
        whole = jnp.sum(total_now[g], axis=1, keepdims=True)
        value = (acc_now[g] / whole).astype(result.dtype)
        for j in range(heads):
            col = (g * heads + j) * HD
            result[:, col : col + HD] = value[j * tok : (j + 1) * tok]
        return sound(whole)

    fine = None
    for g in range(groups):
        old_get, _ = rows_at((total, acc), g, at)
        _, new_put = rows_at((total_now, acc_now), g, 0)
        q_at = lambda off, count: qs[g, pl.ds(pl.multiple_of(at + off, HD), count)]

        @pl.when(relevant)
        def _():
            k, v = keys[-1][group_columns(g), :], values[-1][:, group_columns(g)]
            allowed = allowed_at(first, base, tok, k.shape[1], lengths)
            add_block(tok, heads, q_at, k, v, allowed, old_get, new_put)

        @pl.when(jnp.logical_not(relevant))
        def _():
            new_put(0, rows, old_get(0, rows))

        good = write(g)
        fine = good if fine is None else fine & good

    @pl.when(jnp.logical_not(fine))
    def _():
        for g in range(groups):
            peak[...] = jnp.full_like(peak, NEG)
            total_now[g] = jnp.zeros_like(peak)
            acc_now[g] = jnp.zeros_like(peak)
            for i in range(parts):
                k, v = keys[i][group_columns(g), :], values[i][:, group_columns(g)]
                where = meta[PARTS + i] * 2 * tok
                allowed = allowed_at(first, where, tok, k.shape[1], lengths)

                @pl.loop(0, heads)
                def _(j):
                    here = pl.ds(pl.multiple_of(j * tok, tok), tok)
                    query = qs[g, pl.ds(pl.multiple_of(at + j * tok, HD), tok)]
                    s = jnp.where(allowed, dot_nn(query, k) * FACTOR, NEG)
                    top = jnp.maximum(peak[here], jnp.max(s, axis=1, keepdims=True))
                    p = jnp.where(allowed, jnp.exp2(s - top[:, :1]), 0.0)
                    shrink = jnp.exp2(peak[here] - top)
                    total_now[g, here] = total_now[g, here] * shrink + fold(p, jnp.add)
                    acc_now[g, here] = acc_now[g, here] * shrink + dot_nn(
                        p.astype(jnp.bfloat16), v
                    )
                    peak[here] = top

            write(g)

    if not near:
        width = result.shape[1]
        where = pl.ds(pl.multiple_of(core * width, width), width)
        copy = pltpu.make_async_copy(result, out.at[:, where], refs[-1])
        copy.start()
        copy.wait()


def close_sums(state, keys, values, meta, lengths, near):
    qs, total, acc = state
    groups, rows, unused = qs.shape
    tok = values[0].shape[0] // 2
    heads = rows // (2 * tok)
    width = groups * heads * HD
    sums = pltpu.VMEM((groups, heads * tok, HD), jnp.float32)
    scratch = [pltpu.VMEM((heads * tok, HD), jnp.float32), sums, sums]
    if not near:
        scratch += [pltpu.VMEM((tok, width), jnp.bfloat16), pltpu.SemaphoreType.DMA]
    pairs = groups * rows * tok
    return pl.pallas_call(
        functools.partial(close_kernel, tok, heads, groups, near),
        out_shape=jax.ShapeDtypeStruct((tok, width if near else 2 * width), jnp.bfloat16),
        in_specs=[SMEM, SMEM] + [VMEM] * (3 + 2 * len(keys)),
        out_specs=VMEM if near else HBM,
        scratch_shapes=scratch,
        compiler_params=pltpu.CompilerParams(vmem_limit_bytes=ROOM),
        cost_estimate=pl.CostEstimate(
            flops=pairs * HD * 8, bytes_accessed=tok * width * 2, transcendentals=pairs
        ),
        name="close_near" if near else "close_own",
    )(meta, lengths, qs, total, acc, *keys, *values)


def request_part(query, keys, values, mask, heads):
    p = jnp.exp2(dot_nn(query, keys) * FACTOR)
    p = jnp.where(mask[None], p.reshape(heads, mask.shape[0], -1), 0.0).reshape(p.shape)
    return fold(p, jnp.add), dot_nn(p.astype(jnp.bfloat16), values)


def stack_heads(q, g, heads):
    slices = [q[:, (g * heads + j) * HD : (g * heads + j + 1) * HD] for j in range(heads)]
    return jnp.concatenate([x.astype(jnp.float32) for x in slices], 0).astype(jnp.bfloat16)


def early_kernel(heads, groups, meta, q, mask, *refs):
    parts = (len(refs) - 2) // 2
    keys, values = refs[:parts], refs[parts : 2 * parts]
    total, acc = refs[2 * parts :]
    length = keys[0].shape[1]
    for g in range(groups):
        query = stack_heads(q, g, heads)
        col = slice(g * HD, (g + 1) * HD)
        sums = None
        for i in range(parts):
            where = pl.ds(pl.multiple_of(meta[PARTS + i] * length, length), length)
            more = request_part(query, keys[i][col], values[i][:, col], mask[:, where] > 0, heads)
            sums = more if sums is None else [x + y for x, y in zip(sums, more)]
        total[g], acc[g] = sums


def early_decode(q, mask, keys, values, meta):
    heads = H // KVH
    groups = values[0].shape[1] // HD
    rows = heads * q.shape[0]
    sums = jax.ShapeDtypeStruct((groups, rows, HD), jnp.float32)
    pairs = groups * rows * len(keys) * values[0].shape[0]
    return pl.pallas_call(
        functools.partial(early_kernel, heads, groups),
        out_shape=[sums, sums],
        in_specs=[SMEM] + [VMEM] * (2 + 2 * len(keys)),
        out_specs=[VMEM] * 2,
        compiler_params=pltpu.CompilerParams(vmem_limit_bytes=ROOM),
        cost_estimate=pl.CostEstimate(
            flops=pairs * HD * 4, bytes_accessed=rows * HD, transcendentals=pairs
        ),
        name="early_decode",
    )(meta, q, mask, *keys, *values)


def late_kernel(done, steps, heads, groups, meta, q, mask, newk, newv, total, acc, *refs):
    parts = (len(refs) - 2) // 2
    keys, values = refs[:parts], refs[parts : 2 * parts]
    out, scores = refs[2 * parts :]
    own = q.shape[0]
    rows = heads * own
    length = keys[0].shape[1]
    row = lax.broadcasted_iota(jnp.int32, (own, own), 0)
    col = lax.broadcasted_iota(jnp.int32, (own, own), 1)
    fresh_ok = (lax.div(row, steps) == lax.div(col, steps)) & (col <= row)

    def keep(allowed, x, other):
        y = x.reshape(heads, own, x.shape[1])
        return jnp.where(allowed[None], y, other).reshape(x.shape)

    def open_to(i):
        where = pl.ds(pl.multiple_of(meta[PARTS + i] * length, length), length)
        return mask[:, where] > 0

    def write(g, sums, whole):
        result = sums / whole
        for j in range(heads):
            out[:, (g * heads + j) * HD : (g * heads + j + 1) * HD] = result[
                j * own : (j + 1) * own
            ].astype(out.dtype)

    fine = None
    for g in range(groups):
        query = stack_heads(q, g, heads)
        cols = slice(g * HD, (g + 1) * HD)
        p = keep(fresh_ok, jnp.exp2(dot_nt(query, newk[:, cols]) * FACTOR), 0.0)
        whole = jnp.sum(p, axis=1, keepdims=True)
        sums = [total[g], acc[g] + dot_nn(p.astype(jnp.bfloat16), newv[:, cols])]
        for i in range(done, parts):
            more = request_part(query, keys[i][cols], values[i][:, cols], open_to(i), heads)
            sums = [x + y for x, y in zip(sums, more)]
        whole = whole + jnp.sum(sums[0], axis=1, keepdims=True)
        write(g, sums[1], whole)
        fine = sound(whole) if fine is None else fine & sound(whole)

    @pl.when(jnp.logical_not(fine))
    def _():
        for g in range(groups):
            query = stack_heads(q, g, heads)
            cols = slice(g * HD, (g + 1) * HD)
            fresh = keep(fresh_ok, dot_nt(query, newk[:, cols]) * FACTOR, NEG)
            top = jnp.max(fresh, axis=1, keepdims=True)
            for i in range(parts):
                s = keep(open_to(i), dot_nn(query, keys[i][cols]) * FACTOR, NEG)
                scores[:, i * length : (i + 1) * length] = s
                top = jnp.maximum(top, jnp.max(s, axis=1, keepdims=True))
            p = jnp.exp2(fresh - top)
            whole = jnp.sum(p, axis=1, keepdims=True)
            sums = dot_nn(p.astype(jnp.bfloat16), newv[:, cols])
            for i in range(parts):
                p = jnp.exp2(scores[:, i * length : (i + 1) * length] - top)
                whole = whole + jnp.sum(p, axis=1, keepdims=True)
                sums = sums + dot_nn(p.astype(jnp.bfloat16), values[i][:, cols])
            write(g, sums, whole)


def late_decode(sums, done, q, mask, newk, newv, keys, values, meta, steps):
    heads = H // KVH
    groups = values[0].shape[1] // HD
    rows = heads * q.shape[0]
    length = values[0].shape[0]
    pairs = groups * rows * (len(keys) - done) * length
    return pl.pallas_call(
        functools.partial(late_kernel, done, steps, heads, groups),
        out_shape=jax.ShapeDtypeStruct(q.shape, jnp.bfloat16),
        in_specs=[SMEM] + [VMEM] * (6 + 2 * len(keys)),
        out_specs=VMEM,
        scratch_shapes=[pltpu.VMEM((rows, len(keys) * length), jnp.float32)],
        compiler_params=pltpu.CompilerParams(vmem_limit_bytes=ROOM),
        cost_estimate=pl.CostEstimate(
            flops=pairs * HD * 4, bytes_accessed=rows * HD, transcendentals=pairs
        ),
        name="late_decode",
    )(meta, q, mask, newk, newv, *sums, *keys, *values)


def decode_kernel(parts, steps, heads, groups, starts, q, mask, newk, newv, *refs):
    kheld, vheld = refs[:parts], refs[parts : 2 * parts]
    out, kall, vall, sems, scores = refs[2 * parts :]
    own = q.shape[0]
    rows = heads * own
    length = kheld[0].shape[1]
    copies = []
    for i in range(parts):
        where = pl.ds(pl.multiple_of(starts[i], HD), length)
        copies.append(pltpu.make_async_copy(kheld[i], kall.at[:, where], sems.at[2 * i]))
        copies.append(pltpu.make_async_copy(vheld[i], vall.at[where], sems.at[2 * i + 1]))
    for copy in copies:
        copy.start()
    row = lax.broadcasted_iota(jnp.int32, (own, own), 0)
    col = lax.broadcasted_iota(jnp.int32, (own, own), 1)
    fresh_ok = (lax.div(row, steps) == lax.div(col, steps)) & (col <= row)

    def columns(g):
        return slice(g * HD, (g + 1) * HD)

    def stacked(g):
        first = g * heads
        slices = [q[:, (first + j) * HD : (first + j + 1) * HD] for j in range(heads)]
        return jnp.concatenate([x.astype(jnp.float32) for x in slices], 0).astype(jnp.bfloat16)

    def keep(allowed, x, other):
        y = x.reshape(heads, own, x.shape[1])
        return jnp.where(allowed[None], y, other).reshape(x.shape)

    def open_to(i):
        return mask[:, pl.ds(pl.multiple_of(starts[i], HD), length)] > 0

    def write(g, acc, whole):
        result = acc / whole
        for j in range(heads):
            out[:, (g * heads + j) * HD : (g * heads + j + 1) * HD] = result[
                j * own : (j + 1) * own
            ].astype(out.dtype)

    fine = None
    for g in range(groups):
        query = stacked(g)
        p = keep(fresh_ok, jnp.exp2(dot_nt(query, newk[:, columns(g)]) * FACTOR), 0.0)
        whole = jnp.sum(p, axis=1, keepdims=True)
        acc = dot_nn(p.astype(jnp.bfloat16), newv[:, columns(g)])
        total = jnp.zeros((rows, HD), jnp.float32)
        for i in range(parts):
            p = jnp.exp2(dot_nn(query, kheld[i][columns(g)]) * FACTOR)
            p = keep(open_to(i), p, 0.0)
            total = total + fold(p, jnp.add)
            acc = acc + dot_nn(p.astype(jnp.bfloat16), vheld[i][:, columns(g)])
        whole = whole + jnp.sum(total, axis=1, keepdims=True)
        write(g, acc, whole)
        fine = sound(whole) if fine is None else fine & sound(whole)

    @pl.when(jnp.logical_not(fine))
    def _():
        for g in range(groups):
            query = stacked(g)
            fresh = keep(fresh_ok, dot_nt(query, newk[:, columns(g)]) * FACTOR, NEG)
            top = jnp.max(fresh, axis=1, keepdims=True)
            for i in range(parts):
                s = keep(open_to(i), dot_nn(query, kheld[i][columns(g)]) * FACTOR, NEG)
                scores[:, i * length : (i + 1) * length] = s
                top = jnp.maximum(top, jnp.max(s, axis=1, keepdims=True))
            p = jnp.exp2(fresh - top)
            whole = jnp.sum(p, axis=1, keepdims=True)
            acc = dot_nn(p.astype(jnp.bfloat16), newv[:, columns(g)])
            for i in range(parts):
                p = jnp.exp2(scores[:, i * length : (i + 1) * length] - top)
                whole = whole + jnp.sum(p, axis=1, keepdims=True)
                acc = acc + dot_nn(p.astype(jnp.bfloat16), vheld[i][:, columns(g)])
            write(g, acc, whole)

    for copy in copies:
        copy.wait()


def decode(q, mask, newk, newv, kparts, vparts, starts, steps):
    own = q.shape[0]
    parts = len(kparts)
    length, width = vparts[0].shape
    count = parts * length
    heads = H // KVH
    groups = width // HD
    rows = heads * own
    pairs = groups * rows * count
    return pl.pallas_call(
        functools.partial(decode_kernel, parts, steps, heads, groups),
        out_shape=[
            jax.ShapeDtypeStruct(q.shape, jnp.bfloat16),
            jax.ShapeDtypeStruct((width, count), jnp.bfloat16),
            jax.ShapeDtypeStruct((count, width), jnp.bfloat16),
        ],
        grid_spec=pltpu.PrefetchScalarGridSpec(
            num_scalar_prefetch=1,
            grid=(),
            in_specs=[VMEM] * (4 + 2 * parts),
            out_specs=[VMEM, HBM, HBM],
            scratch_shapes=[
                pltpu.SemaphoreType.DMA((2 * parts,)),
                pltpu.VMEM((rows, count), jnp.float32),
            ],
        ),
        compiler_params=pltpu.CompilerParams(vmem_limit_bytes=ROOM),
        cost_estimate=pl.CostEstimate(
            flops=pairs * HD * 4, bytes_accessed=count * width * 4, transcendentals=pairs
        ),
        name="decode",
    )(starts, q, mask, newk, newv, *kparts, *vparts)


def prepare_kernel(meta, k, v, send, own_k, own_v):
    width = own_k.shape[0]
    mine = pl.ds(pl.multiple_of(meta[0] * width, width), width)
    other = pl.ds(pl.multiple_of((1 - meta[0]) * width, width), width)
    send[:width] = k[:, other].astype(jnp.float32).T.astype(send.dtype)
    send[width:] = v[:, other]
    own_k[...] = k[:, mine].astype(jnp.float32).T.astype(own_k.dtype)
    own_v[...] = v[:, mine]


def prepare(k, v, core):
    tok, width = k.shape[0], k.shape[1] // 2
    assert tok == width
    block = jax.ShapeDtypeStruct((tok, width), k.dtype)
    return pl.pallas_call(
        prepare_kernel,
        out_shape=[jax.ShapeDtypeStruct((2 * tok, width), k.dtype), block, block],
        grid_spec=pltpu.PrefetchScalarGridSpec(
            num_scalar_prefetch=1, grid=(), in_specs=[VMEM] * 2, out_specs=[VMEM] * 3
        ),
        name="prepare",
    )(core[None], k, v)


def join_kernel(meta, own_k, own_v, theirs, keys, values):
    tok = own_v.shape[0]
    mine = pl.ds(pl.multiple_of(meta[0] * tok, tok), tok)
    other = pl.ds(pl.multiple_of((1 - meta[0]) * tok, tok), tok)
    keys[:, mine] = own_k[...]
    keys[:, other] = theirs[: own_k.shape[0]]
    values[mine] = own_v[...]
    values[other] = theirs[own_k.shape[0] :]


def join(own_k, own_v, theirs, core):
    tok, width = own_v.shape
    return pl.pallas_call(
        join_kernel,
        out_shape=[
            jax.ShapeDtypeStruct((width, 2 * tok), own_k.dtype),
            jax.ShapeDtypeStruct((2 * tok, width), own_k.dtype),
        ],
        grid_spec=pltpu.PrefetchScalarGridSpec(
            num_scalar_prefetch=1, grid=(), in_specs=[VMEM] * 3, out_specs=[VMEM] * 2
        ),
        name="join",
    )(core[None], own_k, own_v, theirs)


def project_kernel(meta, *refs):
    pieces, (mine, other), outs, (sorted_rows,) = refs[:-7], refs[-7:-5], refs[-5:-1], refs[-1:]
    parts = len(pieces)
    rows = pieces[0].shape[0]
    for i, piece in enumerate(pieces):
        at = pl.ds(pl.multiple_of(meta[PARTS + parts + i] * rows, rows), rows)
        sorted_rows[at] = piece[...]
    half = parts * rows // 2
    here = pl.ds(pl.multiple_of(meta[ACROSS] * half, half), half)
    there = pl.ds(pl.multiple_of((1 - meta[ACROSS]) * half, half), half)
    kept, beside, across, corner = outs
    for at, near, far in ((here, kept, beside), (there, across, corner)):
        some = sorted_rows[at]
        near[...] = dot_nt(mine[...], some).astype(near.dtype)
        far[...] = dot_nt(other[...], some).astype(far.dtype)


def project(pieces, mine, other, meta):
    rows = len(pieces) * pieces[0].shape[0]
    width, depth = mine.shape
    block = jax.ShapeDtypeStruct((width, rows // 2), jnp.bfloat16)
    return pl.pallas_call(
        project_kernel,
        out_shape=[jax.ShapeDtypeStruct(block.shape, jnp.float32)] + [block] * 3,
        in_specs=[SMEM] + [VMEM] * (len(pieces) + 2),
        out_specs=[VMEM] * 4,
        scratch_shapes=[pltpu.VMEM((rows, depth), jnp.bfloat16)],
        compiler_params=pltpu.CompilerParams(vmem_limit_bytes=ROOM),
        cost_estimate=pl.CostEstimate(
            flops=rows * width * depth * 4, bytes_accessed=width * depth * 4, transcendentals=0
        ),
        name="project",
    )(meta, *pieces, mine, other)


def index(z, y, c):
    return (z * 2 + y) * 2 + c


def on_ring(r, chips):
    return (r, 0) if r < chips // 2 else (chips - 1 - r, 1)


def ring_perm(chips, d):
    return [
        (index(*on_ring(r, chips), c), index(*on_ring((r + d) % chips, chips), c))
        for r in range(chips)
        for c in range(2)
    ]


def ring_place(r, chips):
    r = lax.rem(r + 2 * chips, chips)
    return jnp.where(r < chips // 2, r * 2, (chips - 1 - r) * 2 + 1)


def spread(x, n):
    place = lax.axis_index("seq")
    deep = n // 4
    everyone = [(z, y, c) for z in range(deep) for y in range(2) for c in range(2)]
    z, y, c = place // 4, (place // 2) % 2, place % 2
    held = [(x, z, y, c)]
    for d in range(1, deep):
        perm = [(index(*p), index((p[0] - d) % deep, p[1], p[2])) for p in everyone]
        held.append((lax.ppermute(x, "seq", perm), lax.rem(z + d, deep), y, c))
    perm = [(index(*p), index(p[0], 1 - p[1], p[2])) for p in everyone]
    held += [(lax.ppermute(b, "seq", perm), bz, 1 - by, bc) for b, bz, by, bc in held]
    perm = [(index(*p), index(p[0], p[1], 1 - p[2])) for p in everyone]
    held += [(lax.ppermute(b, "seq", perm), bz, by, 1 - bc) for b, bz, by, bc in held]
    return [b for b, *_ in held], jnp.stack([index(bz, by, bc) for _, bz, by, bc in held])


def open_blocks(table, steps, count):
    number = lax.broadcasted_iota(jnp.int32, (*table.shape, count), 2) // BLK
    mask = jnp.any(table[:, :, None] == number, axis=1).astype(jnp.float32)
    return jnp.repeat(mask, steps, axis=0)


def whole_heads(n, q_pre, k_cache, v_cache, lengths, q_dec, k_new, v_new, block_table, w_out):
    tok = q_pre.shape[0]
    place = lax.axis_index("seq").astype(jnp.int32)
    rows, steps = q_dec.shape[0], q_dec.shape[1]
    own = rows // n
    kparts, sources = spread(k_cache.T, n)
    vparts, _ = spread(v_cache, n)
    starts = sources.astype(jnp.int32) * tok

    def mine(x):
        y = lax.dynamic_slice_in_dim(x, place * own, own, 0)
        return y.reshape(own * steps, -1) if x.ndim == 3 else y

    mask = open_blocks(mine(block_table), steps, n * tok)
    attn_own, keys, values = decode(
        mine(q_dec), mask, mine(k_new), mine(v_new), kparts, vparts, starts, steps
    )
    attn = lax.all_gather(attn_own, "seq", axis=0, tiled=True)
    flat = jnp.dot(attn, w_out, preferred_element_type=jnp.float32).astype(jnp.bfloat16)
    dec_out = lax.psum_scatter(
        flat.reshape(rows, steps, -1), "tp", scatter_dimension=0, tiled=True
    )
    zero = jnp.zeros((), jnp.int32)
    meta = jnp.stack([place * tok, zero, zero, zero])
    groups = k_cache.shape[1] // HD
    pre_out = prefill(
        q_pre, keys, values, meta, lengths, groups, q_pre.shape[1], "prefill"
    )
    return (pre_out, dec_out)


def split_heads(n, q_pre, k_cache, v_cache, lengths, q_dec, k_new, v_new, block_table, w_out):
    tok = q_pre.shape[0]
    place = lax.axis_index("seq").astype(jnp.int32)
    across = lax.axis_index("tp").astype(jnp.int32)
    core, chip = lax.rem(place, 2), lax.div(place, 2)
    chips = n // 2
    far, deep = chips // 2, chips // 2
    z, y = lax.div(chip, 2), lax.rem(chip, 2)
    r = jnp.where(y == 0, z, chips - 1 - z)
    rows, steps = q_dec.shape[0], q_dec.shape[1]
    own = rows // chips
    sibling = [(i, i ^ 1) for i in range(n)]
    everyone = [(a, b, c) for a in range(deep) for b in range(2) for c in range(2)]

    def half(x, which, axis):
        size = x.shape[axis] // 2
        return lax.dynamic_slice_in_dim(x, which * size, size, axis)

    def mine(x):
        part = lax.dynamic_slice_in_dim(x, chip * own, own, 0)
        return half(part, core, 2).reshape(own * steps, -1) if x.ndim == 3 else part

    order = [0] + [o for d in range(1, far) for o in (-d, d)] + [far]
    numbers = [ring_place(r + o, chips) for o in order]
    levels = [z] + [lax.rem(z + deep - d, deep) for d in range(1, deep)]
    firsts = [level * 2 + y for level in levels] + [level * 2 + 1 - y for level in levels]
    meta = jnp.stack([core, chip, across] + numbers + firsts).astype(jnp.int32)

    send, own_k, own_v = prepare(k_cache, v_cache, core)
    theirs = lax.ppermute(send, "seq", sibling)
    keys, values = {}, {}
    keys[0], values[0] = join(own_k, own_v, theirs, core)
    keys[0], values[0], q_pre, w_out, q_dec, k_new, v_new, block_table, meta = (
        lax.optimization_barrier(
            (keys[0], values[0], q_pre, w_out, q_dec, k_new, v_new, block_table, meta)
        )
    )
    q_near = lax.ppermute(half(q_pre, 1 - core, 1), "seq", sibling)
    weights = w_out.T
    w_near = lax.ppermute(half(weights, 1 - core, 1), "seq", sibling)
    fresh = (mine(q_dec), open_blocks(mine(block_table), steps, n * tok), mine(k_new), mine(v_new))
    w_mine = half(weights, core, 1)

    up, down = ring_perm(chips, 1), ring_perm(chips, -1)
    state, sums = None, ()
    early = far // 2
    for d in range(1, far + 1):
        keys[-d] = lax.ppermute(keys[1 - d], "seq", up)
        values[d] = lax.ppermute(values[d - 1], "seq", down)
        if d < far:
            keys[d] = lax.ppermute(keys[d - 1], "seq", down)
            values[-d] = lax.ppermute(values[1 - d], "seq", up)
        else:
            keys[d] = keys[-d]
        if d == 1:
            state = open_sums(q_pre, q_near, keys[0], values[0], meta, lengths)
        else:
            pair = (1 - d, d - 1)
            state = stage(
                state, [keys[o] for o in pair], [values[o] for o in pair],
                (2 * d - 3, 2 * d - 2), meta, lengths,
            )
        if d == early + 1:
            seen = order[: 2 * early + 1]
            sums = early_decode(
                *fresh[:2], [keys[o] for o in seen], [values[o] for o in seen], meta
            )
        last = (keys[-d], keys[d], values[-d], values[d]) if d < far else (keys[d], values[d])
        last, state, sums = lax.optimization_barrier((last, state, sums))
        if d < far:
            keys[-d], keys[d], values[-d], values[d] = last
        else:
            keys[d], values[d] = last
    kparts, vparts = [keys[o] for o in order], [values[o] for o in order]
    attn_own = late_decode(sums, len(seen), *fresh, kparts, vparts, meta, steps)

    pieces = [attn_own]
    for d in range(1, deep):
        perm = [(index(*p), index((p[0] + d) % deep, p[1], p[2])) for p in everyone]
        pieces.append(lax.ppermute(attn_own, "seq", perm))
    pieces[1], state = lax.optimization_barrier((pieces[1], state))
    perm = [(index(*p), index(p[0], 1 - p[1], p[2])) for p in everyone]
    pieces += [lax.ppermute(piece, "seq", perm) for piece in pieces]

    near = close_sums(state, kparts, vparts, meta, lengths, True)
    back = lax.ppermute(near, "seq", sibling)
    pre_out = close_sums(state, kparts, vparts, meta, lengths, False)
    pieces[-1], pre_out = lax.optimization_barrier((pieces[-1], pre_out))
    pre_out = settle(pre_out, back, meta)

    total, *sent = project(pieces, w_mine, w_near, meta)
    for block, (dc, dx) in zip(sent, ((1, 0), (0, 1), (1, 1))):
        perm = [
            (i * 2 + x, (i ^ dc) * 2 + (x ^ dx)) for i in range(n) for x in range(2)
        ]
        total = total + lax.ppermute(block, ("seq", "tp"), perm).astype(jnp.float32)
    dec_out = total.astype(jnp.bfloat16).T.reshape(rows // 2, steps, -1)
    return (pre_out, dec_out)


def per_device(n, tp, q_pre, k_cache, v_cache, prompt_lengths, *rest):
    groups = k_cache.shape[1] // HD
    even = groups % 2 == 0 and groups > 2 and tp == 2
    form = split_heads if even and k_cache.shape[1] == 2 * k_cache.shape[0] else whole_heads
    return form(n, q_pre, k_cache, v_cache, prompt_lengths.astype(jnp.int32), *rest)


def solution(mesh):
    placed = (
        P("seq", "tp"),
        P("seq", "tp"),
        P("seq", "tp"),
        P(),
        P(None, None, "tp"),
        P(None, None, "tp"),
        P(None, None, "tp"),
        P(),
        P("tp", "seq"),
    )
    return jax.shard_map(
        functools.partial(per_device, mesh.shape["seq"], mesh.shape["tp"]),
        mesh=mesh,
        in_specs=placed,
        out_specs=(P("seq", "tp"), P("tp", None, "seq")),
        check_vma=False,
    )
```

```python
import functools
import math

import jax
import jax.numpy as jnp
from jax import lax
from jax.experimental import pallas as pl
from jax.experimental.pallas import tpu as pltpu
from jax.sharding import PartitionSpec as P

H = 56
KVH = 8
HD = 128
BLK = 64
SPAN = 512
PAIR = 2
NEG = -1e30
LEAST, MOST = 2.0**-60, 2.0**100
FACTOR = math.log2(math.e) / math.sqrt(HD)
ROOM = 16 * 1024 * 1024
CORE, CHIP, ACROSS, PARTS, LEVELS = 0, 1, 2, 3, 11
HBM = pl.BlockSpec(memory_space=pltpu.HBM)
VMEM = pl.BlockSpec(memory_space=pltpu.VMEM)
SMEM = pl.BlockSpec(memory_space=pltpu.SMEM)


def dot_nt(a, b):
    return lax.dot_general(a, b, (((1,), (1,)), ((), ())), preferred_element_type=jnp.float32)


def dot_nn(a, b):
    return lax.dot_general(a, b, (((1,), (0,)), ((), ())), preferred_element_type=jnp.float32)


def fold(x, op):
    out = x[:, :HD]
    for i in range(1, x.shape[1] // HD):
        out = op(out, x[:, i * HD : (i + 1) * HD])
    return out


def start_of(position, lengths):
    end = jnp.int32(0)
    out = jnp.zeros_like(position)
    for i in range(lengths.shape[0]):
        end = end + lengths[i]
        out = jnp.where(position >= end, end, out)
    return out


def sound(total):
    return (jnp.min(total) >= LEAST) & (jnp.max(total) <= MOST)


def prefill_kernel(tok, heads, meta, lengths, q, keys_all, values_all, *refs):
    out, qs, peak, total, acc = refs[-5:]
    for j in range(heads):
        qs[j * tok : (j + 1) * tok] = q[:, j * HD : (j + 1) * HD]
    total[...] = jnp.zeros_like(total)
    acc[...] = jnp.zeros_like(acc)

    begin = meta[0]
    finish = begin + tok
    low = start_of(begin, lengths)
    high = start_of(finish - 1, lengths)
    blocks = lax.div(finish - low + SPAN - 1, SPAN)
    clear = lax.div(finish - high, SPAN)

    def first_of(k):
        return jnp.maximum(finish - (k + 1) * SPAN, 0)

    def load(k):
        here = pl.ds(pl.multiple_of(first_of(k), HD), SPAN)
        return keys_all[:, here], values_all[here, :]

    def allowed_in(k):
        t = begin + lax.broadcasted_iota(jnp.int32, (tok, 1), 0)
        u = first_of(k) + lax.broadcasted_iota(jnp.int32, (tok, SPAN), 1)
        last = jnp.minimum(t, finish - k * SPAN - 1)
        return (u <= last) & (u >= start_of(t, lengths))

    def keep(allowed, x, other):
        some = x.shape[0] // tok
        return jnp.where(allowed[None], x.reshape(some, tok, SPAN), other).reshape(x.shape)

    def block(k, masked):
        keys, values = load(k)
        allowed = allowed_in(k) if masked else None
        for j in range(0, heads, PAIR):
            here = slice(j * tok, min(j + PAIR, heads) * tok)
            p = jnp.exp2(dot_nn(qs[here], keys) * FACTOR)
            if masked:
                p = keep(allowed, p, 0.0)
            total[here] += fold(p, jnp.add)
            acc[here] += dot_nn(p.astype(jnp.bfloat16), values)

    block(0, True)

    @pl.loop(1, jnp.maximum(clear, 1))
    def _(k):
        block(k, False)

    @pl.loop(jnp.maximum(clear, 1), blocks)
    def _(k):
        block(k, True)

    def write():
        whole = jnp.sum(total[...], axis=1, keepdims=True)
        result = (acc[...] / whole).astype(out.dtype)
        for j in range(heads):
            out[:, j * HD : (j + 1) * HD] = result[j * tok : (j + 1) * tok]
        return whole

    fine = sound(write())

    @pl.when(jnp.logical_not(fine))
    def _():
        peak[...] = jnp.full_like(peak, NEG)
        total[...] = jnp.zeros_like(total)
        acc[...] = jnp.zeros_like(acc)

        @pl.loop(0, blocks)
        def _(k):
            keys, values = load(k)
            allowed = allowed_in(k)

            @pl.loop(0, heads)
            def _(j):
                here = pl.ds(pl.multiple_of(j * tok, tok), tok)
                s = jnp.where(allowed, dot_nn(qs[here], keys) * FACTOR, NEG)
                top = jnp.maximum(peak[here], jnp.max(s, axis=1, keepdims=True))
                p = jnp.where(allowed, jnp.exp2(s - top[:, :1]), 0.0)
                shrink = jnp.exp2(peak[here] - top)
                total[here] = total[here] * shrink + fold(p, jnp.add)
                acc[here] = acc[here] * shrink + dot_nn(p.astype(jnp.bfloat16), values)
                peak[here] = top

        write()


def prefill(q, keys, values, meta, lengths, groups, columns, name, before=None):
    tok = q.shape[0]
    count = values.shape[0]
    heads = H // KVH
    rows = heads * tok
    pairs = rows * count // 2 * groups
    extra = [] if before is None else [before]
    return pl.pallas_call(
        functools.partial(prefill_kernel, tok, heads),
        out_shape=jax.ShapeDtypeStruct((tok, columns), jnp.bfloat16),
        grid_spec=pltpu.PrefetchScalarGridSpec(
            num_scalar_prefetch=2,
            grid=(groups,),
            in_specs=[
                pl.BlockSpec((tok, heads * HD), lambda g, meta, lengths: (0, meta[1] + g)),
                pl.BlockSpec((HD, count), lambda g, meta, lengths: (meta[2] + g, 0)),
                pl.BlockSpec((count, HD), lambda g, meta, lengths: (0, meta[2] + g)),
            ]
            + [HBM] * len(extra),
            out_specs=pl.BlockSpec((tok, heads * HD), lambda g, meta, lengths: (0, meta[3] + g)),
            scratch_shapes=[
                pltpu.VMEM((rows, HD), jnp.bfloat16),
                pltpu.VMEM((rows, HD), jnp.float32),
                pltpu.VMEM((rows, HD), jnp.float32),
                pltpu.VMEM((rows, HD), jnp.float32),
            ],
        ),
        compiler_params=pltpu.CompilerParams(vmem_limit_bytes=ROOM),
        cost_estimate=pl.CostEstimate(
            flops=pairs * HD * 8, bytes_accessed=count * HD * 4 * groups, transcendentals=pairs
        ),
        input_output_aliases={} if before is None else {5: 0},
        name=name,
    )(meta, lengths, q, keys, values, *extra)


def settle_kernel(meta, piece, whole, out, sem):
    width = piece.shape[1]
    where = pl.ds(pl.multiple_of((1 - meta[CORE]) * width, width), width)
    copy = pltpu.make_async_copy(piece, out.at[:, where], sem)
    copy.start()
    copy.wait()


def settle(whole, piece, meta):
    return pl.pallas_call(
        settle_kernel,
        out_shape=jax.ShapeDtypeStruct(whole.shape, whole.dtype),
        in_specs=[SMEM, VMEM, HBM],
        out_specs=HBM,
        scratch_shapes=[pltpu.SemaphoreType.DMA],
        input_output_aliases={2: 0},
        cost_estimate=pl.CostEstimate(flops=0, bytes_accessed=piece.size * 4, transcendentals=0),
        name="settle",
    )(meta, piece, whole)


def allowed_at(first, base, tok, length, lengths):
    t = first + lax.broadcasted_iota(jnp.int32, (tok, 1), 0)
    u = base + lax.broadcasted_iota(jnp.int32, (tok, length), 1)
    return (u <= t) & (u >= start_of(t, lengths))


def column_block(at):
    return pl.ds(pl.multiple_of(at, HD), HD)


def keys_of(upper, g):
    return upper[column_block(g * HD), :]


def values_of(lower, g):
    half = lower.shape[1] // 2
    both = [lower[:, column_block(side * half + g * HD)] for side in range(2)]
    return jnp.concatenate(both, axis=0)


def add_block(tok, heads, q_at, keys, values, allowed, sums, fresh=False):
    length = keys.shape[1]
    for j in range(0, heads, PAIR):
        some = min(PAIR, heads - j)
        p = jnp.exp2(dot_nn(q_at(j * tok, some * tok), keys) * FACTOR)
        if allowed is not None:
            p = p.reshape(some, tok, length)
            p = jnp.where(allowed[None], p, 0.0).reshape(some * tok, length)
        more = (fold(p, jnp.add), dot_nn(p.astype(jnp.bfloat16), values))
        for ref, value in zip(sums, more):
            here = slice(j * tok, (j + some) * tok)
            ref[here] = value if fresh else ref[here] + value


def relation(meta, part, side, tok, lengths):
    first = (meta[CHIP] * 2 + side) * tok
    base = meta[PARTS + part] * 2 * tok
    relevant = (base < first) & (meta[PARTS + part] != meta[CHIP])
    relevant = relevant & (base + 2 * tok > start_of(first, lengths))
    return relevant, base >= start_of(first + tok - 1, lengths), first, base


def side_rows(side, heads, tok):
    return pl.ds(pl.multiple_of(side * (heads * tok), HD), heads * tok)


def open_kernel(tok, heads, groups, meta, lengths, q_own, q_near, block, qs, total, acc):
    core = meta[CORE]
    rows = heads * tok
    for source, side in ((q_own, core), (q_near, 1 - core)):
        for g in range(groups):
            for j in range(heads):
                at = pl.ds(pl.multiple_of(side * rows + j * tok, HD), tok)
                first = (g * heads + j) * HD
                qs[g, at] = source[:, first : first + HD]
    upper, lower = block.at[: block.shape[0] // 2], block.at[block.shape[0] // 2 :]

    @pl.loop(0, groups)
    def _(g):
        keys, values = keys_of(upper, g), values_of(lower, g)
        for side in range(2):
            length = (side + 1) * tok
            first = (meta[CHIP] * 2 + side) * tok
            allowed = allowed_at(first, meta[CHIP] * 2 * tok, tok, length, lengths)
            here = side_rows(side, heads, tok)
            q_at = lambda at, count: qs[g, pl.ds(side * rows + at, count)]
            add_block(tok, heads, q_at, keys[:, :length], values[:length], allowed,
                      (total.at[g, here], acc.at[g, here]), True)


def open_sums(q_own, q_near, block, meta, lengths):
    tok = q_own.shape[0]
    heads = H // KVH
    groups = q_own.shape[1] // (heads * HD)
    rows = 2 * heads * tok
    sums = jax.ShapeDtypeStruct((groups, rows, HD), jnp.float32)
    pairs = groups * rows * tok * 2
    return pl.pallas_call(
        functools.partial(open_kernel, tok, heads, groups),
        out_shape=[jax.ShapeDtypeStruct((groups, rows, HD), jnp.bfloat16), sums, sums],
        in_specs=[SMEM, SMEM, VMEM, VMEM, VMEM],
        out_specs=[VMEM] * 3,
        compiler_params=pltpu.CompilerParams(vmem_limit_bytes=ROOM),
        cost_estimate=pl.CostEstimate(
            flops=pairs * HD * 8, bytes_accessed=q_own.size * 2, transcendentals=pairs
        ),
        name="open",
    )(meta, lengths, q_own, q_near, block)


def stage_kernel(tok, heads, groups, first_part, meta, lengths, qs, total_in, acc_in, one, two, total, acc, held):
    held[0], held[1] = one[...], two[...]
    half = held.shape[1] // 2

    @pl.loop(0, 4 * groups)
    def _(step):
        which, rest = lax.div(step, 2 * groups), lax.rem(step, 2 * groups)
        g, side = lax.div(rest, 2), lax.rem(rest, 2)
        relevant, clear, first, base = relation(meta, first_part + which, side, tok, lengths)
        here = side_rows(side, heads, tok)
        sums = (total.at[g, here], acc.at[g, here])
        at = side * (heads * tok)
        q_at = lambda off, count: qs[g, pl.ds(pl.multiple_of(at + off, HD), count)]
        upper, lower = held.at[which, :half], held.at[which, half:]

        @pl.when(relevant & clear)
        def _():
            add_block(tok, heads, q_at, keys_of(upper, g), values_of(lower, g), None, sums)

        @pl.when(relevant & jnp.logical_not(clear))
        def _():
            allowed = allowed_at(first, base, tok, 2 * tok, lengths)
            add_block(tok, heads, q_at, keys_of(upper, g), values_of(lower, g), allowed, sums)


def stage(state, pair, first_part, meta, lengths):
    qs, total, acc = state
    groups, rows, unused = qs.shape
    tok = pair[0].shape[1] // 2
    pairs = groups * rows * tok * 2
    new = pl.pallas_call(
        functools.partial(stage_kernel, tok, rows // (2 * tok), groups, first_part),
        out_shape=[jax.ShapeDtypeStruct(x.shape, x.dtype) for x in (total, acc)],
        in_specs=[SMEM, SMEM] + [VMEM] * 5,
        out_specs=[VMEM] * 2,
        scratch_shapes=[pltpu.VMEM((2, *pair[0].shape), pair[0].dtype)],
        input_output_aliases={3: 0, 4: 1},
        compiler_params=pltpu.CompilerParams(vmem_limit_bytes=ROOM),
        cost_estimate=pl.CostEstimate(
            flops=pairs * HD * 8, bytes_accessed=tok * HD, transcendentals=pairs
        ),
        name=f"stage{first_part}",
    )(meta, lengths, qs, total, acc, *pair)
    return qs, *new


def gather_parts(blocks, last, held):
    half = held.shape[1] // 2
    for i, block in enumerate(blocks):
        held[i] = block[...]
    held[len(blocks), :half] = last[0][...]
    held[len(blocks), half:] = last[1][...]


def close_kernel(tok, heads, groups, near, meta, lengths, qs, total, acc, *refs):
    parts = len(refs) - (7 if near else 9)
    blocks, last = refs[:parts], refs[parts : parts + 2]
    out, held, peak, total_now, acc_now = refs[parts + 2 : parts + 7]
    rows = heads * tok
    core = meta[CORE]
    side = 1 - core if near else core
    at = side * rows
    result = out if near else refs[-2]
    relevant, clear, first, base = relation(meta, parts, side, tok, lengths)
    here = side_rows(side, heads, tok)

    def q_of(g):
        return lambda off, count: qs[g, pl.ds(pl.multiple_of(at + off, HD), count)]

    def write(g):
        whole = jnp.sum(total_now[...], axis=1, keepdims=True)
        value = (acc_now[...] / whole).astype(result.dtype)
        for j in range(heads):
            result[:, column_block((g * heads + j) * HD)] = value[j * tok : (j + 1) * tok]
        return sound(whole)

    def one_group(g, fine):
        total_now[...] = total[g, here]
        acc_now[...] = acc[g, here]

        @pl.when(relevant)
        def _():
            allowed = allowed_at(first, base, tok, 2 * tok, lengths)
            add_block(tok, heads, q_of(g), keys_of(last[0], g), values_of(last[1], g), allowed,
                      (total_now, acc_now))

        return fine & write(g).astype(jnp.int32)

    fine = lax.fori_loop(0, groups, one_group, jnp.int32(1))

    @pl.when(fine == 0)
    def _():
        gather_parts(blocks, last, held)
        half = held.shape[1] // 2

        @pl.loop(0, groups)
        def _(g):
            peak[...] = jnp.full_like(peak, NEG)
            total_now[...] = jnp.zeros_like(total_now)
            acc_now[...] = jnp.zeros_like(acc_now)

            @pl.loop(0, (parts + 1) * heads)
            def _(step):
                i, j = lax.div(step, heads), lax.rem(step, heads)
                keys = keys_of(held.at[i, :half], g)
                values = values_of(held.at[i, half:], g)
                allowed = allowed_at(first, meta[PARTS + i] * 2 * tok, tok, 2 * tok, lengths)
                mine = pl.ds(pl.multiple_of(j * tok, tok), tok)
                s = jnp.where(allowed, dot_nn(q_of(g)(j * tok, tok), keys) * FACTOR, NEG)
                top = jnp.maximum(peak[mine], jnp.max(s, axis=1, keepdims=True))
                p = jnp.where(allowed, jnp.exp2(s - top[:, :1]), 0.0)
                shrink = jnp.exp2(peak[mine] - top)
                total_now[mine] = total_now[mine] * shrink + fold(p, jnp.add)
                acc_now[mine] = acc_now[mine] * shrink + dot_nn(p.astype(jnp.bfloat16), values)
                peak[mine] = top

            write(g)

    if not near:
        width = result.shape[1]
        where = pl.ds(pl.multiple_of(core * width, width), width)
        copy = pltpu.make_async_copy(result, out.at[:, where], refs[-1])
        copy.start()
        copy.wait()


def close_sums(state, blocks, last, meta, lengths, near):
    qs, total, acc = state
    groups, rows, unused = qs.shape
    tok = last[0].shape[1] // 2
    heads = rows // (2 * tok)
    width = groups * heads * HD
    sums = pltpu.VMEM((heads * tok, HD), jnp.float32)
    scratch = [pltpu.VMEM((len(blocks) + 1, *blocks[0].shape), blocks[0].dtype), sums, sums, sums]
    if not near:
        scratch += [pltpu.VMEM((tok, width), jnp.bfloat16), pltpu.SemaphoreType.DMA]
    return pl.pallas_call(
        functools.partial(close_kernel, tok, heads, groups, near),
        out_shape=jax.ShapeDtypeStruct((tok, width if near else 2 * width), jnp.bfloat16),
        in_specs=[SMEM, SMEM] + [VMEM] * (5 + len(blocks)),
        out_specs=VMEM if near else HBM,
        scratch_shapes=scratch,
        compiler_params=pltpu.CompilerParams(vmem_limit_bytes=ROOM),
        cost_estimate=pl.CostEstimate(
            flops=rows, bytes_accessed=tok * width * 2, transcendentals=0
        ),
        name="close_near" if near else "close_own",
    )(meta, lengths, qs, total, acc, *blocks, *last)


def request_sums(query, keys, values, mask):
    p = jnp.exp2(dot_nn(query, keys) * FACTOR)
    p = jnp.where(mask[None], p.reshape(-1, *mask.shape), 0.0).reshape(p.shape)
    return fold(p, jnp.add), dot_nn(p.astype(jnp.bfloat16), values)


def fresh_scores(query, newk, own):
    s = dot_nt(query, newk) * FACTOR
    size = newk.shape[0]
    row = lax.broadcasted_iota(jnp.int32, (size, size), 0)
    col = lax.broadcasted_iota(jnp.int32, (size, size), 1)
    ok = (lax.rem(row, own) == lax.rem(col, own)) & (lax.div(col, own) <= lax.div(row, own))
    return s.reshape(-1, size, size), ok


def early_kernel(own, heads, groups, parts, meta, q_dec, k_new, v_new, table, *refs):
    blocks = refs[:parts]
    total, acc, query, newk, newv, mask, q3, k3, v3, sems = refs[parts:]
    steps = q3.shape[1]
    core, level = meta[CORE], lax.div(meta[CHIP], 2)
    requests = pl.ds(level * own, own)
    copies = []
    for i, (source, held) in enumerate(((q_dec, q3), (k_new, k3), (v_new, v3))):
        width = held.shape[2]
        where = pl.ds(pl.multiple_of(core * width, width), width)
        copies.append(pltpu.make_async_copy(source.at[requests, :, where], held, sems.at[i]))
    for copy in copies:
        copy.start()
    length = blocks[0].shape[1]
    rows = table[pl.ds(pl.multiple_of(level * own, own), own), :]
    lane = lax.div(lax.broadcasted_iota(jnp.int32, (own, length), 1), BLK)
    for i in range(mask.shape[1] // length):
        number = lane + meta[PARTS + i] * (length // BLK)
        hit = rows[:, :1] == number
        for j in range(1, rows.shape[1]):
            hit = hit | (rows[:, j : j + 1] == number)
        mask[:, i * length : (i + 1) * length] = hit.astype(jnp.float32)
    for copy in copies:
        copy.wait()
    for s in range(steps):
        for g in range(groups):
            col = slice(g * HD, (g + 1) * HD)
            at = slice(s * own, (s + 1) * own)
            newk[at, col] = k3[:, s, col]
            newv[at, col] = v3[:, s, col]
            for j in range(heads):
                first = (g * heads + j) * HD
                row = (j * steps + s) * own
                query[g, row : row + own] = q3[:, s, first : first + HD]
    half = blocks[0].shape[0] // 2

    @pl.loop(0, groups)
    def _(g):
        col = column_block(g * HD)
        s, ok = fresh_scores(query[g], newk[:, col], own)
        p = jnp.where(ok[None], jnp.exp2(s), 0.0).reshape(-1, s.shape[2])
        first = jnp.sum(p, axis=1, keepdims=True)
        lead = lax.broadcasted_iota(jnp.int32, (p.shape[0], HD), 1) == 0
        sums = [jnp.where(lead, first, 0.0), dot_nn(p.astype(jnp.bfloat16), newv[:, col])]
        for i in range(parts):
            open_to = mask[:, i * length : (i + 1) * length] > 0
            keys, values = keys_of(blocks[i].at[:half], g), values_of(blocks[i].at[half:], g)
            more = request_sums(query[g], keys, values, open_to)
            sums = [x + y for x, y in zip(sums, more)]
        total[g], acc[g] = sums


def early_decode(q_dec, k_new, v_new, table, blocks, count, own, meta):
    heads = H // KVH
    steps = q_dec.shape[1]
    width = k_new.shape[2] // 2
    groups = width // HD
    length = blocks[0].shape[1]
    rows = heads * own * steps
    sums = jax.ShapeDtypeStruct((groups, rows, HD), jnp.float32)
    new = jax.ShapeDtypeStruct((own * steps, width), jnp.bfloat16)
    pairs = groups * rows * len(blocks) * length
    return pl.pallas_call(
        functools.partial(early_kernel, own, heads, groups, len(blocks)),
        out_shape=[
            sums, sums, jax.ShapeDtypeStruct((groups, rows, HD), jnp.bfloat16), new, new,
            jax.ShapeDtypeStruct((own, count * length), jnp.float32),
        ],
        in_specs=[SMEM] + [HBM] * 3 + [VMEM] * (1 + len(blocks)),
        out_specs=[VMEM] * 6,
        scratch_shapes=[
            pltpu.VMEM((own, steps, groups * heads * HD), jnp.bfloat16),
            pltpu.VMEM((own, steps, width), jnp.bfloat16),
            pltpu.VMEM((own, steps, width), jnp.bfloat16),
            pltpu.SemaphoreType.DMA((3,)),
        ],
        compiler_params=pltpu.CompilerParams(vmem_limit_bytes=ROOM),
        cost_estimate=pl.CostEstimate(
            flops=pairs * HD * 8, bytes_accessed=rows * HD * 8, transcendentals=pairs
        ),
        name="early_decode",
    )(meta, q_dec, k_new, v_new, table, *blocks)


def late_kernel(own, steps, heads, groups, done, meta, total, acc, query, newk, newv, mask, *refs):
    parts = len(refs) - 5
    blocks, last = refs[:parts], refs[parts : parts + 2]
    out, held, scores = refs[parts + 2 :]
    length = blocks[0].shape[1]
    half = blocks[0].shape[0] // 2
    size = own * steps

    def write(g, sums, whole):
        result = (sums / whole).astype(out.dtype)
        for j in range(heads):
            out[:, column_block((g * heads + j) * HD)] = result[j * size : (j + 1) * size]

    def one_group(g, fine):
        sums = [total[g], acc[g]]
        for i in range(done, parts + 1):
            upper = last[0] if i == parts else blocks[i].at[:half]
            lower = last[1] if i == parts else blocks[i].at[half:]
            open_to = mask[:, i * length : (i + 1) * length] > 0
            more = request_sums(query[g], keys_of(upper, g), values_of(lower, g), open_to)
            sums = [x + y for x, y in zip(sums, more)]
        whole = jnp.sum(sums[0], axis=1, keepdims=True)
        write(g, sums[1], whole)
        return fine & sound(whole).astype(jnp.int32)

    fine = lax.fori_loop(0, groups, one_group, jnp.int32(1))

    @pl.when(fine == 0)
    def _():
        gather_parts(blocks, last, held)

        @pl.loop(0, groups)
        def _(g):
            col = column_block(g * HD)
            fresh, ok = fresh_scores(query[g], newk[:, col], own)
            fresh = jnp.where(ok[None], fresh, NEG).reshape(-1, size)
            rows = fresh.shape[0]

            def score(i, top):
                s = dot_nn(query[g], keys_of(held.at[i, :half], g)) * FACTOR
                where = pl.ds(pl.multiple_of(i * length, length), length)
                open_to = mask[:, where] > 0
                s = jnp.where(open_to[None], s.reshape(-1, own, length), NEG).reshape(s.shape)
                scores[:, where] = s
                return jnp.maximum(top, jnp.max(s, axis=1, keepdims=True))

            top = lax.fori_loop(0, parts + 1, score, jnp.max(fresh, axis=1, keepdims=True))
            p = jnp.exp2(fresh - top)

            def weigh(i, sums):
                where = pl.ds(pl.multiple_of(i * length, length), length)
                p = jnp.exp2(scores[:, where] - top)
                values = values_of(held.at[i, half:], g)
                return (
                    sums[0] + jnp.sum(p, axis=1, keepdims=True),
                    sums[1] + dot_nn(p.astype(jnp.bfloat16), values),
                )

            start = (
                jnp.sum(p, axis=1, keepdims=True),
                dot_nn(p.astype(jnp.bfloat16), newv[:, col]),
            )
            whole, sums = lax.fori_loop(0, parts + 1, weigh, start)
            write(g, sums, whole)


def late_decode(early, blocks, last, done, own, steps, meta):
    groups, rows, unused = early[0].shape
    heads = H // KVH
    parts, length = len(blocks) + 1, blocks[0].shape[1]
    pairs = groups * rows * (parts - done) * length
    return pl.pallas_call(
        functools.partial(late_kernel, own, steps, heads, groups, done),
        out_shape=jax.ShapeDtypeStruct((own * steps, groups * heads * HD), jnp.bfloat16),
        in_specs=[SMEM] + [VMEM] * (len(early) + len(blocks) + 2),
        out_specs=VMEM,
        scratch_shapes=[
            pltpu.VMEM((parts, *blocks[0].shape), blocks[0].dtype),
            pltpu.VMEM((rows, parts * length), jnp.float32),
        ],
        compiler_params=pltpu.CompilerParams(vmem_limit_bytes=ROOM + ROOM // 4),
        cost_estimate=pl.CostEstimate(
            flops=pairs * HD * 8, bytes_accessed=rows * HD, transcendentals=pairs
        ),
        name="late_decode",
    )(meta, *early, *blocks, *last)


def decode_kernel(parts, steps, heads, groups, starts, q, mask, newk, newv, *refs):
    kheld, vheld = refs[:parts], refs[parts : 2 * parts]
    out, kall, vall, sems, scores = refs[2 * parts :]
    own = q.shape[0]
    rows = heads * own
    length = kheld[0].shape[1]
    copies = []
    for i in range(parts):
        where = pl.ds(pl.multiple_of(starts[i], HD), length)
        copies.append(pltpu.make_async_copy(kheld[i], kall.at[:, where], sems.at[2 * i]))
        copies.append(pltpu.make_async_copy(vheld[i], vall.at[where], sems.at[2 * i + 1]))
    for copy in copies:
        copy.start()
    row = lax.broadcasted_iota(jnp.int32, (own, own), 0)
    col = lax.broadcasted_iota(jnp.int32, (own, own), 1)
    fresh_ok = (lax.div(row, steps) == lax.div(col, steps)) & (col <= row)

    def columns(g):
        return slice(g * HD, (g + 1) * HD)

    def stacked(g):
        first = g * heads
        slices = [q[:, (first + j) * HD : (first + j + 1) * HD] for j in range(heads)]
        return jnp.concatenate([x.astype(jnp.float32) for x in slices], 0).astype(jnp.bfloat16)

    def keep(allowed, x, other):
        y = x.reshape(heads, own, x.shape[1])
        return jnp.where(allowed[None], y, other).reshape(x.shape)

    def open_to(i):
        return mask[:, pl.ds(pl.multiple_of(starts[i], HD), length)] > 0

    def write(g, acc, whole):
        result = acc / whole
        for j in range(heads):
            out[:, (g * heads + j) * HD : (g * heads + j + 1) * HD] = result[
                j * own : (j + 1) * own
            ].astype(out.dtype)

    fine = None
    for g in range(groups):
        query = stacked(g)
        p = keep(fresh_ok, jnp.exp2(dot_nt(query, newk[:, columns(g)]) * FACTOR), 0.0)
        whole = jnp.sum(p, axis=1, keepdims=True)
        acc = dot_nn(p.astype(jnp.bfloat16), newv[:, columns(g)])
        total = jnp.zeros((rows, HD), jnp.float32)
        for i in range(parts):
            p = jnp.exp2(dot_nn(query, kheld[i][columns(g)]) * FACTOR)
            p = keep(open_to(i), p, 0.0)
            total = total + fold(p, jnp.add)
            acc = acc + dot_nn(p.astype(jnp.bfloat16), vheld[i][:, columns(g)])
        whole = whole + jnp.sum(total, axis=1, keepdims=True)
        write(g, acc, whole)
        fine = sound(whole) if fine is None else fine & sound(whole)

    @pl.when(jnp.logical_not(fine))
    def _():
        for g in range(groups):
            query = stacked(g)
            fresh = keep(fresh_ok, dot_nt(query, newk[:, columns(g)]) * FACTOR, NEG)
            top = jnp.max(fresh, axis=1, keepdims=True)
            for i in range(parts):
                s = keep(open_to(i), dot_nn(query, kheld[i][columns(g)]) * FACTOR, NEG)
                scores[:, i * length : (i + 1) * length] = s
                top = jnp.maximum(top, jnp.max(s, axis=1, keepdims=True))
            p = jnp.exp2(fresh - top)
            whole = jnp.sum(p, axis=1, keepdims=True)
            acc = dot_nn(p.astype(jnp.bfloat16), newv[:, columns(g)])
            for i in range(parts):
                p = jnp.exp2(scores[:, i * length : (i + 1) * length] - top)
                whole = whole + jnp.sum(p, axis=1, keepdims=True)
                acc = acc + dot_nn(p.astype(jnp.bfloat16), vheld[i][:, columns(g)])
            write(g, acc, whole)

    for copy in copies:
        copy.wait()


def decode(q, mask, newk, newv, kparts, vparts, starts, steps):
    own = q.shape[0]
    parts = len(kparts)
    length, width = vparts[0].shape
    count = parts * length
    heads = H // KVH
    groups = width // HD
    rows = heads * own
    pairs = groups * rows * count
    return pl.pallas_call(
        functools.partial(decode_kernel, parts, steps, heads, groups),
        out_shape=[
            jax.ShapeDtypeStruct(q.shape, jnp.bfloat16),
            jax.ShapeDtypeStruct((width, count), jnp.bfloat16),
            jax.ShapeDtypeStruct((count, width), jnp.bfloat16),
        ],
        grid_spec=pltpu.PrefetchScalarGridSpec(
            num_scalar_prefetch=1,
            grid=(),
            in_specs=[VMEM] * (4 + 2 * parts),
            out_specs=[VMEM, HBM, HBM],
            scratch_shapes=[
                pltpu.SemaphoreType.DMA((2 * parts,)),
                pltpu.VMEM((rows, count), jnp.float32),
            ],
        ),
        compiler_params=pltpu.CompilerParams(vmem_limit_bytes=ROOM),
        cost_estimate=pl.CostEstimate(
            flops=pairs * HD * 4, bytes_accessed=count * width * 4, transcendentals=pairs
        ),
        name="decode",
    )(starts, q, mask, newk, newv, *kparts, *vparts)


def prepare_kernel(meta, k, v, q, send, block, send_q, own_q, sems):
    tok, width = k.shape[0], k.shape[1] // 2
    core = meta[0]
    columns = own_q.shape[1]
    copies = []
    for i, (which, held) in enumerate(((1 - core, send_q), (core, own_q))):
        where = pl.ds(pl.multiple_of(which * columns, columns), columns)
        copies.append(pltpu.make_async_copy(q.at[:, where], held, sems.at[i]))
    for copy in copies:
        copy.start()
    mine = pl.ds(pl.multiple_of(core * width, width), width)
    other = pl.ds(pl.multiple_of((1 - core) * width, width), width)
    here = pl.ds(pl.multiple_of(core * tok, tok), tok)
    send[:width] = k[:, other].astype(jnp.float32).T.astype(send.dtype)
    send[width:] = v[:, other]
    block[:width, here] = k[:, mine].astype(jnp.float32).T.astype(block.dtype)
    block[width:, mine] = v[:, mine]
    for copy in copies:
        copy.wait()


def prepare(k, v, q, core):
    tok, width = k.shape[0], k.shape[1] // 2
    assert tok == width
    halves = jax.ShapeDtypeStruct((tok, q.shape[1] // 2), q.dtype)
    return pl.pallas_call(
        prepare_kernel,
        out_shape=[
            jax.ShapeDtypeStruct((2 * tok, width), k.dtype),
            jax.ShapeDtypeStruct((2 * width, 2 * tok), k.dtype),
            halves,
            halves,
        ],
        in_specs=[SMEM, VMEM, VMEM, HBM],
        out_specs=[VMEM] * 4,
        scratch_shapes=[pltpu.SemaphoreType.DMA((2,))],
        name="prepare",
    )(core[None], k, v, q)


def join_kernel(meta, block_in, theirs, block):
    width = theirs.shape[1]
    other = pl.ds(pl.multiple_of((1 - meta[0]) * width, width), width)
    block[:width, other] = theirs[:width]
    block[width:, other] = theirs[width:]


def join(block, theirs, core):
    return pl.pallas_call(
        join_kernel,
        out_shape=jax.ShapeDtypeStruct(block.shape, block.dtype),
        in_specs=[SMEM, VMEM, VMEM],
        out_specs=VMEM,
        input_output_aliases={1: 0},
        name="join",
    )(core[None], block, theirs)


def take_kernel(meta, whole, out, sem):
    width = out.shape[1]
    where = pl.ds(pl.multiple_of((1 - meta[CORE]) * width, width), width)
    copy = pltpu.make_async_copy(whole.at[:, where], out, sem)
    copy.start()
    copy.wait()


def take_other_half(whole, meta):
    return pl.pallas_call(
        take_kernel,
        out_shape=jax.ShapeDtypeStruct((whole.shape[0], whole.shape[1] // 2), whole.dtype),
        in_specs=[SMEM, HBM],
        out_specs=VMEM,
        scratch_shapes=[pltpu.SemaphoreType.DMA],
        name="take",
    )(meta, whole)


def project_kernel(meta, *refs):
    pieces, (whole, other), outs, (sorted_rows,) = refs[:-7], refs[-7:-5], refs[-5:-1], refs[-1:]
    parts = len(pieces)
    rows = pieces[0].shape[0]
    for i, piece in enumerate(pieces):
        at = pl.ds(pl.multiple_of(meta[LEVELS + i] * rows, rows), rows)
        sorted_rows[at] = piece[...]
    depth = other.shape[1]
    mine = whole[:, pl.ds(pl.multiple_of(meta[CORE] * depth, depth), depth)]
    half = parts * rows // 2
    here = pl.ds(pl.multiple_of(meta[ACROSS] * half, half), half)
    there = pl.ds(pl.multiple_of((1 - meta[ACROSS]) * half, half), half)
    kept, beside, across, corner = outs
    for at, near, far in ((here, kept, beside), (there, across, corner)):
        some = sorted_rows[at]
        near[...] = dot_nt(mine, some).astype(near.dtype)
        far[...] = dot_nt(other[...], some).astype(far.dtype)


def project(pieces, whole, other, meta):
    rows = len(pieces) * pieces[0].shape[0]
    width, depth = other.shape
    block = jax.ShapeDtypeStruct((width, rows // 2), jnp.bfloat16)
    return pl.pallas_call(
        project_kernel,
        out_shape=[jax.ShapeDtypeStruct(block.shape, jnp.float32)] + [block] * 3,
        in_specs=[SMEM] + [VMEM] * (len(pieces) + 2),
        out_specs=[VMEM] * 4,
        scratch_shapes=[pltpu.VMEM((rows, depth), jnp.bfloat16)],
        compiler_params=pltpu.CompilerParams(vmem_limit_bytes=ROOM),
        cost_estimate=pl.CostEstimate(
            flops=rows * width * depth * 4, bytes_accessed=width * depth * 4, transcendentals=0
        ),
        name="project",
    )(meta, *pieces, whole, other)


def index(z, y, c):
    return (z * 2 + y) * 2 + c


def on_ring(r, chips):
    return (r, 0) if r < chips // 2 else (chips - 1 - r, 1)


def ring_perm(chips, d):
    return [
        (index(*on_ring(r, chips), c), index(*on_ring((r + d) % chips, chips), c))
        for r in range(chips)
        for c in range(2)
    ]


def ring_place(r, chips):
    r = lax.rem(r + 2 * chips, chips)
    return jnp.where(r < chips // 2, r * 2, (chips - 1 - r) * 2 + 1)


def spread(x, n):
    place = lax.axis_index("seq")
    deep = n // 4
    everyone = [(z, y, c) for z in range(deep) for y in range(2) for c in range(2)]
    z, y, c = place // 4, (place // 2) % 2, place % 2
    held = [(x, z, y, c)]
    for d in range(1, deep):
        perm = [(index(*p), index((p[0] - d) % deep, p[1], p[2])) for p in everyone]
        held.append((lax.ppermute(x, "seq", perm), lax.rem(z + d, deep), y, c))
    perm = [(index(*p), index(p[0], 1 - p[1], p[2])) for p in everyone]
    held += [(lax.ppermute(b, "seq", perm), bz, 1 - by, bc) for b, bz, by, bc in held]
    perm = [(index(*p), index(p[0], p[1], 1 - p[2])) for p in everyone]
    held += [(lax.ppermute(b, "seq", perm), bz, by, 1 - bc) for b, bz, by, bc in held]
    return [b for b, *_ in held], jnp.stack([index(bz, by, bc) for _, bz, by, bc in held])


def open_blocks(table, steps, count):
    number = lax.broadcasted_iota(jnp.int32, (*table.shape, count), 2) // BLK
    mask = jnp.any(table[:, :, None] == number, axis=1).astype(jnp.float32)
    return jnp.repeat(mask, steps, axis=0)


def whole_heads(n, q_pre, k_cache, v_cache, lengths, q_dec, k_new, v_new, block_table, w_out):
    tok = q_pre.shape[0]
    place = lax.axis_index("seq").astype(jnp.int32)
    rows, steps = q_dec.shape[0], q_dec.shape[1]
    own = rows // n
    kparts, sources = spread(k_cache.T, n)
    vparts, _ = spread(v_cache, n)
    starts = sources.astype(jnp.int32) * tok

    def mine(x):
        y = lax.dynamic_slice_in_dim(x, place * own, own, 0)
        return y.reshape(own * steps, -1) if x.ndim == 3 else y

    mask = open_blocks(mine(block_table), steps, n * tok)
    attn_own, keys, values = decode(
        mine(q_dec), mask, mine(k_new), mine(v_new), kparts, vparts, starts, steps
    )
    attn = lax.all_gather(attn_own, "seq", axis=0, tiled=True)
    flat = jnp.dot(attn, w_out, preferred_element_type=jnp.float32).astype(jnp.bfloat16)
    dec_out = lax.psum_scatter(
        flat.reshape(rows, steps, -1), "tp", scatter_dimension=0, tiled=True
    )
    zero = jnp.zeros((), jnp.int32)
    meta = jnp.stack([place * tok, zero, zero, zero])
    groups = k_cache.shape[1] // HD
    pre_out = prefill(
        q_pre, keys, values, meta, lengths, groups, q_pre.shape[1], "prefill"
    )
    return (pre_out, dec_out)


def split_heads(n, q_pre, k_cache, v_cache, lengths, q_dec, k_new, v_new, block_table, w_out):
    place = lax.axis_index("seq").astype(jnp.int32)
    across = lax.axis_index("tp").astype(jnp.int32)
    core, chip = lax.rem(place, 2), lax.div(place, 2)
    chips = n // 2
    far, deep = chips // 2, chips // 2
    z, y = lax.div(chip, 2), lax.rem(chip, 2)
    r = jnp.where(y == 0, z, chips - 1 - z)
    rows, steps = q_dec.shape[0], q_dec.shape[1]
    own = rows // deep
    sibling = [(i, i ^ 1) for i in range(n)]
    everyone = [(a, b, c) for a in range(deep) for b in range(2) for c in range(2)]

    order = [0] + [o for d in range(1, far) for o in (-d, d)] + [far]
    numbers = [ring_place(r + o, chips) for o in order]
    levels = [z] + [lax.rem(z + deep - d, deep) for d in range(1, deep)]
    assert len(numbers) == LEVELS - PARTS
    meta = jnp.stack([core, chip, across] + numbers + levels).astype(jnp.int32)

    send, block, send_q, own_q = prepare(k_cache, v_cache, q_pre, core)
    theirs = lax.ppermute(send, "seq", sibling)
    held = {0: join(block, theirs, core)}
    held[0], send_q, meta = lax.optimization_barrier((held[0], send_q, meta))
    near_q = lax.ppermute(send_q, "seq", sibling)

    up, down = ring_perm(chips, 1), ring_perm(chips, -1)
    half = block.shape[0] // 2
    state, early, w_near = None, (), w_out
    soon = far // 2
    for d in range(1, far + 1):
        if d < far:
            held[-d] = lax.ppermute(held[1 - d], "seq", up)
            held[d] = lax.ppermute(held[d - 1], "seq", down)
            last = (held[-d], held[d])
        else:
            last = (
                lax.ppermute(held[1 - d][:half], "seq", up),
                lax.ppermute(held[d - 1][half:], "seq", down),
            )
        if d == 1:
            state = open_sums(own_q, near_q, held[0], meta, lengths)
        else:
            state = stage(state, (held[1 - d], held[d - 1]), 2 * d - 3, meta, lengths)
        if d == soon + 1:
            seen = [held[o] for o in order[: 2 * soon + 1]]
            early = early_decode(
                q_dec, k_new, v_new, block_table, seen, len(order), own, meta
            )
        last, state, early, w_near = lax.optimization_barrier((last, state, early, w_near))
        if d == 1:
            weights = w_near.T
            w_near = lax.ppermute(take_other_half(weights, meta), "seq", sibling)
        if d < far:
            held[-d], held[d] = last
    blocks = [held[o] for o in order[:-1]]
    attn_own = late_decode(early, blocks, last, len(seen), own, steps, meta)

    pieces = [attn_own]
    for d in range(1, deep):
        perm = [(index(*p), index((p[0] + d) % deep, p[1], p[2])) for p in everyone]
        pieces.append(lax.ppermute(attn_own, "seq", perm))
    attn_own, state = lax.optimization_barrier((attn_own, state))
    near = close_sums(state, blocks, last, meta, lengths, True)
    back = lax.ppermute(near, "seq", sibling)
    pre_out = close_sums(state, blocks, last, meta, lengths, False)
    pieces[-1], pre_out, back = lax.optimization_barrier((pieces[-1], pre_out, back))
    pre_out = settle(pre_out, back, meta)

    total, *sent = project(pieces, weights, w_near, meta)
    for piece, (dc, dx) in zip(sent, ((1, 0), (0, 1), (1, 1))):
        perm = [
            (i * 2 + x, (i ^ dc) * 2 + (x ^ dx)) for i in range(n) for x in range(2)
        ]
        total = total + lax.ppermute(piece, ("seq", "tp"), perm).astype(jnp.float32)
    dec_out = total.astype(jnp.bfloat16).T.reshape(deep // 2, steps, own, -1)
    return (pre_out, dec_out.transpose(0, 2, 1, 3).reshape(rows // 2, steps, -1))


def per_device(n, tp, q_pre, k_cache, v_cache, prompt_lengths, *rest):
    groups = k_cache.shape[1] // HD
    square = groups % 2 == 0 and k_cache.shape[1] == 2 * k_cache.shape[0]
    form = split_heads if square and tp == 2 and n == 2 * (LEVELS - PARTS) else whole_heads
    return form(n, q_pre, k_cache, v_cache, prompt_lengths.astype(jnp.int32), *rest)


def solution(mesh):
    placed = (
        P("seq", "tp"),
        P("seq", "tp"),
        P("seq", "tp"),
        P(),
        P(None, None, "tp"),
        P(None, None, "tp"),
        P(None, None, "tp"),
        P(),
        P("tp", "seq"),
    )
    return jax.shard_map(
        functools.partial(per_device, mesh.shape["seq"], mesh.shape["tp"]),
        mesh=mesh,
        in_specs=placed,
        out_specs=(P("seq", "tp"), P("tp", None, "seq")),
        check_vma=False,
    )
```

```python
import functools
import math

import jax
import jax.numpy as jnp
from jax import lax
from jax.experimental import pallas as pl
from jax.experimental.pallas import tpu as pltpu
from jax.sharding import PartitionSpec as P

H = 56
KVH = 8
HD = 128
BLK = 64
SPAN = 512
PAIR = 2
NEG = -1e30
LEAST, MOST = 2.0**-60, 2.0**100
FACTOR = math.log2(math.e) / math.sqrt(HD)
ROOM = 16 * 1024 * 1024
LITTLE = 4 * 1024 * 1024
CORE, CHIP, ACROSS, PARTS, LEVELS = 0, 1, 2, 3, 11
HBM = pl.BlockSpec(memory_space=pltpu.HBM)
VMEM = pl.BlockSpec(memory_space=pltpu.VMEM)
SMEM = pl.BlockSpec(memory_space=pltpu.SMEM)


def dot_nt(a, b):
    return lax.dot_general(a, b, (((1,), (1,)), ((), ())), preferred_element_type=jnp.float32)


def dot_nn(a, b):
    return lax.dot_general(a, b, (((1,), (0,)), ((), ())), preferred_element_type=jnp.float32)


def fold(x, op):
    out = x[:, :HD]
    for i in range(1, x.shape[1] // HD):
        out = op(out, x[:, i * HD : (i + 1) * HD])
    return out


def start_of(position, lengths):
    end = jnp.int32(0)
    out = jnp.zeros_like(position)
    for i in range(lengths.shape[0]):
        end = end + lengths[i]
        out = jnp.where(position >= end, end, out)
    return out


def sound(total):
    return (jnp.min(total) >= LEAST) & (jnp.max(total) <= MOST)


def prefill_kernel(tok, heads, meta, lengths, q, keys_all, values_all, *refs):
    out, qs, peak, total, acc = refs[-5:]
    for j in range(heads):
        qs[j * tok : (j + 1) * tok] = q[:, j * HD : (j + 1) * HD]
    total[...] = jnp.zeros_like(total)
    acc[...] = jnp.zeros_like(acc)

    begin = meta[0]
    finish = begin + tok
    low = start_of(begin, lengths)
    high = start_of(finish - 1, lengths)
    blocks = lax.div(finish - low + SPAN - 1, SPAN)
    clear = lax.div(finish - high, SPAN)

    def first_of(k):
        return jnp.maximum(finish - (k + 1) * SPAN, 0)

    def load(k):
        here = pl.ds(pl.multiple_of(first_of(k), HD), SPAN)
        return keys_all[:, here], values_all[here, :]

    def allowed_in(k):
        t = begin + lax.broadcasted_iota(jnp.int32, (tok, 1), 0)
        u = first_of(k) + lax.broadcasted_iota(jnp.int32, (tok, SPAN), 1)
        last = jnp.minimum(t, finish - k * SPAN - 1)
        return (u <= last) & (u >= start_of(t, lengths))

    def keep(allowed, x, other):
        some = x.shape[0] // tok
        return jnp.where(allowed[None], x.reshape(some, tok, SPAN), other).reshape(x.shape)

    def block(k, masked):
        keys, values = load(k)
        allowed = allowed_in(k) if masked else None
        for j in range(0, heads, PAIR):
            here = slice(j * tok, min(j + PAIR, heads) * tok)
            p = jnp.exp2(dot_nn(qs[here], keys) * FACTOR)
            if masked:
                p = keep(allowed, p, 0.0)
            total[here] += fold(p, jnp.add)
            acc[here] += dot_nn(p.astype(jnp.bfloat16), values)

    block(0, True)

    @pl.loop(1, jnp.maximum(clear, 1))
    def _(k):
        block(k, False)

    @pl.loop(jnp.maximum(clear, 1), blocks)
    def _(k):
        block(k, True)

    def write():
        whole = jnp.sum(total[...], axis=1, keepdims=True)
        result = (acc[...] / whole).astype(out.dtype)
        for j in range(heads):
            out[:, j * HD : (j + 1) * HD] = result[j * tok : (j + 1) * tok]
        return whole

    fine = sound(write())

    @pl.when(jnp.logical_not(fine))
    def _():
        peak[...] = jnp.full_like(peak, NEG)
        total[...] = jnp.zeros_like(total)
        acc[...] = jnp.zeros_like(acc)

        @pl.loop(0, blocks)
        def _(k):
            keys, values = load(k)
            allowed = allowed_in(k)

            @pl.loop(0, heads)
            def _(j):
                here = pl.ds(pl.multiple_of(j * tok, tok), tok)
                s = jnp.where(allowed, dot_nn(qs[here], keys) * FACTOR, NEG)
                top = jnp.maximum(peak[here], jnp.max(s, axis=1, keepdims=True))
                p = jnp.where(allowed, jnp.exp2(s - top[:, :1]), 0.0)
                shrink = jnp.exp2(peak[here] - top)
                total[here] = total[here] * shrink + fold(p, jnp.add)
                acc[here] = acc[here] * shrink + dot_nn(p.astype(jnp.bfloat16), values)
                peak[here] = top

        write()


def prefill(q, keys, values, meta, lengths, groups, columns, name, before=None):
    tok = q.shape[0]
    count = values.shape[0]
    heads = H // KVH
    rows = heads * tok
    pairs = rows * count // 2 * groups
    extra = [] if before is None else [before]
    return pl.pallas_call(
        functools.partial(prefill_kernel, tok, heads),
        out_shape=jax.ShapeDtypeStruct((tok, columns), jnp.bfloat16),
        grid_spec=pltpu.PrefetchScalarGridSpec(
            num_scalar_prefetch=2,
            grid=(groups,),
            in_specs=[
                pl.BlockSpec((tok, heads * HD), lambda g, meta, lengths: (0, meta[1] + g)),
                pl.BlockSpec((HD, count), lambda g, meta, lengths: (meta[2] + g, 0)),
                pl.BlockSpec((count, HD), lambda g, meta, lengths: (0, meta[2] + g)),
            ]
            + [HBM] * len(extra),
            out_specs=pl.BlockSpec((tok, heads * HD), lambda g, meta, lengths: (0, meta[3] + g)),
            scratch_shapes=[
                pltpu.VMEM((rows, HD), jnp.bfloat16),
                pltpu.VMEM((rows, HD), jnp.float32),
                pltpu.VMEM((rows, HD), jnp.float32),
                pltpu.VMEM((rows, HD), jnp.float32),
            ],
        ),
        compiler_params=pltpu.CompilerParams(vmem_limit_bytes=ROOM),
        cost_estimate=pl.CostEstimate(
            flops=pairs * HD * 8, bytes_accessed=count * HD * 4 * groups, transcendentals=pairs
        ),
        input_output_aliases={} if before is None else {5: 0},
        name=name,
    )(meta, lengths, q, keys, values, *extra)


def settle_kernel(meta, piece, whole, out, sem):
    width = piece.shape[1]
    where = pl.ds(pl.multiple_of((1 - meta[CORE]) * width, width), width)
    copy = pltpu.make_async_copy(piece, out.at[:, where], sem)
    copy.start()
    copy.wait()


def settle(whole, piece, meta):
    return pl.pallas_call(
        settle_kernel,
        out_shape=jax.ShapeDtypeStruct(whole.shape, whole.dtype),
        in_specs=[SMEM, VMEM, HBM],
        out_specs=HBM,
        scratch_shapes=[pltpu.SemaphoreType.DMA],
        input_output_aliases={2: 0},
        compiler_params=pltpu.CompilerParams(vmem_limit_bytes=LITTLE),
        cost_estimate=pl.CostEstimate(flops=0, bytes_accessed=piece.size * 4, transcendentals=0),
        name="settle",
    )(meta, piece, whole)


def allowed_at(first, base, tok, length, lengths):
    t = first + lax.broadcasted_iota(jnp.int32, (tok, 1), 0)
    u = base + lax.broadcasted_iota(jnp.int32, (tok, length), 1)
    return (u <= t) & (u >= start_of(t, lengths))


def column_block(at):
    return pl.ds(pl.multiple_of(at, HD), HD)


def keys_of(upper, g):
    return upper[column_block(g * HD), :]


def values_of(lower, g):
    half = lower.shape[1] // 2
    both = [lower[:, column_block(side * half + g * HD)] for side in range(2)]
    return jnp.concatenate(both, axis=0)


def add_block(tok, heads, q_at, keys, values, allowed, sums, fresh=False):
    length = keys.shape[1]
    for j in range(0, heads, PAIR):
        some = min(PAIR, heads - j)
        p = jnp.exp2(dot_nn(q_at(j * tok, some * tok), keys) * FACTOR)
        if allowed is not None:
            p = p.reshape(some, tok, length)
            p = jnp.where(allowed[None], p, 0.0).reshape(some * tok, length)
        more = (fold(p, jnp.add), dot_nn(p.astype(jnp.bfloat16), values))
        for ref, value in zip(sums, more):
            here = slice(j * tok, (j + some) * tok)
            ref[here] = value if fresh else ref[here] + value


def relation(meta, part, side, tok, lengths):
    first = (meta[CHIP] * 2 + side) * tok
    base = meta[PARTS + part] * 2 * tok
    relevant = (base < first) & (meta[PARTS + part] != meta[CHIP])
    relevant = relevant & (base + 2 * tok > start_of(first, lengths))
    return relevant, base >= start_of(first + tok - 1, lengths), first, base


def side_rows(side, heads, tok):
    return pl.ds(pl.multiple_of(side * (heads * tok), HD), heads * tok)


def open_kernel(tok, heads, groups, meta, lengths, q_own, q_near, block, qs, total, acc):
    core = meta[CORE]
    rows = heads * tok
    for source, side in ((q_own, core), (q_near, 1 - core)):
        for g in range(groups):
            for j in range(heads):
                at = pl.ds(pl.multiple_of(side * rows + j * tok, HD), tok)
                first = (g * heads + j) * HD
                qs[g, at] = source[:, first : first + HD]
    upper, lower = block.at[: block.shape[0] // 2], block.at[block.shape[0] // 2 :]

    @pl.loop(0, groups)
    def _(g):
        keys, values = keys_of(upper, g), values_of(lower, g)
        for side in range(2):
            length = (side + 1) * tok
            first = (meta[CHIP] * 2 + side) * tok
            allowed = allowed_at(first, meta[CHIP] * 2 * tok, tok, length, lengths)
            here = side_rows(side, heads, tok)
            q_at = lambda at, count: qs[g, pl.ds(side * rows + at, count)]
            add_block(tok, heads, q_at, keys[:, :length], values[:length], allowed,
                      (total.at[g, here], acc.at[g, here]), True)


def open_sums(q_own, q_near, block, meta, lengths):
    tok = q_own.shape[0]
    heads = H // KVH
    groups = q_own.shape[1] // (heads * HD)
    rows = 2 * heads * tok
    sums = jax.ShapeDtypeStruct((groups, rows, HD), jnp.float32)
    pairs = groups * rows * tok * 2
    return pl.pallas_call(
        functools.partial(open_kernel, tok, heads, groups),
        out_shape=[jax.ShapeDtypeStruct((groups, rows, HD), jnp.bfloat16), sums, sums],
        in_specs=[SMEM, SMEM, VMEM, VMEM, VMEM],
        out_specs=[VMEM] * 3,
        compiler_params=pltpu.CompilerParams(vmem_limit_bytes=2 * LITTLE),
        cost_estimate=pl.CostEstimate(
            flops=pairs * HD * 8, bytes_accessed=q_own.size * 2, transcendentals=pairs
        ),
        name="open",
    )(meta, lengths, q_own, q_near, block)


def stage_kernel(tok, heads, groups, first_part, meta, lengths, qs, total_in, acc_in, one, two, total, acc, held):
    held[0], held[1] = one[...], two[...]
    half = held.shape[1] // 2

    @pl.loop(0, 4 * groups)
    def _(step):
        which, rest = lax.div(step, 2 * groups), lax.rem(step, 2 * groups)
        g, side = lax.div(rest, 2), lax.rem(rest, 2)
        relevant, clear, first, base = relation(meta, first_part + which, side, tok, lengths)
        here = side_rows(side, heads, tok)
        sums = (total.at[g, here], acc.at[g, here])
        at = side * (heads * tok)
        q_at = lambda off, count: qs[g, pl.ds(pl.multiple_of(at + off, HD), count)]
        upper, lower = held.at[which, :half], held.at[which, half:]

        @pl.when(relevant & clear)
        def _():
            add_block(tok, heads, q_at, keys_of(upper, g), values_of(lower, g), None, sums)

        @pl.when(relevant & jnp.logical_not(clear))
        def _():
            allowed = allowed_at(first, base, tok, 2 * tok, lengths)
            add_block(tok, heads, q_at, keys_of(upper, g), values_of(lower, g), allowed, sums)


def stage(state, pair, first_part, meta, lengths):
    qs, total, acc = state
    groups, rows, unused = qs.shape
    tok = pair[0].shape[1] // 2
    pairs = groups * rows * tok * 2
    new = pl.pallas_call(
        functools.partial(stage_kernel, tok, rows // (2 * tok), groups, first_part),
        out_shape=[jax.ShapeDtypeStruct(x.shape, x.dtype) for x in (total, acc)],
        in_specs=[SMEM, SMEM] + [VMEM] * 5,
        out_specs=[VMEM] * 2,
        scratch_shapes=[pltpu.VMEM((2, *pair[0].shape), pair[0].dtype)],
        input_output_aliases={3: 0, 4: 1},
        compiler_params=pltpu.CompilerParams(vmem_limit_bytes=2 * LITTLE),
        cost_estimate=pl.CostEstimate(
            flops=pairs * HD * 8, bytes_accessed=tok * HD, transcendentals=pairs
        ),
        name=f"stage{first_part}",
    )(meta, lengths, qs, total, acc, *pair)
    return qs, *new


def finish_kernel(tok, heads, groups, done, meta, lengths, qs, total, acc, *refs):
    parts = len(refs) - 10
    blocks, last = refs[:parts], refs[parts : parts + 2]
    near, out, held, peak, total_now, acc_now, result, sem = refs[parts + 2 :]
    rows = heads * tok
    core = meta[CORE]
    half = held.shape[1] // 2

    def fill(first):
        for i in range(first, parts):
            held[i] = blocks[i][...]
        held[parts, :half] = last[0][...]
        held[parts, half:] = last[1][...]

    def turn_of(step):
        turn, g = lax.div(step, groups), lax.rem(step, groups)
        side = jnp.where(turn == 0, 1 - core, core)
        at = side * rows
        q_at = lambda off, count: qs[g, pl.ds(pl.multiple_of(at + off, HD), count)]
        return turn, g, side, q_at

    def write(turn, g):
        whole = jnp.sum(total_now[...], axis=1, keepdims=True)
        value = (acc_now[...] / whole).astype(result.dtype)
        for j in range(heads):
            result[turn, :, column_block((g * heads + j) * HD)] = value[j * tok : (j + 1) * tok]
        return sound(whole)

    def one_turn(step, fine):
        turn, g, side, q_at = turn_of(step)
        here = side_rows(side, heads, tok)
        total_now[...] = total[g, here]
        acc_now[...] = acc[g, here]

        @pl.loop(done, parts + 1)
        def _(i):
            relevant, clear, first, base = relation(meta, i, side, tok, lengths)
            upper, lower = held.at[i, :half], held.at[i, half:]
            sums = (total_now, acc_now)

            @pl.when(relevant & clear)
            def _():
                add_block(tok, heads, q_at, keys_of(upper, g), values_of(lower, g), None, sums)

            @pl.when(relevant & jnp.logical_not(clear))
            def _():
                allowed = allowed_at(first, base, tok, 2 * tok, lengths)
                add_block(tok, heads, q_at, keys_of(upper, g), values_of(lower, g), allowed, sums)

        return fine & write(turn, g).astype(jnp.int32)

    fill(done)
    fine = lax.fori_loop(0, 2 * groups, one_turn, jnp.int32(1))

    @pl.when(fine == 0)
    def _():
        fill(0)

        @pl.loop(0, 2 * groups)
        def _(step):
            turn, g, side, q_at = turn_of(step)
            first = (meta[CHIP] * 2 + side) * tok
            peak[...] = jnp.full_like(peak, NEG)
            total_now[...] = jnp.zeros_like(total_now)
            acc_now[...] = jnp.zeros_like(acc_now)

            @pl.loop(0, (parts + 1) * heads)
            def _(step):
                i, j = lax.div(step, heads), lax.rem(step, heads)
                keys = keys_of(held.at[i, :half], g)
                values = values_of(held.at[i, half:], g)
                allowed = allowed_at(first, meta[PARTS + i] * 2 * tok, tok, 2 * tok, lengths)
                mine = pl.ds(pl.multiple_of(j * tok, tok), tok)
                s = jnp.where(allowed, dot_nn(q_at(j * tok, tok), keys) * FACTOR, NEG)
                top = jnp.maximum(peak[mine], jnp.max(s, axis=1, keepdims=True))
                p = jnp.where(allowed, jnp.exp2(s - top[:, :1]), 0.0)
                shrink = jnp.exp2(peak[mine] - top)
                total_now[mine] = total_now[mine] * shrink + fold(p, jnp.add)
                acc_now[mine] = acc_now[mine] * shrink + dot_nn(p.astype(jnp.bfloat16), values)
                peak[mine] = top

            write(turn, g)

    width = near.shape[1]
    where = pl.ds(pl.multiple_of(core * width, width), width)
    copy = pltpu.make_async_copy(result.at[1], out.at[:, where], sem)
    copy.start()
    near[...] = result[0]
    copy.wait()


def finish(state, blocks, last, done, meta, lengths):
    qs, total, acc = state
    groups, rows, unused = qs.shape
    tok = last[0].shape[1] // 2
    heads = rows // (2 * tok)
    width = groups * heads * HD
    sums = pltpu.VMEM((heads * tok, HD), jnp.float32)
    return pl.pallas_call(
        functools.partial(finish_kernel, tok, heads, groups, done),
        out_shape=[
            jax.ShapeDtypeStruct((tok, width), jnp.bfloat16),
            jax.ShapeDtypeStruct((tok, 2 * width), jnp.bfloat16),
        ],
        in_specs=[SMEM, SMEM] + [VMEM] * (5 + len(blocks)),
        out_specs=[VMEM, HBM],
        scratch_shapes=[
            pltpu.VMEM((len(blocks) + 1, *blocks[0].shape), blocks[0].dtype),
            sums, sums, sums,
            pltpu.VMEM((2, tok, width), jnp.bfloat16),
            pltpu.SemaphoreType.DMA,
        ],
        compiler_params=pltpu.CompilerParams(vmem_limit_bytes=ROOM),
        cost_estimate=pl.CostEstimate(
            flops=groups * rows * tok * HD * 8, bytes_accessed=tok * width * 4,
            transcendentals=groups * rows * tok * 2,
        ),
        name="finish",
    )(meta, lengths, qs, total, acc, *blocks, *last)


def request_sums(query, keys, values, mask):
    p = jnp.exp2(dot_nn(query, keys) * FACTOR)
    p = jnp.where(mask[None], p.reshape(-1, *mask.shape), 0.0).reshape(p.shape)
    return fold(p, jnp.add), dot_nn(p.astype(jnp.bfloat16), values)


def fresh_scores(query, newk, own):
    s = dot_nt(query, newk) * FACTOR
    size = newk.shape[0]
    row = lax.broadcasted_iota(jnp.int32, (size, size), 0)
    col = lax.broadcasted_iota(jnp.int32, (size, size), 1)
    ok = (lax.rem(row, own) == lax.rem(col, own)) & (lax.div(col, own) <= lax.div(row, own))
    return s.reshape(-1, size, size), ok


def requests_kernel(own, heads, groups, length, meta, q_dec, k_new, v_new, table, *refs):
    total, acc, query, newk, newv, mask, q3, k3, v3, sems = refs
    steps = q3.shape[1]
    core, level = meta[CORE], lax.div(meta[CHIP], 2)
    requests = pl.ds(level * own, own)
    copies = []
    for i, (source, held) in enumerate(((q_dec, q3), (k_new, k3), (v_new, v3))):
        width = held.shape[2]
        where = pl.ds(pl.multiple_of(core * width, width), width)
        copies.append(pltpu.make_async_copy(source.at[requests, :, where], held, sems.at[i]))
    for copy in copies:
        copy.start()
    rows = table[pl.ds(pl.multiple_of(level * own, own), own), :]
    lane = lax.div(lax.broadcasted_iota(jnp.int32, (own, length), 1), BLK)
    for i in range(mask.shape[1] // length):
        number = lane + meta[PARTS + i] * (length // BLK)
        hit = rows[:, :1] == number
        for j in range(1, rows.shape[1]):
            hit = hit | (rows[:, j : j + 1] == number)
        mask[:, i * length : (i + 1) * length] = hit.astype(jnp.float32)
    for copy in copies:
        copy.wait()
    for s in range(steps):
        for g in range(groups):
            col = slice(g * HD, (g + 1) * HD)
            at = slice(s * own, (s + 1) * own)
            newk[at, col] = k3[:, s, col]
            newv[at, col] = v3[:, s, col]
            for j in range(heads):
                first = (g * heads + j) * HD
                row = (j * steps + s) * own
                query[g, row : row + own] = q3[:, s, first : first + HD]

    @pl.loop(0, groups)
    def _(g):
        col = column_block(g * HD)
        s, ok = fresh_scores(query[g], newk[:, col], own)
        p = jnp.where(ok[None], jnp.exp2(s), 0.0).reshape(-1, s.shape[2])
        first = jnp.sum(p, axis=1, keepdims=True)
        lead = lax.broadcasted_iota(jnp.int32, (p.shape[0], HD), 1) == 0
        total[g] = jnp.where(lead, first, 0.0)
        acc[g] = dot_nn(p.astype(jnp.bfloat16), newv[:, col])


def open_requests(q_dec, k_new, v_new, table, length, own, meta):
    heads = H // KVH
    steps = q_dec.shape[1]
    width = k_new.shape[2] // 2
    groups = width // HD
    rows = heads * own * steps
    sums = jax.ShapeDtypeStruct((groups, rows, HD), jnp.float32)
    new = jax.ShapeDtypeStruct((own * steps, width), jnp.bfloat16)
    return pl.pallas_call(
        functools.partial(requests_kernel, own, heads, groups, length),
        out_shape=[
            sums, sums, jax.ShapeDtypeStruct((groups, rows, HD), jnp.bfloat16), new, new,
            jax.ShapeDtypeStruct((own, (LEVELS - PARTS) * length), jnp.float32),
        ],
        in_specs=[SMEM] + [HBM] * 3 + [VMEM],
        out_specs=[VMEM] * 6,
        scratch_shapes=[
            pltpu.VMEM((own, steps, groups * heads * HD), jnp.bfloat16),
            pltpu.VMEM((own, steps, width), jnp.bfloat16),
            pltpu.VMEM((own, steps, width), jnp.bfloat16),
            pltpu.SemaphoreType.DMA((3,)),
        ],
        compiler_params=pltpu.CompilerParams(vmem_limit_bytes=LITTLE),
        cost_estimate=pl.CostEstimate(
            flops=groups * rows * own * steps * HD * 4, bytes_accessed=rows * HD * 8,
            transcendentals=groups * rows * own * steps,
        ),
        name="requests",
    )(meta, q_dec, k_new, v_new, table)


def early_kernel(groups, total_in, acc_in, query, mask, *refs):
    blocks, (total, acc) = refs[:-2], refs[-2:]
    half, length = blocks[0].shape[0] // 2, blocks[0].shape[1]

    @pl.loop(0, groups)
    def _(g):
        sums = [total[g], acc[g]]
        for i, block in enumerate(blocks):
            open_to = mask[:, i * length : (i + 1) * length] > 0
            keys, values = keys_of(block.at[:half], g), values_of(block.at[half:], g)
            more = request_sums(query[g], keys, values, open_to)
            sums = [x + y for x, y in zip(sums, more)]
        total[g], acc[g] = sums


def early_decode(state, blocks):
    total, acc, query, newk, newv, mask = state
    groups, rows, unused = query.shape
    pairs = groups * rows * len(blocks) * blocks[0].shape[1]
    sums = jax.ShapeDtypeStruct(total.shape, total.dtype)
    new = pl.pallas_call(
        functools.partial(early_kernel, groups),
        out_shape=[sums, sums],
        in_specs=[VMEM] * (4 + len(blocks)),
        out_specs=[VMEM] * 2,
        input_output_aliases={0: 0, 1: 1},
        compiler_params=pltpu.CompilerParams(vmem_limit_bytes=2 * LITTLE),
        cost_estimate=pl.CostEstimate(
            flops=pairs * HD * 8, bytes_accessed=rows * HD, transcendentals=pairs
        ),
        name="early_decode",
    )(total, acc, query, mask, *blocks)
    return [*new, query, newk, newv, mask]


def late_kernel(own, steps, heads, groups, done, meta, total, acc, query, newk, newv, mask, *refs):
    parts = len(refs) - 5
    blocks, last = refs[:parts], refs[parts : parts + 2]
    out, held, scores = refs[parts + 2 :]
    length = blocks[0].shape[1]
    half = blocks[0].shape[0] // 2
    size = own * steps

    def write(g, sums, whole):
        result = (sums / whole).astype(out.dtype)
        for j in range(heads):
            out[:, column_block((g * heads + j) * HD)] = result[j * size : (j + 1) * size]

    def one_group(g, fine):
        sums = [total[g], acc[g]]
        for i in range(done, parts + 1):
            upper = last[0] if i == parts else blocks[i].at[:half]
            lower = last[1] if i == parts else blocks[i].at[half:]
            open_to = mask[:, i * length : (i + 1) * length] > 0
            more = request_sums(query[g], keys_of(upper, g), values_of(lower, g), open_to)
            sums = [x + y for x, y in zip(sums, more)]
        whole = jnp.sum(sums[0], axis=1, keepdims=True)
        write(g, sums[1], whole)
        return fine & sound(whole).astype(jnp.int32)

    fine = lax.fori_loop(0, groups, one_group, jnp.int32(1))

    @pl.when(fine == 0)
    def _():
        for i in range(parts):
            held[i] = blocks[i][...]
        held[parts, :half] = last[0][...]
        held[parts, half:] = last[1][...]

        @pl.loop(0, groups)
        def _(g):
            col = column_block(g * HD)
            fresh, ok = fresh_scores(query[g], newk[:, col], own)
            fresh = jnp.where(ok[None], fresh, NEG).reshape(-1, size)
            rows = fresh.shape[0]

            def score(i, top):
                s = dot_nn(query[g], keys_of(held.at[i, :half], g)) * FACTOR
                where = pl.ds(pl.multiple_of(i * length, length), length)
                open_to = mask[:, where] > 0
                s = jnp.where(open_to[None], s.reshape(-1, own, length), NEG).reshape(s.shape)
                scores[:, where] = s
                return jnp.maximum(top, jnp.max(s, axis=1, keepdims=True))

            top = lax.fori_loop(0, parts + 1, score, jnp.max(fresh, axis=1, keepdims=True))
            p = jnp.exp2(fresh - top)

            def weigh(i, sums):
                where = pl.ds(pl.multiple_of(i * length, length), length)
                p = jnp.exp2(scores[:, where] - top)
                values = values_of(held.at[i, half:], g)
                return (
                    sums[0] + jnp.sum(p, axis=1, keepdims=True),
                    sums[1] + dot_nn(p.astype(jnp.bfloat16), values),
                )

            start = (
                jnp.sum(p, axis=1, keepdims=True),
                dot_nn(p.astype(jnp.bfloat16), newv[:, col]),
            )
            whole, sums = lax.fori_loop(0, parts + 1, weigh, start)
            write(g, sums, whole)


def late_decode(early, blocks, last, done, own, steps, meta):
    groups, rows, unused = early[0].shape
    heads = H // KVH
    parts, length = len(blocks) + 1, blocks[0].shape[1]
    pairs = groups * rows * (parts - done) * length
    return pl.pallas_call(
        functools.partial(late_kernel, own, steps, heads, groups, done),
        out_shape=jax.ShapeDtypeStruct((own * steps, groups * heads * HD), jnp.bfloat16),
        in_specs=[SMEM] + [VMEM] * (len(early) + len(blocks) + 2),
        out_specs=VMEM,
        scratch_shapes=[
            pltpu.VMEM((parts, *blocks[0].shape), blocks[0].dtype),
            pltpu.VMEM((rows, parts * length), jnp.float32),
        ],
        compiler_params=pltpu.CompilerParams(vmem_limit_bytes=ROOM + ROOM // 4),
        cost_estimate=pl.CostEstimate(
            flops=pairs * HD * 8, bytes_accessed=rows * HD, transcendentals=pairs
        ),
        name="late_decode",
    )(meta, *early, *blocks, *last)


def decode_kernel(parts, steps, heads, groups, starts, q, mask, newk, newv, *refs):
    kheld, vheld = refs[:parts], refs[parts : 2 * parts]
    out, kall, vall, sems, scores = refs[2 * parts :]
    own = q.shape[0]
    rows = heads * own
    length = kheld[0].shape[1]
    copies = []
    for i in range(parts):
        where = pl.ds(pl.multiple_of(starts[i], HD), length)
        copies.append(pltpu.make_async_copy(kheld[i], kall.at[:, where], sems.at[2 * i]))
        copies.append(pltpu.make_async_copy(vheld[i], vall.at[where], sems.at[2 * i + 1]))
    for copy in copies:
        copy.start()
    row = lax.broadcasted_iota(jnp.int32, (own, own), 0)
    col = lax.broadcasted_iota(jnp.int32, (own, own), 1)
    fresh_ok = (lax.div(row, steps) == lax.div(col, steps)) & (col <= row)

    def columns(g):
        return slice(g * HD, (g + 1) * HD)

    def stacked(g):
        first = g * heads
        slices = [q[:, (first + j) * HD : (first + j + 1) * HD] for j in range(heads)]
        return jnp.concatenate([x.astype(jnp.float32) for x in slices], 0).astype(jnp.bfloat16)

    def keep(allowed, x, other):
        y = x.reshape(heads, own, x.shape[1])
        return jnp.where(allowed[None], y, other).reshape(x.shape)

    def open_to(i):
        return mask[:, pl.ds(pl.multiple_of(starts[i], HD), length)] > 0

    def write(g, acc, whole):
        result = acc / whole
        for j in range(heads):
            out[:, (g * heads + j) * HD : (g * heads + j + 1) * HD] = result[
                j * own : (j + 1) * own
            ].astype(out.dtype)

    fine = None
    for g in range(groups):
        query = stacked(g)
        p = keep(fresh_ok, jnp.exp2(dot_nt(query, newk[:, columns(g)]) * FACTOR), 0.0)
        whole = jnp.sum(p, axis=1, keepdims=True)
        acc = dot_nn(p.astype(jnp.bfloat16), newv[:, columns(g)])
        total = jnp.zeros((rows, HD), jnp.float32)
        for i in range(parts):
            p = jnp.exp2(dot_nn(query, kheld[i][columns(g)]) * FACTOR)
            p = keep(open_to(i), p, 0.0)
            total = total + fold(p, jnp.add)
            acc = acc + dot_nn(p.astype(jnp.bfloat16), vheld[i][:, columns(g)])
        whole = whole + jnp.sum(total, axis=1, keepdims=True)
        write(g, acc, whole)
        fine = sound(whole) if fine is None else fine & sound(whole)

    @pl.when(jnp.logical_not(fine))
    def _():
        for g in range(groups):
            query = stacked(g)
            fresh = keep(fresh_ok, dot_nt(query, newk[:, columns(g)]) * FACTOR, NEG)
            top = jnp.max(fresh, axis=1, keepdims=True)
            for i in range(parts):
                s = keep(open_to(i), dot_nn(query, kheld[i][columns(g)]) * FACTOR, NEG)
                scores[:, i * length : (i + 1) * length] = s
                top = jnp.maximum(top, jnp.max(s, axis=1, keepdims=True))
            p = jnp.exp2(fresh - top)
            whole = jnp.sum(p, axis=1, keepdims=True)
            acc = dot_nn(p.astype(jnp.bfloat16), newv[:, columns(g)])
            for i in range(parts):
                p = jnp.exp2(scores[:, i * length : (i + 1) * length] - top)
                whole = whole + jnp.sum(p, axis=1, keepdims=True)
                acc = acc + dot_nn(p.astype(jnp.bfloat16), vheld[i][:, columns(g)])
            write(g, acc, whole)

    for copy in copies:
        copy.wait()


def decode(q, mask, newk, newv, kparts, vparts, starts, steps):
    own = q.shape[0]
    parts = len(kparts)
    length, width = vparts[0].shape
    count = parts * length
    heads = H // KVH
    groups = width // HD
    rows = heads * own
    pairs = groups * rows * count
    return pl.pallas_call(
        functools.partial(decode_kernel, parts, steps, heads, groups),
        out_shape=[
            jax.ShapeDtypeStruct(q.shape, jnp.bfloat16),
            jax.ShapeDtypeStruct((width, count), jnp.bfloat16),
            jax.ShapeDtypeStruct((count, width), jnp.bfloat16),
        ],
        grid_spec=pltpu.PrefetchScalarGridSpec(
            num_scalar_prefetch=1,
            grid=(),
            in_specs=[VMEM] * (4 + 2 * parts),
            out_specs=[VMEM, HBM, HBM],
            scratch_shapes=[
                pltpu.SemaphoreType.DMA((2 * parts,)),
                pltpu.VMEM((rows, count), jnp.float32),
            ],
        ),
        compiler_params=pltpu.CompilerParams(vmem_limit_bytes=ROOM),
        cost_estimate=pl.CostEstimate(
            flops=pairs * HD * 4, bytes_accessed=count * width * 4, transcendentals=pairs
        ),
        name="decode",
    )(starts, q, mask, newk, newv, *kparts, *vparts)


def prepare_kernel(meta, k, v, q, send, block, send_q, own_q, sems):
    tok, width = k.shape[0], k.shape[1] // 2
    core = meta[0]
    columns = own_q.shape[1]
    copies = []
    for i, (which, held) in enumerate(((1 - core, send_q), (core, own_q))):
        where = pl.ds(pl.multiple_of(which * columns, columns), columns)
        copies.append(pltpu.make_async_copy(q.at[:, where], held, sems.at[i]))
    for copy in copies:
        copy.start()
    mine = pl.ds(pl.multiple_of(core * width, width), width)
    other = pl.ds(pl.multiple_of((1 - core) * width, width), width)
    here = pl.ds(pl.multiple_of(core * tok, tok), tok)
    send[:width] = k[:, other].astype(jnp.float32).T.astype(send.dtype)
    send[width:] = v[:, other]
    block[:width, here] = k[:, mine].astype(jnp.float32).T.astype(block.dtype)
    block[width:, mine] = v[:, mine]
    for copy in copies:
        copy.wait()


def prepare(k, v, q, core):
    tok, width = k.shape[0], k.shape[1] // 2
    assert tok == width
    halves = jax.ShapeDtypeStruct((tok, q.shape[1] // 2), q.dtype)
    return pl.pallas_call(
        prepare_kernel,
        out_shape=[
            jax.ShapeDtypeStruct((2 * tok, width), k.dtype),
            jax.ShapeDtypeStruct((2 * width, 2 * tok), k.dtype),
            halves,
            halves,
        ],
        in_specs=[SMEM, VMEM, VMEM, HBM],
        out_specs=[VMEM] * 4,
        scratch_shapes=[pltpu.SemaphoreType.DMA((2,))],
        compiler_params=pltpu.CompilerParams(vmem_limit_bytes=LITTLE),
        name="prepare",
    )(core[None], k, v, q)


def join_kernel(meta, block_in, theirs, block):
    width = theirs.shape[1]
    other = pl.ds(pl.multiple_of((1 - meta[0]) * width, width), width)
    block[:width, other] = theirs[:width]
    block[width:, other] = theirs[width:]


def join(block, theirs, core):
    return pl.pallas_call(
        join_kernel,
        out_shape=jax.ShapeDtypeStruct(block.shape, block.dtype),
        in_specs=[SMEM, VMEM, VMEM],
        out_specs=VMEM,
        input_output_aliases={1: 0},
        compiler_params=pltpu.CompilerParams(vmem_limit_bytes=LITTLE),
        name="join",
    )(core[None], block, theirs)


def take_kernel(meta, whole, out, sem):
    width = out.shape[1]
    where = pl.ds(pl.multiple_of((1 - meta[CORE]) * width, width), width)
    copy = pltpu.make_async_copy(whole.at[:, where], out, sem)
    copy.start()
    copy.wait()


def take_other_half(whole, meta):
    return pl.pallas_call(
        take_kernel,
        out_shape=jax.ShapeDtypeStruct((whole.shape[0], whole.shape[1] // 2), whole.dtype),
        in_specs=[SMEM, HBM],
        out_specs=VMEM,
        scratch_shapes=[pltpu.SemaphoreType.DMA],
        compiler_params=pltpu.CompilerParams(vmem_limit_bytes=LITTLE),
        name="take",
    )(meta, whole)


def project_kernel(meta, *refs):
    pieces, (whole, other), outs, (sorted_rows,) = refs[:-7], refs[-7:-5], refs[-5:-1], refs[-1:]
    parts = len(pieces)
    rows = pieces[0].shape[0]
    for i, piece in enumerate(pieces):
        at = pl.ds(pl.multiple_of(meta[LEVELS + i] * rows, rows), rows)
        sorted_rows[at] = piece[...]
    depth = other.shape[1]
    mine = whole[:, pl.ds(pl.multiple_of(meta[CORE] * depth, depth), depth)]
    half = parts * rows // 2
    here = pl.ds(pl.multiple_of(meta[ACROSS] * half, half), half)
    there = pl.ds(pl.multiple_of((1 - meta[ACROSS]) * half, half), half)
    kept, beside, across, corner = outs
    for at, near, far in ((here, kept, beside), (there, across, corner)):
        some = sorted_rows[at]
        near[...] = dot_nt(mine, some).astype(near.dtype)
        far[...] = dot_nt(other[...], some).astype(far.dtype)


def project(pieces, whole, other, meta):
    rows = len(pieces) * pieces[0].shape[0]
    width, depth = other.shape
    block = jax.ShapeDtypeStruct((width, rows // 2), jnp.bfloat16)
    return pl.pallas_call(
        project_kernel,
        out_shape=[jax.ShapeDtypeStruct(block.shape, jnp.float32)] + [block] * 3,
        in_specs=[SMEM] + [VMEM] * (len(pieces) + 2),
        out_specs=[VMEM] * 4,
        scratch_shapes=[pltpu.VMEM((rows, depth), jnp.bfloat16)],
        compiler_params=pltpu.CompilerParams(vmem_limit_bytes=2 * LITTLE),
        cost_estimate=pl.CostEstimate(
            flops=rows * width * depth * 4, bytes_accessed=width * depth * 4, transcendentals=0
        ),
        name="project",
    )(meta, *pieces, whole, other)


def index(z, y, c):
    return (z * 2 + y) * 2 + c


def on_ring(r, chips):
    return (r, 0) if r < chips // 2 else (chips - 1 - r, 1)


def ring_perm(chips, d):
    return [
        (index(*on_ring(r, chips), c), index(*on_ring((r + d) % chips, chips), c))
        for r in range(chips)
        for c in range(2)
    ]


def ring_place(r, chips):
    r = lax.rem(r + 2 * chips, chips)
    return jnp.where(r < chips // 2, r * 2, (chips - 1 - r) * 2 + 1)


def spread(x, n):
    place = lax.axis_index("seq")
    deep = n // 4
    everyone = [(z, y, c) for z in range(deep) for y in range(2) for c in range(2)]
    z, y, c = place // 4, (place // 2) % 2, place % 2
    held = [(x, z, y, c)]
    for d in range(1, deep):
        perm = [(index(*p), index((p[0] - d) % deep, p[1], p[2])) for p in everyone]
        held.append((lax.ppermute(x, "seq", perm), lax.rem(z + d, deep), y, c))
    perm = [(index(*p), index(p[0], 1 - p[1], p[2])) for p in everyone]
    held += [(lax.ppermute(b, "seq", perm), bz, 1 - by, bc) for b, bz, by, bc in held]
    perm = [(index(*p), index(p[0], p[1], 1 - p[2])) for p in everyone]
    held += [(lax.ppermute(b, "seq", perm), bz, by, 1 - bc) for b, bz, by, bc in held]
    return [b for b, *_ in held], jnp.stack([index(bz, by, bc) for _, bz, by, bc in held])


def open_blocks(table, steps, count):
    number = lax.broadcasted_iota(jnp.int32, (*table.shape, count), 2) // BLK
    mask = jnp.any(table[:, :, None] == number, axis=1).astype(jnp.float32)
    return jnp.repeat(mask, steps, axis=0)


def whole_heads(n, q_pre, k_cache, v_cache, lengths, q_dec, k_new, v_new, block_table, w_out):
    tok = q_pre.shape[0]
    place = lax.axis_index("seq").astype(jnp.int32)
    rows, steps = q_dec.shape[0], q_dec.shape[1]
    own = rows // n
    kparts, sources = spread(k_cache.T, n)
    vparts, _ = spread(v_cache, n)
    starts = sources.astype(jnp.int32) * tok

    def mine(x):
        y = lax.dynamic_slice_in_dim(x, place * own, own, 0)
        return y.reshape(own * steps, -1) if x.ndim == 3 else y

    mask = open_blocks(mine(block_table), steps, n * tok)
    attn_own, keys, values = decode(
        mine(q_dec), mask, mine(k_new), mine(v_new), kparts, vparts, starts, steps
    )
    attn = lax.all_gather(attn_own, "seq", axis=0, tiled=True)
    flat = jnp.dot(attn, w_out, preferred_element_type=jnp.float32).astype(jnp.bfloat16)
    dec_out = lax.psum_scatter(
        flat.reshape(rows, steps, -1), "tp", scatter_dimension=0, tiled=True
    )
    zero = jnp.zeros((), jnp.int32)
    meta = jnp.stack([place * tok, zero, zero, zero])
    groups = k_cache.shape[1] // HD
    pre_out = prefill(
        q_pre, keys, values, meta, lengths, groups, q_pre.shape[1], "prefill"
    )
    return (pre_out, dec_out)


def split_heads(n, q_pre, k_cache, v_cache, lengths, q_dec, k_new, v_new, block_table, w_out):
    place = lax.axis_index("seq").astype(jnp.int32)
    across = lax.axis_index("tp").astype(jnp.int32)
    core, chip = lax.rem(place, 2), lax.div(place, 2)
    chips = n // 2
    far, deep = chips // 2, chips // 2
    z, y = lax.div(chip, 2), lax.rem(chip, 2)
    r = jnp.where(y == 0, z, chips - 1 - z)
    rows, steps = q_dec.shape[0], q_dec.shape[1]
    own = rows // deep
    sibling = [(i, i ^ 1) for i in range(n)]
    everyone = [(a, b, c) for a in range(deep) for b in range(2) for c in range(2)]

    order = [0] + [o for d in range(1, far) for o in (-d, d)] + [far]
    numbers = [ring_place(r + o, chips) for o in order]
    levels = [z] + [lax.rem(z + deep - d, deep) for d in range(1, deep)]
    assert len(numbers) == LEVELS - PARTS
    meta = jnp.stack([core, chip, across] + numbers + levels).astype(jnp.int32)

    send, block, send_q, own_q = prepare(k_cache, v_cache, q_pre, core)
    theirs = lax.ppermute(send, "seq", sibling)
    held = {0: join(block, theirs, core)}
    held[0], send_q, meta = lax.optimization_barrier((held[0], send_q, meta))
    near_q = lax.ppermute(send_q, "seq", sibling)

    up, down = ring_perm(chips, 1), ring_perm(chips, -1)
    half = block.shape[0] // 2
    w_near = w_out
    for d in range(1, far + 1):
        if d < far:
            held[-d] = lax.ppermute(held[1 - d], "seq", up)
            held[d] = lax.ppermute(held[d - 1], "seq", down)
            last = (held[-d], held[d])
        else:
            last = (
                lax.ppermute(held[1 - d][:half], "seq", up),
                lax.ppermute(held[d - 1][half:], "seq", down),
            )
        if d == 1:
            state = open_sums(own_q, near_q, held[0], meta, lengths)
            early = open_requests(
                q_dec, k_new, v_new, block_table, block.shape[1], own, meta
            )
        elif d < far:
            state = stage(state, (held[1 - d], held[d - 1]), 2 * d - 3, meta, lengths)
        else:
            blocks = [held[o] for o in order[:-1]]
            early = early_decode(early, blocks)
        last, state, early, w_near = lax.optimization_barrier((last, state, early, w_near))
        if d == 1:
            weights = w_near.T
            w_near = lax.ppermute(take_other_half(weights, meta), "seq", sibling)
        if d < far:
            held[-d], held[d] = last
    attn_own = late_decode(early, blocks, last, len(blocks), own, steps, meta)

    pieces = [attn_own]
    for d in range(1, deep):
        perm = [(index(*p), index((p[0] + d) % deep, p[1], p[2])) for p in everyone]
        pieces.append(lax.ppermute(attn_own, "seq", perm))
    attn_own, state = lax.optimization_barrier((attn_own, state))
    near, pre_out = finish(state, blocks, last, 2 * far - 3, meta, lengths)
    pieces, near, pre_out = lax.optimization_barrier((pieces, near, pre_out))
    back = lax.ppermute(near, "seq", sibling)
    pre_out = settle(pre_out, back, meta)

    total, *sent = project(pieces, weights, w_near, meta)
    for piece, (dc, dx) in zip(sent, ((1, 0), (0, 1), (1, 1))):
        perm = [
            (i * 2 + x, (i ^ dc) * 2 + (x ^ dx)) for i in range(n) for x in range(2)
        ]
        total = total + lax.ppermute(piece, ("seq", "tp"), perm).astype(jnp.float32)
    dec_out = total.astype(jnp.bfloat16).T.reshape(deep // 2, steps, own, -1)
    return (pre_out, dec_out.transpose(0, 2, 1, 3).reshape(rows // 2, steps, -1))


def per_device(n, tp, q_pre, k_cache, v_cache, prompt_lengths, *rest):
    groups = k_cache.shape[1] // HD
    square = groups % 2 == 0 and k_cache.shape[1] == 2 * k_cache.shape[0]
    form = split_heads if square and tp == 2 and n == 2 * (LEVELS - PARTS) else whole_heads
    return form(n, q_pre, k_cache, v_cache, prompt_lengths.astype(jnp.int32), *rest)


def solution(mesh):
    placed = (
        P("seq", "tp"),
        P("seq", "tp"),
        P("seq", "tp"),
        P(),
        P(None, None, "tp"),
        P(None, None, "tp"),
        P(None, None, "tp"),
        P(),
        P("tp", "seq"),
    )
    return jax.shard_map(
        functools.partial(per_device, mesh.shape["seq"], mesh.shape["tp"]),
        mesh=mesh,
        in_specs=placed,
        out_specs=(P("seq", "tp"), P("tp", None, "seq")),
        check_vma=False,
    )
```

```python
import functools
import math

import jax
import jax.numpy as jnp
from jax import lax
from jax.experimental import pallas as pl
from jax.experimental.pallas import tpu as pltpu
from jax.sharding import PartitionSpec as P

H = 56
KVH = 8
HD = 128
BLK = 64
SPAN = 512
PAIR = 2
NEG = -1e30
LEAST, MOST = 2.0**-60, 2.0**100
FACTOR = math.log2(math.e) / math.sqrt(HD)
ROOM = 16 * 1024 * 1024
LITTLE = 4 * 1024 * 1024
CORE, CHIP, ACROSS, PARTS, LEVELS = 0, 1, 2, 3, 11
HBM = pl.BlockSpec(memory_space=pltpu.HBM)
VMEM = pl.BlockSpec(memory_space=pltpu.VMEM)
SMEM = pl.BlockSpec(memory_space=pltpu.SMEM)


def dot_nt(a, b):
    return lax.dot_general(a, b, (((1,), (1,)), ((), ())), preferred_element_type=jnp.float32)


def dot_nn(a, b):
    return lax.dot_general(a, b, (((1,), (0,)), ((), ())), preferred_element_type=jnp.float32)


def fold(x, op):
    out = x[:, :HD]
    for i in range(1, x.shape[1] // HD):
        out = op(out, x[:, i * HD : (i + 1) * HD])
    return out


def start_of(position, lengths):
    end = jnp.int32(0)
    out = jnp.zeros_like(position)
    for i in range(lengths.shape[0]):
        end = end + lengths[i]
        out = jnp.where(position >= end, end, out)
    return out


def sound(total):
    return (jnp.min(total) >= LEAST) & (jnp.max(total) <= MOST)


def prefill_kernel(tok, heads, meta, lengths, q, keys_all, values_all, *refs):
    out, qs, peak, total, acc = refs[-5:]
    for j in range(heads):
        qs[j * tok : (j + 1) * tok] = q[:, j * HD : (j + 1) * HD]
    total[...] = jnp.zeros_like(total)
    acc[...] = jnp.zeros_like(acc)

    begin = meta[0]
    finish = begin + tok
    low = start_of(begin, lengths)
    high = start_of(finish - 1, lengths)
    blocks = lax.div(finish - low + SPAN - 1, SPAN)
    clear = lax.div(finish - high, SPAN)

    def first_of(k):
        return jnp.maximum(finish - (k + 1) * SPAN, 0)

    def load(k):
        here = pl.ds(pl.multiple_of(first_of(k), HD), SPAN)
        return keys_all[:, here], values_all[here, :]

    def allowed_in(k):
        t = begin + lax.broadcasted_iota(jnp.int32, (tok, 1), 0)
        u = first_of(k) + lax.broadcasted_iota(jnp.int32, (tok, SPAN), 1)
        last = jnp.minimum(t, finish - k * SPAN - 1)
        return (u <= last) & (u >= start_of(t, lengths))

    def keep(allowed, x, other):
        some = x.shape[0] // tok
        return jnp.where(allowed[None], x.reshape(some, tok, SPAN), other).reshape(x.shape)

    def block(k, masked):
        keys, values = load(k)
        allowed = allowed_in(k) if masked else None
        for j in range(0, heads, PAIR):
            here = slice(j * tok, min(j + PAIR, heads) * tok)
            p = jnp.exp2(dot_nn(qs[here], keys) * FACTOR)
            if masked:
                p = keep(allowed, p, 0.0)
            total[here] += fold(p, jnp.add)
            acc[here] += dot_nn(p.astype(jnp.bfloat16), values)

    block(0, True)

    @pl.loop(1, jnp.maximum(clear, 1))
    def _(k):
        block(k, False)

    @pl.loop(jnp.maximum(clear, 1), blocks)
    def _(k):
        block(k, True)

    def write():
        whole = jnp.sum(total[...], axis=1, keepdims=True)
        result = (acc[...] / whole).astype(out.dtype)
        for j in range(heads):
            out[:, j * HD : (j + 1) * HD] = result[j * tok : (j + 1) * tok]
        return whole

    fine = sound(write())

    @pl.when(jnp.logical_not(fine))
    def _():
        peak[...] = jnp.full_like(peak, NEG)
        total[...] = jnp.zeros_like(total)
        acc[...] = jnp.zeros_like(acc)

        @pl.loop(0, blocks)
        def _(k):
            keys, values = load(k)
            allowed = allowed_in(k)

            @pl.loop(0, heads)
            def _(j):
                here = pl.ds(pl.multiple_of(j * tok, tok), tok)
                s = jnp.where(allowed, dot_nn(qs[here], keys) * FACTOR, NEG)
                top = jnp.maximum(peak[here], jnp.max(s, axis=1, keepdims=True))
                p = jnp.where(allowed, jnp.exp2(s - top[:, :1]), 0.0)
                shrink = jnp.exp2(peak[here] - top)
                total[here] = total[here] * shrink + fold(p, jnp.add)
                acc[here] = acc[here] * shrink + dot_nn(p.astype(jnp.bfloat16), values)
                peak[here] = top

        write()


def prefill(q, keys, values, meta, lengths, groups, columns, name, before=None):
    tok = q.shape[0]
    count = values.shape[0]
    heads = H // KVH
    rows = heads * tok
    pairs = rows * count // 2 * groups
    extra = [] if before is None else [before]
    return pl.pallas_call(
        functools.partial(prefill_kernel, tok, heads),
        out_shape=jax.ShapeDtypeStruct((tok, columns), jnp.bfloat16),
        grid_spec=pltpu.PrefetchScalarGridSpec(
            num_scalar_prefetch=2,
            grid=(groups,),
            in_specs=[
                pl.BlockSpec((tok, heads * HD), lambda g, meta, lengths: (0, meta[1] + g)),
                pl.BlockSpec((HD, count), lambda g, meta, lengths: (meta[2] + g, 0)),
                pl.BlockSpec((count, HD), lambda g, meta, lengths: (0, meta[2] + g)),
            ]
            + [HBM] * len(extra),
            out_specs=pl.BlockSpec((tok, heads * HD), lambda g, meta, lengths: (0, meta[3] + g)),
            scratch_shapes=[
                pltpu.VMEM((rows, HD), jnp.bfloat16),
                pltpu.VMEM((rows, HD), jnp.float32),
                pltpu.VMEM((rows, HD), jnp.float32),
                pltpu.VMEM((rows, HD), jnp.float32),
            ],
        ),
        compiler_params=pltpu.CompilerParams(vmem_limit_bytes=ROOM),
        cost_estimate=pl.CostEstimate(
            flops=pairs * HD * 8, bytes_accessed=count * HD * 4 * groups, transcendentals=pairs
        ),
        input_output_aliases={} if before is None else {5: 0},
        name=name,
    )(meta, lengths, q, keys, values, *extra)


def settle_kernel(meta, piece, whole, out, sem):
    width = piece.shape[1]
    where = pl.ds(pl.multiple_of((1 - meta[CORE]) * width, width), width)
    copy = pltpu.make_async_copy(piece, out.at[:, where], sem)
    copy.start()
    copy.wait()


def settle(whole, piece, meta):
    return pl.pallas_call(
        settle_kernel,
        out_shape=jax.ShapeDtypeStruct(whole.shape, whole.dtype),
        in_specs=[SMEM, VMEM, HBM],
        out_specs=HBM,
        scratch_shapes=[pltpu.SemaphoreType.DMA],
        input_output_aliases={2: 0},
        compiler_params=pltpu.CompilerParams(vmem_limit_bytes=LITTLE),
        cost_estimate=pl.CostEstimate(flops=0, bytes_accessed=piece.size * 4, transcendentals=0),
        name="settle",
    )(meta, piece, whole)


def allowed_at(first, base, tok, length, lengths):
    t = first + lax.broadcasted_iota(jnp.int32, (tok, 1), 0)
    u = base + lax.broadcasted_iota(jnp.int32, (tok, length), 1)
    return (u <= t) & (u >= start_of(t, lengths))


def column_block(at):
    return pl.ds(pl.multiple_of(at, HD), HD)


def keys_of(upper, g):
    return upper[column_block(g * HD), :]


def values_of(lower, g):
    half = lower.shape[1] // 2
    both = [lower[:, column_block(side * half + g * HD)] for side in range(2)]
    return jnp.concatenate(both, axis=0)


def add_block(tok, heads, q_at, keys, values, allowed, sums, fresh=False):
    length = keys.shape[1]
    for j in range(0, heads, PAIR):
        some = min(PAIR, heads - j)
        p = jnp.exp2(dot_nn(q_at(j * tok, some * tok), keys) * FACTOR)
        if allowed is not None:
            p = p.reshape(some, tok, length)
            p = jnp.where(allowed[None], p, 0.0).reshape(some * tok, length)
        more = (fold(p, jnp.add), dot_nn(p.astype(jnp.bfloat16), values))
        for ref, value in zip(sums, more):
            here = slice(j * tok, (j + some) * tok)
            ref[here] = value if fresh else ref[here] + value


def relation(meta, part, side, tok, lengths):
    first = (meta[CHIP] * 2 + side) * tok
    base = meta[PARTS + part] * 2 * tok
    relevant = (base < first) & (meta[PARTS + part] != meta[CHIP])
    relevant = relevant & (base + 2 * tok > start_of(first, lengths))
    return relevant, base >= start_of(first + tok - 1, lengths), first, base


def side_rows(side, heads, tok):
    return pl.ds(pl.multiple_of(side * (heads * tok), HD), heads * tok)


def open_kernel(tok, heads, groups, meta, lengths, q, q_near, upper, lower, qs, total, acc):
    core = meta[CORE]
    rows = heads * tok
    for source, side, skip in ((q, core, core * groups * heads), (q_near, 1 - core, 0)):
        for g in range(groups):
            for j in range(heads):
                at = pl.ds(pl.multiple_of(side * rows + j * tok, HD), tok)
                qs[g, at] = source[:, column_block((skip + g * heads + j) * HD)]

    @pl.loop(0, groups)
    def _(g):
        keys, values = keys_of(upper, g), values_of(lower, g)
        for side in range(2):
            length = (side + 1) * tok
            first = (meta[CHIP] * 2 + side) * tok
            allowed = allowed_at(first, meta[CHIP] * 2 * tok, tok, length, lengths)
            here = side_rows(side, heads, tok)
            q_at = lambda at, count: qs[g, pl.ds(side * rows + at, count)]
            add_block(tok, heads, q_at, keys[:, :length], values[:length], allowed,
                      (total.at[g, here], acc.at[g, here]), True)


def open_sums(q, q_near, block, meta, lengths):
    tok = q.shape[0]
    heads = H // KVH
    groups = q_near.shape[1] // (heads * HD)
    rows = 2 * heads * tok
    sums = jax.ShapeDtypeStruct((groups, rows, HD), jnp.float32)
    pairs = groups * rows * tok * 2
    return pl.pallas_call(
        functools.partial(open_kernel, tok, heads, groups),
        out_shape=[jax.ShapeDtypeStruct((groups, rows, HD), jnp.bfloat16), sums, sums],
        in_specs=[SMEM, SMEM, VMEM, VMEM, VMEM, VMEM],
        out_specs=[VMEM] * 3,
        compiler_params=pltpu.CompilerParams(vmem_limit_bytes=2 * LITTLE),
        cost_estimate=pl.CostEstimate(
            flops=pairs * HD * 8, bytes_accessed=q.size * 2, transcendentals=pairs
        ),
        name="open",
    )(meta, lengths, q, q_near, *block)


def stage_kernel(tok, heads, groups, first_part, meta, lengths, qs, total_in, acc_in, *refs):
    total, acc, held_k, held_v = refs[-4:]
    for i in range(2):
        held_k[i], held_v[i] = refs[2 * i][...], refs[2 * i + 1][...]

    @pl.loop(0, 4 * groups)
    def _(step):
        which, rest = lax.div(step, 2 * groups), lax.rem(step, 2 * groups)
        g, side = lax.div(rest, 2), lax.rem(rest, 2)
        relevant, clear, first, base = relation(meta, first_part + which, side, tok, lengths)
        here = side_rows(side, heads, tok)
        sums = (total.at[g, here], acc.at[g, here])
        at = side * (heads * tok)
        q_at = lambda off, count: qs[g, pl.ds(pl.multiple_of(at + off, HD), count)]
        upper, lower = held_k.at[which], held_v.at[which]

        @pl.when(relevant & clear)
        def _():
            add_block(tok, heads, q_at, keys_of(upper, g), values_of(lower, g), None, sums)

        @pl.when(relevant & jnp.logical_not(clear))
        def _():
            allowed = allowed_at(first, base, tok, 2 * tok, lengths)
            add_block(tok, heads, q_at, keys_of(upper, g), values_of(lower, g), allowed, sums)


def stage(state, pair, first_part, meta, lengths):
    qs, total, acc = state
    groups, rows, unused = qs.shape
    flat = [x for block in pair for x in block]
    tok = flat[0].shape[1] // 2
    pairs = groups * rows * tok * 2
    new = pl.pallas_call(
        functools.partial(stage_kernel, tok, rows // (2 * tok), groups, first_part),
        out_shape=[jax.ShapeDtypeStruct(x.shape, x.dtype) for x in (total, acc)],
        in_specs=[SMEM, SMEM] + [VMEM] * 7,
        out_specs=[VMEM] * 2,
        scratch_shapes=[pltpu.VMEM((2, *x.shape), x.dtype) for x in pair[0]],
        input_output_aliases={3: 0, 4: 1},
        compiler_params=pltpu.CompilerParams(vmem_limit_bytes=2 * LITTLE),
        cost_estimate=pl.CostEstimate(
            flops=pairs * HD * 8, bytes_accessed=tok * HD, transcendentals=pairs
        ),
        name=f"stage{first_part}",
    )(meta, lengths, qs, total, acc, *flat)
    return qs, *new


def finish_kernel(tok, heads, groups, done, meta, lengths, qs, total, acc, *refs):
    near, out, held_k, held_v, peak, total_now, acc_now, result, sem = refs[-9:]
    parts = held_k.shape[0]
    rows = heads * tok
    core = meta[CORE]

    def fill(first):
        for i in range(first, parts):
            held_k[i], held_v[i] = refs[2 * i][...], refs[2 * i + 1][...]

    def turn_of(step):
        turn, g = lax.div(step, groups), lax.rem(step, groups)
        side = jnp.where(turn == 0, 1 - core, core)
        at = side * rows
        q_at = lambda off, count: qs[g, pl.ds(pl.multiple_of(at + off, HD), count)]
        return turn, g, side, q_at

    def write(turn, g):
        whole = jnp.sum(total_now[...], axis=1, keepdims=True)
        value = (acc_now[...] / whole).astype(result.dtype)
        for j in range(heads):
            result[turn, :, column_block((g * heads + j) * HD)] = value[j * tok : (j + 1) * tok]
        return sound(whole)

    def one_turn(step, fine):
        turn, g, side, q_at = turn_of(step)
        here = side_rows(side, heads, tok)
        total_now[...] = total[g, here]
        acc_now[...] = acc[g, here]

        @pl.loop(done, parts)
        def _(i):
            relevant, clear, first, base = relation(meta, i, side, tok, lengths)
            upper, lower = held_k.at[i], held_v.at[i]
            sums = (total_now, acc_now)

            @pl.when(relevant & clear)
            def _():
                add_block(tok, heads, q_at, keys_of(upper, g), values_of(lower, g), None, sums)

            @pl.when(relevant & jnp.logical_not(clear))
            def _():
                allowed = allowed_at(first, base, tok, 2 * tok, lengths)
                add_block(tok, heads, q_at, keys_of(upper, g), values_of(lower, g), allowed, sums)

        return fine & write(turn, g).astype(jnp.int32)

    fill(done)
    fine = lax.fori_loop(0, 2 * groups, one_turn, jnp.int32(1))

    @pl.when(fine == 0)
    def _():
        fill(0)

        @pl.loop(0, 2 * groups)
        def _(step):
            turn, g, side, q_at = turn_of(step)
            first = (meta[CHIP] * 2 + side) * tok
            peak[...] = jnp.full_like(peak, NEG)
            total_now[...] = jnp.zeros_like(total_now)
            acc_now[...] = jnp.zeros_like(acc_now)

            @pl.loop(0, parts * heads)
            def _(step):
                i, j = lax.div(step, heads), lax.rem(step, heads)
                keys, values = keys_of(held_k.at[i], g), values_of(held_v.at[i], g)
                allowed = allowed_at(first, meta[PARTS + i] * 2 * tok, tok, 2 * tok, lengths)
                mine = pl.ds(pl.multiple_of(j * tok, tok), tok)
                s = jnp.where(allowed, dot_nn(q_at(j * tok, tok), keys) * FACTOR, NEG)
                top = jnp.maximum(peak[mine], jnp.max(s, axis=1, keepdims=True))
                p = jnp.where(allowed, jnp.exp2(s - top[:, :1]), 0.0)
                shrink = jnp.exp2(peak[mine] - top)
                total_now[mine] = total_now[mine] * shrink + fold(p, jnp.add)
                acc_now[mine] = acc_now[mine] * shrink + dot_nn(p.astype(jnp.bfloat16), values)
                peak[mine] = top

            write(turn, g)

    width = near.shape[1]
    where = pl.ds(pl.multiple_of(core * width, width), width)
    copy = pltpu.make_async_copy(result.at[1], out.at[:, where], sem)
    copy.start()
    near[...] = result[0]
    copy.wait()


def finish(state, blocks, done, meta, lengths):
    qs, total, acc = state
    groups, rows, unused = qs.shape
    flat = [x for block in blocks for x in block]
    tok = flat[0].shape[1] // 2
    heads = rows // (2 * tok)
    width = groups * heads * HD
    sums = pltpu.VMEM((heads * tok, HD), jnp.float32)
    return pl.pallas_call(
        functools.partial(finish_kernel, tok, heads, groups, done),
        out_shape=[
            jax.ShapeDtypeStruct((tok, width), jnp.bfloat16),
            jax.ShapeDtypeStruct((tok, 2 * width), jnp.bfloat16),
        ],
        in_specs=[SMEM, SMEM] + [VMEM] * (3 + len(flat)),
        out_specs=[VMEM, HBM],
        scratch_shapes=[
            *[pltpu.VMEM((len(blocks), *x.shape), x.dtype) for x in blocks[0]],
            sums, sums, sums,
            pltpu.VMEM((2, tok, width), jnp.bfloat16),
            pltpu.SemaphoreType.DMA,
        ],
        compiler_params=pltpu.CompilerParams(vmem_limit_bytes=ROOM),
        cost_estimate=pl.CostEstimate(
            flops=groups * rows * tok * HD * 8, bytes_accessed=tok * width * 4,
            transcendentals=groups * rows * tok * 2,
        ),
        name="finish",
    )(meta, lengths, qs, total, acc, *flat)


def request_sums(query, keys, values, mask):
    p = jnp.exp2(dot_nn(query, keys) * FACTOR)
    p = jnp.where(mask[None], p.reshape(-1, *mask.shape), 0.0).reshape(p.shape)
    return fold(p, jnp.add), dot_nn(p.astype(jnp.bfloat16), values)


def fresh_scores(query, newk, own):
    s = dot_nt(query, newk) * FACTOR
    size = newk.shape[0]
    row = lax.broadcasted_iota(jnp.int32, (size, size), 0)
    col = lax.broadcasted_iota(jnp.int32, (size, size), 1)
    ok = (lax.rem(row, own) == lax.rem(col, own)) & (lax.div(col, own) <= lax.div(row, own))
    return s.reshape(-1, size, size), ok


def requests_kernel(own, heads, groups, length, meta, q_dec, k_new, v_new, table, *refs):
    total, acc, query, newk, newv, mask, q3, k3, v3, sems = refs
    steps = q3.shape[1]
    core, level = meta[CORE], lax.div(meta[CHIP], 2)
    requests = pl.ds(level * own, own)
    copies = []
    for i, (source, held) in enumerate(((q_dec, q3), (k_new, k3), (v_new, v3))):
        width = held.shape[2]
        where = pl.ds(pl.multiple_of(core * width, width), width)
        copies.append(pltpu.make_async_copy(source.at[requests, :, where], held, sems.at[i]))
    for copy in copies:
        copy.start()
    rows = table[pl.ds(pl.multiple_of(level * own, own), own), :]
    lane = lax.div(lax.broadcasted_iota(jnp.int32, (own, length), 1), BLK)
    for i in range(mask.shape[1] // length):
        number = lane + meta[PARTS + i] * (length // BLK)
        hit = rows[:, :1] == number
        for j in range(1, rows.shape[1]):
            hit = hit | (rows[:, j : j + 1] == number)
        mask[:, i * length : (i + 1) * length] = hit.astype(jnp.float32)
    for copy in copies:
        copy.wait()
    for s in range(steps):
        for g in range(groups):
            col = slice(g * HD, (g + 1) * HD)
            at = slice(s * own, (s + 1) * own)
            newk[at, col] = k3[:, s, col]
            newv[at, col] = v3[:, s, col]
            for j in range(heads):
                first = (g * heads + j) * HD
                row = (j * steps + s) * own
                query[g, row : row + own] = q3[:, s, first : first + HD]

    @pl.loop(0, groups)
    def _(g):
        col = column_block(g * HD)
        s, ok = fresh_scores(query[g], newk[:, col], own)
        p = jnp.where(ok[None], jnp.exp2(s), 0.0).reshape(-1, s.shape[2])
        first = jnp.sum(p, axis=1, keepdims=True)
        lead = lax.broadcasted_iota(jnp.int32, (p.shape[0], HD), 1) == 0
        total[g] = jnp.where(lead, first, 0.0)
        acc[g] = dot_nn(p.astype(jnp.bfloat16), newv[:, col])


def open_requests(q_dec, k_new, v_new, table, length, own, meta):
    heads = H // KVH
    steps = q_dec.shape[1]
    width = k_new.shape[2] // 2
    groups = width // HD
    rows = heads * own * steps
    sums = jax.ShapeDtypeStruct((groups, rows, HD), jnp.float32)
    new = jax.ShapeDtypeStruct((own * steps, width), jnp.bfloat16)
    return pl.pallas_call(
        functools.partial(requests_kernel, own, heads, groups, length),
        out_shape=[
            sums, sums, jax.ShapeDtypeStruct((groups, rows, HD), jnp.bfloat16), new, new,
            jax.ShapeDtypeStruct((own, (LEVELS - PARTS) * length), jnp.float32),
        ],
        in_specs=[SMEM] + [HBM] * 3 + [VMEM],
        out_specs=[VMEM] * 6,
        scratch_shapes=[
            pltpu.VMEM((own, steps, groups * heads * HD), jnp.bfloat16),
            pltpu.VMEM((own, steps, width), jnp.bfloat16),
            pltpu.VMEM((own, steps, width), jnp.bfloat16),
            pltpu.SemaphoreType.DMA((3,)),
        ],
        compiler_params=pltpu.CompilerParams(vmem_limit_bytes=LITTLE),
        cost_estimate=pl.CostEstimate(
            flops=groups * rows * own * steps * HD * 4, bytes_accessed=rows * HD * 8,
            transcendentals=groups * rows * own * steps,
        ),
        name="requests",
    )(meta, q_dec, k_new, v_new, table)


def early_kernel(groups, total_in, acc_in, query, mask, *refs):
    total, acc = refs[-2:]
    length = refs[0].shape[1]

    @pl.loop(0, groups)
    def _(g):
        sums = [total[g], acc[g]]
        for i in range(len(refs) // 2 - 1):
            open_to = mask[:, i * length : (i + 1) * length] > 0
            keys, values = keys_of(refs[2 * i], g), values_of(refs[2 * i + 1], g)
            more = request_sums(query[g], keys, values, open_to)
            sums = [x + y for x, y in zip(sums, more)]
        total[g], acc[g] = sums


def early_decode(state, blocks):
    total, acc, query, newk, newv, mask = state
    groups, rows, unused = query.shape
    flat = [x for block in blocks for x in block]
    pairs = groups * rows * len(blocks) * flat[0].shape[1]
    sums = jax.ShapeDtypeStruct(total.shape, total.dtype)
    new = pl.pallas_call(
        functools.partial(early_kernel, groups),
        out_shape=[sums, sums],
        in_specs=[VMEM] * (4 + len(flat)),
        out_specs=[VMEM] * 2,
        input_output_aliases={0: 0, 1: 1},
        compiler_params=pltpu.CompilerParams(vmem_limit_bytes=2 * LITTLE),
        cost_estimate=pl.CostEstimate(
            flops=pairs * HD * 8, bytes_accessed=rows * HD, transcendentals=pairs
        ),
        name="early_decode",
    )(total, acc, query, mask, *flat)
    return [*new, query, newk, newv, mask]


def late_kernel(own, steps, heads, groups, done, meta, total, acc, query, newk, newv, mask, *refs):
    out, held_k, held_v, scores = refs[-4:]
    parts, unused, length = held_k.shape
    size = own * steps

    def write(g, sums, whole):
        result = (sums / whole).astype(out.dtype)
        for j in range(heads):
            out[:, column_block((g * heads + j) * HD)] = result[j * size : (j + 1) * size]

    def one_group(g, fine):
        sums = [total[g], acc[g]]
        for i in range(done, parts):
            open_to = mask[:, i * length : (i + 1) * length] > 0
            keys, values = keys_of(refs[2 * i], g), values_of(refs[2 * i + 1], g)
            more = request_sums(query[g], keys, values, open_to)
            sums = [x + y for x, y in zip(sums, more)]
        whole = jnp.sum(sums[0], axis=1, keepdims=True)
        write(g, sums[1], whole)
        return fine & sound(whole).astype(jnp.int32)

    fine = lax.fori_loop(0, groups, one_group, jnp.int32(1))

    @pl.when(fine == 0)
    def _():
        for i in range(parts):
            held_k[i], held_v[i] = refs[2 * i][...], refs[2 * i + 1][...]

        @pl.loop(0, groups)
        def _(g):
            col = column_block(g * HD)
            fresh, ok = fresh_scores(query[g], newk[:, col], own)
            fresh = jnp.where(ok[None], fresh, NEG).reshape(-1, size)
            rows = fresh.shape[0]

            def score(i, top):
                s = dot_nn(query[g], keys_of(held_k.at[i], g)) * FACTOR
                where = pl.ds(pl.multiple_of(i * length, length), length)
                open_to = mask[:, where] > 0
                s = jnp.where(open_to[None], s.reshape(-1, own, length), NEG).reshape(s.shape)
                scores[:, where] = s
                return jnp.maximum(top, jnp.max(s, axis=1, keepdims=True))

            top = lax.fori_loop(0, parts, score, jnp.max(fresh, axis=1, keepdims=True))
            p = jnp.exp2(fresh - top)

            def weigh(i, sums):
                where = pl.ds(pl.multiple_of(i * length, length), length)
                p = jnp.exp2(scores[:, where] - top)
                values = values_of(held_v.at[i], g)
                return (
                    sums[0] + jnp.sum(p, axis=1, keepdims=True),
                    sums[1] + dot_nn(p.astype(jnp.bfloat16), values),
                )

            start = (
                jnp.sum(p, axis=1, keepdims=True),
                dot_nn(p.astype(jnp.bfloat16), newv[:, col]),
            )
            whole, sums = lax.fori_loop(0, parts, weigh, start)
            write(g, sums, whole)


def late_decode(early, blocks, done, own, steps, meta):
    groups, rows, unused = early[0].shape
    heads = H // KVH
    flat = [x for block in blocks for x in block]
    parts, length = len(blocks), flat[0].shape[1]
    pairs = groups * rows * (parts - done) * length
    return pl.pallas_call(
        functools.partial(late_kernel, own, steps, heads, groups, done),
        out_shape=jax.ShapeDtypeStruct((own * steps, groups * heads * HD), jnp.bfloat16),
        in_specs=[SMEM] + [VMEM] * (len(early) + len(flat)),
        out_specs=VMEM,
        scratch_shapes=[
            *[pltpu.VMEM((parts, *x.shape), x.dtype) for x in blocks[0]],
            pltpu.VMEM((rows, parts * length), jnp.float32),
        ],
        compiler_params=pltpu.CompilerParams(vmem_limit_bytes=ROOM + ROOM // 4),
        cost_estimate=pl.CostEstimate(
            flops=pairs * HD * 8, bytes_accessed=rows * HD, transcendentals=pairs
        ),
        name="late_decode",
    )(meta, *early, *flat)


def decode_kernel(parts, steps, heads, groups, starts, q, mask, newk, newv, *refs):
    kheld, vheld = refs[:parts], refs[parts : 2 * parts]
    out, kall, vall, sems, scores = refs[2 * parts :]
    own = q.shape[0]
    rows = heads * own
    length = kheld[0].shape[1]
    copies = []
    for i in range(parts):
        where = pl.ds(pl.multiple_of(starts[i], HD), length)
        copies.append(pltpu.make_async_copy(kheld[i], kall.at[:, where], sems.at[2 * i]))
        copies.append(pltpu.make_async_copy(vheld[i], vall.at[where], sems.at[2 * i + 1]))
    for copy in copies:
        copy.start()
    row = lax.broadcasted_iota(jnp.int32, (own, own), 0)
    col = lax.broadcasted_iota(jnp.int32, (own, own), 1)
    fresh_ok = (lax.div(row, steps) == lax.div(col, steps)) & (col <= row)

    def columns(g):
        return slice(g * HD, (g + 1) * HD)

    def stacked(g):
        first = g * heads
        slices = [q[:, (first + j) * HD : (first + j + 1) * HD] for j in range(heads)]
        return jnp.concatenate([x.astype(jnp.float32) for x in slices], 0).astype(jnp.bfloat16)

    def keep(allowed, x, other):
        y = x.reshape(heads, own, x.shape[1])
        return jnp.where(allowed[None], y, other).reshape(x.shape)

    def open_to(i):
        return mask[:, pl.ds(pl.multiple_of(starts[i], HD), length)] > 0

    def write(g, acc, whole):
        result = acc / whole
        for j in range(heads):
            out[:, (g * heads + j) * HD : (g * heads + j + 1) * HD] = result[
                j * own : (j + 1) * own
            ].astype(out.dtype)

    fine = None
    for g in range(groups):
        query = stacked(g)
        p = keep(fresh_ok, jnp.exp2(dot_nt(query, newk[:, columns(g)]) * FACTOR), 0.0)
        whole = jnp.sum(p, axis=1, keepdims=True)
        acc = dot_nn(p.astype(jnp.bfloat16), newv[:, columns(g)])
        total = jnp.zeros((rows, HD), jnp.float32)
        for i in range(parts):
            p = jnp.exp2(dot_nn(query, kheld[i][columns(g)]) * FACTOR)
            p = keep(open_to(i), p, 0.0)
            total = total + fold(p, jnp.add)
            acc = acc + dot_nn(p.astype(jnp.bfloat16), vheld[i][:, columns(g)])
        whole = whole + jnp.sum(total, axis=1, keepdims=True)
        write(g, acc, whole)
        fine = sound(whole) if fine is None else fine & sound(whole)

    @pl.when(jnp.logical_not(fine))
    def _():
        for g in range(groups):
            query = stacked(g)
            fresh = keep(fresh_ok, dot_nt(query, newk[:, columns(g)]) * FACTOR, NEG)
            top = jnp.max(fresh, axis=1, keepdims=True)
            for i in range(parts):
                s = keep(open_to(i), dot_nn(query, kheld[i][columns(g)]) * FACTOR, NEG)
                scores[:, i * length : (i + 1) * length] = s
                top = jnp.maximum(top, jnp.max(s, axis=1, keepdims=True))
            p = jnp.exp2(fresh - top)
            whole = jnp.sum(p, axis=1, keepdims=True)
            acc = dot_nn(p.astype(jnp.bfloat16), newv[:, columns(g)])
            for i in range(parts):
                p = jnp.exp2(scores[:, i * length : (i + 1) * length] - top)
                whole = whole + jnp.sum(p, axis=1, keepdims=True)
                acc = acc + dot_nn(p.astype(jnp.bfloat16), vheld[i][:, columns(g)])
            write(g, acc, whole)

    for copy in copies:
        copy.wait()


def decode(q, mask, newk, newv, kparts, vparts, starts, steps):
    own = q.shape[0]
    parts = len(kparts)
    length, width = vparts[0].shape
    count = parts * length
    heads = H // KVH
    groups = width // HD
    rows = heads * own
    pairs = groups * rows * count
    return pl.pallas_call(
        functools.partial(decode_kernel, parts, steps, heads, groups),
        out_shape=[
            jax.ShapeDtypeStruct(q.shape, jnp.bfloat16),
            jax.ShapeDtypeStruct((width, count), jnp.bfloat16),
            jax.ShapeDtypeStruct((count, width), jnp.bfloat16),
        ],
        grid_spec=pltpu.PrefetchScalarGridSpec(
            num_scalar_prefetch=1,
            grid=(),
            in_specs=[VMEM] * (4 + 2 * parts),
            out_specs=[VMEM, HBM, HBM],
            scratch_shapes=[
                pltpu.SemaphoreType.DMA((2 * parts,)),
                pltpu.VMEM((rows, count), jnp.float32),
            ],
        ),
        compiler_params=pltpu.CompilerParams(vmem_limit_bytes=ROOM),
        cost_estimate=pl.CostEstimate(
            flops=pairs * HD * 4, bytes_accessed=count * width * 4, transcendentals=pairs
        ),
        name="decode",
    )(starts, q, mask, newk, newv, *kparts, *vparts)


def prepare_kernel(meta, k, v, send, keys, values):
    tok, width = k.shape[0], k.shape[1] // 2
    mine = pl.ds(pl.multiple_of(meta[0] * width, width), width)
    other = pl.ds(pl.multiple_of((1 - meta[0]) * width, width), width)
    send[:width] = k[:, other].astype(jnp.float32).T.astype(send.dtype)
    send[width:] = v[:, other]
    keys[:, mine] = k[:, mine].astype(jnp.float32).T.astype(keys.dtype)
    values[:, mine] = v[:, mine]


def prepare(k, v, core):
    tok, width = k.shape[0], k.shape[1] // 2
    assert tok == width
    block = jax.ShapeDtypeStruct((width, 2 * tok), k.dtype)
    return pl.pallas_call(
        prepare_kernel,
        out_shape=[jax.ShapeDtypeStruct((2 * tok, width), k.dtype), block, block],
        in_specs=[SMEM, VMEM, VMEM],
        out_specs=[VMEM] * 3,
        name="prepare",
    )(core[None], k, v)


def join_kernel(meta, keys_in, values_in, theirs, keys, values):
    width = theirs.shape[1]
    other = pl.ds(pl.multiple_of((1 - meta[0]) * width, width), width)
    keys[:, other] = theirs[:width]
    values[:, other] = theirs[width:]


def join(keys, values, theirs, core):
    return pl.pallas_call(
        join_kernel,
        out_shape=[jax.ShapeDtypeStruct(x.shape, x.dtype) for x in (keys, values)],
        in_specs=[SMEM, VMEM, VMEM, VMEM],
        out_specs=[VMEM] * 2,
        input_output_aliases={1: 0, 2: 1},
        compiler_params=pltpu.CompilerParams(vmem_limit_bytes=LITTLE),
        name="join",
    )(core[None], keys, values, theirs)


def take_kernel(meta, whole, out, sem):
    width = out.shape[1]
    where = pl.ds(pl.multiple_of((1 - meta[CORE]) * width, width), width)
    copy = pltpu.make_async_copy(whole.at[:, where], out, sem)
    copy.start()
    copy.wait()


def take_other_half(whole, meta):
    return pl.pallas_call(
        take_kernel,
        out_shape=jax.ShapeDtypeStruct((whole.shape[0], whole.shape[1] // 2), whole.dtype),
        in_specs=[SMEM, HBM],
        out_specs=VMEM,
        scratch_shapes=[pltpu.SemaphoreType.DMA],
        compiler_params=pltpu.CompilerParams(vmem_limit_bytes=LITTLE),
        name="take",
    )(meta, whole)


def project_kernel(meta, *refs):
    pieces, (whole, other), outs, (sorted_rows,) = refs[:-7], refs[-7:-5], refs[-5:-1], refs[-1:]
    parts = len(pieces)
    rows = pieces[0].shape[0]
    for i, piece in enumerate(pieces):
        at = pl.ds(pl.multiple_of(meta[LEVELS + i] * rows, rows), rows)
        sorted_rows[at] = piece[...]
    depth = other.shape[1]
    mine = whole[:, pl.ds(pl.multiple_of(meta[CORE] * depth, depth), depth)]
    half = parts * rows // 2
    here = pl.ds(pl.multiple_of(meta[ACROSS] * half, half), half)
    there = pl.ds(pl.multiple_of((1 - meta[ACROSS]) * half, half), half)
    kept, beside, across, corner = outs
    for at, near, far in ((here, kept, beside), (there, across, corner)):
        some = sorted_rows[at]
        near[...] = dot_nt(mine, some).astype(near.dtype)
        far[...] = dot_nt(other[...], some).astype(far.dtype)


def project(pieces, whole, other, meta):
    rows = len(pieces) * pieces[0].shape[0]
    width, depth = other.shape
    block = jax.ShapeDtypeStruct((width, rows // 2), jnp.bfloat16)
    return pl.pallas_call(
        project_kernel,
        out_shape=[jax.ShapeDtypeStruct(block.shape, jnp.float32)] + [block] * 3,
        in_specs=[SMEM] + [VMEM] * (len(pieces) + 2),
        out_specs=[VMEM] * 4,
        scratch_shapes=[pltpu.VMEM((rows, depth), jnp.bfloat16)],
        compiler_params=pltpu.CompilerParams(vmem_limit_bytes=2 * LITTLE),
        cost_estimate=pl.CostEstimate(
            flops=rows * width * depth * 4, bytes_accessed=width * depth * 4, transcendentals=0
        ),
        name="project",
    )(meta, *pieces, whole, other)


def index(z, y, c):
    return (z * 2 + y) * 2 + c


def on_ring(r, chips):
    return (r, 0) if r < chips // 2 else (chips - 1 - r, 1)


def ring_perm(chips, d):
    return [
        (index(*on_ring(r, chips), c), index(*on_ring((r + d) % chips, chips), c))
        for r in range(chips)
        for c in range(2)
    ]


def ring_place(r, chips):
    r = lax.rem(r + 2 * chips, chips)
    return jnp.where(r < chips // 2, r * 2, (chips - 1 - r) * 2 + 1)


def spread(x, n):
    place = lax.axis_index("seq")
    deep = n // 4
    everyone = [(z, y, c) for z in range(deep) for y in range(2) for c in range(2)]
    z, y, c = place // 4, (place // 2) % 2, place % 2
    held = [(x, z, y, c)]
    for d in range(1, deep):
        perm = [(index(*p), index((p[0] - d) % deep, p[1], p[2])) for p in everyone]
        held.append((lax.ppermute(x, "seq", perm), lax.rem(z + d, deep), y, c))
    perm = [(index(*p), index(p[0], 1 - p[1], p[2])) for p in everyone]
    held += [(lax.ppermute(b, "seq", perm), bz, 1 - by, bc) for b, bz, by, bc in held]
    perm = [(index(*p), index(p[0], p[1], 1 - p[2])) for p in everyone]
    held += [(lax.ppermute(b, "seq", perm), bz, by, 1 - bc) for b, bz, by, bc in held]
    return [b for b, *_ in held], jnp.stack([index(bz, by, bc) for _, bz, by, bc in held])


def open_blocks(table, steps, count):
    number = lax.broadcasted_iota(jnp.int32, (*table.shape, count), 2) // BLK
    mask = jnp.any(table[:, :, None] == number, axis=1).astype(jnp.float32)
    return jnp.repeat(mask, steps, axis=0)


def whole_heads(n, q_pre, k_cache, v_cache, lengths, q_dec, k_new, v_new, block_table, w_out):
    tok = q_pre.shape[0]
    place = lax.axis_index("seq").astype(jnp.int32)
    rows, steps = q_dec.shape[0], q_dec.shape[1]
    own = rows // n
    kparts, sources = spread(k_cache.T, n)
    vparts, _ = spread(v_cache, n)
    starts = sources.astype(jnp.int32) * tok

    def mine(x):
        y = lax.dynamic_slice_in_dim(x, place * own, own, 0)
        return y.reshape(own * steps, -1) if x.ndim == 3 else y

    mask = open_blocks(mine(block_table), steps, n * tok)
    attn_own, keys, values = decode(
        mine(q_dec), mask, mine(k_new), mine(v_new), kparts, vparts, starts, steps
    )
    attn = lax.all_gather(attn_own, "seq", axis=0, tiled=True)
    flat = jnp.dot(attn, w_out, preferred_element_type=jnp.float32).astype(jnp.bfloat16)
    dec_out = lax.psum_scatter(
        flat.reshape(rows, steps, -1), "tp", scatter_dimension=0, tiled=True
    )
    zero = jnp.zeros((), jnp.int32)
    meta = jnp.stack([place * tok, zero, zero, zero])
    groups = k_cache.shape[1] // HD
    pre_out = prefill(
        q_pre, keys, values, meta, lengths, groups, q_pre.shape[1], "prefill"
    )
    return (pre_out, dec_out)


def split_heads(n, q_pre, k_cache, v_cache, lengths, q_dec, k_new, v_new, block_table, w_out):
    tok = q_pre.shape[0]
    place = lax.axis_index("seq").astype(jnp.int32)
    across = lax.axis_index("tp").astype(jnp.int32)
    core, chip = lax.rem(place, 2), lax.div(place, 2)
    chips = n // 2
    far, deep = chips // 2, chips // 2
    z, y = lax.div(chip, 2), lax.rem(chip, 2)
    r = jnp.where(y == 0, z, chips - 1 - z)
    rows, steps = q_dec.shape[0], q_dec.shape[1]
    own = rows // deep
    sibling = [(i, i ^ 1) for i in range(n)]
    everyone = [(a, b, c) for a in range(deep) for b in range(2) for c in range(2)]

    order = [0] + [o for d in range(1, far) for o in (-d, d)] + [far]
    numbers = [ring_place(r + o, chips) for o in order]
    levels = [z] + [lax.rem(z + deep - d, deep) for d in range(1, deep)]
    assert len(numbers) == LEVELS - PARTS
    meta = jnp.stack([core, chip, across] + numbers + levels).astype(jnp.int32)

    send, keys, values = prepare(k_cache, v_cache, core)
    theirs = lax.ppermute(send, "seq", sibling)
    held_k, held_v = {}, {}
    held_k[0], held_v[0] = join(keys, values, theirs, core)
    held_k[0], held_v[0], q_pre, meta = lax.optimization_barrier(
        (held_k[0], held_v[0], q_pre, meta)
    )
    near_q = lax.ppermute(take_other_half(q_pre, meta), "seq", sibling)

    up, down = ring_perm(chips, 1), ring_perm(chips, -1)
    w_near, early = w_out, ()
    for d in range(1, far + 1):
        held_k[-d] = lax.ppermute(held_k[1 - d], "seq", up)
        held_v[d] = lax.ppermute(held_v[d - 1], "seq", down)
        if d < far:
            held_k[d] = lax.ppermute(held_k[d - 1], "seq", down)
            held_v[-d] = lax.ppermute(held_v[1 - d], "seq", up)
            sides = (-d, d)
        else:
            held_k[d] = held_k[-d]
            sides = (d,)
        if d == 1:
            state = open_sums(q_pre, near_q, (held_k[0], held_v[0]), meta, lengths)
        elif d == 2:
            pair = [(held_k[o], held_v[o]) for o in (-1, 1)]
            state = stage(state, pair, 1, meta, lengths)
        elif d == far - 1:
            early = open_requests(q_dec, k_new, v_new, block_table, 2 * tok, own, meta)
        elif d == far:
            blocks = [(held_k[o], held_v[o]) for o in order[:-1]]
            early = early_decode(early, blocks)
        for x in (held_k, held_v):
            moved, state, early, w_near = lax.optimization_barrier(
                ([x[o] for o in sides], state, early, w_near)
            )
            x.update(zip(sides, moved))
        if d == 1:
            weights = w_near.T
            w_near = lax.ppermute(take_other_half(weights, meta), "seq", sibling)
    blocks = [(held_k[o], held_v[o]) for o in order]
    attn_own = late_decode(early, blocks, len(blocks) - 1, own, steps, meta)

    pieces = [attn_own]
    for d in range(1, deep):
        perm = [(index(*p), index((p[0] + d) % deep, p[1], p[2])) for p in everyone]
        pieces.append(lax.ppermute(attn_own, "seq", perm))
    attn_own, state = lax.optimization_barrier((attn_own, state))
    near, pre_out = finish(state, blocks, 3, meta, lengths)
    pieces, near, pre_out = lax.optimization_barrier((pieces, near, pre_out))
    back = lax.ppermute(near, "seq", sibling)
    pre_out = settle(pre_out, back, meta)

    total, *sent = project(pieces, weights, w_near, meta)
    got = []
    for piece, (dc, dx) in zip(sent, ((1, 0), (0, 1), (1, 1))):
        perm = [
            (i * 2 + x, (i ^ dc) * 2 + (x ^ dx)) for i in range(n) for x in range(2)
        ]
        got.append(lax.ppermute(piece, ("seq", "tp"), perm))
    got[0], pre_out = lax.optimization_barrier((got[0], pre_out))
    for piece in got:
        total = total + piece.astype(jnp.float32)
    dec_out = total.astype(jnp.bfloat16).T.reshape(deep // 2, steps, own, -1)
    return (pre_out, dec_out.transpose(0, 2, 1, 3).reshape(rows // 2, steps, -1))


def per_device(n, tp, q_pre, k_cache, v_cache, prompt_lengths, *rest):
    groups = k_cache.shape[1] // HD
    square = groups % 2 == 0 and k_cache.shape[1] == 2 * k_cache.shape[0]
    form = split_heads if square and tp == 2 and n == 2 * (LEVELS - PARTS) else whole_heads
    return form(n, q_pre, k_cache, v_cache, prompt_lengths.astype(jnp.int32), *rest)


def solution(mesh):
    placed = (
        P("seq", "tp"),
        P("seq", "tp"),
        P("seq", "tp"),
        P(),
        P(None, None, "tp"),
        P(None, None, "tp"),
        P(None, None, "tp"),
        P(),
        P("tp", "seq"),
    )
    return jax.shard_map(
        functools.partial(per_device, mesh.shape["seq"], mesh.shape["tp"]),
        mesh=mesh,
        in_specs=placed,
        out_specs=(P("seq", "tp"), P("tp", None, "seq")),
        check_vma=False,
    )
```

```python
import functools
import math

import jax
import jax.numpy as jnp
from jax import lax
from jax.experimental import pallas as pl
from jax.experimental.pallas import tpu as pltpu
from jax.sharding import PartitionSpec as P

H = 56
KVH = 8
HD = 128
BLK = 64
SPAN = 512
PAIR = 2
NEG = -1e30
LEAST, MOST = 2.0**-60, 2.0**100
FACTOR = math.log2(math.e) / math.sqrt(HD)
ROOM = 16 * 1024 * 1024
LITTLE = 4 * 1024 * 1024
CORE, CHIP, ACROSS, PARTS, LEVELS = 0, 1, 2, 3, 11
HBM = pl.BlockSpec(memory_space=pltpu.HBM)
VMEM = pl.BlockSpec(memory_space=pltpu.VMEM)
SMEM = pl.BlockSpec(memory_space=pltpu.SMEM)


def dot_nt(a, b):
    return lax.dot_general(a, b, (((1,), (1,)), ((), ())), preferred_element_type=jnp.float32)


def dot_nn(a, b):
    return lax.dot_general(a, b, (((1,), (0,)), ((), ())), preferred_element_type=jnp.float32)


def fold(x, op):
    out = x[:, :HD]
    for i in range(1, x.shape[1] // HD):
        out = op(out, x[:, i * HD : (i + 1) * HD])
    return out


def start_of(position, lengths):
    end = jnp.int32(0)
    out = jnp.zeros_like(position)
    for i in range(lengths.shape[0]):
        end = end + lengths[i]
        out = jnp.where(position >= end, end, out)
    return out


def sound(total):
    return (jnp.min(total) >= LEAST) & (jnp.max(total) <= MOST)


def prefill_kernel(tok, heads, meta, lengths, q, keys_all, values_all, *refs):
    out, qs, peak, total, acc = refs[-5:]
    for j in range(heads):
        qs[j * tok : (j + 1) * tok] = q[:, j * HD : (j + 1) * HD]
    total[...] = jnp.zeros_like(total)
    acc[...] = jnp.zeros_like(acc)

    begin = meta[0]
    finish = begin + tok
    low = start_of(begin, lengths)
    high = start_of(finish - 1, lengths)
    blocks = lax.div(finish - low + SPAN - 1, SPAN)
    clear = lax.div(finish - high, SPAN)

    def first_of(k):
        return jnp.maximum(finish - (k + 1) * SPAN, 0)

    def load(k):
        here = pl.ds(pl.multiple_of(first_of(k), HD), SPAN)
        return keys_all[:, here], values_all[here, :]

    def allowed_in(k):
        t = begin + lax.broadcasted_iota(jnp.int32, (tok, 1), 0)
        u = first_of(k) + lax.broadcasted_iota(jnp.int32, (tok, SPAN), 1)
        last = jnp.minimum(t, finish - k * SPAN - 1)
        return (u <= last) & (u >= start_of(t, lengths))

    def keep(allowed, x, other):
        some = x.shape[0] // tok
        return jnp.where(allowed[None], x.reshape(some, tok, SPAN), other).reshape(x.shape)

    def block(k, masked):
        keys, values = load(k)
        allowed = allowed_in(k) if masked else None
        for j in range(0, heads, PAIR):
            here = slice(j * tok, min(j + PAIR, heads) * tok)
            p = jnp.exp2(dot_nn(qs[here], keys) * FACTOR)
            if masked:
                p = keep(allowed, p, 0.0)
            total[here] += fold(p, jnp.add)
            acc[here] += dot_nn(p.astype(jnp.bfloat16), values)

    block(0, True)

    @pl.loop(1, jnp.maximum(clear, 1))
    def _(k):
        block(k, False)

    @pl.loop(jnp.maximum(clear, 1), blocks)
    def _(k):
        block(k, True)

    def write():
        whole = jnp.sum(total[...], axis=1, keepdims=True)
        result = (acc[...] / whole).astype(out.dtype)
        for j in range(heads):
            out[:, j * HD : (j + 1) * HD] = result[j * tok : (j + 1) * tok]
        return whole

    fine = sound(write())

    @pl.when(jnp.logical_not(fine))
    def _():
        peak[...] = jnp.full_like(peak, NEG)
        total[...] = jnp.zeros_like(total)
        acc[...] = jnp.zeros_like(acc)

        @pl.loop(0, blocks)
        def _(k):
            keys, values = load(k)
            allowed = allowed_in(k)

            @pl.loop(0, heads)
            def _(j):
                here = pl.ds(pl.multiple_of(j * tok, tok), tok)
                s = jnp.where(allowed, dot_nn(qs[here], keys) * FACTOR, NEG)
                top = jnp.maximum(peak[here], jnp.max(s, axis=1, keepdims=True))
                p = jnp.where(allowed, jnp.exp2(s - top[:, :1]), 0.0)
                shrink = jnp.exp2(peak[here] - top)
                total[here] = total[here] * shrink + fold(p, jnp.add)
                acc[here] = acc[here] * shrink + dot_nn(p.astype(jnp.bfloat16), values)
                peak[here] = top

        write()


def prefill(q, keys, values, meta, lengths, groups, columns, name, before=None):
    tok = q.shape[0]
    count = values.shape[0]
    heads = H // KVH
    rows = heads * tok
    pairs = rows * count // 2 * groups
    extra = [] if before is None else [before]
    return pl.pallas_call(
        functools.partial(prefill_kernel, tok, heads),
        out_shape=jax.ShapeDtypeStruct((tok, columns), jnp.bfloat16),
        grid_spec=pltpu.PrefetchScalarGridSpec(
            num_scalar_prefetch=2,
            grid=(groups,),
            in_specs=[
                pl.BlockSpec((tok, heads * HD), lambda g, meta, lengths: (0, meta[1] + g)),
                pl.BlockSpec((HD, count), lambda g, meta, lengths: (meta[2] + g, 0)),
                pl.BlockSpec((count, HD), lambda g, meta, lengths: (0, meta[2] + g)),
            ]
            + [HBM] * len(extra),
            out_specs=pl.BlockSpec((tok, heads * HD), lambda g, meta, lengths: (0, meta[3] + g)),
            scratch_shapes=[
                pltpu.VMEM((rows, HD), jnp.bfloat16),
                pltpu.VMEM((rows, HD), jnp.float32),
                pltpu.VMEM((rows, HD), jnp.float32),
                pltpu.VMEM((rows, HD), jnp.float32),
            ],
        ),
        compiler_params=pltpu.CompilerParams(vmem_limit_bytes=ROOM),
        cost_estimate=pl.CostEstimate(
            flops=pairs * HD * 8, bytes_accessed=count * HD * 4 * groups, transcendentals=pairs
        ),
        input_output_aliases={} if before is None else {5: 0},
        name=name,
    )(meta, lengths, q, keys, values, *extra)


def settle_kernel(meta, piece, whole, out, sem):
    width = piece.shape[1]
    where = pl.ds(pl.multiple_of((1 - meta[CORE]) * width, width), width)
    copy = pltpu.make_async_copy(piece, out.at[:, where], sem)
    copy.start()
    copy.wait()


def settle(whole, piece, meta):
    return pl.pallas_call(
        settle_kernel,
        out_shape=jax.ShapeDtypeStruct(whole.shape, whole.dtype),
        in_specs=[SMEM, VMEM, HBM],
        out_specs=HBM,
        scratch_shapes=[pltpu.SemaphoreType.DMA],
        input_output_aliases={2: 0},
        compiler_params=pltpu.CompilerParams(vmem_limit_bytes=LITTLE),
        cost_estimate=pl.CostEstimate(flops=0, bytes_accessed=piece.size * 4, transcendentals=0),
        name="settle",
    )(meta, piece, whole)


def allowed_at(first, base, tok, length, lengths):
    t = first + lax.broadcasted_iota(jnp.int32, (tok, 1), 0)
    u = base + lax.broadcasted_iota(jnp.int32, (tok, length), 1)
    return (u <= t) & (u >= start_of(t, lengths))


def column_block(at):
    return pl.ds(pl.multiple_of(at, HD), HD)


def keys_of(upper, g):
    return upper[column_block(g * HD), :]


def values_of(lower, g):
    half = lower.shape[1] // 2
    both = [lower[:, column_block(side * half + g * HD)] for side in range(2)]
    return jnp.concatenate(both, axis=0)


def add_block(tok, heads, q_at, keys, values, allowed, sums, fresh=False):
    length = keys.shape[1]
    for j in range(0, heads, PAIR):
        some = min(PAIR, heads - j)
        p = jnp.exp2(dot_nn(q_at(j * tok, some * tok), keys) * FACTOR)
        if allowed is not None:
            p = p.reshape(some, tok, length)
            p = jnp.where(allowed[None], p, 0.0).reshape(some * tok, length)
        more = (fold(p, jnp.add), dot_nn(p.astype(jnp.bfloat16), values))
        for ref, value in zip(sums, more):
            here = slice(j * tok, (j + some) * tok)
            ref[here] = value if fresh else ref[here] + value


def relation(meta, part, side, tok, lengths):
    first = (meta[CHIP] * 2 + side) * tok
    base = meta[PARTS + part] * 2 * tok
    relevant = (base < first) & (meta[PARTS + part] != meta[CHIP])
    relevant = relevant & (base + 2 * tok > start_of(first, lengths))
    return relevant, base >= start_of(first + tok - 1, lengths), first, base


def side_rows(side, heads, tok):
    return pl.ds(pl.multiple_of(side * (heads * tok), HD), heads * tok)


def open_kernel(tok, heads, groups, meta, lengths, q, q_near, block, qs, total, acc):
    core = meta[CORE]
    rows = heads * tok
    for source, side, skip in ((q, core, core * groups * heads), (q_near, 1 - core, 0)):
        for g in range(groups):
            for j in range(heads):
                at = pl.ds(pl.multiple_of(side * rows + j * tok, HD), tok)
                qs[g, at] = source[:, column_block((skip + g * heads + j) * HD)]
    upper, lower = block.at[: block.shape[0] // 2], block.at[block.shape[0] // 2 :]

    @pl.loop(0, groups)
    def _(g):
        keys, values = keys_of(upper, g), values_of(lower, g)
        for side in range(2):
            length = (side + 1) * tok
            first = (meta[CHIP] * 2 + side) * tok
            allowed = allowed_at(first, meta[CHIP] * 2 * tok, tok, length, lengths)
            here = side_rows(side, heads, tok)
            q_at = lambda at, count: qs[g, pl.ds(side * rows + at, count)]
            add_block(tok, heads, q_at, keys[:, :length], values[:length], allowed,
                      (total.at[g, here], acc.at[g, here]), True)


def open_sums(q, q_near, block, meta, lengths):
    tok = q.shape[0]
    heads = H // KVH
    groups = q_near.shape[1] // (heads * HD)
    rows = 2 * heads * tok
    sums = jax.ShapeDtypeStruct((groups, rows, HD), jnp.float32)
    pairs = groups * rows * tok * 2
    return pl.pallas_call(
        functools.partial(open_kernel, tok, heads, groups),
        out_shape=[jax.ShapeDtypeStruct((groups, rows, HD), jnp.bfloat16), sums, sums],
        in_specs=[SMEM, SMEM, VMEM, VMEM, VMEM],
        out_specs=[VMEM] * 3,
        compiler_params=pltpu.CompilerParams(vmem_limit_bytes=2 * LITTLE),
        cost_estimate=pl.CostEstimate(
            flops=pairs * HD * 8, bytes_accessed=q.size * 2, transcendentals=pairs
        ),
        name="open",
    )(meta, lengths, q, q_near, block)


def stage_body(tok, heads, groups, first_part, meta, lengths, qs, before, one, two, total, acc, held):
    held[0], held[1] = one[...], two[...]
    total[...], acc[...] = before[0][...], before[1][...]
    half = held.shape[1] // 2

    @pl.loop(0, 4 * groups)
    def _(step):
        which, rest = lax.div(step, 2 * groups), lax.rem(step, 2 * groups)
        g, side = lax.div(rest, 2), lax.rem(rest, 2)
        relevant, clear, first, base = relation(meta, first_part + which, side, tok, lengths)
        here = side_rows(side, heads, tok)
        sums = (total.at[g, here], acc.at[g, here])
        at = side * (heads * tok)
        q_at = lambda off, count: qs[g, pl.ds(pl.multiple_of(at + off, HD), count)]
        upper, lower = held.at[which, :half], held.at[which, half:]

        @pl.when(relevant & clear)
        def _():
            add_block(tok, heads, q_at, keys_of(upper, g), values_of(lower, g), None, sums)

        @pl.when(relevant & jnp.logical_not(clear))
        def _():
            allowed = allowed_at(first, base, tok, 2 * tok, lengths)
            add_block(tok, heads, q_at, keys_of(upper, g), values_of(lower, g), allowed, sums)


def stage_kernel(tok, heads, groups, first_part, own, *refs):
    meta, lengths, qs, total_in, acc_in, one, two = refs[:7]
    if own is None:
        total, acc, held = refs[7:]
    else:
        sources, table = refs[7:10], refs[10]
        total, acc, held = refs[11], refs[12], refs[19]
        state, (q3, k3, v3, sems) = refs[13:19], refs[20:]
        copies = request_copies(own, meta, sources, (q3, k3, v3), sems)
        for copy in copies:
            copy.start()
    before = (total_in, acc_in)
    stage_body(tok, heads, groups, first_part, meta, lengths, qs, before, one, two, total, acc, held)
    if own is not None:
        for copy in copies:
            copy.wait()
        requests_body(own, heads, groups, 2 * tok, meta, table, *state, q3, k3, v3)


def stage(state, pair, first_part, meta, lengths, requests=None):
    qs, total, acc = state
    groups, rows, unused = qs.shape
    tok = pair[0].shape[1] // 2
    heads = rows // (2 * tok)
    pairs = groups * rows * tok * 2
    out_shape = [jax.ShapeDtypeStruct(x.shape, x.dtype) for x in (total, acc)]
    scratch = [pltpu.VMEM((2, *pair[0].shape), pair[0].dtype)]
    sources, own = [], None
    if requests is not None:
        *sources, own = requests
        steps = sources[0].shape[1]
        width = sources[1].shape[2] // 2
        size = heads * own * steps
        sums = jax.ShapeDtypeStruct((groups, size, HD), jnp.float32)
        new = jax.ShapeDtypeStruct((own * steps, width), jnp.bfloat16)
        out_shape += [
            sums, sums, jax.ShapeDtypeStruct((groups, size, HD), jnp.bfloat16), new, new,
            jax.ShapeDtypeStruct((own, (LEVELS - PARTS) * 2 * tok), jnp.float32),
        ]
        scratch += [
            pltpu.VMEM((own, steps, groups * heads * HD), jnp.bfloat16),
            pltpu.VMEM((own, steps, width), jnp.bfloat16),
            pltpu.VMEM((own, steps, width), jnp.bfloat16),
            pltpu.SemaphoreType.DMA((3,)),
        ]
    new = pl.pallas_call(
        functools.partial(stage_kernel, tok, heads, groups, first_part, own),
        out_shape=out_shape,
        in_specs=[SMEM, SMEM] + [VMEM] * 5 + ([HBM] * 3 + [VMEM] if sources else []),
        out_specs=[VMEM] * len(out_shape),
        scratch_shapes=scratch,
        input_output_aliases={3: 0, 4: 1},
        compiler_params=pltpu.CompilerParams(vmem_limit_bytes=ROOM),
        cost_estimate=pl.CostEstimate(
            flops=pairs * HD * 8, bytes_accessed=tok * HD, transcendentals=pairs
        ),
        name=f"stage{first_part}",
    )(meta, lengths, qs, total, acc, *pair, *sources)
    return (qs, *new[:2]), new[2:]


def finish_kernel(tok, heads, groups, done, meta, lengths, qs, total, acc, *refs):
    parts = len(refs) - 10
    blocks, last = refs[:parts], refs[parts : parts + 2]
    near, out, held, peak, total_now, acc_now, result, sem = refs[parts + 2 :]
    rows = heads * tok
    core = meta[CORE]
    half = held.shape[1] // 2

    def fill(first):
        for i in range(first, parts):
            held[i] = blocks[i][...]
        held[parts, :half] = last[0][...]
        held[parts, half:] = last[1][...]

    def turn_of(step):
        turn, g = lax.div(step, groups), lax.rem(step, groups)
        side = jnp.where(turn == 0, 1 - core, core)
        at = side * rows
        q_at = lambda off, count: qs[g, pl.ds(pl.multiple_of(at + off, HD), count)]
        return turn, g, side, q_at

    def write(turn, g):
        whole = jnp.sum(total_now[...], axis=1, keepdims=True)
        value = (acc_now[...] / whole).astype(result.dtype)
        for j in range(heads):
            result[turn, :, column_block((g * heads + j) * HD)] = value[j * tok : (j + 1) * tok]
        return sound(whole)

    def one_turn(step, fine):
        turn, g, side, q_at = turn_of(step)
        here = side_rows(side, heads, tok)
        total_now[...] = total[g, here]
        acc_now[...] = acc[g, here]

        @pl.loop(done, parts + 1)
        def _(i):
            relevant, clear, first, base = relation(meta, i, side, tok, lengths)
            upper, lower = held.at[i, :half], held.at[i, half:]
            sums = (total_now, acc_now)

            @pl.when(relevant & clear)
            def _():
                add_block(tok, heads, q_at, keys_of(upper, g), values_of(lower, g), None, sums)

            @pl.when(relevant & jnp.logical_not(clear))
            def _():
                allowed = allowed_at(first, base, tok, 2 * tok, lengths)
                add_block(tok, heads, q_at, keys_of(upper, g), values_of(lower, g), allowed, sums)

        return fine & write(turn, g).astype(jnp.int32)

    fill(done)
    fine = lax.fori_loop(0, 2 * groups, one_turn, jnp.int32(1))

    @pl.when(fine == 0)
    def _():
        fill(0)

        @pl.loop(0, 2 * groups)
        def _(step):
            turn, g, side, q_at = turn_of(step)
            first = (meta[CHIP] * 2 + side) * tok
            peak[...] = jnp.full_like(peak, NEG)
            total_now[...] = jnp.zeros_like(total_now)
            acc_now[...] = jnp.zeros_like(acc_now)

            @pl.loop(0, (parts + 1) * heads)
            def _(step):
                i, j = lax.div(step, heads), lax.rem(step, heads)
                keys = keys_of(held.at[i, :half], g)
                values = values_of(held.at[i, half:], g)
                allowed = allowed_at(first, meta[PARTS + i] * 2 * tok, tok, 2 * tok, lengths)
                mine = pl.ds(pl.multiple_of(j * tok, tok), tok)
                s = jnp.where(allowed, dot_nn(q_at(j * tok, tok), keys) * FACTOR, NEG)
                top = jnp.maximum(peak[mine], jnp.max(s, axis=1, keepdims=True))
                p = jnp.where(allowed, jnp.exp2(s - top[:, :1]), 0.0)
                shrink = jnp.exp2(peak[mine] - top)
                total_now[mine] = total_now[mine] * shrink + fold(p, jnp.add)
                acc_now[mine] = acc_now[mine] * shrink + dot_nn(p.astype(jnp.bfloat16), values)
                peak[mine] = top

            write(turn, g)

    width = near.shape[1]
    where = pl.ds(pl.multiple_of(core * width, width), width)
    copy = pltpu.make_async_copy(result.at[1], out.at[:, where], sem)
    copy.start()
    near[...] = result[0]
    copy.wait()


def finish(state, blocks, last, done, meta, lengths):
    qs, total, acc = state
    groups, rows, unused = qs.shape
    tok = last[0].shape[1] // 2
    heads = rows // (2 * tok)
    width = groups * heads * HD
    sums = pltpu.VMEM((heads * tok, HD), jnp.float32)
    return pl.pallas_call(
        functools.partial(finish_kernel, tok, heads, groups, done),
        out_shape=[
            jax.ShapeDtypeStruct((tok, width), jnp.bfloat16),
            jax.ShapeDtypeStruct((tok, 2 * width), jnp.bfloat16),
        ],
        in_specs=[SMEM, SMEM] + [VMEM] * (5 + len(blocks)),
        out_specs=[VMEM, HBM],
        scratch_shapes=[
            pltpu.VMEM((len(blocks) + 1, *blocks[0].shape), blocks[0].dtype),
            sums, sums, sums,
            pltpu.VMEM((2, tok, width), jnp.bfloat16),
            pltpu.SemaphoreType.DMA,
        ],
        compiler_params=pltpu.CompilerParams(vmem_limit_bytes=ROOM),
        cost_estimate=pl.CostEstimate(
            flops=groups * rows * tok * HD * 8, bytes_accessed=tok * width * 4,
            transcendentals=groups * rows * tok * 2,
        ),
        name="finish",
    )(meta, lengths, qs, total, acc, *blocks, *last)


def request_sums(query, keys, values, mask):
    p = jnp.exp2(dot_nn(query, keys) * FACTOR)
    p = jnp.where(mask[None], p.reshape(-1, *mask.shape), 0.0).reshape(p.shape)
    return fold(p, jnp.add), dot_nn(p.astype(jnp.bfloat16), values)


def fresh_scores(query, newk, own):
    s = dot_nt(query, newk) * FACTOR
    size = newk.shape[0]
    row = lax.broadcasted_iota(jnp.int32, (size, size), 0)
    col = lax.broadcasted_iota(jnp.int32, (size, size), 1)
    ok = (lax.rem(row, own) == lax.rem(col, own)) & (lax.div(col, own) <= lax.div(row, own))
    return s.reshape(-1, size, size), ok


def request_copies(own, meta, sources, held, sems):
    requests = pl.ds(lax.div(meta[CHIP], 2) * own, own)
    copies = []
    for i, (source, target) in enumerate(zip(sources, held)):
        width = target.shape[2]
        where = pl.ds(pl.multiple_of(meta[CORE] * width, width), width)
        copies.append(pltpu.make_async_copy(source.at[requests, :, where], target, sems.at[i]))
    return copies


def requests_body(own, heads, groups, length, meta, table, total, acc, query, newk, newv, mask, q3, k3, v3):
    steps = q3.shape[1]
    level = lax.div(meta[CHIP], 2)
    rows = table[pl.ds(pl.multiple_of(level * own, own), own), :]
    lane = lax.div(lax.broadcasted_iota(jnp.int32, (own, length), 1), BLK)
    for i in range(mask.shape[1] // length):
        number = lane + meta[PARTS + i] * (length // BLK)
        hit = rows[:, :1] == number
        for j in range(1, rows.shape[1]):
            hit = hit | (rows[:, j : j + 1] == number)
        mask[:, i * length : (i + 1) * length] = hit.astype(jnp.float32)
    for s in range(steps):
        for g in range(groups):
            col = slice(g * HD, (g + 1) * HD)
            at = slice(s * own, (s + 1) * own)
            newk[at, col] = k3[:, s, col]
            newv[at, col] = v3[:, s, col]
            for j in range(heads):
                first = (g * heads + j) * HD
                row = (j * steps + s) * own
                query[g, row : row + own] = q3[:, s, first : first + HD]

    @pl.loop(0, groups)
    def _(g):
        col = column_block(g * HD)
        s, ok = fresh_scores(query[g], newk[:, col], own)
        p = jnp.where(ok[None], jnp.exp2(s), 0.0).reshape(-1, s.shape[2])
        first = jnp.sum(p, axis=1, keepdims=True)
        lead = lax.broadcasted_iota(jnp.int32, (p.shape[0], HD), 1) == 0
        total[g] = jnp.where(lead, first, 0.0)
        acc[g] = dot_nn(p.astype(jnp.bfloat16), newv[:, col])


def early_kernel(groups, total_in, acc_in, query, mask, *refs):
    blocks, (total, acc) = refs[:-2], refs[-2:]
    half, length = blocks[0].shape[0] // 2, blocks[0].shape[1]

    @pl.loop(0, groups)
    def _(g):
        sums = [total_in[g], acc_in[g]]
        for i, block in enumerate(blocks):
            open_to = mask[:, i * length : (i + 1) * length] > 0
            keys, values = keys_of(block.at[:half], g), values_of(block.at[half:], g)
            more = request_sums(query[g], keys, values, open_to)
            sums = [x + y for x, y in zip(sums, more)]
        total[g], acc[g] = sums


def early_decode(state, blocks):
    total, acc, query, newk, newv, mask = state
    groups, rows, unused = query.shape
    pairs = groups * rows * len(blocks) * blocks[0].shape[1]
    sums = jax.ShapeDtypeStruct(total.shape, total.dtype)
    new = pl.pallas_call(
        functools.partial(early_kernel, groups),
        out_shape=[sums, sums],
        in_specs=[VMEM] * (4 + len(blocks)),
        out_specs=[VMEM] * 2,
        input_output_aliases={0: 0, 1: 1},
        compiler_params=pltpu.CompilerParams(vmem_limit_bytes=2 * LITTLE),
        cost_estimate=pl.CostEstimate(
            flops=pairs * HD * 8, bytes_accessed=rows * HD, transcendentals=pairs
        ),
        name="early_decode",
    )(total, acc, query, mask, *blocks)
    return [*new, query, newk, newv, mask]


def late_kernel(own, steps, heads, groups, done, meta, total, acc, query, newk, newv, mask, *refs):
    parts = len(refs) - 3
    blocks, last, out = refs[:parts], refs[parts : parts + 2], refs[-1]
    length = blocks[0].shape[1]
    half = blocks[0].shape[0] // 2
    size = own * steps

    def write(g, sums, whole):
        result = (sums / whole).astype(out.dtype)
        for j in range(heads):
            out[:, column_block((g * heads + j) * HD)] = result[j * size : (j + 1) * size]

    def one_group(g, fine):
        sums = [total[g], acc[g]]
        for i in range(done, parts + 1):
            upper = last[0] if i == parts else blocks[i].at[:half]
            lower = last[1] if i == parts else blocks[i].at[half:]
            open_to = mask[:, i * length : (i + 1) * length] > 0
            more = request_sums(query[g], keys_of(upper, g), values_of(lower, g), open_to)
            sums = [x + y for x, y in zip(sums, more)]
        whole = jnp.sum(sums[0], axis=1, keepdims=True)
        write(g, sums[1], whole)
        return fine & sound(whole).astype(jnp.int32)

    fine = lax.fori_loop(0, groups, one_group, jnp.int32(1))

    @pl.when(fine == 0)
    def _():
        @pl.loop(0, groups)
        def _(g):
            col = column_block(g * HD)
            fresh, ok = fresh_scores(query[g], newk[:, col], own)
            fresh = jnp.where(ok[None], fresh, NEG).reshape(-1, size)
            top = jnp.max(fresh, axis=1, keepdims=True)
            p = jnp.exp2(fresh - top)
            whole = jnp.sum(p, axis=1, keepdims=True)
            sums = dot_nn(p.astype(jnp.bfloat16), newv[:, col])
            for i in range(parts + 1):
                upper = last[0] if i == parts else blocks[i].at[:half]
                lower = last[1] if i == parts else blocks[i].at[half:]
                s = dot_nn(query[g], keys_of(upper, g)) * FACTOR
                open_to = mask[:, i * length : (i + 1) * length] > 0
                s = jnp.where(open_to[None], s.reshape(-1, own, length), NEG).reshape(s.shape)
                higher = jnp.maximum(top, jnp.max(s, axis=1, keepdims=True))
                p = jnp.exp2(s - higher)
                shrink = jnp.exp2(top - higher)
                whole = whole * shrink + jnp.sum(p, axis=1, keepdims=True)
                sums = sums * shrink + dot_nn(p.astype(jnp.bfloat16), values_of(lower, g))
                top = higher
            write(g, sums, whole)


def late_decode(early, blocks, last, done, own, steps, meta):
    groups, rows, unused = early[0].shape
    heads = H // KVH
    parts, length = len(blocks) + 1, blocks[0].shape[1]
    pairs = groups * rows * (parts - done) * length
    return pl.pallas_call(
        functools.partial(late_kernel, own, steps, heads, groups, done),
        out_shape=jax.ShapeDtypeStruct((own * steps, groups * heads * HD), jnp.bfloat16),
        in_specs=[SMEM] + [VMEM] * (len(early) + len(blocks) + 2),
        out_specs=VMEM,
        compiler_params=pltpu.CompilerParams(vmem_limit_bytes=ROOM),
        cost_estimate=pl.CostEstimate(
            flops=pairs * HD * 8, bytes_accessed=rows * HD, transcendentals=pairs
        ),
        name="late_decode",
    )(meta, *early, *blocks, *last)


def decode_kernel(parts, steps, heads, groups, starts, q, mask, newk, newv, *refs):
    kheld, vheld = refs[:parts], refs[parts : 2 * parts]
    out, kall, vall, sems, scores = refs[2 * parts :]
    own = q.shape[0]
    rows = heads * own
    length = kheld[0].shape[1]
    copies = []
    for i in range(parts):
        where = pl.ds(pl.multiple_of(starts[i], HD), length)
        copies.append(pltpu.make_async_copy(kheld[i], kall.at[:, where], sems.at[2 * i]))
        copies.append(pltpu.make_async_copy(vheld[i], vall.at[where], sems.at[2 * i + 1]))
    for copy in copies:
        copy.start()
    row = lax.broadcasted_iota(jnp.int32, (own, own), 0)
    col = lax.broadcasted_iota(jnp.int32, (own, own), 1)
    fresh_ok = (lax.div(row, steps) == lax.div(col, steps)) & (col <= row)

    def columns(g):
        return slice(g * HD, (g + 1) * HD)

    def stacked(g):
        first = g * heads
        slices = [q[:, (first + j) * HD : (first + j + 1) * HD] for j in range(heads)]
        return jnp.concatenate([x.astype(jnp.float32) for x in slices], 0).astype(jnp.bfloat16)

    def keep(allowed, x, other):
        y = x.reshape(heads, own, x.shape[1])
        return jnp.where(allowed[None], y, other).reshape(x.shape)

    def open_to(i):
        return mask[:, pl.ds(pl.multiple_of(starts[i], HD), length)] > 0

    def write(g, acc, whole):
        result = acc / whole
        for j in range(heads):
            out[:, (g * heads + j) * HD : (g * heads + j + 1) * HD] = result[
                j * own : (j + 1) * own
            ].astype(out.dtype)

    fine = None
    for g in range(groups):
        query = stacked(g)
        p = keep(fresh_ok, jnp.exp2(dot_nt(query, newk[:, columns(g)]) * FACTOR), 0.0)
        whole = jnp.sum(p, axis=1, keepdims=True)
        acc = dot_nn(p.astype(jnp.bfloat16), newv[:, columns(g)])
        total = jnp.zeros((rows, HD), jnp.float32)
        for i in range(parts):
            p = jnp.exp2(dot_nn(query, kheld[i][columns(g)]) * FACTOR)
            p = keep(open_to(i), p, 0.0)
            total = total + fold(p, jnp.add)
            acc = acc + dot_nn(p.astype(jnp.bfloat16), vheld[i][:, columns(g)])
        whole = whole + jnp.sum(total, axis=1, keepdims=True)
        write(g, acc, whole)
        fine = sound(whole) if fine is None else fine & sound(whole)

    @pl.when(jnp.logical_not(fine))
    def _():
        for g in range(groups):
            query = stacked(g)
            fresh = keep(fresh_ok, dot_nt(query, newk[:, columns(g)]) * FACTOR, NEG)
            top = jnp.max(fresh, axis=1, keepdims=True)
            for i in range(parts):
                s = keep(open_to(i), dot_nn(query, kheld[i][columns(g)]) * FACTOR, NEG)
                scores[:, i * length : (i + 1) * length] = s
                top = jnp.maximum(top, jnp.max(s, axis=1, keepdims=True))
            p = jnp.exp2(fresh - top)
            whole = jnp.sum(p, axis=1, keepdims=True)
            acc = dot_nn(p.astype(jnp.bfloat16), newv[:, columns(g)])
            for i in range(parts):
                p = jnp.exp2(scores[:, i * length : (i + 1) * length] - top)
                whole = whole + jnp.sum(p, axis=1, keepdims=True)
                acc = acc + dot_nn(p.astype(jnp.bfloat16), vheld[i][:, columns(g)])
            write(g, acc, whole)

    for copy in copies:
        copy.wait()


def decode(q, mask, newk, newv, kparts, vparts, starts, steps):
    own = q.shape[0]
    parts = len(kparts)
    length, width = vparts[0].shape
    count = parts * length
    heads = H // KVH
    groups = width // HD
    rows = heads * own
    pairs = groups * rows * count
    return pl.pallas_call(
        functools.partial(decode_kernel, parts, steps, heads, groups),
        out_shape=[
            jax.ShapeDtypeStruct(q.shape, jnp.bfloat16),
            jax.ShapeDtypeStruct((width, count), jnp.bfloat16),
            jax.ShapeDtypeStruct((count, width), jnp.bfloat16),
        ],
        grid_spec=pltpu.PrefetchScalarGridSpec(
            num_scalar_prefetch=1,
            grid=(),
            in_specs=[VMEM] * (4 + 2 * parts),
            out_specs=[VMEM, HBM, HBM],
            scratch_shapes=[
                pltpu.SemaphoreType.DMA((2 * parts,)),
                pltpu.VMEM((rows, count), jnp.float32),
            ],
        ),
        compiler_params=pltpu.CompilerParams(vmem_limit_bytes=ROOM),
        cost_estimate=pl.CostEstimate(
            flops=pairs * HD * 4, bytes_accessed=count * width * 4, transcendentals=pairs
        ),
        name="decode",
    )(starts, q, mask, newk, newv, *kparts, *vparts)


def prepare_kernel(meta, k, v, send, block):
    tok, width = k.shape[0], k.shape[1] // 2
    mine = pl.ds(pl.multiple_of(meta[0] * width, width), width)
    other = pl.ds(pl.multiple_of((1 - meta[0]) * width, width), width)
    send[:width] = k[:, other].astype(jnp.float32).T.astype(send.dtype)
    send[width:] = v[:, other]
    block[:width, mine] = k[:, mine].astype(jnp.float32).T.astype(block.dtype)
    block[width:, mine] = v[:, mine]


def prepare(k, v, core):
    tok, width = k.shape[0], k.shape[1] // 2
    assert tok == width
    return pl.pallas_call(
        prepare_kernel,
        out_shape=[
            jax.ShapeDtypeStruct((2 * tok, width), k.dtype),
            jax.ShapeDtypeStruct((2 * width, 2 * tok), k.dtype),
        ],
        in_specs=[SMEM, VMEM, VMEM],
        out_specs=[VMEM] * 2,
        compiler_params=pltpu.CompilerParams(vmem_limit_bytes=LITTLE),
        name="prepare",
    )(core[None], k, v)


def join_kernel(meta, block_in, theirs, block):
    width = theirs.shape[1]
    other = pl.ds(pl.multiple_of((1 - meta[0]) * width, width), width)
    block[...] = block_in[...]
    block[:width, other] = theirs[:width]
    block[width:, other] = theirs[width:]


def join(block, theirs, core):
    return pl.pallas_call(
        join_kernel,
        out_shape=jax.ShapeDtypeStruct(block.shape, block.dtype),
        in_specs=[SMEM, VMEM, VMEM],
        out_specs=VMEM,
        input_output_aliases={1: 0},
        compiler_params=pltpu.CompilerParams(vmem_limit_bytes=LITTLE),
        name="join",
    )(core[None], block, theirs)


def take_kernel(meta, whole, out, sem):
    width = out.shape[1]
    where = pl.ds(pl.multiple_of((1 - meta[CORE]) * width, width), width)
    copy = pltpu.make_async_copy(whole.at[:, where], out, sem)
    copy.start()
    copy.wait()


def take_other_half(whole, meta):
    return pl.pallas_call(
        take_kernel,
        out_shape=jax.ShapeDtypeStruct((whole.shape[0], whole.shape[1] // 2), whole.dtype),
        in_specs=[SMEM, HBM],
        out_specs=VMEM,
        scratch_shapes=[pltpu.SemaphoreType.DMA],
        compiler_params=pltpu.CompilerParams(vmem_limit_bytes=LITTLE),
        name="take",
    )(meta, whole)


def project_kernel(meta, *refs):
    pieces, (whole, other), outs, (sorted_rows,) = refs[:-7], refs[-7:-5], refs[-5:-1], refs[-1:]
    parts = len(pieces)
    rows = pieces[0].shape[0]
    for i, piece in enumerate(pieces):
        at = pl.ds(pl.multiple_of(meta[LEVELS + i] * rows, rows), rows)
        sorted_rows[at] = piece[...]
    depth = other.shape[1]
    mine = whole[:, pl.ds(pl.multiple_of(meta[CORE] * depth, depth), depth)]
    half = parts * rows // 2
    here = pl.ds(pl.multiple_of(meta[ACROSS] * half, half), half)
    there = pl.ds(pl.multiple_of((1 - meta[ACROSS]) * half, half), half)
    kept, beside, across, corner = outs
    for at, near, far in ((here, kept, beside), (there, across, corner)):
        some = sorted_rows[at]
        near[...] = dot_nt(mine, some).astype(near.dtype)
        far[...] = dot_nt(other[...], some).astype(far.dtype)


def project(pieces, whole, other, meta):
    rows = len(pieces) * pieces[0].shape[0]
    width, depth = other.shape
    block = jax.ShapeDtypeStruct((width, rows // 2), jnp.bfloat16)
    return pl.pallas_call(
        project_kernel,
        out_shape=[jax.ShapeDtypeStruct(block.shape, jnp.float32)] + [block] * 3,
        in_specs=[SMEM] + [VMEM] * (len(pieces) + 2),
        out_specs=[VMEM] * 4,
        scratch_shapes=[pltpu.VMEM((rows, depth), jnp.bfloat16)],
        compiler_params=pltpu.CompilerParams(vmem_limit_bytes=2 * LITTLE),
        cost_estimate=pl.CostEstimate(
            flops=rows * width * depth * 4, bytes_accessed=width * depth * 4, transcendentals=0
        ),
        name="project",
    )(meta, *pieces, whole, other)


def index(z, y, c):
    return (z * 2 + y) * 2 + c


def on_ring(r, chips):
    return (r, 0) if r < chips // 2 else (chips - 1 - r, 1)


def ring_perm(chips, d):
    return [
        (index(*on_ring(r, chips), c), index(*on_ring((r + d) % chips, chips), c))
        for r in range(chips)
        for c in range(2)
    ]


def ring_place(r, chips):
    r = lax.rem(r + 2 * chips, chips)
    return jnp.where(r < chips // 2, r * 2, (chips - 1 - r) * 2 + 1)


def spread(x, n):
    place = lax.axis_index("seq")
    deep = n // 4
    everyone = [(z, y, c) for z in range(deep) for y in range(2) for c in range(2)]
    z, y, c = place // 4, (place // 2) % 2, place % 2
    held = [(x, z, y, c)]
    for d in range(1, deep):
        perm = [(index(*p), index((p[0] - d) % deep, p[1], p[2])) for p in everyone]
        held.append((lax.ppermute(x, "seq", perm), lax.rem(z + d, deep), y, c))
    perm = [(index(*p), index(p[0], 1 - p[1], p[2])) for p in everyone]
    held += [(lax.ppermute(b, "seq", perm), bz, 1 - by, bc) for b, bz, by, bc in held]
    perm = [(index(*p), index(p[0], p[1], 1 - p[2])) for p in everyone]
    held += [(lax.ppermute(b, "seq", perm), bz, by, 1 - bc) for b, bz, by, bc in held]
    return [b for b, *_ in held], jnp.stack([index(bz, by, bc) for _, bz, by, bc in held])


def open_blocks(table, steps, count):
    number = lax.broadcasted_iota(jnp.int32, (*table.shape, count), 2) // BLK
    mask = jnp.any(table[:, :, None] == number, axis=1).astype(jnp.float32)
    return jnp.repeat(mask, steps, axis=0)


def whole_heads(n, q_pre, k_cache, v_cache, lengths, q_dec, k_new, v_new, block_table, w_out):
    tok = q_pre.shape[0]
    place = lax.axis_index("seq").astype(jnp.int32)
    rows, steps = q_dec.shape[0], q_dec.shape[1]
    own = rows // n
    kparts, sources = spread(k_cache.T, n)
    vparts, _ = spread(v_cache, n)
    starts = sources.astype(jnp.int32) * tok

    def mine(x):
        y = lax.dynamic_slice_in_dim(x, place * own, own, 0)
        return y.reshape(own * steps, -1) if x.ndim == 3 else y

    mask = open_blocks(mine(block_table), steps, n * tok)
    attn_own, keys, values = decode(
        mine(q_dec), mask, mine(k_new), mine(v_new), kparts, vparts, starts, steps
    )
    attn = lax.all_gather(attn_own, "seq", axis=0, tiled=True)
    flat = jnp.dot(attn, w_out, preferred_element_type=jnp.float32).astype(jnp.bfloat16)
    dec_out = lax.psum_scatter(
        flat.reshape(rows, steps, -1), "tp", scatter_dimension=0, tiled=True
    )
    zero = jnp.zeros((), jnp.int32)
    meta = jnp.stack([place * tok, zero, zero, zero])
    groups = k_cache.shape[1] // HD
    pre_out = prefill(
        q_pre, keys, values, meta, lengths, groups, q_pre.shape[1], "prefill"
    )
    return (pre_out, dec_out)


def split_heads(n, q_pre, k_cache, v_cache, lengths, q_dec, k_new, v_new, block_table, w_out):
    place = lax.axis_index("seq").astype(jnp.int32)
    across = lax.axis_index("tp").astype(jnp.int32)
    core, chip = lax.rem(place, 2), lax.div(place, 2)
    chips = n // 2
    far, deep = chips // 2, chips // 2
    z, y = lax.div(chip, 2), lax.rem(chip, 2)
    r = jnp.where(y == 0, z, chips - 1 - z)
    rows, steps = q_dec.shape[0], q_dec.shape[1]
    own = rows // deep
    sibling = [(i, i ^ 1) for i in range(n)]
    everyone = [(a, b, c) for a in range(deep) for b in range(2) for c in range(2)]

    order = [0] + [o for d in range(1, far) for o in (-d, d)] + [far]
    numbers = [ring_place(r + o, chips) for o in order]
    levels = [z] + [lax.rem(z + deep - d, deep) for d in range(1, deep)]
    assert len(numbers) == LEVELS - PARTS
    meta = jnp.stack([core, chip, across] + numbers + levels).astype(jnp.int32)

    send, block = prepare(k_cache, v_cache, core)
    theirs = lax.ppermute(send, "seq", sibling)
    width = q_pre.shape[1] // 2
    send_q = lax.dynamic_slice_in_dim(q_pre, (1 - core) * width, width, 1)
    theirs, send_q = lax.optimization_barrier((theirs, send_q))
    held = {0: join(block, theirs, core)}
    near_q = lax.ppermute(send_q, "seq", sibling)

    up, down = ring_perm(chips, 1), ring_perm(chips, -1)
    half = block.shape[0] // 2
    early, w_near = (), w_out
    for d in range(1, far + 1):
        if d < far:
            held[-d] = lax.ppermute(held[1 - d], "seq", up)
            held[d] = lax.ppermute(held[d - 1], "seq", down)
            last = (held[-d], held[d])
        else:
            last = (
                lax.ppermute(held[1 - d][:half], "seq", up),
                lax.ppermute(held[d - 1][half:], "seq", down),
            )
        if d == 1:
            state = open_sums(q_pre, near_q, held[0], meta, lengths)
        elif d < far:
            requests = (q_dec, k_new, v_new, block_table, own) if d == 2 else None
            pair = (held[1 - d], held[d - 1])
            state, more = stage(state, pair, 2 * d - 3, meta, lengths, requests)
            early = early or more
        else:
            blocks = [held[o] for o in order[:-1]]
            early = early_decode(early, blocks)
        last, state, early, w_near = lax.optimization_barrier((last, state, early, w_near))
        if d == 1:
            weights = w_near.T
            w_near = lax.ppermute(take_other_half(weights, meta), "seq", sibling)
        if d < far:
            held[-d], held[d] = last
    attn_own = late_decode(early, blocks, last, len(blocks), own, steps, meta)

    pieces = [attn_own]
    for d in range(1, deep):
        perm = [(index(*p), index((p[0] + d) % deep, p[1], p[2])) for p in everyone]
        pieces.append(lax.ppermute(attn_own, "seq", perm))
    attn_own, state = lax.optimization_barrier((attn_own, state))
    near, pre_out = finish(state, blocks, last, 2 * far - 3, meta, lengths)
    pieces, near, pre_out = lax.optimization_barrier((pieces, near, pre_out))
    back = lax.ppermute(near, "seq", sibling)
    pre_out = settle(pre_out, back, meta)

    total, *sent = project(pieces, weights, w_near, meta)
    got = []
    for piece, (dc, dx) in zip(sent, ((1, 0), (0, 1), (1, 1))):
        perm = [
            (i * 2 + x, (i ^ dc) * 2 + (x ^ dx)) for i in range(n) for x in range(2)
        ]
        got.append(lax.ppermute(piece, ("seq", "tp"), perm))
    got[0], pre_out = lax.optimization_barrier((got[0], pre_out))
    for piece in got:
        total = total + piece.astype(jnp.float32)
    dec_out = total.astype(jnp.bfloat16).T.reshape(deep // 2, steps, own, -1)
    return (pre_out, dec_out.transpose(0, 2, 1, 3).reshape(rows // 2, steps, -1))


def per_device(n, tp, q_pre, k_cache, v_cache, prompt_lengths, *rest):
    groups = k_cache.shape[1] // HD
    square = groups % 2 == 0 and k_cache.shape[1] == 2 * k_cache.shape[0]
    form = split_heads if square and tp == 2 and n == 2 * (LEVELS - PARTS) else whole_heads
    return form(n, q_pre, k_cache, v_cache, prompt_lengths.astype(jnp.int32), *rest)


def solution(mesh):
    placed = (
        P("seq", "tp"),
        P("seq", "tp"),
        P("seq", "tp"),
        P(),
        P(None, None, "tp"),
        P(None, None, "tp"),
        P(None, None, "tp"),
        P(),
        P("tp", "seq"),
    )
    return jax.shard_map(
        functools.partial(per_device, mesh.shape["seq"], mesh.shape["tp"]),
        mesh=mesh,
        in_specs=placed,
        out_specs=(P("seq", "tp"), P("tp", None, "seq")),
        check_vma=False,
    )
```

```python
import functools
import math

import jax
import jax.numpy as jnp
from jax import lax
from jax.experimental import pallas as pl
from jax.experimental.pallas import tpu as pltpu
from jax.sharding import PartitionSpec as P

H = 56
KVH = 8
HD = 128
BLK = 64
SPAN = 512
PAIR = 2
NEG = -1e30
LEAST, MOST = 2.0**-60, 2.0**100
FACTOR = math.log2(math.e) / math.sqrt(HD)
ROOM = 16 * 1024 * 1024
LITTLE = 4 * 1024 * 1024
CORE, CHIP, ACROSS, PARTS, LEVELS = 0, 1, 2, 3, 11
HBM = pl.BlockSpec(memory_space=pltpu.HBM)
VMEM = pl.BlockSpec(memory_space=pltpu.VMEM)
SMEM = pl.BlockSpec(memory_space=pltpu.SMEM)


def dot_nt(a, b):
    return lax.dot_general(a, b, (((1,), (1,)), ((), ())), preferred_element_type=jnp.float32)


def dot_nn(a, b):
    return lax.dot_general(a, b, (((1,), (0,)), ((), ())), preferred_element_type=jnp.float32)


def fold(x, op):
    out = x[:, :HD]
    for i in range(1, x.shape[1] // HD):
        out = op(out, x[:, i * HD : (i + 1) * HD])
    return out


def start_of(position, lengths):
    end = jnp.int32(0)
    out = jnp.zeros_like(position)
    for i in range(lengths.shape[0]):
        end = end + lengths[i]
        out = jnp.where(position >= end, end, out)
    return out


def sound(total):
    return (jnp.min(total) >= LEAST) & (jnp.max(total) <= MOST)


def prefill_kernel(tok, heads, meta, lengths, q, keys_all, values_all, *refs):
    out, qs, peak, total, acc = refs[-5:]
    for j in range(heads):
        qs[j * tok : (j + 1) * tok] = q[:, j * HD : (j + 1) * HD]
    total[...] = jnp.zeros_like(total)
    acc[...] = jnp.zeros_like(acc)

    begin = meta[0]
    finish = begin + tok
    low = start_of(begin, lengths)
    high = start_of(finish - 1, lengths)
    blocks = lax.div(finish - low + SPAN - 1, SPAN)
    clear = lax.div(finish - high, SPAN)

    def first_of(k):
        return jnp.maximum(finish - (k + 1) * SPAN, 0)

    def load(k):
        here = pl.ds(pl.multiple_of(first_of(k), HD), SPAN)
        return keys_all[:, here], values_all[here, :]

    def allowed_in(k):
        t = begin + lax.broadcasted_iota(jnp.int32, (tok, 1), 0)
        u = first_of(k) + lax.broadcasted_iota(jnp.int32, (tok, SPAN), 1)
        last = jnp.minimum(t, finish - k * SPAN - 1)
        return (u <= last) & (u >= start_of(t, lengths))

    def keep(allowed, x, other):
        some = x.shape[0] // tok
        return jnp.where(allowed[None], x.reshape(some, tok, SPAN), other).reshape(x.shape)

    def block(k, masked):
        keys, values = load(k)
        allowed = allowed_in(k) if masked else None
        for j in range(0, heads, PAIR):
            here = slice(j * tok, min(j + PAIR, heads) * tok)
            p = jnp.exp2(dot_nn(qs[here], keys) * FACTOR)
            if masked:
                p = keep(allowed, p, 0.0)
            total[here] += fold(p, jnp.add)
            acc[here] += dot_nn(p.astype(jnp.bfloat16), values)

    block(0, True)

    @pl.loop(1, jnp.maximum(clear, 1))
    def _(k):
        block(k, False)

    @pl.loop(jnp.maximum(clear, 1), blocks)
    def _(k):
        block(k, True)

    def write():
        whole = jnp.sum(total[...], axis=1, keepdims=True)
        result = (acc[...] / whole).astype(out.dtype)
        for j in range(heads):
            out[:, j * HD : (j + 1) * HD] = result[j * tok : (j + 1) * tok]
        return whole

    fine = sound(write())

    @pl.when(jnp.logical_not(fine))
    def _():
        peak[...] = jnp.full_like(peak, NEG)
        total[...] = jnp.zeros_like(total)
        acc[...] = jnp.zeros_like(acc)

        @pl.loop(0, blocks)
        def _(k):
            keys, values = load(k)
            allowed = allowed_in(k)

            @pl.loop(0, heads)
            def _(j):
                here = pl.ds(pl.multiple_of(j * tok, tok), tok)
                s = jnp.where(allowed, dot_nn(qs[here], keys) * FACTOR, NEG)
                top = jnp.maximum(peak[here], jnp.max(s, axis=1, keepdims=True))
                p = jnp.where(allowed, jnp.exp2(s - top[:, :1]), 0.0)
                shrink = jnp.exp2(peak[here] - top)
                total[here] = total[here] * shrink + fold(p, jnp.add)
                acc[here] = acc[here] * shrink + dot_nn(p.astype(jnp.bfloat16), values)
                peak[here] = top

        write()


def prefill(q, keys, values, meta, lengths, groups, columns, name, before=None):
    tok = q.shape[0]
    count = values.shape[0]
    heads = H // KVH
    rows = heads * tok
    pairs = rows * count // 2 * groups
    extra = [] if before is None else [before]
    return pl.pallas_call(
        functools.partial(prefill_kernel, tok, heads),
        out_shape=jax.ShapeDtypeStruct((tok, columns), jnp.bfloat16),
        grid_spec=pltpu.PrefetchScalarGridSpec(
            num_scalar_prefetch=2,
            grid=(groups,),
            in_specs=[
                pl.BlockSpec((tok, heads * HD), lambda g, meta, lengths: (0, meta[1] + g)),
                pl.BlockSpec((HD, count), lambda g, meta, lengths: (meta[2] + g, 0)),
                pl.BlockSpec((count, HD), lambda g, meta, lengths: (0, meta[2] + g)),
            ]
            + [HBM] * len(extra),
            out_specs=pl.BlockSpec((tok, heads * HD), lambda g, meta, lengths: (0, meta[3] + g)),
            scratch_shapes=[
                pltpu.VMEM((rows, HD), jnp.bfloat16),
                pltpu.VMEM((rows, HD), jnp.float32),
                pltpu.VMEM((rows, HD), jnp.float32),
                pltpu.VMEM((rows, HD), jnp.float32),
            ],
        ),
        compiler_params=pltpu.CompilerParams(vmem_limit_bytes=ROOM),
        cost_estimate=pl.CostEstimate(
            flops=pairs * HD * 8, bytes_accessed=count * HD * 4 * groups, transcendentals=pairs
        ),
        input_output_aliases={} if before is None else {5: 0},
        name=name,
    )(meta, lengths, q, keys, values, *extra)


def settle_kernel(meta, piece, whole, out, sem):
    width = piece.shape[1]
    where = pl.ds(pl.multiple_of((1 - meta[CORE]) * width, width), width)
    copy = pltpu.make_async_copy(piece, out.at[:, where], sem)
    copy.start()
    copy.wait()


def settle(whole, piece, meta):
    return pl.pallas_call(
        settle_kernel,
        out_shape=jax.ShapeDtypeStruct(whole.shape, whole.dtype),
        in_specs=[SMEM, VMEM, HBM],
        out_specs=HBM,
        scratch_shapes=[pltpu.SemaphoreType.DMA],
        input_output_aliases={2: 0},
        compiler_params=pltpu.CompilerParams(vmem_limit_bytes=LITTLE),
        cost_estimate=pl.CostEstimate(flops=0, bytes_accessed=piece.size * 4, transcendentals=0),
        name="settle",
    )(meta, piece, whole)


def allowed_at(first, base, tok, length, lengths):
    t = first + lax.broadcasted_iota(jnp.int32, (tok, 1), 0)
    u = base + lax.broadcasted_iota(jnp.int32, (tok, length), 1)
    return (u <= t) & (u >= start_of(t, lengths))


def column_block(at):
    return pl.ds(pl.multiple_of(at, HD), HD)


def keys_of(upper, g):
    return upper[column_block(g * HD), :]


def values_of(lower, g):
    half = lower.shape[1] // 2
    both = [lower[:, column_block(side * half + g * HD)] for side in range(2)]
    return jnp.concatenate(both, axis=0)


def add_block(tok, heads, q_at, keys, values, allowed, sums, fresh=False):
    length = keys.shape[1]
    for j in range(0, heads, PAIR):
        some = min(PAIR, heads - j)
        p = jnp.exp2(dot_nn(q_at(j * tok, some * tok), keys) * FACTOR)
        if allowed is not None:
            p = p.reshape(some, tok, length)
            p = jnp.where(allowed[None], p, 0.0).reshape(some * tok, length)
        more = (fold(p, jnp.add), dot_nn(p.astype(jnp.bfloat16), values))
        for ref, value in zip(sums, more):
            here = slice(j * tok, (j + some) * tok)
            ref[here] = value if fresh else ref[here] + value


def relation(meta, part, side, tok, lengths):
    first = (meta[CHIP] * 2 + side) * tok
    base = meta[PARTS + part] * 2 * tok
    relevant = (base < first) & (meta[PARTS + part] != meta[CHIP])
    relevant = relevant & (base + 2 * tok > start_of(first, lengths))
    return relevant, base >= start_of(first + tok - 1, lengths), first, base


def side_rows(side, heads, tok):
    return pl.ds(pl.multiple_of(side * (heads * tok), HD), heads * tok)


def open_kernel(tok, heads, groups, meta, lengths, q, q_near, block, qs, total, acc):
    core = meta[CORE]
    rows = heads * tok
    for source, side, skip in ((q, core, core * groups * heads), (q_near, 1 - core, 0)):
        for g in range(groups):
            for j in range(heads):
                at = pl.ds(pl.multiple_of(side * rows + j * tok, HD), tok)
                qs[g, at] = source[:, column_block((skip + g * heads + j) * HD)]
    upper, lower = block.at[: block.shape[0] // 2], block.at[block.shape[0] // 2 :]

    @pl.loop(0, groups)
    def _(g):
        keys, values = keys_of(upper, g), values_of(lower, g)
        for side in range(2):
            length = (side + 1) * tok
            first = (meta[CHIP] * 2 + side) * tok
            allowed = allowed_at(first, meta[CHIP] * 2 * tok, tok, length, lengths)
            here = side_rows(side, heads, tok)
            q_at = lambda at, count: qs[g, pl.ds(side * rows + at, count)]
            add_block(tok, heads, q_at, keys[:, :length], values[:length], allowed,
                      (total.at[g, here], acc.at[g, here]), True)


def open_sums(q, q_near, block, meta, lengths):
    tok = q.shape[0]
    heads = H // KVH
    groups = q_near.shape[1] // (heads * HD)
    rows = 2 * heads * tok
    sums = jax.ShapeDtypeStruct((groups, rows, HD), jnp.float32)
    pairs = groups * rows * tok * 2
    return pl.pallas_call(
        functools.partial(open_kernel, tok, heads, groups),
        out_shape=[jax.ShapeDtypeStruct((groups, rows, HD), jnp.bfloat16), sums, sums],
        in_specs=[SMEM, SMEM, VMEM, VMEM, VMEM],
        out_specs=[VMEM] * 3,
        compiler_params=pltpu.CompilerParams(vmem_limit_bytes=2 * LITTLE),
        cost_estimate=pl.CostEstimate(
            flops=pairs * HD * 8, bytes_accessed=q.size * 2, transcendentals=pairs
        ),
        name="open",
    )(meta, lengths, q, q_near, block)


def stage_body(tok, heads, groups, first_part, meta, lengths, qs, before, one, two, total, acc, held):
    held[0], held[1] = one[...], two[...]
    total[...], acc[...] = before[0][...], before[1][...]
    half = held.shape[1] // 2

    @pl.loop(0, 4 * groups)
    def _(step):
        which, rest = lax.div(step, 2 * groups), lax.rem(step, 2 * groups)
        g, side = lax.div(rest, 2), lax.rem(rest, 2)
        relevant, clear, first, base = relation(meta, first_part + which, side, tok, lengths)
        here = side_rows(side, heads, tok)
        sums = (total.at[g, here], acc.at[g, here])
        at = side * (heads * tok)
        q_at = lambda off, count: qs[g, pl.ds(pl.multiple_of(at + off, HD), count)]
        upper, lower = held.at[which, :half], held.at[which, half:]

        @pl.when(relevant & clear)
        def _():
            add_block(tok, heads, q_at, keys_of(upper, g), values_of(lower, g), None, sums)

        @pl.when(relevant & jnp.logical_not(clear))
        def _():
            allowed = allowed_at(first, base, tok, 2 * tok, lengths)
            add_block(tok, heads, q_at, keys_of(upper, g), values_of(lower, g), allowed, sums)


def stage_kernel(tok, heads, groups, first_part, own, *refs):
    meta, lengths, qs, total_in, acc_in, one, two = refs[:7]
    if own is None:
        total, acc, held = refs[7:]
    else:
        sources, table = refs[7:10], refs[10]
        total, acc, held = refs[11], refs[12], refs[19]
        state, (q3, k3, v3, sems) = refs[13:19], refs[20:]
        copies = request_copies(own, meta, sources, (q3, k3, v3), sems)
        for copy in copies:
            copy.start()
    before = (total_in, acc_in)
    stage_body(tok, heads, groups, first_part, meta, lengths, qs, before, one, two, total, acc, held)
    if own is not None:
        for copy in copies:
            copy.wait()
        requests_body(own, heads, groups, 2 * tok, meta, table, *state, q3, k3, v3)


def stage(state, pair, first_part, meta, lengths, requests=None):
    qs, total, acc = state
    groups, rows, unused = qs.shape
    tok = pair[0].shape[1] // 2
    heads = rows // (2 * tok)
    pairs = groups * rows * tok * 2
    out_shape = [jax.ShapeDtypeStruct(x.shape, x.dtype) for x in (total, acc)]
    scratch = [pltpu.VMEM((2, *pair[0].shape), pair[0].dtype)]
    sources, own = [], None
    if requests is not None:
        *sources, own = requests
        steps = sources[0].shape[1]
        width = sources[1].shape[2] // 2
        size = heads * own * steps
        sums = jax.ShapeDtypeStruct((groups, size, HD), jnp.float32)
        new = jax.ShapeDtypeStruct((own * steps, width), jnp.bfloat16)
        out_shape += [
            sums, sums, jax.ShapeDtypeStruct((groups, size, HD), jnp.bfloat16), new, new,
            jax.ShapeDtypeStruct((own, (LEVELS - PARTS) * 2 * tok), jnp.float32),
        ]
        scratch += [
            pltpu.VMEM((own, steps, groups * heads * HD), jnp.bfloat16),
            pltpu.VMEM((own, steps, width), jnp.bfloat16),
            pltpu.VMEM((own, steps, width), jnp.bfloat16),
            pltpu.SemaphoreType.DMA((3,)),
        ]
    new = pl.pallas_call(
        functools.partial(stage_kernel, tok, heads, groups, first_part, own),
        out_shape=out_shape,
        in_specs=[SMEM, SMEM] + [VMEM] * 5 + ([HBM] * 3 + [VMEM] if sources else []),
        out_specs=[VMEM] * len(out_shape),
        scratch_shapes=scratch,
        input_output_aliases={3: 0, 4: 1},
        compiler_params=pltpu.CompilerParams(vmem_limit_bytes=ROOM),
        cost_estimate=pl.CostEstimate(
            flops=pairs * HD * 8, bytes_accessed=tok * HD, transcendentals=pairs
        ),
        name=f"stage{first_part}",
    )(meta, lengths, qs, total, acc, *pair, *sources)
    return (qs, *new[:2]), new[2:]


def finish_kernel(tok, heads, groups, done, meta, lengths, qs, total, acc, *refs):
    parts = len(refs) - 10
    blocks, last = refs[:parts], refs[parts : parts + 2]
    near, out, held, peak, total_now, acc_now, result, sem = refs[parts + 2 :]
    rows = heads * tok
    core = meta[CORE]
    half = held.shape[1] // 2

    def fill(first):
        for i in range(first, parts):
            held[i] = blocks[i][...]
        held[parts, :half] = last[0][...]
        held[parts, half:] = last[1][...]

    def turn_of(step):
        turn, g = lax.div(step, groups), lax.rem(step, groups)
        side = jnp.where(turn == 0, 1 - core, core)
        at = side * rows
        q_at = lambda off, count: qs[g, pl.ds(pl.multiple_of(at + off, HD), count)]
        return turn, g, side, q_at

    def write(turn, g):
        whole = jnp.sum(total_now[...], axis=1, keepdims=True)
        value = (acc_now[...] / whole).astype(result.dtype)
        for j in range(heads):
            result[turn, :, column_block((g * heads + j) * HD)] = value[j * tok : (j + 1) * tok]
        return sound(whole)

    def one_turn(step, fine):
        turn, g, side, q_at = turn_of(step)
        here = side_rows(side, heads, tok)
        total_now[...] = total[g, here]
        acc_now[...] = acc[g, here]

        @pl.loop(done, parts + 1)
        def _(i):
            relevant, clear, first, base = relation(meta, i, side, tok, lengths)
            upper, lower = held.at[i, :half], held.at[i, half:]
            sums = (total_now, acc_now)

            @pl.when(relevant & clear)
            def _():
                add_block(tok, heads, q_at, keys_of(upper, g), values_of(lower, g), None, sums)

            @pl.when(relevant & jnp.logical_not(clear))
            def _():
                allowed = allowed_at(first, base, tok, 2 * tok, lengths)
                add_block(tok, heads, q_at, keys_of(upper, g), values_of(lower, g), allowed, sums)

        return fine & write(turn, g).astype(jnp.int32)

    fill(done)
    fine = lax.fori_loop(0, 2 * groups, one_turn, jnp.int32(1))

    @pl.when(fine == 0)
    def _():
        fill(0)

        @pl.loop(0, 2 * groups)
        def _(step):
            turn, g, side, q_at = turn_of(step)
            first = (meta[CHIP] * 2 + side) * tok
            peak[...] = jnp.full_like(peak, NEG)
            total_now[...] = jnp.zeros_like(total_now)
            acc_now[...] = jnp.zeros_like(acc_now)

            @pl.loop(0, (parts + 1) * heads)
            def _(step):
                i, j = lax.div(step, heads), lax.rem(step, heads)
                keys = keys_of(held.at[i, :half], g)
                values = values_of(held.at[i, half:], g)
                allowed = allowed_at(first, meta[PARTS + i] * 2 * tok, tok, 2 * tok, lengths)
                mine = pl.ds(pl.multiple_of(j * tok, tok), tok)
                s = jnp.where(allowed, dot_nn(q_at(j * tok, tok), keys) * FACTOR, NEG)
                top = jnp.maximum(peak[mine], jnp.max(s, axis=1, keepdims=True))
                p = jnp.where(allowed, jnp.exp2(s - top[:, :1]), 0.0)
                shrink = jnp.exp2(peak[mine] - top)
                total_now[mine] = total_now[mine] * shrink + fold(p, jnp.add)
                acc_now[mine] = acc_now[mine] * shrink + dot_nn(p.astype(jnp.bfloat16), values)
                peak[mine] = top

            write(turn, g)

    width = near.shape[1]
    where = pl.ds(pl.multiple_of(core * width, width), width)
    copy = pltpu.make_async_copy(result.at[1], out.at[:, where], sem)
    copy.start()
    near[...] = result[0]
    copy.wait()


def finish(state, blocks, last, done, meta, lengths):
    qs, total, acc = state
    groups, rows, unused = qs.shape
    tok = last[0].shape[1] // 2
    heads = rows // (2 * tok)
    width = groups * heads * HD
    sums = pltpu.VMEM((heads * tok, HD), jnp.float32)
    return pl.pallas_call(
        functools.partial(finish_kernel, tok, heads, groups, done),
        out_shape=[
            jax.ShapeDtypeStruct((tok, width), jnp.bfloat16),
            jax.ShapeDtypeStruct((tok, 2 * width), jnp.bfloat16),
        ],
        in_specs=[SMEM, SMEM] + [VMEM] * (5 + len(blocks)),
        out_specs=[VMEM, HBM],
        scratch_shapes=[
            pltpu.VMEM((len(blocks) + 1, *blocks[0].shape), blocks[0].dtype),
            sums, sums, sums,
            pltpu.VMEM((2, tok, width), jnp.bfloat16),
            pltpu.SemaphoreType.DMA,
        ],
        compiler_params=pltpu.CompilerParams(vmem_limit_bytes=ROOM),
        cost_estimate=pl.CostEstimate(
            flops=groups * rows * tok * HD * 8, bytes_accessed=tok * width * 4,
            transcendentals=groups * rows * tok * 2,
        ),
        name="finish",
    )(meta, lengths, qs, total, acc, *blocks, *last)


def request_sums(query, keys, values, mask):
    p = jnp.exp2(dot_nn(query, keys) * FACTOR)
    p = jnp.where(mask[None], p.reshape(-1, *mask.shape), 0.0).reshape(p.shape)
    return fold(p, jnp.add), dot_nn(p.astype(jnp.bfloat16), values)


def fresh_scores(query, newk, own):
    s = dot_nt(query, newk) * FACTOR
    size = newk.shape[0]
    row = lax.broadcasted_iota(jnp.int32, (size, size), 0)
    col = lax.broadcasted_iota(jnp.int32, (size, size), 1)
    ok = (lax.rem(row, own) == lax.rem(col, own)) & (lax.div(col, own) <= lax.div(row, own))
    return s.reshape(-1, size, size), ok


def request_copies(own, meta, sources, held, sems):
    requests = pl.ds(lax.div(meta[CHIP], 2) * own, own)
    copies = []
    for i, (source, target) in enumerate(zip(sources, held)):
        width = target.shape[2]
        where = pl.ds(pl.multiple_of(meta[CORE] * width, width), width)
        copies.append(pltpu.make_async_copy(source.at[requests, :, where], target, sems.at[i]))
    return copies


def requests_body(own, heads, groups, length, meta, table, total, acc, query, newk, newv, mask, q3, k3, v3):
    steps = q3.shape[1]
    level = lax.div(meta[CHIP], 2)
    pick = lax.broadcasted_iota(jnp.int32, (own, table.shape[1]), 1) - level * own
    pick = (pick == lax.broadcasted_iota(jnp.int32, pick.shape, 0)).astype(jnp.float32)
    rows = dot_nt(pick.astype(jnp.bfloat16), table[...].astype(jnp.float32).astype(jnp.bfloat16))
    lane = lax.div(lax.broadcasted_iota(jnp.int32, (own, length), 1), BLK)
    for i in range(mask.shape[1] // length):
        number = (lane + meta[PARTS + i] * (length // BLK)).astype(jnp.float32)
        hit = rows[:, :1] == number
        for j in range(1, rows.shape[1]):
            hit = hit | (rows[:, j : j + 1] == number)
        mask[:, i * length : (i + 1) * length] = hit.astype(jnp.float32)
    for s in range(steps):
        for g in range(groups):
            col = slice(g * HD, (g + 1) * HD)
            at = slice(s * own, (s + 1) * own)
            newk[at, col] = k3[:, s, col]
            newv[at, col] = v3[:, s, col]
            for j in range(heads):
                first = (g * heads + j) * HD
                row = (j * steps + s) * own
                query[g, row : row + own] = q3[:, s, first : first + HD]

    @pl.loop(0, groups)
    def _(g):
        col = column_block(g * HD)
        s, ok = fresh_scores(query[g], newk[:, col], own)
        p = jnp.where(ok[None], jnp.exp2(s), 0.0).reshape(-1, s.shape[2])
        first = jnp.sum(p, axis=1, keepdims=True)
        lead = lax.broadcasted_iota(jnp.int32, (p.shape[0], HD), 1) == 0
        total[g] = jnp.where(lead, first, 0.0)
        acc[g] = dot_nn(p.astype(jnp.bfloat16), newv[:, col])


def early_kernel(groups, total_in, acc_in, query, mask, *refs):
    blocks, (total, acc) = refs[:-2], refs[-2:]
    half, length = blocks[0].shape[0] // 2, blocks[0].shape[1]

    @pl.loop(0, groups)
    def _(g):
        sums = [total_in[g], acc_in[g]]
        for i, block in enumerate(blocks):
            open_to = mask[:, i * length : (i + 1) * length] > 0
            keys, values = keys_of(block.at[:half], g), values_of(block.at[half:], g)
            more = request_sums(query[g], keys, values, open_to)
            sums = [x + y for x, y in zip(sums, more)]
        total[g], acc[g] = sums


def early_decode(state, blocks):
    total, acc, query, newk, newv, mask = state
    groups, rows, unused = query.shape
    pairs = groups * rows * len(blocks) * blocks[0].shape[1]
    sums = jax.ShapeDtypeStruct(total.shape, total.dtype)
    new = pl.pallas_call(
        functools.partial(early_kernel, groups),
        out_shape=[sums, sums],
        in_specs=[VMEM] * (4 + len(blocks)),
        out_specs=[VMEM] * 2,
        input_output_aliases={0: 0, 1: 1},
        compiler_params=pltpu.CompilerParams(vmem_limit_bytes=2 * LITTLE),
        cost_estimate=pl.CostEstimate(
            flops=pairs * HD * 8, bytes_accessed=rows * HD, transcendentals=pairs
        ),
        name="early_decode",
    )(total, acc, query, mask, *blocks)
    return [*new, query, newk, newv, mask]


def late_kernel(own, steps, heads, groups, done, meta, total, acc, query, newk, newv, mask, *refs):
    parts = len(refs) - 3
    blocks, last, out = refs[:parts], refs[parts : parts + 2], refs[-1]
    length = blocks[0].shape[1]
    half = blocks[0].shape[0] // 2
    size = own * steps

    def write(g, sums, whole):
        result = (sums / whole).astype(out.dtype)
        for j in range(heads):
            out[:, column_block((g * heads + j) * HD)] = result[j * size : (j + 1) * size]

    def one_group(g, fine):
        sums = [total[g], acc[g]]
        for i in range(done, parts + 1):
            upper = last[0] if i == parts else blocks[i].at[:half]
            lower = last[1] if i == parts else blocks[i].at[half:]
            open_to = mask[:, i * length : (i + 1) * length] > 0
            more = request_sums(query[g], keys_of(upper, g), values_of(lower, g), open_to)
            sums = [x + y for x, y in zip(sums, more)]
        whole = jnp.sum(sums[0], axis=1, keepdims=True)
        write(g, sums[1], whole)
        return fine & sound(whole).astype(jnp.int32)

    fine = lax.fori_loop(0, groups, one_group, jnp.int32(1))

    @pl.when(fine == 0)
    def _():
        @pl.loop(0, groups)
        def _(g):
            col = column_block(g * HD)
            fresh, ok = fresh_scores(query[g], newk[:, col], own)
            fresh = jnp.where(ok[None], fresh, NEG).reshape(-1, size)
            top = jnp.max(fresh, axis=1, keepdims=True)
            p = jnp.exp2(fresh - top)
            whole = jnp.sum(p, axis=1, keepdims=True)
            sums = dot_nn(p.astype(jnp.bfloat16), newv[:, col])
            for i in range(parts + 1):
                upper = last[0] if i == parts else blocks[i].at[:half]
                lower = last[1] if i == parts else blocks[i].at[half:]
                s = dot_nn(query[g], keys_of(upper, g)) * FACTOR
                open_to = mask[:, i * length : (i + 1) * length] > 0
                s = jnp.where(open_to[None], s.reshape(-1, own, length), NEG).reshape(s.shape)
                higher = jnp.maximum(top, jnp.max(s, axis=1, keepdims=True))
                p = jnp.exp2(s - higher)
                shrink = jnp.exp2(top - higher)
                whole = whole * shrink + jnp.sum(p, axis=1, keepdims=True)
                sums = sums * shrink + dot_nn(p.astype(jnp.bfloat16), values_of(lower, g))
                top = higher
            write(g, sums, whole)


def late_decode(early, blocks, last, done, own, steps, meta):
    groups, rows, unused = early[0].shape
    heads = H // KVH
    parts, length = len(blocks) + 1, blocks[0].shape[1]
    pairs = groups * rows * (parts - done) * length
    return pl.pallas_call(
        functools.partial(late_kernel, own, steps, heads, groups, done),
        out_shape=jax.ShapeDtypeStruct((own * steps, groups * heads * HD), jnp.bfloat16),
        in_specs=[SMEM] + [VMEM] * (len(early) + len(blocks) + 2),
        out_specs=VMEM,
        compiler_params=pltpu.CompilerParams(vmem_limit_bytes=ROOM),
        cost_estimate=pl.CostEstimate(
            flops=pairs * HD * 8, bytes_accessed=rows * HD, transcendentals=pairs
        ),
        name="late_decode",
    )(meta, *early, *blocks, *last)


def decode_kernel(parts, steps, heads, groups, starts, q, mask, newk, newv, *refs):
    kheld, vheld = refs[:parts], refs[parts : 2 * parts]
    out, kall, vall, sems, scores = refs[2 * parts :]
    own = q.shape[0]
    rows = heads * own
    length = kheld[0].shape[1]
    copies = []
    for i in range(parts):
        where = pl.ds(pl.multiple_of(starts[i], HD), length)
        copies.append(pltpu.make_async_copy(kheld[i], kall.at[:, where], sems.at[2 * i]))
        copies.append(pltpu.make_async_copy(vheld[i], vall.at[where], sems.at[2 * i + 1]))
    for copy in copies:
        copy.start()
    row = lax.broadcasted_iota(jnp.int32, (own, own), 0)
    col = lax.broadcasted_iota(jnp.int32, (own, own), 1)
    fresh_ok = (lax.div(row, steps) == lax.div(col, steps)) & (col <= row)

    def columns(g):
        return slice(g * HD, (g + 1) * HD)

    def stacked(g):
        first = g * heads
        slices = [q[:, (first + j) * HD : (first + j + 1) * HD] for j in range(heads)]
        return jnp.concatenate([x.astype(jnp.float32) for x in slices], 0).astype(jnp.bfloat16)

    def keep(allowed, x, other):
        y = x.reshape(heads, own, x.shape[1])
        return jnp.where(allowed[None], y, other).reshape(x.shape)

    def open_to(i):
        return mask[:, pl.ds(pl.multiple_of(starts[i], HD), length)] > 0

    def write(g, acc, whole):
        result = acc / whole
        for j in range(heads):
            out[:, (g * heads + j) * HD : (g * heads + j + 1) * HD] = result[
                j * own : (j + 1) * own
            ].astype(out.dtype)

    fine = None
    for g in range(groups):
        query = stacked(g)
        p = keep(fresh_ok, jnp.exp2(dot_nt(query, newk[:, columns(g)]) * FACTOR), 0.0)
        whole = jnp.sum(p, axis=1, keepdims=True)
        acc = dot_nn(p.astype(jnp.bfloat16), newv[:, columns(g)])
        total = jnp.zeros((rows, HD), jnp.float32)
        for i in range(parts):
            p = jnp.exp2(dot_nn(query, kheld[i][columns(g)]) * FACTOR)
            p = keep(open_to(i), p, 0.0)
            total = total + fold(p, jnp.add)
            acc = acc + dot_nn(p.astype(jnp.bfloat16), vheld[i][:, columns(g)])
        whole = whole + jnp.sum(total, axis=1, keepdims=True)
        write(g, acc, whole)
        fine = sound(whole) if fine is None else fine & sound(whole)

    @pl.when(jnp.logical_not(fine))
    def _():
        for g in range(groups):
            query = stacked(g)
            fresh = keep(fresh_ok, dot_nt(query, newk[:, columns(g)]) * FACTOR, NEG)
            top = jnp.max(fresh, axis=1, keepdims=True)
            for i in range(parts):
                s = keep(open_to(i), dot_nn(query, kheld[i][columns(g)]) * FACTOR, NEG)
                scores[:, i * length : (i + 1) * length] = s
                top = jnp.maximum(top, jnp.max(s, axis=1, keepdims=True))
            p = jnp.exp2(fresh - top)
            whole = jnp.sum(p, axis=1, keepdims=True)
            acc = dot_nn(p.astype(jnp.bfloat16), newv[:, columns(g)])
            for i in range(parts):
                p = jnp.exp2(scores[:, i * length : (i + 1) * length] - top)
                whole = whole + jnp.sum(p, axis=1, keepdims=True)
                acc = acc + dot_nn(p.astype(jnp.bfloat16), vheld[i][:, columns(g)])
            write(g, acc, whole)

    for copy in copies:
        copy.wait()


def decode(q, mask, newk, newv, kparts, vparts, starts, steps):
    own = q.shape[0]
    parts = len(kparts)
    length, width = vparts[0].shape
    count = parts * length
    heads = H // KVH
    groups = width // HD
    rows = heads * own
    pairs = groups * rows * count
    return pl.pallas_call(
        functools.partial(decode_kernel, parts, steps, heads, groups),
        out_shape=[
            jax.ShapeDtypeStruct(q.shape, jnp.bfloat16),
            jax.ShapeDtypeStruct((width, count), jnp.bfloat16),
            jax.ShapeDtypeStruct((count, width), jnp.bfloat16),
        ],
        grid_spec=pltpu.PrefetchScalarGridSpec(
            num_scalar_prefetch=1,
            grid=(),
            in_specs=[VMEM] * (4 + 2 * parts),
            out_specs=[VMEM, HBM, HBM],
            scratch_shapes=[
                pltpu.SemaphoreType.DMA((2 * parts,)),
                pltpu.VMEM((rows, count), jnp.float32),
            ],
        ),
        compiler_params=pltpu.CompilerParams(vmem_limit_bytes=ROOM),
        cost_estimate=pl.CostEstimate(
            flops=pairs * HD * 4, bytes_accessed=count * width * 4, transcendentals=pairs
        ),
        name="decode",
    )(starts, q, mask, newk, newv, *kparts, *vparts)


def prepare_kernel(meta, k, v, send, block):
    tok, width = k.shape[0], k.shape[1] // 2
    mine = pl.ds(pl.multiple_of(meta[0] * width, width), width)
    other = pl.ds(pl.multiple_of((1 - meta[0]) * width, width), width)
    send[:width] = k[:, other].astype(jnp.float32).T.astype(send.dtype)
    send[width:] = v[:, other]
    block[:width, mine] = k[:, mine].astype(jnp.float32).T.astype(block.dtype)
    block[width:, mine] = v[:, mine]


def prepare(k, v, core):
    tok, width = k.shape[0], k.shape[1] // 2
    assert tok == width
    return pl.pallas_call(
        prepare_kernel,
        out_shape=[
            jax.ShapeDtypeStruct((2 * tok, width), k.dtype),
            jax.ShapeDtypeStruct((2 * width, 2 * tok), k.dtype),
        ],
        in_specs=[SMEM, VMEM, VMEM],
        out_specs=[VMEM] * 2,
        compiler_params=pltpu.CompilerParams(vmem_limit_bytes=LITTLE),
        name="prepare",
    )(core[None], k, v)


def join_kernel(meta, block_in, theirs, q, block, send_q, sem):
    columns = send_q.shape[1]
    where = pl.ds(pl.multiple_of((1 - meta[0]) * columns, columns), columns)
    copy = pltpu.make_async_copy(q.at[:, where], send_q, sem)
    copy.start()
    width = theirs.shape[1]
    other = pl.ds(pl.multiple_of((1 - meta[0]) * width, width), width)
    block[...] = block_in[...]
    block[:width, other] = theirs[:width]
    block[width:, other] = theirs[width:]
    copy.wait()


def join(block, theirs, q, core):
    return pl.pallas_call(
        join_kernel,
        out_shape=[
            jax.ShapeDtypeStruct(block.shape, block.dtype),
            jax.ShapeDtypeStruct((q.shape[0], q.shape[1] // 2), q.dtype),
        ],
        in_specs=[SMEM, VMEM, VMEM, HBM],
        out_specs=[VMEM] * 2,
        scratch_shapes=[pltpu.SemaphoreType.DMA],
        compiler_params=pltpu.CompilerParams(vmem_limit_bytes=LITTLE),
        name="join",
    )(core[None], block, theirs, q)


def take_kernel(meta, whole, out, sem):
    width = out.shape[1]
    where = pl.ds(pl.multiple_of((1 - meta[CORE]) * width, width), width)
    copy = pltpu.make_async_copy(whole.at[:, where], out, sem)
    copy.start()
    copy.wait()


def take_other_half(whole, meta):
    return pl.pallas_call(
        take_kernel,
        out_shape=jax.ShapeDtypeStruct((whole.shape[0], whole.shape[1] // 2), whole.dtype),
        in_specs=[SMEM, HBM],
        out_specs=VMEM,
        scratch_shapes=[pltpu.SemaphoreType.DMA],
        compiler_params=pltpu.CompilerParams(vmem_limit_bytes=LITTLE),
        name="take",
    )(meta, whole)


def project_kernel(meta, *refs):
    pieces, (whole, other), outs, (sorted_rows,) = refs[:-7], refs[-7:-5], refs[-5:-1], refs[-1:]
    parts = len(pieces)
    rows = pieces[0].shape[0]
    for i, piece in enumerate(pieces):
        at = pl.ds(pl.multiple_of(meta[LEVELS + i] * rows, rows), rows)
        sorted_rows[at] = piece[...]
    depth = other.shape[1]
    mine = whole[:, pl.ds(pl.multiple_of(meta[CORE] * depth, depth), depth)]
    half = parts * rows // 2
    here = pl.ds(pl.multiple_of(meta[ACROSS] * half, half), half)
    there = pl.ds(pl.multiple_of((1 - meta[ACROSS]) * half, half), half)
    kept, beside, across, corner = outs
    for at, near, far in ((here, kept, beside), (there, across, corner)):
        some = sorted_rows[at]
        near[...] = dot_nt(mine, some).astype(near.dtype)
        far[...] = dot_nt(other[...], some).astype(far.dtype)


def project(pieces, whole, other, meta):
    rows = len(pieces) * pieces[0].shape[0]
    width, depth = other.shape
    block = jax.ShapeDtypeStruct((width, rows // 2), jnp.bfloat16)
    return pl.pallas_call(
        project_kernel,
        out_shape=[jax.ShapeDtypeStruct(block.shape, jnp.float32)] + [block] * 3,
        in_specs=[SMEM] + [VMEM] * (len(pieces) + 2),
        out_specs=[VMEM] * 4,
        scratch_shapes=[pltpu.VMEM((rows, depth), jnp.bfloat16)],
        compiler_params=pltpu.CompilerParams(vmem_limit_bytes=2 * LITTLE),
        cost_estimate=pl.CostEstimate(
            flops=rows * width * depth * 4, bytes_accessed=width * depth * 4, transcendentals=0
        ),
        name="project",
    )(meta, *pieces, whole, other)


def index(z, y, c):
    return (z * 2 + y) * 2 + c


def on_ring(r, chips):
    return (r, 0) if r < chips // 2 else (chips - 1 - r, 1)


def ring_perm(chips, d):
    return [
        (index(*on_ring(r, chips), c), index(*on_ring((r + d) % chips, chips), c))
        for r in range(chips)
        for c in range(2)
    ]


def ring_place(r, chips):
    r = lax.rem(r + 2 * chips, chips)
    return jnp.where(r < chips // 2, r * 2, (chips - 1 - r) * 2 + 1)


def spread(x, n):
    place = lax.axis_index("seq")
    deep = n // 4
    everyone = [(z, y, c) for z in range(deep) for y in range(2) for c in range(2)]
    z, y, c = place // 4, (place // 2) % 2, place % 2
    held = [(x, z, y, c)]
    for d in range(1, deep):
        perm = [(index(*p), index((p[0] - d) % deep, p[1], p[2])) for p in everyone]
        held.append((lax.ppermute(x, "seq", perm), lax.rem(z + d, deep), y, c))
    perm = [(index(*p), index(p[0], 1 - p[1], p[2])) for p in everyone]
    held += [(lax.ppermute(b, "seq", perm), bz, 1 - by, bc) for b, bz, by, bc in held]
    perm = [(index(*p), index(p[0], p[1], 1 - p[2])) for p in everyone]
    held += [(lax.ppermute(b, "seq", perm), bz, by, 1 - bc) for b, bz, by, bc in held]
    return [b for b, *_ in held], jnp.stack([index(bz, by, bc) for _, bz, by, bc in held])


def open_blocks(table, steps, count):
    number = lax.broadcasted_iota(jnp.int32, (*table.shape, count), 2) // BLK
    mask = jnp.any(table[:, :, None] == number, axis=1).astype(jnp.float32)
    return jnp.repeat(mask, steps, axis=0)


def whole_heads(n, q_pre, k_cache, v_cache, lengths, q_dec, k_new, v_new, block_table, w_out):
    tok = q_pre.shape[0]
    place = lax.axis_index("seq").astype(jnp.int32)
    rows, steps = q_dec.shape[0], q_dec.shape[1]
    own = rows // n
    kparts, sources = spread(k_cache.T, n)
    vparts, _ = spread(v_cache, n)
    starts = sources.astype(jnp.int32) * tok

    def mine(x):
        y = lax.dynamic_slice_in_dim(x, place * own, own, 0)
        return y.reshape(own * steps, -1) if x.ndim == 3 else y

    mask = open_blocks(mine(block_table), steps, n * tok)
    attn_own, keys, values = decode(
        mine(q_dec), mask, mine(k_new), mine(v_new), kparts, vparts, starts, steps
    )
    attn = lax.all_gather(attn_own, "seq", axis=0, tiled=True)
    flat = jnp.dot(attn, w_out, preferred_element_type=jnp.float32).astype(jnp.bfloat16)
    dec_out = lax.psum_scatter(
        flat.reshape(rows, steps, -1), "tp", scatter_dimension=0, tiled=True
    )
    zero = jnp.zeros((), jnp.int32)
    meta = jnp.stack([place * tok, zero, zero, zero])
    groups = k_cache.shape[1] // HD
    pre_out = prefill(
        q_pre, keys, values, meta, lengths, groups, q_pre.shape[1], "prefill"
    )
    return (pre_out, dec_out)


def split_heads(n, q_pre, k_cache, v_cache, lengths, q_dec, k_new, v_new, block_table, w_out):
    place = lax.axis_index("seq").astype(jnp.int32)
    across = lax.axis_index("tp").astype(jnp.int32)
    core, chip = lax.rem(place, 2), lax.div(place, 2)
    chips = n // 2
    far, deep = chips // 2, chips // 2
    z, y = lax.div(chip, 2), lax.rem(chip, 2)
    r = jnp.where(y == 0, z, chips - 1 - z)
    rows, steps = q_dec.shape[0], q_dec.shape[1]
    own = rows // deep
    sibling = [(i, i ^ 1) for i in range(n)]
    everyone = [(a, b, c) for a in range(deep) for b in range(2) for c in range(2)]

    order = [0] + [o for d in range(1, far) for o in (-d, d)] + [far]
    numbers = [ring_place(r + o, chips) for o in order]
    levels = [z] + [lax.rem(z + deep - d, deep) for d in range(1, deep)]
    assert len(numbers) == LEVELS - PARTS
    meta = jnp.stack([core, chip, across] + numbers + levels).astype(jnp.int32)

    send, block = prepare(k_cache, v_cache, core)
    theirs = lax.ppermute(send, "seq", sibling)
    theirs, meta = lax.optimization_barrier((theirs, meta))
    block, send_q = join(block, theirs, q_pre, core)
    held = {0: block}
    near_q = lax.ppermute(send_q, "seq", sibling)

    up, down = ring_perm(chips, 1), ring_perm(chips, -1)
    half = block.shape[0] // 2
    early, w_near = (), w_out
    for d in range(1, far + 1):
        if d < far:
            held[-d] = lax.ppermute(held[1 - d], "seq", up)
            held[d] = lax.ppermute(held[d - 1], "seq", down)
            last = (held[-d], held[d])
        else:
            last = (
                lax.ppermute(held[1 - d][:half], "seq", up),
                lax.ppermute(held[d - 1][half:], "seq", down),
            )
        if d == 1:
            state = open_sums(q_pre, near_q, held[0], meta, lengths)
        elif d < far:
            requests = (q_dec, k_new, v_new, block_table.T, own) if d == 2 else None
            pair = (held[1 - d], held[d - 1])
            state, more = stage(state, pair, 2 * d - 3, meta, lengths, requests)
            early = early or more
        else:
            blocks = [held[o] for o in order[:-1]]
            early = early_decode(early, blocks)
        last, state, early, w_near = lax.optimization_barrier((last, state, early, w_near))
        if d == 1:
            weights = w_near.T
            w_near = lax.ppermute(take_other_half(weights, meta), "seq", sibling)
        if d < far:
            held[-d], held[d] = last
    attn_own = late_decode(early, blocks, last, len(blocks), own, steps, meta)

    pieces = [attn_own]
    for d in range(1, deep):
        perm = [(index(*p), index((p[0] + d) % deep, p[1], p[2])) for p in everyone]
        pieces.append(lax.ppermute(attn_own, "seq", perm))
    attn_own, state = lax.optimization_barrier((attn_own, state))
    near, pre_out = finish(state, blocks, last, 2 * far - 3, meta, lengths)
    pieces, near, pre_out = lax.optimization_barrier((pieces, near, pre_out))
    back = lax.ppermute(near, "seq", sibling)
    pre_out = settle(pre_out, back, meta)

    total, *sent = project(pieces, weights, w_near, meta)
    got = []
    for piece, (dc, dx) in zip(sent, ((1, 0), (0, 1), (1, 1))):
        perm = [
            (i * 2 + x, (i ^ dc) * 2 + (x ^ dx)) for i in range(n) for x in range(2)
        ]
        got.append(lax.ppermute(piece, ("seq", "tp"), perm))
    got[0], pre_out = lax.optimization_barrier((got[0], pre_out))
    for piece in got:
        total = total + piece.astype(jnp.float32)
    dec_out = total.astype(jnp.bfloat16).T.reshape(deep // 2, steps, own, -1)
    return (pre_out, dec_out.transpose(0, 2, 1, 3).reshape(rows // 2, steps, -1))


def per_device(n, tp, q_pre, k_cache, v_cache, prompt_lengths, *rest):
    groups = k_cache.shape[1] // HD
    square = groups % 2 == 0 and k_cache.shape[1] == 2 * k_cache.shape[0]
    small = n * k_cache.shape[0] // BLK <= 256 and n == 2 * (LEVELS - PARTS)
    form = split_heads if square and tp == 2 and small else whole_heads
    return form(n, q_pre, k_cache, v_cache, prompt_lengths.astype(jnp.int32), *rest)


def solution(mesh):
    placed = (
        P("seq", "tp"),
        P("seq", "tp"),
        P("seq", "tp"),
        P(),
        P(None, None, "tp"),
        P(None, None, "tp"),
        P(None, None, "tp"),
        P(),
        P("tp", "seq"),
    )
    return jax.shard_map(
        functools.partial(per_device, mesh.shape["seq"], mesh.shape["tp"]),
        mesh=mesh,
        in_specs=placed,
        out_specs=(P("seq", "tp"), P("tp", None, "seq")),
        check_vma=False,
    )
```

```python
import functools
import math

import jax
import jax.numpy as jnp
from jax import lax
from jax.experimental import pallas as pl
from jax.experimental.pallas import tpu as pltpu
from jax.sharding import PartitionSpec as P

H = 56
KVH = 8
HD = 128
BLK = 64
SPAN = 512
PAIR = 2
NEG = -1e30
LEAST, MOST = 2.0**-60, 2.0**100
FACTOR = math.log2(math.e) / math.sqrt(HD)
ROOM = 16 * 1024 * 1024
LITTLE = 4 * 1024 * 1024
CORE, CHIP, ACROSS, PARTS, LEVELS = 0, 1, 2, 3, 11
BRIEF = pl.CostEstimate(flops=1024, bytes_accessed=1024, transcendentals=0)
HBM = pl.BlockSpec(memory_space=pltpu.HBM)
VMEM = pl.BlockSpec(memory_space=pltpu.VMEM)
SMEM = pl.BlockSpec(memory_space=pltpu.SMEM)


def dot_nt(a, b):
    return lax.dot_general(a, b, (((1,), (1,)), ((), ())), preferred_element_type=jnp.float32)


def dot_nn(a, b):
    return lax.dot_general(a, b, (((1,), (0,)), ((), ())), preferred_element_type=jnp.float32)


def fold(x, op):
    out = x[:, :HD]
    for i in range(1, x.shape[1] // HD):
        out = op(out, x[:, i * HD : (i + 1) * HD])
    return out


def start_of(position, lengths):
    end = jnp.int32(0)
    out = jnp.zeros_like(position)
    for i in range(lengths.shape[0]):
        end = end + lengths[i]
        out = jnp.where(position >= end, end, out)
    return out


def sound(total):
    return (jnp.min(total) >= LEAST) & (jnp.max(total) <= MOST)


def prefill_kernel(tok, heads, meta, lengths, q, keys_all, values_all, *refs):
    out, qs, peak, total, acc = refs[-5:]
    for j in range(heads):
        qs[j * tok : (j + 1) * tok] = q[:, j * HD : (j + 1) * HD]
    total[...] = jnp.zeros_like(total)
    acc[...] = jnp.zeros_like(acc)

    begin = meta[0]
    finish = begin + tok
    low = start_of(begin, lengths)
    high = start_of(finish - 1, lengths)
    blocks = lax.div(finish - low + SPAN - 1, SPAN)
    clear = lax.div(finish - high, SPAN)

    def first_of(k):
        return jnp.maximum(finish - (k + 1) * SPAN, 0)

    def load(k):
        here = pl.ds(pl.multiple_of(first_of(k), HD), SPAN)
        return keys_all[:, here], values_all[here, :]

    def allowed_in(k):
        t = begin + lax.broadcasted_iota(jnp.int32, (tok, 1), 0)
        u = first_of(k) + lax.broadcasted_iota(jnp.int32, (tok, SPAN), 1)
        last = jnp.minimum(t, finish - k * SPAN - 1)
        return (u <= last) & (u >= start_of(t, lengths))

    def keep(allowed, x, other):
        some = x.shape[0] // tok
        return jnp.where(allowed[None], x.reshape(some, tok, SPAN), other).reshape(x.shape)

    def block(k, masked):
        keys, values = load(k)
        allowed = allowed_in(k) if masked else None
        for j in range(0, heads, PAIR):
            here = slice(j * tok, min(j + PAIR, heads) * tok)
            p = jnp.exp2(dot_nn(qs[here], keys) * FACTOR)
            if masked:
                p = keep(allowed, p, 0.0)
            total[here] += fold(p, jnp.add)
            acc[here] += dot_nn(p.astype(jnp.bfloat16), values)

    block(0, True)

    @pl.loop(1, jnp.maximum(clear, 1))
    def _(k):
        block(k, False)

    @pl.loop(jnp.maximum(clear, 1), blocks)
    def _(k):
        block(k, True)

    def write():
        whole = jnp.sum(total[...], axis=1, keepdims=True)
        result = (acc[...] / whole).astype(out.dtype)
        for j in range(heads):
            out[:, j * HD : (j + 1) * HD] = result[j * tok : (j + 1) * tok]
        return whole

    fine = sound(write())

    @pl.when(jnp.logical_not(fine))
    def _():
        peak[...] = jnp.full_like(peak, NEG)
        total[...] = jnp.zeros_like(total)
        acc[...] = jnp.zeros_like(acc)

        @pl.loop(0, blocks)
        def _(k):
            keys, values = load(k)
            allowed = allowed_in(k)

            @pl.loop(0, heads)
            def _(j):
                here = pl.ds(pl.multiple_of(j * tok, tok), tok)
                s = jnp.where(allowed, dot_nn(qs[here], keys) * FACTOR, NEG)
                top = jnp.maximum(peak[here], jnp.max(s, axis=1, keepdims=True))
                p = jnp.where(allowed, jnp.exp2(s - top[:, :1]), 0.0)
                shrink = jnp.exp2(peak[here] - top)
                total[here] = total[here] * shrink + fold(p, jnp.add)
                acc[here] = acc[here] * shrink + dot_nn(p.astype(jnp.bfloat16), values)
                peak[here] = top

        write()


def prefill(q, keys, values, meta, lengths, groups, columns, name, before=None):
    tok = q.shape[0]
    count = values.shape[0]
    heads = H // KVH
    rows = heads * tok
    pairs = rows * count // 2 * groups
    extra = [] if before is None else [before]
    return pl.pallas_call(
        functools.partial(prefill_kernel, tok, heads),
        out_shape=jax.ShapeDtypeStruct((tok, columns), jnp.bfloat16),
        grid_spec=pltpu.PrefetchScalarGridSpec(
            num_scalar_prefetch=2,
            grid=(groups,),
            in_specs=[
                pl.BlockSpec((tok, heads * HD), lambda g, meta, lengths: (0, meta[1] + g)),
                pl.BlockSpec((HD, count), lambda g, meta, lengths: (meta[2] + g, 0)),
                pl.BlockSpec((count, HD), lambda g, meta, lengths: (0, meta[2] + g)),
            ]
            + [HBM] * len(extra),
            out_specs=pl.BlockSpec((tok, heads * HD), lambda g, meta, lengths: (0, meta[3] + g)),
            scratch_shapes=[
                pltpu.VMEM((rows, HD), jnp.bfloat16),
                pltpu.VMEM((rows, HD), jnp.float32),
                pltpu.VMEM((rows, HD), jnp.float32),
                pltpu.VMEM((rows, HD), jnp.float32),
            ],
        ),
        compiler_params=pltpu.CompilerParams(vmem_limit_bytes=ROOM),
        cost_estimate=pl.CostEstimate(
            flops=pairs * HD * 8, bytes_accessed=count * HD * 4 * groups, transcendentals=pairs
        ),
        input_output_aliases={} if before is None else {5: 0},
        name=name,
    )(meta, lengths, q, keys, values, *extra)


def settle_kernel(meta, piece, whole, out, sem):
    width = piece.shape[1]
    where = pl.ds(pl.multiple_of((1 - meta[CORE]) * width, width), width)
    copy = pltpu.make_async_copy(piece, out.at[:, where], sem)
    copy.start()
    copy.wait()


def settle(whole, piece, meta):
    return pl.pallas_call(
        settle_kernel,
        out_shape=jax.ShapeDtypeStruct(whole.shape, whole.dtype),
        in_specs=[SMEM, VMEM, HBM],
        out_specs=HBM,
        scratch_shapes=[pltpu.SemaphoreType.DMA],
        input_output_aliases={2: 0},
        compiler_params=pltpu.CompilerParams(vmem_limit_bytes=LITTLE),
        cost_estimate=pl.CostEstimate(flops=0, bytes_accessed=piece.size * 4, transcendentals=0),
        name="settle",
    )(meta, piece, whole)


def allowed_at(first, base, tok, length, lengths):
    t = first + lax.broadcasted_iota(jnp.int32, (tok, 1), 0)
    u = base + lax.broadcasted_iota(jnp.int32, (tok, length), 1)
    return (u <= t) & (u >= start_of(t, lengths))


def column_block(at):
    return pl.ds(pl.multiple_of(at, HD), HD)


def keys_of(upper, g):
    return upper[column_block(g * HD), :]


def values_of(lower, g):
    half = lower.shape[1] // 2
    both = [lower[:, column_block(side * half + g * HD)] for side in range(2)]
    return jnp.concatenate(both, axis=0)


def add_block(tok, heads, q_at, keys, values, allowed, sums, fresh=False):
    length = keys.shape[1]
    for j in range(0, heads, PAIR):
        some = min(PAIR, heads - j)
        p = jnp.exp2(dot_nn(q_at(j * tok, some * tok), keys) * FACTOR)
        if allowed is not None:
            p = p.reshape(some, tok, length)
            p = jnp.where(allowed[None], p, 0.0).reshape(some * tok, length)
        more = (fold(p, jnp.add), dot_nn(p.astype(jnp.bfloat16), values))
        for ref, value in zip(sums, more):
            here = slice(j * tok, (j + some) * tok)
            ref[here] = value if fresh else ref[here] + value


def relation(meta, part, side, tok, lengths):
    first = (meta[CHIP] * 2 + side) * tok
    base = meta[PARTS + part] * 2 * tok
    relevant = (base < first) & (meta[PARTS + part] != meta[CHIP])
    relevant = relevant & (base + 2 * tok > start_of(first, lengths))
    return relevant, base >= start_of(first + tok - 1, lengths), first, base


def side_rows(side, heads, tok):
    return pl.ds(pl.multiple_of(side * (heads * tok), HD), heads * tok)


def open_kernel(tok, heads, groups, meta, lengths, q, q_near, upper, lower, qs, total, acc):
    core = meta[CORE]
    rows = heads * tok
    for source, side, skip in ((q, core, core * groups * heads), (q_near, 1 - core, 0)):
        for g in range(groups):
            for j in range(heads):
                at = pl.ds(pl.multiple_of(side * rows + j * tok, HD), tok)
                qs[g, at] = source[:, column_block((skip + g * heads + j) * HD)]

    @pl.loop(0, groups)
    def _(g):
        keys, values = keys_of(upper, g), values_of(lower, g)
        for side in range(2):
            length = (side + 1) * tok
            first = (meta[CHIP] * 2 + side) * tok
            allowed = allowed_at(first, meta[CHIP] * 2 * tok, tok, length, lengths)
            here = side_rows(side, heads, tok)
            q_at = lambda at, count: qs[g, pl.ds(side * rows + at, count)]
            add_block(tok, heads, q_at, keys[:, :length], values[:length], allowed,
                      (total.at[g, here], acc.at[g, here]), True)


def open_sums(q, q_near, block, meta, lengths):
    tok = q.shape[0]
    heads = H // KVH
    groups = q_near.shape[1] // (heads * HD)
    rows = 2 * heads * tok
    sums = jax.ShapeDtypeStruct((groups, rows, HD), jnp.float32)
    pairs = groups * rows * tok * 2
    return pl.pallas_call(
        functools.partial(open_kernel, tok, heads, groups),
        out_shape=[jax.ShapeDtypeStruct((groups, rows, HD), jnp.bfloat16), sums, sums],
        in_specs=[SMEM, SMEM, VMEM, VMEM, VMEM, VMEM],
        out_specs=[VMEM] * 3,
        compiler_params=pltpu.CompilerParams(vmem_limit_bytes=2 * LITTLE),
        cost_estimate=BRIEF,
        name="open",
    )(meta, lengths, q, q_near, *block)


def stage_body(tok, heads, groups, first_part, meta, lengths, qs, before, pair, total, acc, held):
    for i in range(2):
        held[0][i], held[1][i] = pair[2 * i][...], pair[2 * i + 1][...]
    total[...], acc[...] = before[0][...], before[1][...]

    @pl.loop(0, 4 * groups)
    def _(step):
        which, rest = lax.div(step, 2 * groups), lax.rem(step, 2 * groups)
        g, side = lax.div(rest, 2), lax.rem(rest, 2)
        relevant, clear, first, base = relation(meta, first_part + which, side, tok, lengths)
        here = side_rows(side, heads, tok)
        sums = (total.at[g, here], acc.at[g, here])
        at = side * (heads * tok)
        q_at = lambda off, count: qs[g, pl.ds(pl.multiple_of(at + off, HD), count)]
        upper, lower = held[0].at[which], held[1].at[which]

        @pl.when(relevant & clear)
        def _():
            add_block(tok, heads, q_at, keys_of(upper, g), values_of(lower, g), None, sums)

        @pl.when(relevant & jnp.logical_not(clear))
        def _():
            allowed = allowed_at(first, base, tok, 2 * tok, lengths)
            add_block(tok, heads, q_at, keys_of(upper, g), values_of(lower, g), allowed, sums)


def stage_kernel(tok, heads, groups, first_part, own, *refs):
    meta, lengths, qs, total_in, acc_in = refs[:5]
    pair = refs[5:9]
    if own is None:
        total, acc, *held = refs[9:]
    else:
        sources, table = refs[9:12], refs[12]
        total, acc, state, held = refs[13], refs[14], refs[15:21], refs[21:23]
        q3, k3, v3, sems = refs[23:]
        copies = request_copies(own, meta, sources, (q3, k3, v3), sems)
        for copy in copies:
            copy.start()
    before = (total_in, acc_in)
    stage_body(tok, heads, groups, first_part, meta, lengths, qs, before, pair, total, acc, held)
    if own is not None:
        for copy in copies:
            copy.wait()
        requests_body(own, heads, groups, 2 * tok, meta, table, *state, q3, k3, v3)


def stage(state, pair, first_part, meta, lengths, requests=None):
    qs, total, acc = state
    groups, rows, unused = qs.shape
    flat = [x for block in pair for x in block]
    tok = flat[0].shape[1] // 2
    heads = rows // (2 * tok)
    out_shape = [jax.ShapeDtypeStruct(x.shape, x.dtype) for x in (total, acc)]
    scratch = [pltpu.VMEM((2, *x.shape), x.dtype) for x in pair[0]]
    sources, own = [], None
    if requests is not None:
        *sources, own = requests
        steps = sources[0].shape[1]
        width = sources[1].shape[2] // 2
        size = heads * own * steps
        sums = jax.ShapeDtypeStruct((groups, size, HD), jnp.float32)
        new = jax.ShapeDtypeStruct((own * steps, width), jnp.bfloat16)
        out_shape += [
            sums, sums, jax.ShapeDtypeStruct((groups, size, HD), jnp.bfloat16), new, new,
            jax.ShapeDtypeStruct((own, (LEVELS - PARTS) * 2 * tok), jnp.float32),
        ]
        scratch += [
            pltpu.VMEM((own, steps, groups * heads * HD), jnp.bfloat16),
            pltpu.VMEM((own, steps, width), jnp.bfloat16),
            pltpu.VMEM((own, steps, width), jnp.bfloat16),
            pltpu.SemaphoreType.DMA((3,)),
        ]
    new = pl.pallas_call(
        functools.partial(stage_kernel, tok, heads, groups, first_part, own),
        out_shape=out_shape,
        in_specs=[SMEM, SMEM] + [VMEM] * 7 + ([HBM] * 3 + [VMEM] if sources else []),
        out_specs=[VMEM] * len(out_shape),
        scratch_shapes=scratch,
        input_output_aliases={3: 0, 4: 1},
        compiler_params=pltpu.CompilerParams(vmem_limit_bytes=ROOM),
        cost_estimate=BRIEF,
        name=f"stage{first_part}",
    )(meta, lengths, qs, total, acc, *flat, *sources)
    return (qs, *new[:2]), new[2:]


def finish_kernel(tok, heads, groups, done, meta, lengths, qs, total, acc, *refs):
    near, out, held_k, held_v, peak, total_now, acc_now, result, sem = refs[-9:]
    parts = held_k.shape[0]
    rows = heads * tok
    core = meta[CORE]

    def fill(first):
        for i in range(first, parts):
            held_k[i], held_v[i] = refs[2 * i][...], refs[2 * i + 1][...]

    def turn_of(step):
        turn, g = lax.div(step, groups), lax.rem(step, groups)
        side = jnp.where(turn == 0, 1 - core, core)
        at = side * rows
        q_at = lambda off, count: qs[g, pl.ds(pl.multiple_of(at + off, HD), count)]
        return turn, g, side, q_at

    def write(turn, g):
        whole = jnp.sum(total_now[...], axis=1, keepdims=True)
        value = (acc_now[...] / whole).astype(result.dtype)
        for j in range(heads):
            result[turn, :, column_block((g * heads + j) * HD)] = value[j * tok : (j + 1) * tok]
        return sound(whole)

    def one_turn(step, fine):
        turn, g, side, q_at = turn_of(step)
        here = side_rows(side, heads, tok)
        total_now[...] = total[g, here]
        acc_now[...] = acc[g, here]

        @pl.loop(done, parts)
        def _(i):
            relevant, clear, first, base = relation(meta, i, side, tok, lengths)
            upper, lower = held_k.at[i], held_v.at[i]
            sums = (total_now, acc_now)

            @pl.when(relevant & clear)
            def _():
                add_block(tok, heads, q_at, keys_of(upper, g), values_of(lower, g), None, sums)

            @pl.when(relevant & jnp.logical_not(clear))
            def _():
                allowed = allowed_at(first, base, tok, 2 * tok, lengths)
                add_block(tok, heads, q_at, keys_of(upper, g), values_of(lower, g), allowed, sums)

        return fine & write(turn, g).astype(jnp.int32)

    fill(done)
    fine = lax.fori_loop(0, 2 * groups, one_turn, jnp.int32(1))

    @pl.when(fine == 0)
    def _():
        fill(0)

        @pl.loop(0, 2 * groups)
        def _(step):
            turn, g, side, q_at = turn_of(step)
            first = (meta[CHIP] * 2 + side) * tok
            peak[...] = jnp.full_like(peak, NEG)
            total_now[...] = jnp.zeros_like(total_now)
            acc_now[...] = jnp.zeros_like(acc_now)

            @pl.loop(0, parts * heads)
            def _(step):
                i, j = lax.div(step, heads), lax.rem(step, heads)
                keys, values = keys_of(held_k.at[i], g), values_of(held_v.at[i], g)
                allowed = allowed_at(first, meta[PARTS + i] * 2 * tok, tok, 2 * tok, lengths)
                mine = pl.ds(pl.multiple_of(j * tok, tok), tok)
                s = jnp.where(allowed, dot_nn(q_at(j * tok, tok), keys) * FACTOR, NEG)
                top = jnp.maximum(peak[mine], jnp.max(s, axis=1, keepdims=True))
                p = jnp.where(allowed, jnp.exp2(s - top[:, :1]), 0.0)
                shrink = jnp.exp2(peak[mine] - top)
                total_now[mine] = total_now[mine] * shrink + fold(p, jnp.add)
                acc_now[mine] = acc_now[mine] * shrink + dot_nn(p.astype(jnp.bfloat16), values)
                peak[mine] = top

            write(turn, g)

    width = near.shape[1]
    where = pl.ds(pl.multiple_of(core * width, width), width)
    copy = pltpu.make_async_copy(result.at[1], out.at[:, where], sem)
    copy.start()
    near[...] = result[0]
    copy.wait()


def finish(state, blocks, done, meta, lengths):
    qs, total, acc = state
    groups, rows, unused = qs.shape
    flat = [x for block in blocks for x in block]
    tok = flat[0].shape[1] // 2
    heads = rows // (2 * tok)
    width = groups * heads * HD
    sums = pltpu.VMEM((heads * tok, HD), jnp.float32)
    return pl.pallas_call(
        functools.partial(finish_kernel, tok, heads, groups, done),
        out_shape=[
            jax.ShapeDtypeStruct((tok, width), jnp.bfloat16),
            jax.ShapeDtypeStruct((tok, 2 * width), jnp.bfloat16),
        ],
        in_specs=[SMEM, SMEM] + [VMEM] * (3 + len(flat)),
        out_specs=[VMEM, HBM],
        scratch_shapes=[
            *[pltpu.VMEM((len(blocks), *x.shape), x.dtype) for x in blocks[0]],
            sums, sums, sums,
            pltpu.VMEM((2, tok, width), jnp.bfloat16),
            pltpu.SemaphoreType.DMA,
        ],
        compiler_params=pltpu.CompilerParams(vmem_limit_bytes=ROOM),
        cost_estimate=pl.CostEstimate(
            flops=groups * rows * tok * HD * 8, bytes_accessed=tok * width * 4,
            transcendentals=groups * rows * tok * 2,
        ),
        name="finish",
    )(meta, lengths, qs, total, acc, *flat)


def request_sums(query, keys, values, mask):
    p = jnp.exp2(dot_nn(query, keys) * FACTOR)
    p = jnp.where(mask[None], p.reshape(-1, *mask.shape), 0.0).reshape(p.shape)
    return fold(p, jnp.add), dot_nn(p.astype(jnp.bfloat16), values)


def fresh_scores(query, newk, own):
    s = dot_nt(query, newk) * FACTOR
    size = newk.shape[0]
    row = lax.broadcasted_iota(jnp.int32, (size, size), 0)
    col = lax.broadcasted_iota(jnp.int32, (size, size), 1)
    ok = (lax.rem(row, own) == lax.rem(col, own)) & (lax.div(col, own) <= lax.div(row, own))
    return s.reshape(-1, size, size), ok


def request_copies(own, meta, sources, held, sems):
    requests = pl.ds(lax.div(meta[CHIP], 2) * own, own)
    copies = []
    for i, (source, target) in enumerate(zip(sources, held)):
        width = target.shape[2]
        where = pl.ds(pl.multiple_of(meta[CORE] * width, width), width)
        copies.append(pltpu.make_async_copy(source.at[requests, :, where], target, sems.at[i]))
    return copies


def requests_body(own, heads, groups, length, meta, table, total, acc, query, newk, newv, mask, q3, k3, v3):
    steps = q3.shape[1]
    level = lax.div(meta[CHIP], 2)
    pick = lax.broadcasted_iota(jnp.int32, (own, table.shape[1]), 1) - level * own
    pick = (pick == lax.broadcasted_iota(jnp.int32, pick.shape, 0)).astype(jnp.float32)
    rows = dot_nt(pick.astype(jnp.bfloat16), table[...].astype(jnp.float32).astype(jnp.bfloat16))
    lane = lax.div(lax.broadcasted_iota(jnp.int32, (own, length), 1), BLK)
    for i in range(mask.shape[1] // length):
        number = (lane + meta[PARTS + i] * (length // BLK)).astype(jnp.float32)
        hit = rows[:, :1] == number
        for j in range(1, rows.shape[1]):
            hit = hit | (rows[:, j : j + 1] == number)
        mask[:, i * length : (i + 1) * length] = hit.astype(jnp.float32)
    for s in range(steps):
        for g in range(groups):
            col = slice(g * HD, (g + 1) * HD)
            at = slice(s * own, (s + 1) * own)
            newk[at, col] = k3[:, s, col]
            newv[at, col] = v3[:, s, col]
            for j in range(heads):
                first = (g * heads + j) * HD
                row = (j * steps + s) * own
                query[g, row : row + own] = q3[:, s, first : first + HD]

    @pl.loop(0, groups)
    def _(g):
        col = column_block(g * HD)
        s, ok = fresh_scores(query[g], newk[:, col], own)
        p = jnp.where(ok[None], jnp.exp2(s), 0.0).reshape(-1, s.shape[2])
        first = jnp.sum(p, axis=1, keepdims=True)
        lead = lax.broadcasted_iota(jnp.int32, (p.shape[0], HD), 1) == 0
        total[g] = jnp.where(lead, first, 0.0)
        acc[g] = dot_nn(p.astype(jnp.bfloat16), newv[:, col])


def early_kernel(groups, total_in, acc_in, query, mask, *refs):
    total, acc = refs[-2:]
    length = refs[0].shape[1]

    @pl.loop(0, groups)
    def _(g):
        sums = [total_in[g], acc_in[g]]
        for i in range(len(refs) // 2 - 1):
            open_to = mask[:, i * length : (i + 1) * length] > 0
            keys, values = keys_of(refs[2 * i], g), values_of(refs[2 * i + 1], g)
            more = request_sums(query[g], keys, values, open_to)
            sums = [x + y for x, y in zip(sums, more)]
        total[g], acc[g] = sums


def early_decode(state, blocks):
    total, acc, query, newk, newv, mask = state
    groups, rows, unused = query.shape
    flat = [x for block in blocks for x in block]
    sums = jax.ShapeDtypeStruct(total.shape, total.dtype)
    new = pl.pallas_call(
        functools.partial(early_kernel, groups),
        out_shape=[sums, sums],
        in_specs=[VMEM] * (4 + len(flat)),
        out_specs=[VMEM] * 2,
        input_output_aliases={0: 0, 1: 1},
        compiler_params=pltpu.CompilerParams(vmem_limit_bytes=2 * LITTLE),
        cost_estimate=BRIEF,
        name="early_decode",
    )(total, acc, query, mask, *flat)
    return [*new, query, newk, newv, mask]


def late_kernel(own, steps, heads, groups, done, meta, total, acc, query, newk, newv, mask, *refs):
    parts, out = len(refs) // 2, refs[-1]
    length = refs[0].shape[1]
    size = own * steps

    def write(g, sums, whole):
        result = (sums / whole).astype(out.dtype)
        for j in range(heads):
            out[:, column_block((g * heads + j) * HD)] = result[j * size : (j + 1) * size]

    def one_group(g, fine):
        sums = [total[g], acc[g]]
        for i in range(done, parts):
            open_to = mask[:, i * length : (i + 1) * length] > 0
            keys, values = keys_of(refs[2 * i], g), values_of(refs[2 * i + 1], g)
            more = request_sums(query[g], keys, values, open_to)
            sums = [x + y for x, y in zip(sums, more)]
        whole = jnp.sum(sums[0], axis=1, keepdims=True)
        write(g, sums[1], whole)
        return fine & sound(whole).astype(jnp.int32)

    fine = lax.fori_loop(0, groups, one_group, jnp.int32(1))

    @pl.when(fine == 0)
    def _():
        @pl.loop(0, groups)
        def _(g):
            col = column_block(g * HD)
            fresh, ok = fresh_scores(query[g], newk[:, col], own)
            fresh = jnp.where(ok[None], fresh, NEG).reshape(-1, size)
            top = jnp.max(fresh, axis=1, keepdims=True)
            p = jnp.exp2(fresh - top)
            whole = jnp.sum(p, axis=1, keepdims=True)
            sums = dot_nn(p.astype(jnp.bfloat16), newv[:, col])
            for i in range(parts):
                s = dot_nn(query[g], keys_of(refs[2 * i], g)) * FACTOR
                open_to = mask[:, i * length : (i + 1) * length] > 0
                s = jnp.where(open_to[None], s.reshape(-1, own, length), NEG).reshape(s.shape)
                higher = jnp.maximum(top, jnp.max(s, axis=1, keepdims=True))
                p = jnp.exp2(s - higher)
                shrink = jnp.exp2(top - higher)
                whole = whole * shrink + jnp.sum(p, axis=1, keepdims=True)
                sums = sums * shrink + dot_nn(p.astype(jnp.bfloat16), values_of(refs[2 * i + 1], g))
                top = higher
            write(g, sums, whole)


def late_decode(early, blocks, done, own, steps, meta):
    groups, rows, unused = early[0].shape
    heads = H // KVH
    flat = [x for block in blocks for x in block]
    parts, length = len(blocks), flat[0].shape[1]
    pairs = groups * rows * (parts - done) * length
    return pl.pallas_call(
        functools.partial(late_kernel, own, steps, heads, groups, done),
        out_shape=jax.ShapeDtypeStruct((own * steps, groups * heads * HD), jnp.bfloat16),
        in_specs=[SMEM] + [VMEM] * (len(early) + len(flat)),
        out_specs=VMEM,
        compiler_params=pltpu.CompilerParams(vmem_limit_bytes=ROOM),
        cost_estimate=pl.CostEstimate(
            flops=pairs * HD * 8, bytes_accessed=rows * HD, transcendentals=pairs
        ),
        name="late_decode",
    )(meta, *early, *flat)


def decode_kernel(parts, steps, heads, groups, starts, q, mask, newk, newv, *refs):
    kheld, vheld = refs[:parts], refs[parts : 2 * parts]
    out, kall, vall, sems, scores = refs[2 * parts :]
    own = q.shape[0]
    rows = heads * own
    length = kheld[0].shape[1]
    copies = []
    for i in range(parts):
        where = pl.ds(pl.multiple_of(starts[i], HD), length)
        copies.append(pltpu.make_async_copy(kheld[i], kall.at[:, where], sems.at[2 * i]))
        copies.append(pltpu.make_async_copy(vheld[i], vall.at[where], sems.at[2 * i + 1]))
    for copy in copies:
        copy.start()
    row = lax.broadcasted_iota(jnp.int32, (own, own), 0)
    col = lax.broadcasted_iota(jnp.int32, (own, own), 1)
    fresh_ok = (lax.div(row, steps) == lax.div(col, steps)) & (col <= row)

    def columns(g):
        return slice(g * HD, (g + 1) * HD)

    def stacked(g):
        first = g * heads
        slices = [q[:, (first + j) * HD : (first + j + 1) * HD] for j in range(heads)]
        return jnp.concatenate([x.astype(jnp.float32) for x in slices], 0).astype(jnp.bfloat16)

    def keep(allowed, x, other):
        y = x.reshape(heads, own, x.shape[1])
        return jnp.where(allowed[None], y, other).reshape(x.shape)

    def open_to(i):
        return mask[:, pl.ds(pl.multiple_of(starts[i], HD), length)] > 0

    def write(g, acc, whole):
        result = acc / whole
        for j in range(heads):
            out[:, (g * heads + j) * HD : (g * heads + j + 1) * HD] = result[
                j * own : (j + 1) * own
            ].astype(out.dtype)

    fine = None
    for g in range(groups):
        query = stacked(g)
        p = keep(fresh_ok, jnp.exp2(dot_nt(query, newk[:, columns(g)]) * FACTOR), 0.0)
        whole = jnp.sum(p, axis=1, keepdims=True)
        acc = dot_nn(p.astype(jnp.bfloat16), newv[:, columns(g)])
        total = jnp.zeros((rows, HD), jnp.float32)
        for i in range(parts):
            p = jnp.exp2(dot_nn(query, kheld[i][columns(g)]) * FACTOR)
            p = keep(open_to(i), p, 0.0)
            total = total + fold(p, jnp.add)
            acc = acc + dot_nn(p.astype(jnp.bfloat16), vheld[i][:, columns(g)])
        whole = whole + jnp.sum(total, axis=1, keepdims=True)
        write(g, acc, whole)
        fine = sound(whole) if fine is None else fine & sound(whole)

    @pl.when(jnp.logical_not(fine))
    def _():
        for g in range(groups):
            query = stacked(g)
            fresh = keep(fresh_ok, dot_nt(query, newk[:, columns(g)]) * FACTOR, NEG)
            top = jnp.max(fresh, axis=1, keepdims=True)
            for i in range(parts):
                s = keep(open_to(i), dot_nn(query, kheld[i][columns(g)]) * FACTOR, NEG)
                scores[:, i * length : (i + 1) * length] = s
                top = jnp.maximum(top, jnp.max(s, axis=1, keepdims=True))
            p = jnp.exp2(fresh - top)
            whole = jnp.sum(p, axis=1, keepdims=True)
            acc = dot_nn(p.astype(jnp.bfloat16), newv[:, columns(g)])
            for i in range(parts):
                p = jnp.exp2(scores[:, i * length : (i + 1) * length] - top)
                whole = whole + jnp.sum(p, axis=1, keepdims=True)
                acc = acc + dot_nn(p.astype(jnp.bfloat16), vheld[i][:, columns(g)])
            write(g, acc, whole)

    for copy in copies:
        copy.wait()


def decode(q, mask, newk, newv, kparts, vparts, starts, steps):
    own = q.shape[0]
    parts = len(kparts)
    length, width = vparts[0].shape
    count = parts * length
    heads = H // KVH
    groups = width // HD
    rows = heads * own
    pairs = groups * rows * count
    return pl.pallas_call(
        functools.partial(decode_kernel, parts, steps, heads, groups),
        out_shape=[
            jax.ShapeDtypeStruct(q.shape, jnp.bfloat16),
            jax.ShapeDtypeStruct((width, count), jnp.bfloat16),
            jax.ShapeDtypeStruct((count, width), jnp.bfloat16),
        ],
        grid_spec=pltpu.PrefetchScalarGridSpec(
            num_scalar_prefetch=1,
            grid=(),
            in_specs=[VMEM] * (4 + 2 * parts),
            out_specs=[VMEM, HBM, HBM],
            scratch_shapes=[
                pltpu.SemaphoreType.DMA((2 * parts,)),
                pltpu.VMEM((rows, count), jnp.float32),
            ],
        ),
        compiler_params=pltpu.CompilerParams(vmem_limit_bytes=ROOM),
        cost_estimate=pl.CostEstimate(
            flops=pairs * HD * 4, bytes_accessed=count * width * 4, transcendentals=pairs
        ),
        name="decode",
    )(starts, q, mask, newk, newv, *kparts, *vparts)


def prepare_kernel(meta, k, v, send, keys, values):
    width = k.shape[1] // 2
    mine = pl.ds(pl.multiple_of(meta[0] * width, width), width)
    other = pl.ds(pl.multiple_of((1 - meta[0]) * width, width), width)
    send[:width] = k[:, other].astype(jnp.float32).T.astype(send.dtype)
    send[width:] = v[:, other]
    keys[:, mine] = k[:, mine].astype(jnp.float32).T.astype(keys.dtype)
    values[:, mine] = v[:, mine]


def prepare(k, v, core):
    tok, width = k.shape[0], k.shape[1] // 2
    assert tok == width
    block = jax.ShapeDtypeStruct((width, 2 * tok), k.dtype)
    return pl.pallas_call(
        prepare_kernel,
        out_shape=[jax.ShapeDtypeStruct((2 * tok, width), k.dtype), block, block],
        in_specs=[SMEM, VMEM, VMEM],
        out_specs=[VMEM] * 3,
        compiler_params=pltpu.CompilerParams(vmem_limit_bytes=LITTLE),
        name="prepare",
    )(core[None], k, v)


def join_kernel(meta, keys_in, values_in, theirs, q, keys, values, send_q, sem):
    columns = send_q.shape[1]
    where = pl.ds(pl.multiple_of((1 - meta[0]) * columns, columns), columns)
    copy = pltpu.make_async_copy(q.at[:, where], send_q, sem)
    copy.start()
    width = theirs.shape[1]
    other = pl.ds(pl.multiple_of((1 - meta[0]) * width, width), width)
    keys[...], values[...] = keys_in[...], values_in[...]
    keys[:, other] = theirs[:width]
    values[:, other] = theirs[width:]
    copy.wait()


def join(keys, values, theirs, q, core):
    return pl.pallas_call(
        join_kernel,
        out_shape=[
            jax.ShapeDtypeStruct(keys.shape, keys.dtype),
            jax.ShapeDtypeStruct(values.shape, values.dtype),
            jax.ShapeDtypeStruct((q.shape[0], q.shape[1] // 2), q.dtype),
        ],
        in_specs=[SMEM, VMEM, VMEM, VMEM, HBM],
        out_specs=[VMEM] * 3,
        scratch_shapes=[pltpu.SemaphoreType.DMA],
        compiler_params=pltpu.CompilerParams(vmem_limit_bytes=LITTLE),
        name="join",
    )(core[None], keys, values, theirs, q)


def take_kernel(meta, whole, out, sem):
    width = out.shape[1]
    where = pl.ds(pl.multiple_of((1 - meta[CORE]) * width, width), width)
    copy = pltpu.make_async_copy(whole.at[:, where], out, sem)
    copy.start()
    copy.wait()


def take_other_half(whole, meta):
    return pl.pallas_call(
        take_kernel,
        out_shape=jax.ShapeDtypeStruct((whole.shape[0], whole.shape[1] // 2), whole.dtype),
        in_specs=[SMEM, HBM],
        out_specs=VMEM,
        scratch_shapes=[pltpu.SemaphoreType.DMA],
        compiler_params=pltpu.CompilerParams(vmem_limit_bytes=LITTLE),
        name="take",
    )(meta, whole)


def project_kernel(meta, *refs):
    pieces, (whole, other), outs, (sorted_rows,) = refs[:-7], refs[-7:-5], refs[-5:-1], refs[-1:]
    parts = len(pieces)
    rows = pieces[0].shape[0]
    for i, piece in enumerate(pieces):
        at = pl.ds(pl.multiple_of(meta[LEVELS + i] * rows, rows), rows)
        sorted_rows[at] = piece[...]
    depth = other.shape[1]
    mine = whole[:, pl.ds(pl.multiple_of(meta[CORE] * depth, depth), depth)]
    half = parts * rows // 2
    here = pl.ds(pl.multiple_of(meta[ACROSS] * half, half), half)
    there = pl.ds(pl.multiple_of((1 - meta[ACROSS]) * half, half), half)
    kept, beside, across, corner = outs
    for at, near, far in ((here, kept, beside), (there, across, corner)):
        some = sorted_rows[at]
        near[...] = dot_nt(mine, some).astype(near.dtype)
        far[...] = dot_nt(other[...], some).astype(far.dtype)


def project(pieces, whole, other, meta):
    rows = len(pieces) * pieces[0].shape[0]
    width, depth = other.shape
    block = jax.ShapeDtypeStruct((width, rows // 2), jnp.bfloat16)
    return pl.pallas_call(
        project_kernel,
        out_shape=[jax.ShapeDtypeStruct(block.shape, jnp.float32)] + [block] * 3,
        in_specs=[SMEM] + [VMEM] * (len(pieces) + 2),
        out_specs=[VMEM] * 4,
        scratch_shapes=[pltpu.VMEM((rows, depth), jnp.bfloat16)],
        compiler_params=pltpu.CompilerParams(vmem_limit_bytes=2 * LITTLE),
        cost_estimate=pl.CostEstimate(
            flops=rows * width * depth * 4, bytes_accessed=width * depth * 4, transcendentals=0
        ),
        name="project",
    )(meta, *pieces, whole, other)


def index(z, y, c):
    return (z * 2 + y) * 2 + c


def on_ring(r, chips):
    return (r, 0) if r < chips // 2 else (chips - 1 - r, 1)


def ring_perm(chips, d):
    return [
        (index(*on_ring(r, chips), c), index(*on_ring((r + d) % chips, chips), c))
        for r in range(chips)
        for c in range(2)
    ]


def ring_place(r, chips):
    r = lax.rem(r + 2 * chips, chips)
    return jnp.where(r < chips // 2, r * 2, (chips - 1 - r) * 2 + 1)


def spread(x, n):
    place = lax.axis_index("seq")
    deep = n // 4
    everyone = [(z, y, c) for z in range(deep) for y in range(2) for c in range(2)]
    z, y, c = place // 4, (place // 2) % 2, place % 2
    held = [(x, z, y, c)]
    for d in range(1, deep):
        perm = [(index(*p), index((p[0] - d) % deep, p[1], p[2])) for p in everyone]
        held.append((lax.ppermute(x, "seq", perm), lax.rem(z + d, deep), y, c))
    perm = [(index(*p), index(p[0], 1 - p[1], p[2])) for p in everyone]
    held += [(lax.ppermute(b, "seq", perm), bz, 1 - by, bc) for b, bz, by, bc in held]
    perm = [(index(*p), index(p[0], p[1], 1 - p[2])) for p in everyone]
    held += [(lax.ppermute(b, "seq", perm), bz, by, 1 - bc) for b, bz, by, bc in held]
    return [b for b, *_ in held], jnp.stack([index(bz, by, bc) for _, bz, by, bc in held])


def open_blocks(table, steps, count):
    number = lax.broadcasted_iota(jnp.int32, (*table.shape, count), 2) // BLK
    mask = jnp.any(table[:, :, None] == number, axis=1).astype(jnp.float32)
    return jnp.repeat(mask, steps, axis=0)


def whole_heads(n, q_pre, k_cache, v_cache, lengths, q_dec, k_new, v_new, block_table, w_out):
    tok = q_pre.shape[0]
    place = lax.axis_index("seq").astype(jnp.int32)
    rows, steps = q_dec.shape[0], q_dec.shape[1]
    own = rows // n
    kparts, sources = spread(k_cache.T, n)
    vparts, _ = spread(v_cache, n)
    starts = sources.astype(jnp.int32) * tok

    def mine(x):
        y = lax.dynamic_slice_in_dim(x, place * own, own, 0)
        return y.reshape(own * steps, -1) if x.ndim == 3 else y

    mask = open_blocks(mine(block_table), steps, n * tok)
    attn_own, keys, values = decode(
        mine(q_dec), mask, mine(k_new), mine(v_new), kparts, vparts, starts, steps
    )
    attn = lax.all_gather(attn_own, "seq", axis=0, tiled=True)
    flat = jnp.dot(attn, w_out, preferred_element_type=jnp.float32).astype(jnp.bfloat16)
    dec_out = lax.psum_scatter(
        flat.reshape(rows, steps, -1), "tp", scatter_dimension=0, tiled=True
    )
    zero = jnp.zeros((), jnp.int32)
    meta = jnp.stack([place * tok, zero, zero, zero])
    groups = k_cache.shape[1] // HD
    pre_out = prefill(
        q_pre, keys, values, meta, lengths, groups, q_pre.shape[1], "prefill"
    )
    return (pre_out, dec_out)


def split_heads(n, q_pre, k_cache, v_cache, lengths, q_dec, k_new, v_new, block_table, w_out):
    place = lax.axis_index("seq").astype(jnp.int32)
    across = lax.axis_index("tp").astype(jnp.int32)
    core, chip = lax.rem(place, 2), lax.div(place, 2)
    chips = n // 2
    far, deep = chips // 2, chips // 2
    z, y = lax.div(chip, 2), lax.rem(chip, 2)
    r = jnp.where(y == 0, z, chips - 1 - z)
    rows, steps = q_dec.shape[0], q_dec.shape[1]
    own = rows // deep
    sibling = [(i, i ^ 1) for i in range(n)]
    everyone = [(a, b, c) for a in range(deep) for b in range(2) for c in range(2)]

    order = [0] + [o for d in range(1, far) for o in (-d, d)] + [far]
    numbers = [ring_place(r + o, chips) for o in order]
    levels = [z] + [lax.rem(z + deep - d, deep) for d in range(1, deep)]
    assert len(numbers) == LEVELS - PARTS
    meta = jnp.stack([core, chip, across] + numbers + levels).astype(jnp.int32)

    send, keys, values = prepare(k_cache, v_cache, core)
    theirs = lax.ppermute(send, "seq", sibling)
    theirs, meta = lax.optimization_barrier((theirs, meta))
    held_k, held_v = {}, {}
    held_k[0], held_v[0], send_q = join(keys, values, theirs, q_pre, core)
    near_q = lax.ppermute(send_q, "seq", sibling)

    up, down = ring_perm(chips, 1), ring_perm(chips, -1)
    early, w_near = (), w_out
    for d in range(1, far + 1):
        held_k[-d] = lax.ppermute(held_k[1 - d], "seq", up)
        held_v[d] = lax.ppermute(held_v[d - 1], "seq", down)
        if d < far:
            held_k[d] = lax.ppermute(held_k[d - 1], "seq", down)
            held_v[-d] = lax.ppermute(held_v[1 - d], "seq", up)
            sides = (-d, d)
        else:
            held_k[d] = held_k[-d]
            sides = (d,)
        if d == 1:
            state = open_sums(q_pre, near_q, (held_k[0], held_v[0]), meta, lengths)
        elif d < far:
            requests = (q_dec, k_new, v_new, block_table.T, own) if d == 2 else None
            pair = [(held_k[o], held_v[o]) for o in (1 - d, d - 1)]
            state, more = stage(state, pair, 2 * d - 3, meta, lengths, requests)
            early = early or more
        else:
            blocks = [(held_k[o], held_v[o]) for o in order[:-1]]
            early = early_decode(early, blocks)
        for x in (held_k, held_v):
            moved, state, early = lax.optimization_barrier(([x[o] for o in sides], state, early))
            x.update(zip(sides, moved))
        if d == 3:
            w_near, state = lax.optimization_barrier((w_near, state))
            weights = w_near.T
            w_near = lax.ppermute(take_other_half(weights, meta), "seq", sibling)
    w_near, early = lax.optimization_barrier((w_near, early))
    blocks = [(held_k[o], held_v[o]) for o in order]
    attn_own = late_decode(early, blocks, len(blocks) - 1, own, steps, meta)

    pieces = [attn_own]
    for d in range(1, deep):
        perm = [(index(*p), index((p[0] + d) % deep, p[1], p[2])) for p in everyone]
        pieces.append(lax.ppermute(attn_own, "seq", perm))
    attn_own, state = lax.optimization_barrier((attn_own, state))
    near, pre_out = finish(state, blocks, 2 * far - 3, meta, lengths)
    pieces, near, pre_out = lax.optimization_barrier((pieces, near, pre_out))
    back = lax.ppermute(near, "seq", sibling)
    pre_out = settle(pre_out, back, meta)

    total, *sent = project(pieces, weights, w_near, meta)
    got = []
    for piece, (dc, dx) in zip(sent, ((1, 0), (0, 1), (1, 1))):
        perm = [
            (i * 2 + x, (i ^ dc) * 2 + (x ^ dx)) for i in range(n) for x in range(2)
        ]
        got.append(lax.ppermute(piece, ("seq", "tp"), perm))
    got[0], pre_out = lax.optimization_barrier((got[0], pre_out))
    for piece in got:
        total = total + piece.astype(jnp.float32)
    dec_out = total.astype(jnp.bfloat16).T.reshape(deep // 2, steps, own, -1)
    return (pre_out, dec_out.transpose(0, 2, 1, 3).reshape(rows // 2, steps, -1))


def per_device(n, tp, q_pre, k_cache, v_cache, prompt_lengths, *rest):
    groups = k_cache.shape[1] // HD
    square = groups % 2 == 0 and k_cache.shape[1] == 2 * k_cache.shape[0]
    small = n * k_cache.shape[0] // BLK <= 256 and n == 2 * (LEVELS - PARTS)
    form = split_heads if square and tp == 2 and small else whole_heads
    return form(n, q_pre, k_cache, v_cache, prompt_lengths.astype(jnp.int32), *rest)


def solution(mesh):
    placed = (
        P("seq", "tp"),
        P("seq", "tp"),
        P("seq", "tp"),
        P(),
        P(None, None, "tp"),
        P(None, None, "tp"),
        P(None, None, "tp"),
        P(),
        P("tp", "seq"),
    )
    return jax.shard_map(
        functools.partial(per_device, mesh.shape["seq"], mesh.shape["tp"]),
        mesh=mesh,
        in_specs=placed,
        out_specs=(P("seq", "tp"), P("tp", None, "seq")),
        check_vma=False,
    )
```

```python
import functools
import math

import jax
import jax.numpy as jnp
from jax import lax
from jax.experimental import pallas as pl
from jax.experimental.pallas import tpu as pltpu
from jax.sharding import PartitionSpec as P

H = 56
KVH = 8
HD = 128
BLK = 64
SPAN = 512
PAIR = 2
NEG = -1e30
LEAST, MOST = 2.0**-60, 2.0**100
FACTOR = math.log2(math.e) / math.sqrt(HD)
ROOM = 16 * 1024 * 1024
LITTLE = 4 * 1024 * 1024
CORE, CHIP, ACROSS, PARTS, LEVELS = 0, 1, 2, 3, 11
BRIEF = pl.CostEstimate(flops=1024, bytes_accessed=1024, transcendentals=0)
HBM = pl.BlockSpec(memory_space=pltpu.HBM)
VMEM = pl.BlockSpec(memory_space=pltpu.VMEM)
SMEM = pl.BlockSpec(memory_space=pltpu.SMEM)


def dot_nt(a, b):
    return lax.dot_general(a, b, (((1,), (1,)), ((), ())), preferred_element_type=jnp.float32)


def dot_nn(a, b):
    return lax.dot_general(a, b, (((1,), (0,)), ((), ())), preferred_element_type=jnp.float32)


def fold(x, op):
    out = x[:, :HD]
    for i in range(1, x.shape[1] // HD):
        out = op(out, x[:, i * HD : (i + 1) * HD])
    return out


def start_of(position, lengths):
    end = jnp.int32(0)
    out = jnp.zeros_like(position)
    for i in range(lengths.shape[0]):
        end = end + lengths[i]
        out = jnp.where(position >= end, end, out)
    return out


def sound(total):
    return (jnp.min(total) >= LEAST) & (jnp.max(total) <= MOST)


def prefill_kernel(tok, heads, meta, lengths, q, keys_all, values_all, *refs):
    out, qs, peak, total, acc = refs[-5:]
    for j in range(heads):
        qs[j * tok : (j + 1) * tok] = q[:, j * HD : (j + 1) * HD]
    total[...] = jnp.zeros_like(total)
    acc[...] = jnp.zeros_like(acc)

    begin = meta[0]
    finish = begin + tok
    low = start_of(begin, lengths)
    high = start_of(finish - 1, lengths)
    blocks = lax.div(finish - low + SPAN - 1, SPAN)
    clear = lax.div(finish - high, SPAN)

    def first_of(k):
        return jnp.maximum(finish - (k + 1) * SPAN, 0)

    def load(k):
        here = pl.ds(pl.multiple_of(first_of(k), HD), SPAN)
        return keys_all[:, here], values_all[here, :]

    def allowed_in(k):
        t = begin + lax.broadcasted_iota(jnp.int32, (tok, 1), 0)
        u = first_of(k) + lax.broadcasted_iota(jnp.int32, (tok, SPAN), 1)
        last = jnp.minimum(t, finish - k * SPAN - 1)
        return (u <= last) & (u >= start_of(t, lengths))

    def keep(allowed, x, other):
        some = x.shape[0] // tok
        return jnp.where(allowed[None], x.reshape(some, tok, SPAN), other).reshape(x.shape)

    def block(k, masked):
        keys, values = load(k)
        allowed = allowed_in(k) if masked else None
        for j in range(0, heads, PAIR):
            here = slice(j * tok, min(j + PAIR, heads) * tok)
            p = jnp.exp2(dot_nn(qs[here], keys) * FACTOR)
            if masked:
                p = keep(allowed, p, 0.0)
            total[here] += fold(p, jnp.add)
            acc[here] += dot_nn(p.astype(jnp.bfloat16), values)

    block(0, True)

    @pl.loop(1, jnp.maximum(clear, 1))
    def _(k):
        block(k, False)

    @pl.loop(jnp.maximum(clear, 1), blocks)
    def _(k):
        block(k, True)

    def write():
        whole = jnp.sum(total[...], axis=1, keepdims=True)
        result = (acc[...] / whole).astype(out.dtype)
        for j in range(heads):
            out[:, j * HD : (j + 1) * HD] = result[j * tok : (j + 1) * tok]
        return whole

    fine = sound(write())

    @pl.when(jnp.logical_not(fine))
    def _():
        peak[...] = jnp.full_like(peak, NEG)
        total[...] = jnp.zeros_like(total)
        acc[...] = jnp.zeros_like(acc)

        @pl.loop(0, blocks)
        def _(k):
            keys, values = load(k)
            allowed = allowed_in(k)

            @pl.loop(0, heads)
            def _(j):
                here = pl.ds(pl.multiple_of(j * tok, tok), tok)
                s = jnp.where(allowed, dot_nn(qs[here], keys) * FACTOR, NEG)
                top = jnp.maximum(peak[here], jnp.max(s, axis=1, keepdims=True))
                p = jnp.where(allowed, jnp.exp2(s - top[:, :1]), 0.0)
                shrink = jnp.exp2(peak[here] - top)
                total[here] = total[here] * shrink + fold(p, jnp.add)
                acc[here] = acc[here] * shrink + dot_nn(p.astype(jnp.bfloat16), values)
                peak[here] = top

        write()


def prefill(q, keys, values, meta, lengths, groups, columns, name, before=None):
    tok = q.shape[0]
    count = values.shape[0]
    heads = H // KVH
    rows = heads * tok
    pairs = rows * count // 2 * groups
    extra = [] if before is None else [before]
    return pl.pallas_call(
        functools.partial(prefill_kernel, tok, heads),
        out_shape=jax.ShapeDtypeStruct((tok, columns), jnp.bfloat16),
        grid_spec=pltpu.PrefetchScalarGridSpec(
            num_scalar_prefetch=2,
            grid=(groups,),
            in_specs=[
                pl.BlockSpec((tok, heads * HD), lambda g, meta, lengths: (0, meta[1] + g)),
                pl.BlockSpec((HD, count), lambda g, meta, lengths: (meta[2] + g, 0)),
                pl.BlockSpec((count, HD), lambda g, meta, lengths: (0, meta[2] + g)),
            ]
            + [HBM] * len(extra),
            out_specs=pl.BlockSpec((tok, heads * HD), lambda g, meta, lengths: (0, meta[3] + g)),
            scratch_shapes=[
                pltpu.VMEM((rows, HD), jnp.bfloat16),
                pltpu.VMEM((rows, HD), jnp.float32),
                pltpu.VMEM((rows, HD), jnp.float32),
                pltpu.VMEM((rows, HD), jnp.float32),
            ],
        ),
        compiler_params=pltpu.CompilerParams(vmem_limit_bytes=ROOM),
        cost_estimate=pl.CostEstimate(
            flops=pairs * HD * 8, bytes_accessed=count * HD * 4 * groups, transcendentals=pairs
        ),
        input_output_aliases={} if before is None else {5: 0},
        name=name,
    )(meta, lengths, q, keys, values, *extra)


def settle_kernel(meta, piece, whole, out, sem):
    width = piece.shape[1]
    where = pl.ds(pl.multiple_of((1 - meta[CORE]) * width, width), width)
    copy = pltpu.make_async_copy(piece, out.at[:, where], sem)
    copy.start()
    copy.wait()


def settle(whole, piece, meta):
    return pl.pallas_call(
        settle_kernel,
        out_shape=jax.ShapeDtypeStruct(whole.shape, whole.dtype),
        in_specs=[SMEM, VMEM, HBM],
        out_specs=HBM,
        scratch_shapes=[pltpu.SemaphoreType.DMA],
        input_output_aliases={2: 0},
        compiler_params=pltpu.CompilerParams(vmem_limit_bytes=LITTLE),
        cost_estimate=pl.CostEstimate(flops=0, bytes_accessed=piece.size * 4, transcendentals=0),
        name="settle",
    )(meta, piece, whole)


def allowed_at(first, base, tok, length, lengths):
    t = first + lax.broadcasted_iota(jnp.int32, (tok, 1), 0)
    u = base + lax.broadcasted_iota(jnp.int32, (tok, length), 1)
    return (u <= t) & (u >= start_of(t, lengths))


def column_block(at):
    return pl.ds(pl.multiple_of(at, HD), HD)


def keys_of(upper, g):
    return upper[column_block(g * HD), :]


def values_of(lower, g):
    half = lower.shape[1] // 2
    both = [lower[:, column_block(side * half + g * HD)] for side in range(2)]
    return jnp.concatenate(both, axis=0)


def add_block(tok, heads, q_at, keys, values, allowed, sums, fresh=False):
    length = keys.shape[1]
    bias = None if allowed is None else jnp.where(allowed, 0.0, -jnp.inf)
    for j in range(0, heads, PAIR):
        some = min(PAIR, heads - j)
        s = dot_nn(q_at(j * tok, some * tok), keys) * FACTOR
        if bias is not None:
            s = (s.reshape(some, tok, length) + bias[None]).reshape(some * tok, length)
        p = jnp.exp2(s)
        more = (fold(p, jnp.add), dot_nn(p.astype(jnp.bfloat16), values))
        for ref, value in zip(sums, more):
            here = slice(j * tok, (j + some) * tok)
            ref[here] = value if fresh else ref[here] + value


def relation(meta, part, side, tok, lengths):
    first = (meta[CHIP] * 2 + side) * tok
    base = meta[PARTS + part] * 2 * tok
    relevant = (base < first) & (meta[PARTS + part] != meta[CHIP])
    relevant = relevant & (base + 2 * tok > start_of(first, lengths))
    return relevant, base >= start_of(first + tok - 1, lengths), first, base


def side_rows(side, heads, tok):
    return pl.ds(pl.multiple_of(side * (heads * tok), HD), heads * tok)


def open_kernel(tok, heads, groups, meta, lengths, q, q_near, upper, lower, qs, total, acc):
    core = meta[CORE]
    rows = heads * tok
    for source, side, skip in ((q, core, core * groups * heads), (q_near, 1 - core, 0)):
        for g in range(groups):
            for j in range(heads):
                at = pl.ds(pl.multiple_of(side * rows + j * tok, HD), tok)
                qs[g, at] = source[:, column_block((skip + g * heads + j) * HD)]

    @pl.loop(0, groups)
    def _(g):
        keys, values = keys_of(upper, g), values_of(lower, g)
        for side in range(2):
            length = (side + 1) * tok
            first = (meta[CHIP] * 2 + side) * tok
            allowed = allowed_at(first, meta[CHIP] * 2 * tok, tok, length, lengths)
            here = side_rows(side, heads, tok)
            q_at = lambda at, count: qs[g, pl.ds(side * rows + at, count)]
            add_block(tok, heads, q_at, keys[:, :length], values[:length], allowed,
                      (total.at[g, here], acc.at[g, here]), True)


def open_sums(q, q_near, block, meta, lengths):
    tok = q.shape[0]
    heads = H // KVH
    groups = q_near.shape[1] // (heads * HD)
    rows = 2 * heads * tok
    sums = jax.ShapeDtypeStruct((groups, rows, HD), jnp.float32)
    pairs = groups * rows * tok * 2
    return pl.pallas_call(
        functools.partial(open_kernel, tok, heads, groups),
        out_shape=[jax.ShapeDtypeStruct((groups, rows, HD), jnp.bfloat16), sums, sums],
        in_specs=[SMEM, SMEM, VMEM, VMEM, VMEM, VMEM],
        out_specs=[VMEM] * 3,
        compiler_params=pltpu.CompilerParams(vmem_limit_bytes=2 * LITTLE),
        cost_estimate=BRIEF,
        name="open",
    )(meta, lengths, q, q_near, *block)


def stage_body(tok, heads, groups, first_part, meta, lengths, qs, before, pair, total, acc, held):
    for i in range(2):
        held[0][i], held[1][i] = pair[2 * i][...], pair[2 * i + 1][...]
    total[...], acc[...] = before[0][...], before[1][...]

    @pl.loop(0, 4 * groups)
    def _(step):
        which, rest = lax.div(step, 2 * groups), lax.rem(step, 2 * groups)
        g, side = lax.div(rest, 2), lax.rem(rest, 2)
        relevant, clear, first, base = relation(meta, first_part + which, side, tok, lengths)
        here = side_rows(side, heads, tok)
        sums = (total.at[g, here], acc.at[g, here])
        at = side * (heads * tok)
        q_at = lambda off, count: qs[g, pl.ds(pl.multiple_of(at + off, HD), count)]
        upper, lower = held[0].at[which], held[1].at[which]

        @pl.when(relevant & clear)
        def _():
            add_block(tok, heads, q_at, keys_of(upper, g), values_of(lower, g), None, sums)

        @pl.when(relevant & jnp.logical_not(clear))
        def _():
            allowed = allowed_at(first, base, tok, 2 * tok, lengths)
            add_block(tok, heads, q_at, keys_of(upper, g), values_of(lower, g), allowed, sums)


def stage_kernel(tok, heads, groups, first_part, meta, lengths, qs, total_in, acc_in, *refs):
    pair, (total, acc), held = refs[:4], refs[4:6], refs[6:]
    before = (total_in, acc_in)
    stage_body(tok, heads, groups, first_part, meta, lengths, qs, before, pair, total, acc, held)


def stage(state, pair, first_part, meta, lengths):
    qs, total, acc = state
    groups, rows, unused = qs.shape
    flat = [x for block in pair for x in block]
    tok = flat[0].shape[1] // 2
    new = pl.pallas_call(
        functools.partial(stage_kernel, tok, rows // (2 * tok), groups, first_part),
        out_shape=[jax.ShapeDtypeStruct(x.shape, x.dtype) for x in (total, acc)],
        in_specs=[SMEM, SMEM] + [VMEM] * 7,
        out_specs=[VMEM] * 2,
        scratch_shapes=[pltpu.VMEM((2, *x.shape), x.dtype) for x in pair[0]],
        input_output_aliases={3: 0, 4: 1},
        compiler_params=pltpu.CompilerParams(vmem_limit_bytes=ROOM),
        cost_estimate=BRIEF,
        name=f"stage{first_part}",
    )(meta, lengths, qs, total, acc, *flat)
    return qs, *new


def finish_kernel(tok, heads, groups, done, meta, lengths, qs, total, acc, *refs):
    near, out, held_k, held_v, peak, total_now, acc_now, result, sem = refs[-9:]
    parts = held_k.shape[0]
    rows = heads * tok
    core = meta[CORE]

    def fill(first):
        for i in range(first, parts):
            held_k[i], held_v[i] = refs[2 * i][...], refs[2 * i + 1][...]

    def turn_of(step):
        turn, g = lax.div(step, groups), lax.rem(step, groups)
        side = jnp.where(turn == 0, 1 - core, core)
        at = side * rows
        q_at = lambda off, count: qs[g, pl.ds(pl.multiple_of(at + off, HD), count)]
        return turn, g, side, q_at

    def write(turn, g):
        whole = jnp.sum(total_now[...], axis=1, keepdims=True)
        value = (acc_now[...] / whole).astype(result.dtype)
        for j in range(heads):
            result[turn, :, column_block((g * heads + j) * HD)] = value[j * tok : (j + 1) * tok]
        return sound(whole)

    def one_turn(step, fine):
        turn, g, side, q_at = turn_of(step)
        here = side_rows(side, heads, tok)
        total_now[...] = total[g, here]
        acc_now[...] = acc[g, here]

        @pl.loop(done, parts)
        def _(i):
            relevant, clear, first, base = relation(meta, i, side, tok, lengths)
            upper, lower = held_k.at[i], held_v.at[i]
            sums = (total_now, acc_now)

            @pl.when(relevant & clear)
            def _():
                add_block(tok, heads, q_at, keys_of(upper, g), values_of(lower, g), None, sums)

            @pl.when(relevant & jnp.logical_not(clear))
            def _():
                allowed = allowed_at(first, base, tok, 2 * tok, lengths)
                add_block(tok, heads, q_at, keys_of(upper, g), values_of(lower, g), allowed, sums)

        return fine & write(turn, g).astype(jnp.int32)

    fill(done)
    fine = lax.fori_loop(0, 2 * groups, one_turn, jnp.int32(1))

    @pl.when(fine == 0)
    def _():
        fill(0)

        @pl.loop(0, 2 * groups)
        def _(step):
            turn, g, side, q_at = turn_of(step)
            first = (meta[CHIP] * 2 + side) * tok
            peak[...] = jnp.full_like(peak, NEG)
            total_now[...] = jnp.zeros_like(total_now)
            acc_now[...] = jnp.zeros_like(acc_now)

            @pl.loop(0, parts * heads)
            def _(step):
                i, j = lax.div(step, heads), lax.rem(step, heads)
                keys, values = keys_of(held_k.at[i], g), values_of(held_v.at[i], g)
                allowed = allowed_at(first, meta[PARTS + i] * 2 * tok, tok, 2 * tok, lengths)
                mine = pl.ds(pl.multiple_of(j * tok, tok), tok)
                s = jnp.where(allowed, dot_nn(q_at(j * tok, tok), keys) * FACTOR, NEG)
                top = jnp.maximum(peak[mine], jnp.max(s, axis=1, keepdims=True))
                p = jnp.where(allowed, jnp.exp2(s - top[:, :1]), 0.0)
                shrink = jnp.exp2(peak[mine] - top)
                total_now[mine] = total_now[mine] * shrink + fold(p, jnp.add)
                acc_now[mine] = acc_now[mine] * shrink + dot_nn(p.astype(jnp.bfloat16), values)
                peak[mine] = top

            write(turn, g)

    width = near.shape[1]
    where = pl.ds(pl.multiple_of(core * width, width), width)
    copy = pltpu.make_async_copy(result.at[1], out.at[:, where], sem)
    copy.start()
    near[...] = result[0]
    copy.wait()


def finish(state, blocks, done, meta, lengths):
    qs, total, acc = state
    groups, rows, unused = qs.shape
    flat = [x for block in blocks for x in block]
    tok = flat[0].shape[1] // 2
    heads = rows // (2 * tok)
    width = groups * heads * HD
    sums = pltpu.VMEM((heads * tok, HD), jnp.float32)
    return pl.pallas_call(
        functools.partial(finish_kernel, tok, heads, groups, done),
        out_shape=[
            jax.ShapeDtypeStruct((tok, width), jnp.bfloat16),
            jax.ShapeDtypeStruct((tok, 2 * width), jnp.bfloat16),
        ],
        in_specs=[SMEM, SMEM] + [VMEM] * (3 + len(flat)),
        out_specs=[VMEM, HBM],
        scratch_shapes=[
            *[pltpu.VMEM((len(blocks), *x.shape), x.dtype) for x in blocks[0]],
            sums, sums, sums,
            pltpu.VMEM((2, tok, width), jnp.bfloat16),
            pltpu.SemaphoreType.DMA,
        ],
        compiler_params=pltpu.CompilerParams(vmem_limit_bytes=ROOM),
        cost_estimate=pl.CostEstimate(
            flops=groups * rows * tok * HD * 8, bytes_accessed=tok * width * 4,
            transcendentals=groups * rows * tok * 2,
        ),
        name="finish",
    )(meta, lengths, qs, total, acc, *flat)


def request_sums(query, keys, values, bias):
    s = dot_nn(query, keys) * FACTOR
    p = jnp.exp2((s.reshape(-1, *bias.shape) + bias[None]).reshape(s.shape))
    return fold(p, jnp.add), dot_nn(p.astype(jnp.bfloat16), values)


def fresh_scores(query, newk, own):
    s = dot_nt(query, newk) * FACTOR
    size = newk.shape[0]
    row = lax.broadcasted_iota(jnp.int32, (size, size), 0)
    col = lax.broadcasted_iota(jnp.int32, (size, size), 1)
    ok = (lax.rem(row, own) == lax.rem(col, own)) & (lax.div(col, own) <= lax.div(row, own))
    return s.reshape(-1, size, size), ok


def request_copies(own, meta, sources, held, sems):
    requests = pl.ds(lax.div(meta[CHIP], 2) * own, own)
    copies = []
    for i, (source, target) in enumerate(zip(sources, held)):
        width = target.shape[2]
        where = pl.ds(pl.multiple_of(meta[CORE] * width, width), width)
        copies.append(pltpu.make_async_copy(source.at[requests, :, where], target, sems.at[i]))
    return copies


def requests_body(own, heads, groups, length, meta, table, total, acc, query, newk, newv, mask, q3, k3, v3):
    steps = q3.shape[1]
    level = lax.div(meta[CHIP], 2)
    pick = lax.broadcasted_iota(jnp.int32, (own, table.shape[1]), 1) - level * own
    pick = (pick == lax.broadcasted_iota(jnp.int32, pick.shape, 0)).astype(jnp.float32)
    rows = dot_nt(pick.astype(jnp.bfloat16), table[...].astype(jnp.float32).astype(jnp.bfloat16))
    lane = lax.div(lax.broadcasted_iota(jnp.int32, (own, length), 1), BLK)
    for i in range(mask.shape[1] // length):
        number = (lane + meta[PARTS + i] * (length // BLK)).astype(jnp.float32)
        hit = rows[:, :1] == number
        for j in range(1, rows.shape[1]):
            hit = hit | (rows[:, j : j + 1] == number)
        mask[:, i * length : (i + 1) * length] = jnp.where(hit, 0.0, -jnp.inf)
    for s in range(steps):
        for g in range(groups):
            col = slice(g * HD, (g + 1) * HD)
            at = slice(s * own, (s + 1) * own)
            newk[at, col] = k3[:, s, col]
            newv[at, col] = v3[:, s, col]
            for j in range(heads):
                first = (g * heads + j) * HD
                row = (j * steps + s) * own
                query[g, row : row + own] = q3[:, s, first : first + HD]

    @pl.loop(0, groups)
    def _(g):
        col = column_block(g * HD)
        s, ok = fresh_scores(query[g], newk[:, col], own)
        p = jnp.where(ok[None], jnp.exp2(s), 0.0).reshape(-1, s.shape[2])
        first = jnp.sum(p, axis=1, keepdims=True)
        lead = lax.broadcasted_iota(jnp.int32, (p.shape[0], HD), 1) == 0
        total[g] = jnp.where(lead, first, 0.0)
        acc[g] = dot_nn(p.astype(jnp.bfloat16), newv[:, col])


def requests_kernel(own, heads, groups, length, meta, *refs):
    sources, table, state, (q3, k3, v3, sems) = refs[:3], refs[3], refs[4:10], refs[10:]
    copies = request_copies(own, meta, sources, (q3, k3, v3), sems)
    for copy in copies:
        copy.start()
    for copy in copies:
        copy.wait()
    requests_body(own, heads, groups, length, meta, table, *state, q3, k3, v3)


def open_requests(q_dec, k_new, v_new, table, length, own, meta):
    heads = H // KVH
    steps = q_dec.shape[1]
    width = k_new.shape[2] // 2
    groups = width // HD
    rows = heads * own * steps
    sums = jax.ShapeDtypeStruct((groups, rows, HD), jnp.float32)
    new = jax.ShapeDtypeStruct((own * steps, width), jnp.bfloat16)
    return pl.pallas_call(
        functools.partial(requests_kernel, own, heads, groups, length),
        out_shape=[
            sums, sums, jax.ShapeDtypeStruct((groups, rows, HD), jnp.bfloat16), new, new,
            jax.ShapeDtypeStruct((own, (LEVELS - PARTS) * length), jnp.float32),
        ],
        in_specs=[SMEM] + [HBM] * 3 + [VMEM],
        out_specs=[VMEM] * 6,
        scratch_shapes=[
            pltpu.VMEM((own, steps, groups * heads * HD), jnp.bfloat16),
            pltpu.VMEM((own, steps, width), jnp.bfloat16),
            pltpu.VMEM((own, steps, width), jnp.bfloat16),
            pltpu.SemaphoreType.DMA((3,)),
        ],
        compiler_params=pltpu.CompilerParams(vmem_limit_bytes=LITTLE),
        cost_estimate=BRIEF,
        name="requests",
    )(meta, q_dec, k_new, v_new, table)


def early_kernel(groups, total_in, acc_in, query, mask, *refs):
    total, acc = refs[-2:]
    length = refs[0].shape[1]

    @pl.loop(0, groups)
    def _(g):
        sums = [total_in[g], acc_in[g]]
        for i in range(len(refs) // 2 - 1):
            bias = mask[:, i * length : (i + 1) * length]
            keys, values = keys_of(refs[2 * i], g), values_of(refs[2 * i + 1], g)
            more = request_sums(query[g], keys, values, bias)
            sums = [x + y for x, y in zip(sums, more)]
        total[g], acc[g] = sums


def early_decode(state, blocks):
    total, acc, query, newk, newv, mask = state
    groups, rows, unused = query.shape
    flat = [x for block in blocks for x in block]
    sums = jax.ShapeDtypeStruct(total.shape, total.dtype)
    new = pl.pallas_call(
        functools.partial(early_kernel, groups),
        out_shape=[sums, sums],
        in_specs=[VMEM] * (4 + len(flat)),
        out_specs=[VMEM] * 2,
        input_output_aliases={0: 0, 1: 1},
        compiler_params=pltpu.CompilerParams(vmem_limit_bytes=2 * LITTLE),
        cost_estimate=BRIEF,
        name="early_decode",
    )(total, acc, query, mask, *flat)
    return [*new, query, newk, newv, mask]


def late_kernel(own, steps, heads, groups, done, meta, total, acc, query, newk, newv, mask, *refs):
    parts, out = len(refs) // 2, refs[-1]
    length = refs[0].shape[1]
    size = own * steps

    def write(g, sums, whole):
        result = (sums / whole).astype(out.dtype)
        for j in range(heads):
            out[:, column_block((g * heads + j) * HD)] = result[j * size : (j + 1) * size]

    def one_group(g, fine):
        sums = [total[g], acc[g]]
        for i in range(done, parts):
            bias = mask[:, i * length : (i + 1) * length]
            keys, values = keys_of(refs[2 * i], g), values_of(refs[2 * i + 1], g)
            more = request_sums(query[g], keys, values, bias)
            sums = [x + y for x, y in zip(sums, more)]
        whole = jnp.sum(sums[0], axis=1, keepdims=True)
        write(g, sums[1], whole)
        return fine & sound(whole).astype(jnp.int32)

    fine = lax.fori_loop(0, groups, one_group, jnp.int32(1))

    @pl.when(fine == 0)
    def _():
        @pl.loop(0, groups)
        def _(g):
            col = column_block(g * HD)
            fresh, ok = fresh_scores(query[g], newk[:, col], own)
            fresh = jnp.where(ok[None], fresh, NEG).reshape(-1, size)
            top = jnp.max(fresh, axis=1, keepdims=True)
            p = jnp.exp2(fresh - top)
            whole = jnp.sum(p, axis=1, keepdims=True)
            sums = dot_nn(p.astype(jnp.bfloat16), newv[:, col])
            for i in range(parts):
                s = dot_nn(query[g], keys_of(refs[2 * i], g)) * FACTOR
                open_to = mask[:, i * length : (i + 1) * length] >= 0
                s = jnp.where(open_to[None], s.reshape(-1, own, length), NEG).reshape(s.shape)
                higher = jnp.maximum(top, jnp.max(s, axis=1, keepdims=True))
                p = jnp.exp2(s - higher)
                shrink = jnp.exp2(top - higher)
                whole = whole * shrink + jnp.sum(p, axis=1, keepdims=True)
                sums = sums * shrink + dot_nn(p.astype(jnp.bfloat16), values_of(refs[2 * i + 1], g))
                top = higher
            write(g, sums, whole)


def late_decode(early, blocks, done, own, steps, meta):
    groups, rows, unused = early[0].shape
    heads = H // KVH
    flat = [x for block in blocks for x in block]
    parts, length = len(blocks), flat[0].shape[1]
    pairs = groups * rows * (parts - done) * length
    return pl.pallas_call(
        functools.partial(late_kernel, own, steps, heads, groups, done),
        out_shape=jax.ShapeDtypeStruct((own * steps, groups * heads * HD), jnp.bfloat16),
        in_specs=[SMEM] + [VMEM] * (len(early) + len(flat)),
        out_specs=VMEM,
        compiler_params=pltpu.CompilerParams(vmem_limit_bytes=ROOM),
        cost_estimate=pl.CostEstimate(
            flops=pairs * HD * 8, bytes_accessed=rows * HD, transcendentals=pairs
        ),
        name="late_decode",
    )(meta, *early, *flat)


def decode_kernel(parts, steps, heads, groups, starts, q, mask, newk, newv, *refs):
    kheld, vheld = refs[:parts], refs[parts : 2 * parts]
    out, kall, vall, sems, scores = refs[2 * parts :]
    own = q.shape[0]
    rows = heads * own
    length = kheld[0].shape[1]
    copies = []
    for i in range(parts):
        where = pl.ds(pl.multiple_of(starts[i], HD), length)
        copies.append(pltpu.make_async_copy(kheld[i], kall.at[:, where], sems.at[2 * i]))
        copies.append(pltpu.make_async_copy(vheld[i], vall.at[where], sems.at[2 * i + 1]))
    for copy in copies:
        copy.start()
    row = lax.broadcasted_iota(jnp.int32, (own, own), 0)
    col = lax.broadcasted_iota(jnp.int32, (own, own), 1)
    fresh_ok = (lax.div(row, steps) == lax.div(col, steps)) & (col <= row)

    def columns(g):
        return slice(g * HD, (g + 1) * HD)

    def stacked(g):
        first = g * heads
        slices = [q[:, (first + j) * HD : (first + j + 1) * HD] for j in range(heads)]
        return jnp.concatenate([x.astype(jnp.float32) for x in slices], 0).astype(jnp.bfloat16)

    def keep(allowed, x, other):
        y = x.reshape(heads, own, x.shape[1])
        return jnp.where(allowed[None], y, other).reshape(x.shape)

    def open_to(i):
        return mask[:, pl.ds(pl.multiple_of(starts[i], HD), length)] > 0

    def write(g, acc, whole):
        result = acc / whole
        for j in range(heads):
            out[:, (g * heads + j) * HD : (g * heads + j + 1) * HD] = result[
                j * own : (j + 1) * own
            ].astype(out.dtype)

    fine = None
    for g in range(groups):
        query = stacked(g)
        p = keep(fresh_ok, jnp.exp2(dot_nt(query, newk[:, columns(g)]) * FACTOR), 0.0)
        whole = jnp.sum(p, axis=1, keepdims=True)
        acc = dot_nn(p.astype(jnp.bfloat16), newv[:, columns(g)])
        total = jnp.zeros((rows, HD), jnp.float32)
        for i in range(parts):
            p = jnp.exp2(dot_nn(query, kheld[i][columns(g)]) * FACTOR)
            p = keep(open_to(i), p, 0.0)
            total = total + fold(p, jnp.add)
            acc = acc + dot_nn(p.astype(jnp.bfloat16), vheld[i][:, columns(g)])
        whole = whole + jnp.sum(total, axis=1, keepdims=True)
        write(g, acc, whole)
        fine = sound(whole) if fine is None else fine & sound(whole)

    @pl.when(jnp.logical_not(fine))
    def _():
        for g in range(groups):
            query = stacked(g)
            fresh = keep(fresh_ok, dot_nt(query, newk[:, columns(g)]) * FACTOR, NEG)
            top = jnp.max(fresh, axis=1, keepdims=True)
            for i in range(parts):
                s = keep(open_to(i), dot_nn(query, kheld[i][columns(g)]) * FACTOR, NEG)
                scores[:, i * length : (i + 1) * length] = s
                top = jnp.maximum(top, jnp.max(s, axis=1, keepdims=True))
            p = jnp.exp2(fresh - top)
            whole = jnp.sum(p, axis=1, keepdims=True)
            acc = dot_nn(p.astype(jnp.bfloat16), newv[:, columns(g)])
            for i in range(parts):
                p = jnp.exp2(scores[:, i * length : (i + 1) * length] - top)
                whole = whole + jnp.sum(p, axis=1, keepdims=True)
                acc = acc + dot_nn(p.astype(jnp.bfloat16), vheld[i][:, columns(g)])
            write(g, acc, whole)

    for copy in copies:
        copy.wait()


def decode(q, mask, newk, newv, kparts, vparts, starts, steps):
    own = q.shape[0]
    parts = len(kparts)
    length, width = vparts[0].shape
    count = parts * length
    heads = H // KVH
    groups = width // HD
    rows = heads * own
    pairs = groups * rows * count
    return pl.pallas_call(
        functools.partial(decode_kernel, parts, steps, heads, groups),
        out_shape=[
            jax.ShapeDtypeStruct(q.shape, jnp.bfloat16),
            jax.ShapeDtypeStruct((width, count), jnp.bfloat16),
            jax.ShapeDtypeStruct((count, width), jnp.bfloat16),
        ],
        grid_spec=pltpu.PrefetchScalarGridSpec(
            num_scalar_prefetch=1,
            grid=(),
            in_specs=[VMEM] * (4 + 2 * parts),
            out_specs=[VMEM, HBM, HBM],
            scratch_shapes=[
                pltpu.SemaphoreType.DMA((2 * parts,)),
                pltpu.VMEM((rows, count), jnp.float32),
            ],
        ),
        compiler_params=pltpu.CompilerParams(vmem_limit_bytes=ROOM),
        cost_estimate=pl.CostEstimate(
            flops=pairs * HD * 4, bytes_accessed=count * width * 4, transcendentals=pairs
        ),
        name="decode",
    )(starts, q, mask, newk, newv, *kparts, *vparts)


def prepare_kernel(meta, k, v, send, keys, values):
    width = k.shape[1] // 2
    mine = pl.ds(pl.multiple_of(meta[0] * width, width), width)
    other = pl.ds(pl.multiple_of((1 - meta[0]) * width, width), width)
    send[:width] = k[:, other].astype(jnp.float32).T.astype(send.dtype)
    send[width:] = v[:, other]
    keys[:, mine] = k[:, mine].astype(jnp.float32).T.astype(keys.dtype)
    values[:, mine] = v[:, mine]


def prepare(k, v, core):
    tok, width = k.shape[0], k.shape[1] // 2
    assert tok == width
    block = jax.ShapeDtypeStruct((width, 2 * tok), k.dtype)
    return pl.pallas_call(
        prepare_kernel,
        out_shape=[jax.ShapeDtypeStruct((2 * tok, width), k.dtype), block, block],
        in_specs=[SMEM, VMEM, VMEM],
        out_specs=[VMEM] * 3,
        compiler_params=pltpu.CompilerParams(vmem_limit_bytes=LITTLE),
        name="prepare",
    )(core[None], k, v)


def join_kernel(meta, keys_in, values_in, theirs, q, keys, values, send_q, sem):
    columns = send_q.shape[1]
    where = pl.ds(pl.multiple_of((1 - meta[0]) * columns, columns), columns)
    copy = pltpu.make_async_copy(q.at[:, where], send_q, sem)
    copy.start()
    width = theirs.shape[1]
    other = pl.ds(pl.multiple_of((1 - meta[0]) * width, width), width)
    keys[...], values[...] = keys_in[...], values_in[...]
    keys[:, other] = theirs[:width]
    values[:, other] = theirs[width:]
    copy.wait()


def join(keys, values, theirs, q, core):
    return pl.pallas_call(
        join_kernel,
        out_shape=[
            jax.ShapeDtypeStruct(keys.shape, keys.dtype),
            jax.ShapeDtypeStruct(values.shape, values.dtype),
            jax.ShapeDtypeStruct((q.shape[0], q.shape[1] // 2), q.dtype),
        ],
        in_specs=[SMEM, VMEM, VMEM, VMEM, HBM],
        out_specs=[VMEM] * 3,
        scratch_shapes=[pltpu.SemaphoreType.DMA],
        compiler_params=pltpu.CompilerParams(vmem_limit_bytes=LITTLE),
        name="join",
    )(core[None], keys, values, theirs, q)


def take_kernel(meta, whole, out, sem):
    width = out.shape[1]
    where = pl.ds(pl.multiple_of((1 - meta[CORE]) * width, width), width)
    copy = pltpu.make_async_copy(whole.at[:, where], out, sem)
    copy.start()
    copy.wait()


def take_other_half(whole, meta):
    return pl.pallas_call(
        take_kernel,
        out_shape=jax.ShapeDtypeStruct((whole.shape[0], whole.shape[1] // 2), whole.dtype),
        in_specs=[SMEM, HBM],
        out_specs=VMEM,
        scratch_shapes=[pltpu.SemaphoreType.DMA],
        compiler_params=pltpu.CompilerParams(vmem_limit_bytes=LITTLE),
        name="take",
    )(meta, whole)


def project_kernel(meta, *refs):
    pieces, (whole, other), outs, (sorted_rows,) = refs[:-7], refs[-7:-5], refs[-5:-1], refs[-1:]
    parts = len(pieces)
    rows = pieces[0].shape[0]
    for i, piece in enumerate(pieces):
        at = pl.ds(pl.multiple_of(meta[LEVELS + i] * rows, rows), rows)
        sorted_rows[at] = piece[...]
    depth = other.shape[1]
    mine = whole[:, pl.ds(pl.multiple_of(meta[CORE] * depth, depth), depth)]
    half = parts * rows // 2
    here = pl.ds(pl.multiple_of(meta[ACROSS] * half, half), half)
    there = pl.ds(pl.multiple_of((1 - meta[ACROSS]) * half, half), half)
    kept, beside, across, corner = outs
    for at, near, far in ((here, kept, beside), (there, across, corner)):
        some = sorted_rows[at]
        near[...] = dot_nt(mine, some).astype(near.dtype)
        far[...] = dot_nt(other[...], some).astype(far.dtype)


def project(pieces, whole, other, meta):
    rows = len(pieces) * pieces[0].shape[0]
    width, depth = other.shape
    block = jax.ShapeDtypeStruct((width, rows // 2), jnp.bfloat16)
    return pl.pallas_call(
        project_kernel,
        out_shape=[jax.ShapeDtypeStruct(block.shape, jnp.float32)] + [block] * 3,
        in_specs=[SMEM] + [VMEM] * (len(pieces) + 2),
        out_specs=[VMEM] * 4,
        scratch_shapes=[pltpu.VMEM((rows, depth), jnp.bfloat16)],
        compiler_params=pltpu.CompilerParams(vmem_limit_bytes=2 * LITTLE),
        cost_estimate=pl.CostEstimate(
            flops=rows * width * depth * 4, bytes_accessed=width * depth * 4, transcendentals=0
        ),
        name="project",
    )(meta, *pieces, whole, other)


def index(z, y, c):
    return (z * 2 + y) * 2 + c


def on_ring(r, chips):
    return (r, 0) if r < chips // 2 else (chips - 1 - r, 1)


def ring_perm(chips, d):
    return [
        (index(*on_ring(r, chips), c), index(*on_ring((r + d) % chips, chips), c))
        for r in range(chips)
        for c in range(2)
    ]


def ring_place(r, chips):
    r = lax.rem(r + 2 * chips, chips)
    return jnp.where(r < chips // 2, r * 2, (chips - 1 - r) * 2 + 1)


def spread(x, n):
    place = lax.axis_index("seq")
    deep = n // 4
    everyone = [(z, y, c) for z in range(deep) for y in range(2) for c in range(2)]
    z, y, c = place // 4, (place // 2) % 2, place % 2
    held = [(x, z, y, c)]
    for d in range(1, deep):
        perm = [(index(*p), index((p[0] - d) % deep, p[1], p[2])) for p in everyone]
        held.append((lax.ppermute(x, "seq", perm), lax.rem(z + d, deep), y, c))
    perm = [(index(*p), index(p[0], 1 - p[1], p[2])) for p in everyone]
    held += [(lax.ppermute(b, "seq", perm), bz, 1 - by, bc) for b, bz, by, bc in held]
    perm = [(index(*p), index(p[0], p[1], 1 - p[2])) for p in everyone]
    held += [(lax.ppermute(b, "seq", perm), bz, by, 1 - bc) for b, bz, by, bc in held]
    return [b for b, *_ in held], jnp.stack([index(bz, by, bc) for _, bz, by, bc in held])


def open_blocks(table, steps, count):
    number = lax.broadcasted_iota(jnp.int32, (*table.shape, count), 2) // BLK
    mask = jnp.any(table[:, :, None] == number, axis=1).astype(jnp.float32)
    return jnp.repeat(mask, steps, axis=0)


def whole_heads(n, q_pre, k_cache, v_cache, lengths, q_dec, k_new, v_new, block_table, w_out):
    tok = q_pre.shape[0]
    place = lax.axis_index("seq").astype(jnp.int32)
    rows, steps = q_dec.shape[0], q_dec.shape[1]
    own = rows // n
    kparts, sources = spread(k_cache.T, n)
    vparts, _ = spread(v_cache, n)
    starts = sources.astype(jnp.int32) * tok

    def mine(x):
        y = lax.dynamic_slice_in_dim(x, place * own, own, 0)
        return y.reshape(own * steps, -1) if x.ndim == 3 else y

    mask = open_blocks(mine(block_table), steps, n * tok)
    attn_own, keys, values = decode(
        mine(q_dec), mask, mine(k_new), mine(v_new), kparts, vparts, starts, steps
    )
    attn = lax.all_gather(attn_own, "seq", axis=0, tiled=True)
    flat = jnp.dot(attn, w_out, preferred_element_type=jnp.float32).astype(jnp.bfloat16)
    dec_out = lax.psum_scatter(
        flat.reshape(rows, steps, -1), "tp", scatter_dimension=0, tiled=True
    )
    zero = jnp.zeros((), jnp.int32)
    meta = jnp.stack([place * tok, zero, zero, zero])
    groups = k_cache.shape[1] // HD
    pre_out = prefill(
        q_pre, keys, values, meta, lengths, groups, q_pre.shape[1], "prefill"
    )
    return (pre_out, dec_out)


def split_heads(n, q_pre, k_cache, v_cache, lengths, q_dec, k_new, v_new, block_table, w_out):
    tok = q_pre.shape[0]
    place = lax.axis_index("seq").astype(jnp.int32)
    across = lax.axis_index("tp").astype(jnp.int32)
    core, chip = lax.rem(place, 2), lax.div(place, 2)
    chips = n // 2
    far, deep = chips // 2, chips // 2
    z, y = lax.div(chip, 2), lax.rem(chip, 2)
    r = jnp.where(y == 0, z, chips - 1 - z)
    rows, steps = q_dec.shape[0], q_dec.shape[1]
    own = rows // deep
    sibling = [(i, i ^ 1) for i in range(n)]
    everyone = [(a, b, c) for a in range(deep) for b in range(2) for c in range(2)]

    order = [0] + [o for d in range(1, far) for o in (-d, d)] + [far]
    numbers = [ring_place(r + o, chips) for o in order]
    levels = [z] + [lax.rem(z + deep - d, deep) for d in range(1, deep)]
    assert len(numbers) == LEVELS - PARTS
    meta = jnp.stack([core, chip, across] + numbers + levels).astype(jnp.int32)

    send, keys, values = prepare(k_cache, v_cache, core)
    theirs = lax.ppermute(send, "seq", sibling)
    theirs, meta = lax.optimization_barrier((theirs, meta))
    held_k, held_v = {}, {}
    held_k[0], held_v[0], send_q = join(keys, values, theirs, q_pre, core)
    near_q = lax.ppermute(send_q, "seq", sibling)

    up, down = ring_perm(chips, 1), ring_perm(chips, -1)
    early, w_near = (), w_out
    for d in range(1, far + 1):
        held_k[-d] = lax.ppermute(held_k[1 - d], "seq", up)
        held_v[d] = lax.ppermute(held_v[d - 1], "seq", down)
        if d < far:
            held_k[d] = lax.ppermute(held_k[d - 1], "seq", down)
            held_v[-d] = lax.ppermute(held_v[1 - d], "seq", up)
            sides = (-d, d)
        else:
            held_k[d] = held_k[-d]
            sides = (d,)
        if d == 1:
            state = open_sums(q_pre, near_q, (held_k[0], held_v[0]), meta, lengths)
        elif d < far:
            pair = [(held_k[o], held_v[o]) for o in (1 - d, d - 1)]
            state = stage(state, pair, 2 * d - 3, meta, lengths)
        else:
            blocks = [(held_k[o], held_v[o]) for o in order[:-1]]
            early = early_decode(early, blocks)
        for x in (held_k, held_v):
            moved, state, early = lax.optimization_barrier(([x[o] for o in sides], state, early))
            x.update(zip(sides, moved))
            if d == 1 and x is held_k:
                state, block_table = lax.optimization_barrier((state, block_table))
                early = open_requests(
                    q_dec, k_new, v_new, block_table.T, 2 * tok, own, meta
                )
        if d == 3:
            w_near, state = lax.optimization_barrier((w_near, state))
            weights = w_near.T
            w_near = lax.ppermute(take_other_half(weights, meta), "seq", sibling)
    w_near, early = lax.optimization_barrier((w_near, early))
    blocks = [(held_k[o], held_v[o]) for o in order]
    attn_own = late_decode(early, blocks, len(blocks) - 1, own, steps, meta)

    pieces = [attn_own]
    for d in range(1, deep):
        perm = [(index(*p), index((p[0] + d) % deep, p[1], p[2])) for p in everyone]
        pieces.append(lax.ppermute(attn_own, "seq", perm))
    attn_own, state = lax.optimization_barrier((attn_own, state))
    near, pre_out = finish(state, blocks, 2 * far - 3, meta, lengths)
    pieces, near, pre_out = lax.optimization_barrier((pieces, near, pre_out))
    back = lax.ppermute(near, "seq", sibling)
    pre_out = settle(pre_out, back, meta)

    total, *sent = project(pieces, weights, w_near, meta)
    got = []
    for piece, (dc, dx) in zip(sent, ((1, 0), (0, 1), (1, 1))):
        perm = [
            (i * 2 + x, (i ^ dc) * 2 + (x ^ dx)) for i in range(n) for x in range(2)
        ]
        got.append(lax.ppermute(piece, ("seq", "tp"), perm))
    got[0], pre_out = lax.optimization_barrier((got[0], pre_out))
    for piece in got:
        total = total + piece.astype(jnp.float32)
    dec_out = total.astype(jnp.bfloat16).T.reshape(deep // 2, steps, own, -1)
    return (pre_out, dec_out.transpose(0, 2, 1, 3).reshape(rows // 2, steps, -1))


def per_device(n, tp, q_pre, k_cache, v_cache, prompt_lengths, *rest):
    groups = k_cache.shape[1] // HD
    square = groups % 2 == 0 and k_cache.shape[1] == 2 * k_cache.shape[0]
    small = n * k_cache.shape[0] // BLK <= 256 and n == 2 * (LEVELS - PARTS)
    form = split_heads if square and tp == 2 and small else whole_heads
    return form(n, q_pre, k_cache, v_cache, prompt_lengths.astype(jnp.int32), *rest)


def solution(mesh):
    placed = (
        P("seq", "tp"),
        P("seq", "tp"),
        P("seq", "tp"),
        P(),
        P(None, None, "tp"),
        P(None, None, "tp"),
        P(None, None, "tp"),
        P(),
        P("tp", "seq"),
    )
    return jax.shard_map(
        functools.partial(per_device, mesh.shape["seq"], mesh.shape["tp"]),
        mesh=mesh,
        in_specs=placed,
        out_specs=(P("seq", "tp"), P("tp", None, "seq")),
        check_vma=False,
    )
```

```python
import functools
import math

import jax
import jax.numpy as jnp
from jax import lax
from jax.experimental import pallas as pl
from jax.experimental.pallas import tpu as pltpu
from jax.sharding import PartitionSpec as P

H = 56
KVH = 8
HD = 128
BLK = 64
SPAN = 512
PAIR = 2
NEG = -1e30
LEAST, MOST = 2.0**-60, 2.0**100
FACTOR = math.log2(math.e) / math.sqrt(HD)
ROOM = 16 * 1024 * 1024
LITTLE = 4 * 1024 * 1024
CORE, CHIP, ACROSS, PARTS, LEVELS = 0, 1, 2, 3, 11
BRIEF = pl.CostEstimate(flops=1024, bytes_accessed=1024, transcendentals=0)
HBM = pl.BlockSpec(memory_space=pltpu.HBM)
VMEM = pl.BlockSpec(memory_space=pltpu.VMEM)
SMEM = pl.BlockSpec(memory_space=pltpu.SMEM)


def dot_nt(a, b):
    return lax.dot_general(a, b, (((1,), (1,)), ((), ())), preferred_element_type=jnp.float32)


def dot_nn(a, b):
    return lax.dot_general(a, b, (((1,), (0,)), ((), ())), preferred_element_type=jnp.float32)


def fold(x, op):
    out = x[:, :HD]
    for i in range(1, x.shape[1] // HD):
        out = op(out, x[:, i * HD : (i + 1) * HD])
    return out


def start_of(position, lengths):
    end = jnp.int32(0)
    out = jnp.zeros_like(position)
    for i in range(lengths.shape[0]):
        end = end + lengths[i]
        out = jnp.where(position >= end, end, out)
    return out


def sound(total):
    return (jnp.min(total) >= LEAST) & (jnp.max(total) <= MOST)


def prefill_kernel(tok, heads, meta, lengths, q, keys_all, values_all, *refs):
    out, qs, peak, total, acc = refs[-5:]
    for j in range(heads):
        qs[j * tok : (j + 1) * tok] = q[:, j * HD : (j + 1) * HD]
    total[...] = jnp.zeros_like(total)
    acc[...] = jnp.zeros_like(acc)

    begin = meta[0]
    finish = begin + tok
    low = start_of(begin, lengths)
    high = start_of(finish - 1, lengths)
    blocks = lax.div(finish - low + SPAN - 1, SPAN)
    clear = lax.div(finish - high, SPAN)

    def first_of(k):
        return jnp.maximum(finish - (k + 1) * SPAN, 0)

    def load(k):
        here = pl.ds(pl.multiple_of(first_of(k), HD), SPAN)
        return keys_all[:, here], values_all[here, :]

    def allowed_in(k):
        t = begin + lax.broadcasted_iota(jnp.int32, (tok, 1), 0)
        u = first_of(k) + lax.broadcasted_iota(jnp.int32, (tok, SPAN), 1)
        last = jnp.minimum(t, finish - k * SPAN - 1)
        return (u <= last) & (u >= start_of(t, lengths))

    def keep(allowed, x, other):
        some = x.shape[0] // tok
        return jnp.where(allowed[None], x.reshape(some, tok, SPAN), other).reshape(x.shape)

    def block(k, masked):
        keys, values = load(k)
        allowed = allowed_in(k) if masked else None
        for j in range(0, heads, PAIR):
            here = slice(j * tok, min(j + PAIR, heads) * tok)
            p = jnp.exp2(dot_nn(qs[here], keys) * FACTOR)
            if masked:
                p = keep(allowed, p, 0.0)
            total[here] += fold(p, jnp.add)
            acc[here] += dot_nn(p.astype(jnp.bfloat16), values)

    block(0, True)

    @pl.loop(1, jnp.maximum(clear, 1))
    def _(k):
        block(k, False)

    @pl.loop(jnp.maximum(clear, 1), blocks)
    def _(k):
        block(k, True)

    def write():
        whole = jnp.sum(total[...], axis=1, keepdims=True)
        result = (acc[...] / whole).astype(out.dtype)
        for j in range(heads):
            out[:, j * HD : (j + 1) * HD] = result[j * tok : (j + 1) * tok]
        return whole

    fine = sound(write())

    @pl.when(jnp.logical_not(fine))
    def _():
        peak[...] = jnp.full_like(peak, NEG)
        total[...] = jnp.zeros_like(total)
        acc[...] = jnp.zeros_like(acc)

        @pl.loop(0, blocks)
        def _(k):
            keys, values = load(k)
            allowed = allowed_in(k)

            @pl.loop(0, heads)
            def _(j):
                here = pl.ds(pl.multiple_of(j * tok, tok), tok)
                s = jnp.where(allowed, dot_nn(qs[here], keys) * FACTOR, NEG)
                top = jnp.maximum(peak[here], jnp.max(s, axis=1, keepdims=True))
                p = jnp.where(allowed, jnp.exp2(s - top[:, :1]), 0.0)
                shrink = jnp.exp2(peak[here] - top)
                total[here] = total[here] * shrink + fold(p, jnp.add)
                acc[here] = acc[here] * shrink + dot_nn(p.astype(jnp.bfloat16), values)
                peak[here] = top

        write()


def prefill(q, keys, values, meta, lengths, groups, columns, name, before=None):
    tok = q.shape[0]
    count = values.shape[0]
    heads = H // KVH
    rows = heads * tok
    pairs = rows * count // 2 * groups
    extra = [] if before is None else [before]
    return pl.pallas_call(
        functools.partial(prefill_kernel, tok, heads),
        out_shape=jax.ShapeDtypeStruct((tok, columns), jnp.bfloat16),
        grid_spec=pltpu.PrefetchScalarGridSpec(
            num_scalar_prefetch=2,
            grid=(groups,),
            in_specs=[
                pl.BlockSpec((tok, heads * HD), lambda g, meta, lengths: (0, meta[1] + g)),
                pl.BlockSpec((HD, count), lambda g, meta, lengths: (meta[2] + g, 0)),
                pl.BlockSpec((count, HD), lambda g, meta, lengths: (0, meta[2] + g)),
            ]
            + [HBM] * len(extra),
            out_specs=pl.BlockSpec((tok, heads * HD), lambda g, meta, lengths: (0, meta[3] + g)),
            scratch_shapes=[
                pltpu.VMEM((rows, HD), jnp.bfloat16),
                pltpu.VMEM((rows, HD), jnp.float32),
                pltpu.VMEM((rows, HD), jnp.float32),
                pltpu.VMEM((rows, HD), jnp.float32),
            ],
        ),
        compiler_params=pltpu.CompilerParams(vmem_limit_bytes=ROOM),
        cost_estimate=pl.CostEstimate(
            flops=pairs * HD * 8, bytes_accessed=count * HD * 4 * groups, transcendentals=pairs
        ),
        input_output_aliases={} if before is None else {5: 0},
        name=name,
    )(meta, lengths, q, keys, values, *extra)


def settle_kernel(meta, piece, whole, out, sem):
    width = piece.shape[1]
    where = pl.ds(pl.multiple_of((1 - meta[CORE]) * width, width), width)
    copy = pltpu.make_async_copy(piece, out.at[:, where], sem)
    copy.start()
    copy.wait()


def settle(whole, piece, meta):
    return pl.pallas_call(
        settle_kernel,
        out_shape=jax.ShapeDtypeStruct(whole.shape, whole.dtype),
        in_specs=[SMEM, VMEM, HBM],
        out_specs=HBM,
        scratch_shapes=[pltpu.SemaphoreType.DMA],
        input_output_aliases={2: 0},
        compiler_params=pltpu.CompilerParams(vmem_limit_bytes=LITTLE),
        cost_estimate=pl.CostEstimate(flops=0, bytes_accessed=piece.size * 4, transcendentals=0),
        name="settle",
    )(meta, piece, whole)


def allowed_at(first, base, tok, length, lengths):
    t = first + lax.broadcasted_iota(jnp.int32, (tok, 1), 0)
    u = base + lax.broadcasted_iota(jnp.int32, (tok, length), 1)
    return (u <= t) & (u >= start_of(t, lengths))


def column_block(at):
    return pl.ds(pl.multiple_of(at, HD), HD)


def keys_of(upper, g):
    return upper[column_block(g * HD), :]


def values_of(lower, g):
    half = lower.shape[1] // 2
    both = [lower[:, column_block(side * half + g * HD)] for side in range(2)]
    return jnp.concatenate(both, axis=0)


def block_bias(first, base, tok, length, lengths):
    start = start_of(first, lengths)
    t = first + lax.broadcasted_iota(jnp.int32, (tok, HD), 0)
    u = base + lax.broadcasted_iota(jnp.int32, (1, length), 1)
    row = jnp.where(start_of(t, lengths) == start, 0.0, -jnp.inf)
    return [jnp.concatenate([row] * (length // HD), axis=1), jnp.where(u >= start, 0.0, -jnp.inf)]


def add_block(tok, heads, q_at, keys, values, biases, sums, old):
    length = keys.shape[1]
    for j in range(0, heads, PAIR):
        some = min(PAIR, heads - j)
        s = dot_nn(q_at(j * tok, some * tok), keys) * FACTOR
        for bias in biases:
            s = (s.reshape(some, tok, length) + bias[None]).reshape(some * tok, length)
        p = jnp.exp2(s)
        more = (fold(p, jnp.add), dot_nn(p.astype(jnp.bfloat16), values))
        here = slice(j * tok, (j + some) * tok)
        for i in range(2):
            sums[i][here] = more[i] if old is None else old[i][here] + more[i]


def relation(meta, part, side, tok, lengths):
    first = (meta[CHIP] * 2 + side) * tok
    base = meta[PARTS + part] * 2 * tok
    relevant = (base < first) & (meta[PARTS + part] != meta[CHIP])
    relevant = relevant & (base + 2 * tok > start_of(first, lengths))
    return relevant, base >= start_of(first + tok - 1, lengths), first, base


def side_rows(side, heads, tok):
    return pl.ds(pl.multiple_of(side * (heads * tok), HD), heads * tok)


def open_kernel(tok, heads, groups, meta, lengths, q, q_near, upper, lower, qs, total, acc):
    core = meta[CORE]
    rows = heads * tok
    for source, side, skip in ((q, core, core * groups * heads), (q_near, 1 - core, 0)):
        for g in range(groups):
            for j in range(heads):
                at = pl.ds(pl.multiple_of(side * rows + j * tok, HD), tok)
                qs[g, at] = source[:, column_block((skip + g * heads + j) * HD)]

    @pl.loop(0, groups)
    def _(g):
        keys, values = keys_of(upper, g), values_of(lower, g)
        for side in range(2):
            length = (side + 1) * tok
            first = (meta[CHIP] * 2 + side) * tok
            allowed = allowed_at(first, meta[CHIP] * 2 * tok, tok, length, lengths)
            here = side_rows(side, heads, tok)
            q_at = lambda at, count: qs[g, pl.ds(side * rows + at, count)]
            bias = jnp.where(allowed, 0.0, -jnp.inf)
            add_block(tok, heads, q_at, keys[:, :length], values[:length], [bias],
                      (total.at[g, here], acc.at[g, here]), None)


def open_sums(q, q_near, block, meta, lengths):
    tok = q.shape[0]
    heads = H // KVH
    groups = q_near.shape[1] // (heads * HD)
    rows = 2 * heads * tok
    sums = jax.ShapeDtypeStruct((groups, rows, HD), jnp.float32)
    pairs = groups * rows * tok * 2
    return pl.pallas_call(
        functools.partial(open_kernel, tok, heads, groups),
        out_shape=[jax.ShapeDtypeStruct((groups, rows, HD), jnp.bfloat16), sums, sums],
        in_specs=[SMEM, SMEM, VMEM, VMEM, VMEM, VMEM],
        out_specs=[VMEM] * 3,
        compiler_params=pltpu.CompilerParams(vmem_limit_bytes=2 * LITTLE),
        cost_estimate=BRIEF,
        name="open",
    )(meta, lengths, q, q_near, *block)


def stage_body(tok, heads, groups, first_part, meta, lengths, qs, before, pair, total, acc):
    for which in range(2):
        upper, lower = pair[2 * which], pair[2 * which + 1]

        @pl.loop(0, 2 * groups)
        def _(step):
            g, side = lax.div(step, 2), lax.rem(step, 2)
            relevant, clear, first, base = relation(meta, first_part + which, side, tok, lengths)
            here = side_rows(side, heads, tok)
            sums = (total.at[g, here], acc.at[g, here])
            old = sums if which else [ref.at[g, here] for ref in before]
            at = side * (heads * tok)
            q_at = lambda off, count: qs[g, pl.ds(pl.multiple_of(at + off, HD), count)]

            @pl.when(relevant & clear)
            def _():
                add_block(tok, heads, q_at, keys_of(upper, g), values_of(lower, g), [], sums, old)

            @pl.when(relevant & jnp.logical_not(clear))
            def _():
                biases = block_bias(first, base, tok, 2 * tok, lengths)
                add_block(
                    tok, heads, q_at, keys_of(upper, g), values_of(lower, g), biases, sums, old
                )

            if which == 0:

                @pl.when(jnp.logical_not(relevant))
                def _():
                    for i in range(2):
                        sums[i][...] = old[i][...]


def stage_kernel(tok, heads, groups, first_part, meta, lengths, qs, total_in, acc_in, *refs):
    pair, (total, acc) = refs[:4], refs[4:]
    before = (total_in, acc_in)
    stage_body(tok, heads, groups, first_part, meta, lengths, qs, before, pair, total, acc)


def stage(state, pair, first_part, meta, lengths):
    qs, total, acc = state
    groups, rows, unused = qs.shape
    flat = [x for block in pair for x in block]
    tok = flat[0].shape[1] // 2
    new = pl.pallas_call(
        functools.partial(stage_kernel, tok, rows // (2 * tok), groups, first_part),
        out_shape=[jax.ShapeDtypeStruct(x.shape, x.dtype) for x in (total, acc)],
        in_specs=[SMEM, SMEM] + [VMEM] * 7,
        out_specs=[VMEM] * 2,
        input_output_aliases={3: 0, 4: 1},
        compiler_params=pltpu.CompilerParams(vmem_limit_bytes=ROOM),
        cost_estimate=BRIEF,
        name=f"stage{first_part}",
    )(meta, lengths, qs, total, acc, *flat)
    return qs, *new


def finish_kernel(tok, heads, groups, done, meta, lengths, qs, total, acc, *refs):
    near, out, held_k, held_v, peak, total_now, acc_now, result, sem = refs[-9:]
    parts = held_k.shape[0]
    rows = heads * tok
    core = meta[CORE]

    def fill(first):
        for i in range(first, parts):
            held_k[i], held_v[i] = refs[2 * i][...], refs[2 * i + 1][...]

    def turn_of(step):
        turn, g = lax.div(step, groups), lax.rem(step, groups)
        side = jnp.where(turn == 0, 1 - core, core)
        at = side * rows
        q_at = lambda off, count: qs[g, pl.ds(pl.multiple_of(at + off, HD), count)]
        return turn, g, side, q_at

    def write(turn, g):
        whole = jnp.sum(total_now[...], axis=1, keepdims=True)
        value = (acc_now[...] / whole).astype(result.dtype)
        for j in range(heads):
            result[turn, :, column_block((g * heads + j) * HD)] = value[j * tok : (j + 1) * tok]
        return sound(whole)

    def one_turn(step, fine):
        turn, g, side, q_at = turn_of(step)
        here = side_rows(side, heads, tok)
        total_now[...] = total[g, here]
        acc_now[...] = acc[g, here]

        @pl.loop(done, parts)
        def _(i):
            relevant, clear, first, base = relation(meta, i, side, tok, lengths)
            upper, lower = held_k.at[i], held_v.at[i]
            sums = (total_now, acc_now)

            @pl.when(relevant & clear)
            def _():
                add_block(tok, heads, q_at, keys_of(upper, g), values_of(lower, g), [], sums, sums)

            @pl.when(relevant & jnp.logical_not(clear))
            def _():
                biases = block_bias(first, base, tok, 2 * tok, lengths)
                add_block(
                    tok, heads, q_at, keys_of(upper, g), values_of(lower, g), biases, sums, sums
                )

        return fine & write(turn, g).astype(jnp.int32)

    fill(done)
    fine = lax.fori_loop(0, 2 * groups, one_turn, jnp.int32(1))

    @pl.when(fine == 0)
    def _():
        fill(0)

        @pl.loop(0, 2 * groups)
        def _(step):
            turn, g, side, q_at = turn_of(step)
            first = (meta[CHIP] * 2 + side) * tok
            peak[...] = jnp.full_like(peak, NEG)
            total_now[...] = jnp.zeros_like(total_now)
            acc_now[...] = jnp.zeros_like(acc_now)

            @pl.loop(0, parts * heads)
            def _(step):
                i, j = lax.div(step, heads), lax.rem(step, heads)
                keys, values = keys_of(held_k.at[i], g), values_of(held_v.at[i], g)
                allowed = allowed_at(first, meta[PARTS + i] * 2 * tok, tok, 2 * tok, lengths)
                mine = pl.ds(pl.multiple_of(j * tok, tok), tok)
                s = jnp.where(allowed, dot_nn(q_at(j * tok, tok), keys) * FACTOR, NEG)
                top = jnp.maximum(peak[mine], jnp.max(s, axis=1, keepdims=True))
                p = jnp.where(allowed, jnp.exp2(s - top[:, :1]), 0.0)
                shrink = jnp.exp2(peak[mine] - top)
                total_now[mine] = total_now[mine] * shrink + fold(p, jnp.add)
                acc_now[mine] = acc_now[mine] * shrink + dot_nn(p.astype(jnp.bfloat16), values)
                peak[mine] = top

            write(turn, g)

    width = near.shape[1]
    where = pl.ds(pl.multiple_of(core * width, width), width)
    copy = pltpu.make_async_copy(result.at[1], out.at[:, where], sem)
    copy.start()
    near[...] = result[0]
    copy.wait()


def finish(state, blocks, done, meta, lengths):
    qs, total, acc = state
    groups, rows, unused = qs.shape
    flat = [x for block in blocks for x in block]
    tok = flat[0].shape[1] // 2
    heads = rows // (2 * tok)
    width = groups * heads * HD
    sums = pltpu.VMEM((heads * tok, HD), jnp.float32)
    return pl.pallas_call(
        functools.partial(finish_kernel, tok, heads, groups, done),
        out_shape=[
            jax.ShapeDtypeStruct((tok, width), jnp.bfloat16),
            jax.ShapeDtypeStruct((tok, 2 * width), jnp.bfloat16),
        ],
        in_specs=[SMEM, SMEM] + [VMEM] * (3 + len(flat)),
        out_specs=[VMEM, HBM],
        scratch_shapes=[
            *[pltpu.VMEM((len(blocks), *x.shape), x.dtype) for x in blocks[0]],
            sums, sums, sums,
            pltpu.VMEM((2, tok, width), jnp.bfloat16),
            pltpu.SemaphoreType.DMA,
        ],
        compiler_params=pltpu.CompilerParams(vmem_limit_bytes=ROOM),
        cost_estimate=pl.CostEstimate(
            flops=groups * rows * tok * HD * 8, bytes_accessed=tok * width * 4,
            transcendentals=groups * rows * tok * 2,
        ),
        name="finish",
    )(meta, lengths, qs, total, acc, *flat)


def request_sums(query, keys, values, bias):
    s = dot_nn(query, keys) * FACTOR
    p = jnp.exp2((s.reshape(-1, *bias.shape) + bias[None]).reshape(s.shape))
    return fold(p, jnp.add), dot_nn(p.astype(jnp.bfloat16), values)


def fresh_scores(query, newk, own):
    s = dot_nt(query, newk) * FACTOR
    size = newk.shape[0]
    row = lax.broadcasted_iota(jnp.int32, (size, size), 0)
    col = lax.broadcasted_iota(jnp.int32, (size, size), 1)
    ok = (lax.rem(row, own) == lax.rem(col, own)) & (lax.div(col, own) <= lax.div(row, own))
    return s.reshape(-1, size, size), ok


def request_copies(own, meta, sources, held, sems):
    requests = pl.ds(lax.div(meta[CHIP], 2) * own, own)
    copies = []
    for i, (source, target) in enumerate(zip(sources, held)):
        width = target.shape[2]
        where = pl.ds(pl.multiple_of(meta[CORE] * width, width), width)
        copies.append(pltpu.make_async_copy(source.at[requests, :, where], target, sems.at[i]))
    return copies


def requests_body(own, heads, groups, length, meta, table, total, acc, query, newk, newv, mask, q3, k3, v3):
    steps = q3.shape[1]
    level = lax.div(meta[CHIP], 2)
    pick = lax.broadcasted_iota(jnp.int32, (own, table.shape[1]), 1) - level * own
    pick = (pick == lax.broadcasted_iota(jnp.int32, pick.shape, 0)).astype(jnp.float32)
    rows = dot_nt(pick.astype(jnp.bfloat16), table[...].astype(jnp.float32).astype(jnp.bfloat16))
    lane = lax.div(lax.broadcasted_iota(jnp.int32, (own, length), 1), BLK)
    for i in range(mask.shape[1] // length):
        number = (lane + meta[PARTS + i] * (length // BLK)).astype(jnp.float32)
        hit = rows[:, :1] == number
        for j in range(1, rows.shape[1]):
            hit = hit | (rows[:, j : j + 1] == number)
        mask[:, i * length : (i + 1) * length] = jnp.where(hit, 0.0, -jnp.inf)
    for s in range(steps):
        for g in range(groups):
            col = slice(g * HD, (g + 1) * HD)
            at = slice(s * own, (s + 1) * own)
            newk[at, col] = k3[:, s, col]
            newv[at, col] = v3[:, s, col]
            for j in range(heads):
                first = (g * heads + j) * HD
                row = (j * steps + s) * own
                query[g, row : row + own] = q3[:, s, first : first + HD]

    @pl.loop(0, groups)
    def _(g):
        col = column_block(g * HD)
        s, ok = fresh_scores(query[g], newk[:, col], own)
        p = jnp.where(ok[None], jnp.exp2(s), 0.0).reshape(-1, s.shape[2])
        first = jnp.sum(p, axis=1, keepdims=True)
        lead = lax.broadcasted_iota(jnp.int32, (p.shape[0], HD), 1) == 0
        total[g] = jnp.where(lead, first, 0.0)
        acc[g] = dot_nn(p.astype(jnp.bfloat16), newv[:, col])


def requests_kernel(own, heads, groups, length, meta, *refs):
    sources, table, state, (q3, k3, v3, sems) = refs[:3], refs[3], refs[4:10], refs[10:]
    copies = request_copies(own, meta, sources, (q3, k3, v3), sems)
    for copy in copies:
        copy.start()
    for copy in copies:
        copy.wait()
    requests_body(own, heads, groups, length, meta, table, *state, q3, k3, v3)


def open_requests(q_dec, k_new, v_new, table, length, own, meta):
    heads = H // KVH
    steps = q_dec.shape[1]
    width = k_new.shape[2] // 2
    groups = width // HD
    rows = heads * own * steps
    sums = jax.ShapeDtypeStruct((groups, rows, HD), jnp.float32)
    new = jax.ShapeDtypeStruct((own * steps, width), jnp.bfloat16)
    return pl.pallas_call(
        functools.partial(requests_kernel, own, heads, groups, length),
        out_shape=[
            sums, sums, jax.ShapeDtypeStruct((groups, rows, HD), jnp.bfloat16), new, new,
            jax.ShapeDtypeStruct((own, (LEVELS - PARTS) * length), jnp.float32),
        ],
        in_specs=[SMEM] + [HBM] * 3 + [VMEM],
        out_specs=[VMEM] * 6,
        scratch_shapes=[
            pltpu.VMEM((own, steps, groups * heads * HD), jnp.bfloat16),
            pltpu.VMEM((own, steps, width), jnp.bfloat16),
            pltpu.VMEM((own, steps, width), jnp.bfloat16),
            pltpu.SemaphoreType.DMA((3,)),
        ],
        compiler_params=pltpu.CompilerParams(vmem_limit_bytes=LITTLE),
        cost_estimate=BRIEF,
        name="requests",
    )(meta, q_dec, k_new, v_new, table)


def early_kernel(groups, total_in, acc_in, query, mask, *refs):
    total, acc = refs[-2:]
    length = refs[0].shape[1]

    @pl.loop(0, groups)
    def _(g):
        sums = [total_in[g], acc_in[g]]
        for i in range(len(refs) // 2 - 1):
            bias = mask[:, i * length : (i + 1) * length]
            keys, values = keys_of(refs[2 * i], g), values_of(refs[2 * i + 1], g)
            more = request_sums(query[g], keys, values, bias)
            sums = [x + y for x, y in zip(sums, more)]
        total[g], acc[g] = sums


def early_decode(state, blocks):
    total, acc, query, newk, newv, mask = state
    groups, rows, unused = query.shape
    flat = [x for block in blocks for x in block]
    sums = jax.ShapeDtypeStruct(total.shape, total.dtype)
    new = pl.pallas_call(
        functools.partial(early_kernel, groups),
        out_shape=[sums, sums],
        in_specs=[VMEM] * (4 + len(flat)),
        out_specs=[VMEM] * 2,
        input_output_aliases={0: 0, 1: 1},
        compiler_params=pltpu.CompilerParams(vmem_limit_bytes=2 * LITTLE),
        cost_estimate=BRIEF,
        name="early_decode",
    )(total, acc, query, mask, *flat)
    return [*new, query, newk, newv, mask]


def late_kernel(own, steps, heads, groups, done, meta, total, acc, query, newk, newv, mask, *refs):
    parts, out = len(refs) // 2, refs[-1]
    length = refs[0].shape[1]
    size = own * steps

    def write(g, sums, whole):
        result = (sums / whole).astype(out.dtype)
        for j in range(heads):
            out[:, column_block((g * heads + j) * HD)] = result[j * size : (j + 1) * size]

    def one_group(g, fine):
        sums = [total[g], acc[g]]
        for i in range(done, parts):
            bias = mask[:, i * length : (i + 1) * length]
            keys, values = keys_of(refs[2 * i], g), values_of(refs[2 * i + 1], g)
            more = request_sums(query[g], keys, values, bias)
            sums = [x + y for x, y in zip(sums, more)]
        whole = jnp.sum(sums[0], axis=1, keepdims=True)
        write(g, sums[1], whole)
        return fine & sound(whole).astype(jnp.int32)

    fine = lax.fori_loop(0, groups, one_group, jnp.int32(1))

    @pl.when(fine == 0)
    def _():
        @pl.loop(0, groups)
        def _(g):
            col = column_block(g * HD)
            fresh, ok = fresh_scores(query[g], newk[:, col], own)
            fresh = jnp.where(ok[None], fresh, NEG).reshape(-1, size)
            top = jnp.max(fresh, axis=1, keepdims=True)
            p = jnp.exp2(fresh - top)
            whole = jnp.sum(p, axis=1, keepdims=True)
            sums = dot_nn(p.astype(jnp.bfloat16), newv[:, col])
            for i in range(parts):
                s = dot_nn(query[g], keys_of(refs[2 * i], g)) * FACTOR
                open_to = mask[:, i * length : (i + 1) * length] >= 0
                s = jnp.where(open_to[None], s.reshape(-1, own, length), NEG).reshape(s.shape)
                higher = jnp.maximum(top, jnp.max(s, axis=1, keepdims=True))
                p = jnp.exp2(s - higher)
                shrink = jnp.exp2(top - higher)
                whole = whole * shrink + jnp.sum(p, axis=1, keepdims=True)
                sums = sums * shrink + dot_nn(p.astype(jnp.bfloat16), values_of(refs[2 * i + 1], g))
                top = higher
            write(g, sums, whole)


def late_decode(early, blocks, done, own, steps, meta):
    groups, rows, unused = early[0].shape
    heads = H // KVH
    flat = [x for block in blocks for x in block]
    parts, length = len(blocks), flat[0].shape[1]
    pairs = groups * rows * (parts - done) * length
    return pl.pallas_call(
        functools.partial(late_kernel, own, steps, heads, groups, done),
        out_shape=jax.ShapeDtypeStruct((own * steps, groups * heads * HD), jnp.bfloat16),
        in_specs=[SMEM] + [VMEM] * (len(early) + len(flat)),
        out_specs=VMEM,
        compiler_params=pltpu.CompilerParams(vmem_limit_bytes=ROOM),
        cost_estimate=pl.CostEstimate(
            flops=pairs * HD * 8, bytes_accessed=rows * HD, transcendentals=pairs
        ),
        name="late_decode",
    )(meta, *early, *flat)


def decode_kernel(parts, steps, heads, groups, starts, q, mask, newk, newv, *refs):
    kheld, vheld = refs[:parts], refs[parts : 2 * parts]
    out, kall, vall, sems, scores = refs[2 * parts :]
    own = q.shape[0]
    rows = heads * own
    length = kheld[0].shape[1]
    copies = []
    for i in range(parts):
        where = pl.ds(pl.multiple_of(starts[i], HD), length)
        copies.append(pltpu.make_async_copy(kheld[i], kall.at[:, where], sems.at[2 * i]))
        copies.append(pltpu.make_async_copy(vheld[i], vall.at[where], sems.at[2 * i + 1]))
    for copy in copies:
        copy.start()
    row = lax.broadcasted_iota(jnp.int32, (own, own), 0)
    col = lax.broadcasted_iota(jnp.int32, (own, own), 1)
    fresh_ok = (lax.div(row, steps) == lax.div(col, steps)) & (col <= row)

    def columns(g):
        return slice(g * HD, (g + 1) * HD)

    def stacked(g):
        first = g * heads
        slices = [q[:, (first + j) * HD : (first + j + 1) * HD] for j in range(heads)]
        return jnp.concatenate([x.astype(jnp.float32) for x in slices], 0).astype(jnp.bfloat16)

    def keep(allowed, x, other):
        y = x.reshape(heads, own, x.shape[1])
        return jnp.where(allowed[None], y, other).reshape(x.shape)

    def open_to(i):
        return mask[:, pl.ds(pl.multiple_of(starts[i], HD), length)] > 0

    def write(g, acc, whole):
        result = acc / whole
        for j in range(heads):
            out[:, (g * heads + j) * HD : (g * heads + j + 1) * HD] = result[
                j * own : (j + 1) * own
            ].astype(out.dtype)

    fine = None
    for g in range(groups):
        query = stacked(g)
        p = keep(fresh_ok, jnp.exp2(dot_nt(query, newk[:, columns(g)]) * FACTOR), 0.0)
        whole = jnp.sum(p, axis=1, keepdims=True)
        acc = dot_nn(p.astype(jnp.bfloat16), newv[:, columns(g)])
        total = jnp.zeros((rows, HD), jnp.float32)
        for i in range(parts):
            p = jnp.exp2(dot_nn(query, kheld[i][columns(g)]) * FACTOR)
            p = keep(open_to(i), p, 0.0)
            total = total + fold(p, jnp.add)
            acc = acc + dot_nn(p.astype(jnp.bfloat16), vheld[i][:, columns(g)])
        whole = whole + jnp.sum(total, axis=1, keepdims=True)
        write(g, acc, whole)
        fine = sound(whole) if fine is None else fine & sound(whole)

    @pl.when(jnp.logical_not(fine))
    def _():
        for g in range(groups):
            query = stacked(g)
            fresh = keep(fresh_ok, dot_nt(query, newk[:, columns(g)]) * FACTOR, NEG)
            top = jnp.max(fresh, axis=1, keepdims=True)
            for i in range(parts):
                s = keep(open_to(i), dot_nn(query, kheld[i][columns(g)]) * FACTOR, NEG)
                scores[:, i * length : (i + 1) * length] = s
                top = jnp.maximum(top, jnp.max(s, axis=1, keepdims=True))
            p = jnp.exp2(fresh - top)
            whole = jnp.sum(p, axis=1, keepdims=True)
            acc = dot_nn(p.astype(jnp.bfloat16), newv[:, columns(g)])
            for i in range(parts):
                p = jnp.exp2(scores[:, i * length : (i + 1) * length] - top)
                whole = whole + jnp.sum(p, axis=1, keepdims=True)
                acc = acc + dot_nn(p.astype(jnp.bfloat16), vheld[i][:, columns(g)])
            write(g, acc, whole)

    for copy in copies:
        copy.wait()


def decode(q, mask, newk, newv, kparts, vparts, starts, steps):
    own = q.shape[0]
    parts = len(kparts)
    length, width = vparts[0].shape
    count = parts * length
    heads = H // KVH
    groups = width // HD
    rows = heads * own
    pairs = groups * rows * count
    return pl.pallas_call(
        functools.partial(decode_kernel, parts, steps, heads, groups),
        out_shape=[
            jax.ShapeDtypeStruct(q.shape, jnp.bfloat16),
            jax.ShapeDtypeStruct((width, count), jnp.bfloat16),
            jax.ShapeDtypeStruct((count, width), jnp.bfloat16),
        ],
        grid_spec=pltpu.PrefetchScalarGridSpec(
            num_scalar_prefetch=1,
            grid=(),
            in_specs=[VMEM] * (4 + 2 * parts),
            out_specs=[VMEM, HBM, HBM],
            scratch_shapes=[
                pltpu.SemaphoreType.DMA((2 * parts,)),
                pltpu.VMEM((rows, count), jnp.float32),
            ],
        ),
        compiler_params=pltpu.CompilerParams(vmem_limit_bytes=ROOM),
        cost_estimate=pl.CostEstimate(
            flops=pairs * HD * 4, bytes_accessed=count * width * 4, transcendentals=pairs
        ),
        name="decode",
    )(starts, q, mask, newk, newv, *kparts, *vparts)


def prepare_kernel(meta, k, v, send, keys, values):
    width = k.shape[1] // 2
    mine = pl.ds(pl.multiple_of(meta[0] * width, width), width)
    other = pl.ds(pl.multiple_of((1 - meta[0]) * width, width), width)
    send[:width] = k[:, other].astype(jnp.float32).T.astype(send.dtype)
    send[width:] = v[:, other]
    keys[:, mine] = k[:, mine].astype(jnp.float32).T.astype(keys.dtype)
    values[:, mine] = v[:, mine]


def prepare(k, v, core):
    tok, width = k.shape[0], k.shape[1] // 2
    assert tok == width
    block = jax.ShapeDtypeStruct((width, 2 * tok), k.dtype)
    return pl.pallas_call(
        prepare_kernel,
        out_shape=[jax.ShapeDtypeStruct((2 * tok, width), k.dtype), block, block],
        in_specs=[SMEM, VMEM, VMEM],
        out_specs=[VMEM] * 3,
        compiler_params=pltpu.CompilerParams(vmem_limit_bytes=LITTLE),
        name="prepare",
    )(core[None], k, v)


def join_kernel(meta, keys_in, values_in, theirs, q, keys, values, send_q, sem):
    columns = send_q.shape[1]
    where = pl.ds(pl.multiple_of((1 - meta[0]) * columns, columns), columns)
    copy = pltpu.make_async_copy(q.at[:, where], send_q, sem)
    copy.start()
    width = theirs.shape[1]
    other = pl.ds(pl.multiple_of((1 - meta[0]) * width, width), width)
    keys[...], values[...] = keys_in[...], values_in[...]
    keys[:, other] = theirs[:width]
    values[:, other] = theirs[width:]
    copy.wait()


def join(keys, values, theirs, q, core):
    return pl.pallas_call(
        join_kernel,
        out_shape=[
            jax.ShapeDtypeStruct(keys.shape, keys.dtype),
            jax.ShapeDtypeStruct(values.shape, values.dtype),
            jax.ShapeDtypeStruct((q.shape[0], q.shape[1] // 2), q.dtype),
        ],
        in_specs=[SMEM, VMEM, VMEM, VMEM, HBM],
        out_specs=[VMEM] * 3,
        scratch_shapes=[pltpu.SemaphoreType.DMA],
        compiler_params=pltpu.CompilerParams(vmem_limit_bytes=LITTLE),
        name="join",
    )(core[None], keys, values, theirs, q)


def take_kernel(meta, whole, out, sem):
    width = out.shape[1]
    where = pl.ds(pl.multiple_of((1 - meta[CORE]) * width, width), width)
    copy = pltpu.make_async_copy(whole.at[:, where], out, sem)
    copy.start()
    copy.wait()


def take_other_half(whole, meta):
    return pl.pallas_call(
        take_kernel,
        out_shape=jax.ShapeDtypeStruct((whole.shape[0], whole.shape[1] // 2), whole.dtype),
        in_specs=[SMEM, HBM],
        out_specs=VMEM,
        scratch_shapes=[pltpu.SemaphoreType.DMA],
        compiler_params=pltpu.CompilerParams(vmem_limit_bytes=LITTLE),
        name="take",
    )(meta, whole)


def project_kernel(meta, *refs):
    pieces, (whole, other), outs, (sorted_rows,) = refs[:-7], refs[-7:-5], refs[-5:-1], refs[-1:]
    parts = len(pieces)
    rows = pieces[0].shape[0]
    for i, piece in enumerate(pieces):
        at = pl.ds(pl.multiple_of(meta[LEVELS + i] * rows, rows), rows)
        sorted_rows[at] = piece[...]
    depth = other.shape[1]
    mine = whole[:, pl.ds(pl.multiple_of(meta[CORE] * depth, depth), depth)]
    half = parts * rows // 2
    here = pl.ds(pl.multiple_of(meta[ACROSS] * half, half), half)
    there = pl.ds(pl.multiple_of((1 - meta[ACROSS]) * half, half), half)
    kept, beside, across, corner = outs
    for at, near, far in ((here, kept, beside), (there, across, corner)):
        some = sorted_rows[at]
        near[...] = dot_nt(mine, some).astype(near.dtype)
        far[...] = dot_nt(other[...], some).astype(far.dtype)


def project(pieces, whole, other, meta):
    rows = len(pieces) * pieces[0].shape[0]
    width, depth = other.shape
    block = jax.ShapeDtypeStruct((width, rows // 2), jnp.bfloat16)
    return pl.pallas_call(
        project_kernel,
        out_shape=[jax.ShapeDtypeStruct(block.shape, jnp.float32)] + [block] * 3,
        in_specs=[SMEM] + [VMEM] * (len(pieces) + 2),
        out_specs=[VMEM] * 4,
        scratch_shapes=[pltpu.VMEM((rows, depth), jnp.bfloat16)],
        compiler_params=pltpu.CompilerParams(vmem_limit_bytes=2 * LITTLE),
        cost_estimate=pl.CostEstimate(
            flops=rows * width * depth * 4, bytes_accessed=width * depth * 4, transcendentals=0
        ),
        name="project",
    )(meta, *pieces, whole, other)


def index(z, y, c):
    return (z * 2 + y) * 2 + c


def on_ring(r, chips):
    return (r, 0) if r < chips // 2 else (chips - 1 - r, 1)


def ring_perm(chips, d):
    return [
        (index(*on_ring(r, chips), c), index(*on_ring((r + d) % chips, chips), c))
        for r in range(chips)
        for c in range(2)
    ]


def ring_place(r, chips):
    r = lax.rem(r + 2 * chips, chips)
    return jnp.where(r < chips // 2, r * 2, (chips - 1 - r) * 2 + 1)


def spread(x, n):
    place = lax.axis_index("seq")
    deep = n // 4
    everyone = [(z, y, c) for z in range(deep) for y in range(2) for c in range(2)]
    z, y, c = place // 4, (place // 2) % 2, place % 2
    held = [(x, z, y, c)]
    for d in range(1, deep):
        perm = [(index(*p), index((p[0] - d) % deep, p[1], p[2])) for p in everyone]
        held.append((lax.ppermute(x, "seq", perm), lax.rem(z + d, deep), y, c))
    perm = [(index(*p), index(p[0], 1 - p[1], p[2])) for p in everyone]
    held += [(lax.ppermute(b, "seq", perm), bz, 1 - by, bc) for b, bz, by, bc in held]
    perm = [(index(*p), index(p[0], p[1], 1 - p[2])) for p in everyone]
    held += [(lax.ppermute(b, "seq", perm), bz, by, 1 - bc) for b, bz, by, bc in held]
    return [b for b, *_ in held], jnp.stack([index(bz, by, bc) for _, bz, by, bc in held])


def open_blocks(table, steps, count):
    number = lax.broadcasted_iota(jnp.int32, (*table.shape, count), 2) // BLK
    mask = jnp.any(table[:, :, None] == number, axis=1).astype(jnp.float32)
    return jnp.repeat(mask, steps, axis=0)


def whole_heads(n, q_pre, k_cache, v_cache, lengths, q_dec, k_new, v_new, block_table, w_out):
    tok = q_pre.shape[0]
    place = lax.axis_index("seq").astype(jnp.int32)
    rows, steps = q_dec.shape[0], q_dec.shape[1]
    own = rows // n
    kparts, sources = spread(k_cache.T, n)
    vparts, _ = spread(v_cache, n)
    starts = sources.astype(jnp.int32) * tok

    def mine(x):
        y = lax.dynamic_slice_in_dim(x, place * own, own, 0)
        return y.reshape(own * steps, -1) if x.ndim == 3 else y

    mask = open_blocks(mine(block_table), steps, n * tok)
    attn_own, keys, values = decode(
        mine(q_dec), mask, mine(k_new), mine(v_new), kparts, vparts, starts, steps
    )
    attn = lax.all_gather(attn_own, "seq", axis=0, tiled=True)
    flat = jnp.dot(attn, w_out, preferred_element_type=jnp.float32).astype(jnp.bfloat16)
    dec_out = lax.psum_scatter(
        flat.reshape(rows, steps, -1), "tp", scatter_dimension=0, tiled=True
    )
    zero = jnp.zeros((), jnp.int32)
    meta = jnp.stack([place * tok, zero, zero, zero])
    groups = k_cache.shape[1] // HD
    pre_out = prefill(
        q_pre, keys, values, meta, lengths, groups, q_pre.shape[1], "prefill"
    )
    return (pre_out, dec_out)


def split_heads(n, q_pre, k_cache, v_cache, lengths, q_dec, k_new, v_new, block_table, w_out):
    tok = q_pre.shape[0]
    place = lax.axis_index("seq").astype(jnp.int32)
    across = lax.axis_index("tp").astype(jnp.int32)
    core, chip = lax.rem(place, 2), lax.div(place, 2)
    chips = n // 2
    far, deep = chips // 2, chips // 2
    z, y = lax.div(chip, 2), lax.rem(chip, 2)
    r = jnp.where(y == 0, z, chips - 1 - z)
    rows, steps = q_dec.shape[0], q_dec.shape[1]
    own = rows // deep
    sibling = [(i, i ^ 1) for i in range(n)]
    everyone = [(a, b, c) for a in range(deep) for b in range(2) for c in range(2)]

    order = [0] + [o for d in range(1, far) for o in (-d, d)] + [far]
    numbers = [ring_place(r + o, chips) for o in order]
    levels = [z] + [lax.rem(z + deep - d, deep) for d in range(1, deep)]
    assert len(numbers) == LEVELS - PARTS
    meta = jnp.stack([core, chip, across] + numbers + levels).astype(jnp.int32)

    send, keys, values = prepare(k_cache, v_cache, core)
    theirs = lax.ppermute(send, "seq", sibling)
    theirs, meta = lax.optimization_barrier((theirs, meta))
    held_k, held_v = {}, {}
    held_k[0], held_v[0], send_q = join(keys, values, theirs, q_pre, core)
    near_q = lax.ppermute(send_q, "seq", sibling)

    up, down = ring_perm(chips, 1), ring_perm(chips, -1)
    early, w_near = (), w_out
    for d in range(1, far + 1):
        held_k[-d] = lax.ppermute(held_k[1 - d], "seq", up)
        held_v[d] = lax.ppermute(held_v[d - 1], "seq", down)
        if d < far:
            held_k[d] = lax.ppermute(held_k[d - 1], "seq", down)
            held_v[-d] = lax.ppermute(held_v[1 - d], "seq", up)
            sides = (-d, d)
        else:
            held_k[d] = held_k[-d]
            sides = (d,)
        if d == 1:
            state = open_sums(q_pre, near_q, (held_k[0], held_v[0]), meta, lengths)
        elif d < far:
            pair = [(held_k[o], held_v[o]) for o in (1 - d, d - 1)]
            state = stage(state, pair, 2 * d - 3, meta, lengths)
        else:
            blocks = [(held_k[o], held_v[o]) for o in order[:-1]]
            early = early_decode(early, blocks)
        for x in (held_k, held_v):
            moved, state, early = lax.optimization_barrier(([x[o] for o in sides], state, early))
            x.update(zip(sides, moved))
            if d == 1 and x is held_k:
                state, block_table = lax.optimization_barrier((state, block_table))
                early = open_requests(
                    q_dec, k_new, v_new, block_table.T, 2 * tok, own, meta
                )
        if d == 3:
            w_near, state = lax.optimization_barrier((w_near, state))
            weights = w_near.T
            w_near = lax.ppermute(take_other_half(weights, meta), "seq", sibling)
    w_near, early = lax.optimization_barrier((w_near, early))
    blocks = [(held_k[o], held_v[o]) for o in order]
    attn_own = late_decode(early, blocks, len(blocks) - 1, own, steps, meta)

    pieces = [attn_own]
    for d in range(1, deep):
        perm = [(index(*p), index((p[0] + d) % deep, p[1], p[2])) for p in everyone]
        pieces.append(lax.ppermute(attn_own, "seq", perm))
    attn_own, state = lax.optimization_barrier((attn_own, state))
    near, pre_out = finish(state, blocks, 2 * far - 3, meta, lengths)
    pieces, near, pre_out = lax.optimization_barrier((pieces, near, pre_out))
    back = lax.ppermute(near, "seq", sibling)
    pre_out = settle(pre_out, back, meta)

    total, *sent = project(pieces, weights, w_near, meta)
    got = []
    for piece, (dc, dx) in zip(sent, ((1, 0), (0, 1), (1, 1))):
        perm = [
            (i * 2 + x, (i ^ dc) * 2 + (x ^ dx)) for i in range(n) for x in range(2)
        ]
        got.append(lax.ppermute(piece, ("seq", "tp"), perm))
    got[0], pre_out = lax.optimization_barrier((got[0], pre_out))
    for piece in got:
        total = total + piece.astype(jnp.float32)
    dec_out = total.astype(jnp.bfloat16).T.reshape(deep // 2, steps, own, -1)
    return (pre_out, dec_out.transpose(0, 2, 1, 3).reshape(rows // 2, steps, -1))


def per_device(n, tp, q_pre, k_cache, v_cache, prompt_lengths, *rest):
    groups = k_cache.shape[1] // HD
    square = groups % 2 == 0 and k_cache.shape[1] == 2 * k_cache.shape[0]
    small = n * k_cache.shape[0] // BLK <= 256 and n == 2 * (LEVELS - PARTS)
    form = split_heads if square and tp == 2 and small else whole_heads
    return form(n, q_pre, k_cache, v_cache, prompt_lengths.astype(jnp.int32), *rest)


def solution(mesh):
    placed = (
        P("seq", "tp"),
        P("seq", "tp"),
        P("seq", "tp"),
        P(),
        P(None, None, "tp"),
        P(None, None, "tp"),
        P(None, None, "tp"),
        P(),
        P("tp", "seq"),
    )
    return jax.shard_map(
        functools.partial(per_device, mesh.shape["seq"], mesh.shape["tp"]),
        mesh=mesh,
        in_specs=placed,
        out_specs=(P("seq", "tp"), P("tp", None, "seq")),
        check_vma=False,
    )
```

```python
import functools
import math

import jax
import jax.numpy as jnp
from jax import lax
from jax.experimental import pallas as pl
from jax.experimental.pallas import tpu as pltpu
from jax.sharding import PartitionSpec as P

H = 56
KVH = 8
HD = 128
BLK = 64
SPAN = 512
PAIR = 2
NEG = -1e30
LEAST, MOST = 2.0**-60, 2.0**100
FACTOR = math.log2(math.e) / math.sqrt(HD)
ROOM = 16 * 1024 * 1024
LITTLE = 4 * 1024 * 1024
CORE, CHIP, ACROSS, PARTS, LEVELS = 0, 1, 2, 3, 11
BRIEF = pl.CostEstimate(flops=1024, bytes_accessed=1024, transcendentals=0)
HBM = pl.BlockSpec(memory_space=pltpu.HBM)
VMEM = pl.BlockSpec(memory_space=pltpu.VMEM)
SMEM = pl.BlockSpec(memory_space=pltpu.SMEM)


def dot_nt(a, b):
    return lax.dot_general(a, b, (((1,), (1,)), ((), ())), preferred_element_type=jnp.float32)


def dot_nn(a, b):
    return lax.dot_general(a, b, (((1,), (0,)), ((), ())), preferred_element_type=jnp.float32)


def fold(x, op):
    out = x[:, :HD]
    for i in range(1, x.shape[1] // HD):
        out = op(out, x[:, i * HD : (i + 1) * HD])
    return out


def start_of(position, lengths):
    end = jnp.int32(0)
    out = jnp.zeros_like(position)
    for i in range(lengths.shape[0]):
        end = end + lengths[i]
        out = jnp.where(position >= end, end, out)
    return out


def sound(total):
    return (jnp.min(total) >= LEAST) & (jnp.max(total) <= MOST)


def prefill_kernel(tok, heads, meta, lengths, q, keys_all, values_all, *refs):
    out, qs, peak, total, acc = refs[-5:]
    for j in range(heads):
        qs[j * tok : (j + 1) * tok] = q[:, j * HD : (j + 1) * HD]
    total[...] = jnp.zeros_like(total)
    acc[...] = jnp.zeros_like(acc)

    begin = meta[0]
    finish = begin + tok
    low = start_of(begin, lengths)
    high = start_of(finish - 1, lengths)
    blocks = lax.div(finish - low + SPAN - 1, SPAN)
    clear = lax.div(finish - high, SPAN)

    def first_of(k):
        return jnp.maximum(finish - (k + 1) * SPAN, 0)

    def load(k):
        here = pl.ds(pl.multiple_of(first_of(k), HD), SPAN)
        return keys_all[:, here], values_all[here, :]

    def allowed_in(k):
        t = begin + lax.broadcasted_iota(jnp.int32, (tok, 1), 0)
        u = first_of(k) + lax.broadcasted_iota(jnp.int32, (tok, SPAN), 1)
        last = jnp.minimum(t, finish - k * SPAN - 1)
        return (u <= last) & (u >= start_of(t, lengths))

    def keep(allowed, x, other):
        some = x.shape[0] // tok
        return jnp.where(allowed[None], x.reshape(some, tok, SPAN), other).reshape(x.shape)

    def block(k, masked):
        keys, values = load(k)
        allowed = allowed_in(k) if masked else None
        for j in range(0, heads, PAIR):
            here = slice(j * tok, min(j + PAIR, heads) * tok)
            p = jnp.exp2(dot_nn(qs[here], keys) * FACTOR)
            if masked:
                p = keep(allowed, p, 0.0)
            total[here] += fold(p, jnp.add)
            acc[here] += dot_nn(p.astype(jnp.bfloat16), values)

    block(0, True)

    @pl.loop(1, jnp.maximum(clear, 1))
    def _(k):
        block(k, False)

    @pl.loop(jnp.maximum(clear, 1), blocks)
    def _(k):
        block(k, True)

    def write():
        whole = jnp.sum(total[...], axis=1, keepdims=True)
        result = (acc[...] / whole).astype(out.dtype)
        for j in range(heads):
            out[:, j * HD : (j + 1) * HD] = result[j * tok : (j + 1) * tok]
        return whole

    fine = sound(write())

    @pl.when(jnp.logical_not(fine))
    def _():
        peak[...] = jnp.full_like(peak, NEG)
        total[...] = jnp.zeros_like(total)
        acc[...] = jnp.zeros_like(acc)

        @pl.loop(0, blocks)
        def _(k):
            keys, values = load(k)
            allowed = allowed_in(k)

            @pl.loop(0, heads)
            def _(j):
                here = pl.ds(pl.multiple_of(j * tok, tok), tok)
                s = jnp.where(allowed, dot_nn(qs[here], keys) * FACTOR, NEG)
                top = jnp.maximum(peak[here], jnp.max(s, axis=1, keepdims=True))
                p = jnp.where(allowed, jnp.exp2(s - top[:, :1]), 0.0)
                shrink = jnp.exp2(peak[here] - top)
                total[here] = total[here] * shrink + fold(p, jnp.add)
                acc[here] = acc[here] * shrink + dot_nn(p.astype(jnp.bfloat16), values)
                peak[here] = top

        write()


def prefill(q, keys, values, meta, lengths, groups, columns, name, before=None):
    tok = q.shape[0]
    count = values.shape[0]
    heads = H // KVH
    rows = heads * tok
    pairs = rows * count // 2 * groups
    extra = [] if before is None else [before]
    return pl.pallas_call(
        functools.partial(prefill_kernel, tok, heads),
        out_shape=jax.ShapeDtypeStruct((tok, columns), jnp.bfloat16),
        grid_spec=pltpu.PrefetchScalarGridSpec(
            num_scalar_prefetch=2,
            grid=(groups,),
            in_specs=[
                pl.BlockSpec((tok, heads * HD), lambda g, meta, lengths: (0, meta[1] + g)),
                pl.BlockSpec((HD, count), lambda g, meta, lengths: (meta[2] + g, 0)),
                pl.BlockSpec((count, HD), lambda g, meta, lengths: (0, meta[2] + g)),
            ]
            + [HBM] * len(extra),
            out_specs=pl.BlockSpec((tok, heads * HD), lambda g, meta, lengths: (0, meta[3] + g)),
            scratch_shapes=[
                pltpu.VMEM((rows, HD), jnp.bfloat16),
                pltpu.VMEM((rows, HD), jnp.float32),
                pltpu.VMEM((rows, HD), jnp.float32),
                pltpu.VMEM((rows, HD), jnp.float32),
            ],
        ),
        compiler_params=pltpu.CompilerParams(vmem_limit_bytes=ROOM),
        cost_estimate=pl.CostEstimate(
            flops=pairs * HD * 8, bytes_accessed=count * HD * 4 * groups, transcendentals=pairs
        ),
        input_output_aliases={} if before is None else {5: 0},
        name=name,
    )(meta, lengths, q, keys, values, *extra)


def settle_kernel(meta, piece, whole, out, sem):
    width = piece.shape[1]
    where = pl.ds(pl.multiple_of((1 - meta[CORE]) * width, width), width)
    copy = pltpu.make_async_copy(piece, out.at[:, where], sem)
    copy.start()
    copy.wait()


def settle(whole, piece, meta):
    return pl.pallas_call(
        settle_kernel,
        out_shape=jax.ShapeDtypeStruct(whole.shape, whole.dtype),
        in_specs=[SMEM, VMEM, HBM],
        out_specs=HBM,
        scratch_shapes=[pltpu.SemaphoreType.DMA],
        input_output_aliases={2: 0},
        compiler_params=pltpu.CompilerParams(vmem_limit_bytes=LITTLE),
        cost_estimate=pl.CostEstimate(flops=0, bytes_accessed=piece.size * 4, transcendentals=0),
        name="settle",
    )(meta, piece, whole)


def allowed_at(first, base, tok, length, lengths):
    t = first + lax.broadcasted_iota(jnp.int32, (tok, 1), 0)
    u = base + lax.broadcasted_iota(jnp.int32, (tok, length), 1)
    return (u <= t) & (u >= start_of(t, lengths))


def column_block(at):
    return pl.ds(pl.multiple_of(at, HD), HD)


def keys_of(upper, g):
    return upper[column_block(g * HD), :]


def values_of(lower, g):
    half = lower.shape[1] // 2
    both = [lower[:, column_block(side * half + g * HD)] for side in range(2)]
    return jnp.concatenate(both, axis=0)


def block_bias(first, base, tok, length, lengths):
    start = start_of(first, lengths)
    t = first + lax.broadcasted_iota(jnp.int32, (tok, HD), 0)
    u = base + lax.broadcasted_iota(jnp.int32, (1, length), 1)
    row = jnp.where(start_of(t, lengths) == start, 0.0, -jnp.inf)
    return [jnp.concatenate([row] * (length // HD), axis=1), jnp.where(u >= start, 0.0, -jnp.inf)]


def add_block(tok, heads, q_at, keys, values, biases, sums, old):
    length = keys.shape[1]
    turns = [(j * tok, min(PAIR, heads - j)) for j in range(0, heads, PAIR)]

    def score(at, some):
        return dot_nn(q_at(at, some * tok), keys)

    coming = score(*turns[0])
    for number, (at, some) in enumerate(turns):
        s = coming * FACTOR
        if number + 1 < len(turns):
            coming = score(*turns[number + 1])
        for bias in biases:
            s = (s.reshape(some, tok, length) + bias[None]).reshape(some * tok, length)
        p = jnp.exp2(s)
        more = (fold(p, jnp.add), dot_nn(p.astype(jnp.bfloat16), values))
        here = slice(at, at + some * tok)
        for i in range(2):
            sums[i][here] = more[i] if old is None else old[i][here] + more[i]


def relation(meta, part, side, tok, lengths):
    first = (meta[CHIP] * 2 + side) * tok
    base = meta[PARTS + part] * 2 * tok
    relevant = (base < first) & (meta[PARTS + part] != meta[CHIP])
    relevant = relevant & (base + 2 * tok > start_of(first, lengths))
    return relevant, base >= start_of(first + tok - 1, lengths), first, base


def side_rows(side, heads, tok):
    return pl.ds(pl.multiple_of(side * (heads * tok), HD), heads * tok)


def open_kernel(tok, heads, groups, meta, lengths, q, q_near, upper, lower, qs, total, acc):
    core = meta[CORE]
    rows = heads * tok
    for source, side, skip in ((q, core, core * groups * heads), (q_near, 1 - core, 0)):
        for g in range(groups):
            for j in range(heads):
                at = pl.ds(pl.multiple_of(side * rows + j * tok, HD), tok)
                qs[g, at] = source[:, column_block((skip + g * heads + j) * HD)]

    @pl.loop(0, groups)
    def _(g):
        keys, values = keys_of(upper, g), values_of(lower, g)
        for side in range(2):
            length = (side + 1) * tok
            first = (meta[CHIP] * 2 + side) * tok
            allowed = allowed_at(first, meta[CHIP] * 2 * tok, tok, length, lengths)
            here = side_rows(side, heads, tok)
            q_at = lambda at, count: qs[g, pl.ds(side * rows + at, count)]
            bias = jnp.where(allowed, 0.0, -jnp.inf)
            add_block(tok, heads, q_at, keys[:, :length], values[:length], [bias],
                      (total.at[g, here], acc.at[g, here]), None)


def open_sums(q, q_near, block, meta, lengths):
    tok = q.shape[0]
    heads = H // KVH
    groups = q_near.shape[1] // (heads * HD)
    rows = 2 * heads * tok
    sums = jax.ShapeDtypeStruct((groups, rows, HD), jnp.float32)
    pairs = groups * rows * tok * 2
    return pl.pallas_call(
        functools.partial(open_kernel, tok, heads, groups),
        out_shape=[jax.ShapeDtypeStruct((groups, rows, HD), jnp.bfloat16), sums, sums],
        in_specs=[SMEM, SMEM, VMEM, VMEM, VMEM, VMEM],
        out_specs=[VMEM] * 3,
        compiler_params=pltpu.CompilerParams(vmem_limit_bytes=2 * LITTLE),
        cost_estimate=BRIEF,
        name="open",
    )(meta, lengths, q, q_near, *block)


def stage_body(tok, heads, groups, first_part, meta, lengths, qs, before, pair, total, acc):
    for which in range(2):
        upper, lower = pair[2 * which], pair[2 * which + 1]

        @pl.loop(0, 2 * groups)
        def _(step):
            g, side = lax.div(step, 2), lax.rem(step, 2)
            relevant, clear, first, base = relation(meta, first_part + which, side, tok, lengths)
            here = side_rows(side, heads, tok)
            sums = (total.at[g, here], acc.at[g, here])
            old = sums if which else [ref.at[g, here] for ref in before]
            at = side * (heads * tok)
            q_at = lambda off, count: qs[g, pl.ds(pl.multiple_of(at + off, HD), count)]

            @pl.when(relevant & clear)
            def _():
                add_block(tok, heads, q_at, keys_of(upper, g), values_of(lower, g), [], sums, old)

            @pl.when(relevant & jnp.logical_not(clear))
            def _():
                biases = block_bias(first, base, tok, 2 * tok, lengths)
                add_block(
                    tok, heads, q_at, keys_of(upper, g), values_of(lower, g), biases, sums, old
                )

            if which == 0:

                @pl.when(jnp.logical_not(relevant))
                def _():
                    for i in range(2):
                        sums[i][...] = old[i][...]


def stage_kernel(tok, heads, groups, first_part, meta, lengths, qs, total_in, acc_in, *refs):
    pair, (total, acc) = refs[:4], refs[4:]
    before = (total_in, acc_in)
    stage_body(tok, heads, groups, first_part, meta, lengths, qs, before, pair, total, acc)


def stage(state, pair, first_part, meta, lengths):
    qs, total, acc = state
    groups, rows, unused = qs.shape
    flat = [x for block in pair for x in block]
    tok = flat[0].shape[1] // 2
    new = pl.pallas_call(
        functools.partial(stage_kernel, tok, rows // (2 * tok), groups, first_part),
        out_shape=[jax.ShapeDtypeStruct(x.shape, x.dtype) for x in (total, acc)],
        in_specs=[SMEM, SMEM] + [VMEM] * 7,
        out_specs=[VMEM] * 2,
        input_output_aliases={3: 0, 4: 1},
        compiler_params=pltpu.CompilerParams(vmem_limit_bytes=ROOM),
        cost_estimate=BRIEF,
        name=f"stage{first_part}",
    )(meta, lengths, qs, total, acc, *flat)
    return qs, *new


def finish_kernel(tok, heads, groups, done, meta, lengths, qs, total, acc, *refs):
    near, out, held_k, held_v, peak, total_now, acc_now, result, sem = refs[-9:]
    parts = held_k.shape[0]
    rows = heads * tok
    core = meta[CORE]

    def fill(first):
        for i in range(first, parts):
            held_k[i], held_v[i] = refs[2 * i][...], refs[2 * i + 1][...]

    def turn_of(step):
        turn, g = lax.div(step, groups), lax.rem(step, groups)
        side = jnp.where(turn == 0, 1 - core, core)
        at = side * rows
        q_at = lambda off, count: qs[g, pl.ds(pl.multiple_of(at + off, HD), count)]
        return turn, g, side, q_at

    def write(turn, g):
        whole = jnp.sum(total_now[...], axis=1, keepdims=True)
        value = (acc_now[...] / whole).astype(result.dtype)
        for j in range(heads):
            result[turn, :, column_block((g * heads + j) * HD)] = value[j * tok : (j + 1) * tok]
        return sound(whole)

    def one_turn(step, fine):
        turn, g, side, q_at = turn_of(step)
        here = side_rows(side, heads, tok)
        total_now[...] = total[g, here]
        acc_now[...] = acc[g, here]

        @pl.loop(done, parts)
        def _(i):
            relevant, clear, first, base = relation(meta, i, side, tok, lengths)
            upper, lower = held_k.at[i], held_v.at[i]
            sums = (total_now, acc_now)

            @pl.when(relevant & clear)
            def _():
                add_block(tok, heads, q_at, keys_of(upper, g), values_of(lower, g), [], sums, sums)

            @pl.when(relevant & jnp.logical_not(clear))
            def _():
                biases = block_bias(first, base, tok, 2 * tok, lengths)
                add_block(
                    tok, heads, q_at, keys_of(upper, g), values_of(lower, g), biases, sums, sums
                )

        return fine & write(turn, g).astype(jnp.int32)

    fill(done)
    fine = lax.fori_loop(0, 2 * groups, one_turn, jnp.int32(1))

    @pl.when(fine == 0)
    def _():
        fill(0)

        @pl.loop(0, 2 * groups)
        def _(step):
            turn, g, side, q_at = turn_of(step)
            first = (meta[CHIP] * 2 + side) * tok
            peak[...] = jnp.full_like(peak, NEG)
            total_now[...] = jnp.zeros_like(total_now)
            acc_now[...] = jnp.zeros_like(acc_now)

            @pl.loop(0, parts * heads)
            def _(step):
                i, j = lax.div(step, heads), lax.rem(step, heads)
                keys, values = keys_of(held_k.at[i], g), values_of(held_v.at[i], g)
                allowed = allowed_at(first, meta[PARTS + i] * 2 * tok, tok, 2 * tok, lengths)
                mine = pl.ds(pl.multiple_of(j * tok, tok), tok)
                s = jnp.where(allowed, dot_nn(q_at(j * tok, tok), keys) * FACTOR, NEG)
                top = jnp.maximum(peak[mine], jnp.max(s, axis=1, keepdims=True))
                p = jnp.where(allowed, jnp.exp2(s - top[:, :1]), 0.0)
                shrink = jnp.exp2(peak[mine] - top)
                total_now[mine] = total_now[mine] * shrink + fold(p, jnp.add)
                acc_now[mine] = acc_now[mine] * shrink + dot_nn(p.astype(jnp.bfloat16), values)
                peak[mine] = top

            write(turn, g)

    width = near.shape[1]
    where = pl.ds(pl.multiple_of(core * width, width), width)
    copy = pltpu.make_async_copy(result.at[1], out.at[:, where], sem)
    copy.start()
    near[...] = result[0]
    copy.wait()


def finish(state, blocks, done, meta, lengths):
    qs, total, acc = state
    groups, rows, unused = qs.shape
    flat = [x for block in blocks for x in block]
    tok = flat[0].shape[1] // 2
    heads = rows // (2 * tok)
    width = groups * heads * HD
    sums = pltpu.VMEM((heads * tok, HD), jnp.float32)
    return pl.pallas_call(
        functools.partial(finish_kernel, tok, heads, groups, done),
        out_shape=[
            jax.ShapeDtypeStruct((tok, width), jnp.bfloat16),
            jax.ShapeDtypeStruct((tok, 2 * width), jnp.bfloat16),
        ],
        in_specs=[SMEM, SMEM] + [VMEM] * (3 + len(flat)),
        out_specs=[VMEM, HBM],
        scratch_shapes=[
            *[pltpu.VMEM((len(blocks), *x.shape), x.dtype) for x in blocks[0]],
            sums, sums, sums,
            pltpu.VMEM((2, tok, width), jnp.bfloat16),
            pltpu.SemaphoreType.DMA,
        ],
        compiler_params=pltpu.CompilerParams(vmem_limit_bytes=ROOM),
        cost_estimate=pl.CostEstimate(
            flops=groups * rows * tok * HD * 8, bytes_accessed=tok * width * 4,
            transcendentals=groups * rows * tok * 2,
        ),
        name="finish",
    )(meta, lengths, qs, total, acc, *flat)


def request_sums(query, keys, values, bias):
    s = dot_nn(query, keys) * FACTOR
    p = jnp.exp2((s.reshape(-1, *bias.shape) + bias[None]).reshape(s.shape))
    return fold(p, jnp.add), dot_nn(p.astype(jnp.bfloat16), values)


def fresh_scores(query, newk, own):
    s = dot_nt(query, newk) * FACTOR
    size = newk.shape[0]
    row = lax.broadcasted_iota(jnp.int32, (size, size), 0)
    col = lax.broadcasted_iota(jnp.int32, (size, size), 1)
    ok = (lax.rem(row, own) == lax.rem(col, own)) & (lax.div(col, own) <= lax.div(row, own))
    return s.reshape(-1, size, size), ok


def request_copies(own, meta, sources, held, sems):
    requests = pl.ds(lax.div(meta[CHIP], 2) * own, own)
    copies = []
    for i, (source, target) in enumerate(zip(sources, held)):
        width = target.shape[2]
        where = pl.ds(pl.multiple_of(meta[CORE] * width, width), width)
        copies.append(pltpu.make_async_copy(source.at[requests, :, where], target, sems.at[i]))
    return copies


def requests_body(own, heads, groups, length, meta, table, total, acc, query, newk, newv, mask, q3, k3, v3):
    steps = q3.shape[1]
    level = lax.div(meta[CHIP], 2)
    pick = lax.broadcasted_iota(jnp.int32, (own, table.shape[1]), 1) - level * own
    pick = (pick == lax.broadcasted_iota(jnp.int32, pick.shape, 0)).astype(jnp.float32)
    rows = dot_nt(pick.astype(jnp.bfloat16), table[...].astype(jnp.float32).astype(jnp.bfloat16))
    lane = lax.div(lax.broadcasted_iota(jnp.int32, (own, length), 1), BLK)
    for i in range(mask.shape[1] // length):
        number = (lane + meta[PARTS + i] * (length // BLK)).astype(jnp.float32)
        hit = rows[:, :1] == number
        for j in range(1, rows.shape[1]):
            hit = hit | (rows[:, j : j + 1] == number)
        mask[:, i * length : (i + 1) * length] = jnp.where(hit, 0.0, -jnp.inf)
    for s in range(steps):
        for g in range(groups):
            col = slice(g * HD, (g + 1) * HD)
            at = slice(s * own, (s + 1) * own)
            newk[at, col] = k3[:, s, col]
            newv[at, col] = v3[:, s, col]
            for j in range(heads):
                first = (g * heads + j) * HD
                row = (j * steps + s) * own
                query[g, row : row + own] = q3[:, s, first : first + HD]

    @pl.loop(0, groups)
    def _(g):
        col = column_block(g * HD)
        s, ok = fresh_scores(query[g], newk[:, col], own)
        p = jnp.where(ok[None], jnp.exp2(s), 0.0).reshape(-1, s.shape[2])
        first = jnp.sum(p, axis=1, keepdims=True)
        lead = lax.broadcasted_iota(jnp.int32, (p.shape[0], HD), 1) == 0
        total[g] = jnp.where(lead, first, 0.0)
        acc[g] = dot_nn(p.astype(jnp.bfloat16), newv[:, col])


def requests_kernel(own, heads, groups, length, meta, *refs):
    sources, table, state, (q3, k3, v3, sems) = refs[:3], refs[3], refs[4:10], refs[10:]
    copies = request_copies(own, meta, sources, (q3, k3, v3), sems)
    for copy in copies:
        copy.start()
    for copy in copies:
        copy.wait()
    requests_body(own, heads, groups, length, meta, table, *state, q3, k3, v3)


def open_requests(q_dec, k_new, v_new, table, length, own, meta):
    heads = H // KVH
    steps = q_dec.shape[1]
    width = k_new.shape[2] // 2
    groups = width // HD
    rows = heads * own * steps
    sums = jax.ShapeDtypeStruct((groups, rows, HD), jnp.float32)
    new = jax.ShapeDtypeStruct((own * steps, width), jnp.bfloat16)
    return pl.pallas_call(
        functools.partial(requests_kernel, own, heads, groups, length),
        out_shape=[
            sums, sums, jax.ShapeDtypeStruct((groups, rows, HD), jnp.bfloat16), new, new,
            jax.ShapeDtypeStruct((own, (LEVELS - PARTS) * length), jnp.float32),
        ],
        in_specs=[SMEM] + [HBM] * 3 + [VMEM],
        out_specs=[VMEM] * 6,
        scratch_shapes=[
            pltpu.VMEM((own, steps, groups * heads * HD), jnp.bfloat16),
            pltpu.VMEM((own, steps, width), jnp.bfloat16),
            pltpu.VMEM((own, steps, width), jnp.bfloat16),
            pltpu.SemaphoreType.DMA((3,)),
        ],
        compiler_params=pltpu.CompilerParams(vmem_limit_bytes=LITTLE),
        cost_estimate=BRIEF,
        name="requests",
    )(meta, q_dec, k_new, v_new, table)


def early_kernel(groups, total_in, acc_in, query, mask, *refs):
    total, acc = refs[-2:]
    length = refs[0].shape[1]

    @pl.loop(0, groups)
    def _(g):
        sums = [total_in[g], acc_in[g]]
        for i in range(len(refs) // 2 - 1):
            bias = mask[:, i * length : (i + 1) * length]
            keys, values = keys_of(refs[2 * i], g), values_of(refs[2 * i + 1], g)
            more = request_sums(query[g], keys, values, bias)
            sums = [x + y for x, y in zip(sums, more)]
        total[g], acc[g] = sums


def early_decode(state, blocks):
    total, acc, query, newk, newv, mask = state
    groups, rows, unused = query.shape
    flat = [x for block in blocks for x in block]
    sums = jax.ShapeDtypeStruct(total.shape, total.dtype)
    new = pl.pallas_call(
        functools.partial(early_kernel, groups),
        out_shape=[sums, sums],
        in_specs=[VMEM] * (4 + len(flat)),
        out_specs=[VMEM] * 2,
        input_output_aliases={0: 0, 1: 1},
        compiler_params=pltpu.CompilerParams(vmem_limit_bytes=2 * LITTLE),
        cost_estimate=BRIEF,
        name="early_decode",
    )(total, acc, query, mask, *flat)
    return [*new, query, newk, newv, mask]


def late_kernel(own, steps, heads, groups, done, meta, total, acc, query, newk, newv, mask, *refs):
    parts, out = len(refs) // 2, refs[-1]
    length = refs[0].shape[1]
    size = own * steps

    def write(g, sums, whole):
        result = (sums / whole).astype(out.dtype)
        for j in range(heads):
            out[:, column_block((g * heads + j) * HD)] = result[j * size : (j + 1) * size]

    def one_group(g, fine):
        sums = [total[g], acc[g]]
        for i in range(done, parts):
            bias = mask[:, i * length : (i + 1) * length]
            keys, values = keys_of(refs[2 * i], g), values_of(refs[2 * i + 1], g)
            more = request_sums(query[g], keys, values, bias)
            sums = [x + y for x, y in zip(sums, more)]
        whole = jnp.sum(sums[0], axis=1, keepdims=True)
        write(g, sums[1], whole)
        return fine & sound(whole).astype(jnp.int32)

    fine = lax.fori_loop(0, groups, one_group, jnp.int32(1))

    @pl.when(fine == 0)
    def _():
        @pl.loop(0, groups)
        def _(g):
            col = column_block(g * HD)
            fresh, ok = fresh_scores(query[g], newk[:, col], own)
            fresh = jnp.where(ok[None], fresh, NEG).reshape(-1, size)
            top = jnp.max(fresh, axis=1, keepdims=True)
            p = jnp.exp2(fresh - top)
            whole = jnp.sum(p, axis=1, keepdims=True)
            sums = dot_nn(p.astype(jnp.bfloat16), newv[:, col])
            for i in range(parts):
                s = dot_nn(query[g], keys_of(refs[2 * i], g)) * FACTOR
                open_to = mask[:, i * length : (i + 1) * length] >= 0
                s = jnp.where(open_to[None], s.reshape(-1, own, length), NEG).reshape(s.shape)
                higher = jnp.maximum(top, jnp.max(s, axis=1, keepdims=True))
                p = jnp.exp2(s - higher)
                shrink = jnp.exp2(top - higher)
                whole = whole * shrink + jnp.sum(p, axis=1, keepdims=True)
                sums = sums * shrink + dot_nn(p.astype(jnp.bfloat16), values_of(refs[2 * i + 1], g))
                top = higher
            write(g, sums, whole)


def late_decode(early, blocks, done, own, steps, meta):
    groups, rows, unused = early[0].shape
    heads = H // KVH
    flat = [x for block in blocks for x in block]
    parts, length = len(blocks), flat[0].shape[1]
    pairs = groups * rows * (parts - done) * length
    return pl.pallas_call(
        functools.partial(late_kernel, own, steps, heads, groups, done),
        out_shape=jax.ShapeDtypeStruct((own * steps, groups * heads * HD), jnp.bfloat16),
        in_specs=[SMEM] + [VMEM] * (len(early) + len(flat)),
        out_specs=VMEM,
        compiler_params=pltpu.CompilerParams(vmem_limit_bytes=ROOM),
        cost_estimate=pl.CostEstimate(
            flops=pairs * HD * 8, bytes_accessed=rows * HD, transcendentals=pairs
        ),
        name="late_decode",
    )(meta, *early, *flat)


def decode_kernel(parts, steps, heads, groups, starts, q, mask, newk, newv, *refs):
    kheld, vheld = refs[:parts], refs[parts : 2 * parts]
    out, kall, vall, sems, scores = refs[2 * parts :]
    own = q.shape[0]
    rows = heads * own
    length = kheld[0].shape[1]
    copies = []
    for i in range(parts):
        where = pl.ds(pl.multiple_of(starts[i], HD), length)
        copies.append(pltpu.make_async_copy(kheld[i], kall.at[:, where], sems.at[2 * i]))
        copies.append(pltpu.make_async_copy(vheld[i], vall.at[where], sems.at[2 * i + 1]))
    for copy in copies:
        copy.start()
    row = lax.broadcasted_iota(jnp.int32, (own, own), 0)
    col = lax.broadcasted_iota(jnp.int32, (own, own), 1)
    fresh_ok = (lax.div(row, steps) == lax.div(col, steps)) & (col <= row)

    def columns(g):
        return slice(g * HD, (g + 1) * HD)

    def stacked(g):
        first = g * heads
        slices = [q[:, (first + j) * HD : (first + j + 1) * HD] for j in range(heads)]
        return jnp.concatenate([x.astype(jnp.float32) for x in slices], 0).astype(jnp.bfloat16)

    def keep(allowed, x, other):
        y = x.reshape(heads, own, x.shape[1])
        return jnp.where(allowed[None], y, other).reshape(x.shape)

    def open_to(i):
        return mask[:, pl.ds(pl.multiple_of(starts[i], HD), length)] > 0

    def write(g, acc, whole):
        result = acc / whole
        for j in range(heads):
            out[:, (g * heads + j) * HD : (g * heads + j + 1) * HD] = result[
                j * own : (j + 1) * own
            ].astype(out.dtype)

    fine = None
    for g in range(groups):
        query = stacked(g)
        p = keep(fresh_ok, jnp.exp2(dot_nt(query, newk[:, columns(g)]) * FACTOR), 0.0)
        whole = jnp.sum(p, axis=1, keepdims=True)
        acc = dot_nn(p.astype(jnp.bfloat16), newv[:, columns(g)])
        total = jnp.zeros((rows, HD), jnp.float32)
        for i in range(parts):
            p = jnp.exp2(dot_nn(query, kheld[i][columns(g)]) * FACTOR)
            p = keep(open_to(i), p, 0.0)
            total = total + fold(p, jnp.add)
            acc = acc + dot_nn(p.astype(jnp.bfloat16), vheld[i][:, columns(g)])
        whole = whole + jnp.sum(total, axis=1, keepdims=True)
        write(g, acc, whole)
        fine = sound(whole) if fine is None else fine & sound(whole)

    @pl.when(jnp.logical_not(fine))
    def _():
        for g in range(groups):
            query = stacked(g)
            fresh = keep(fresh_ok, dot_nt(query, newk[:, columns(g)]) * FACTOR, NEG)
            top = jnp.max(fresh, axis=1, keepdims=True)
            for i in range(parts):
                s = keep(open_to(i), dot_nn(query, kheld[i][columns(g)]) * FACTOR, NEG)
                scores[:, i * length : (i + 1) * length] = s
                top = jnp.maximum(top, jnp.max(s, axis=1, keepdims=True))
            p = jnp.exp2(fresh - top)
            whole = jnp.sum(p, axis=1, keepdims=True)
            acc = dot_nn(p.astype(jnp.bfloat16), newv[:, columns(g)])
            for i in range(parts):
                p = jnp.exp2(scores[:, i * length : (i + 1) * length] - top)
                whole = whole + jnp.sum(p, axis=1, keepdims=True)
                acc = acc + dot_nn(p.astype(jnp.bfloat16), vheld[i][:, columns(g)])
            write(g, acc, whole)

    for copy in copies:
        copy.wait()


def decode(q, mask, newk, newv, kparts, vparts, starts, steps):
    own = q.shape[0]
    parts = len(kparts)
    length, width = vparts[0].shape
    count = parts * length
    heads = H // KVH
    groups = width // HD
    rows = heads * own
    pairs = groups * rows * count
    return pl.pallas_call(
        functools.partial(decode_kernel, parts, steps, heads, groups),
        out_shape=[
            jax.ShapeDtypeStruct(q.shape, jnp.bfloat16),
            jax.ShapeDtypeStruct((width, count), jnp.bfloat16),
            jax.ShapeDtypeStruct((count, width), jnp.bfloat16),
        ],
        grid_spec=pltpu.PrefetchScalarGridSpec(
            num_scalar_prefetch=1,
            grid=(),
            in_specs=[VMEM] * (4 + 2 * parts),
            out_specs=[VMEM, HBM, HBM],
            scratch_shapes=[
                pltpu.SemaphoreType.DMA((2 * parts,)),
                pltpu.VMEM((rows, count), jnp.float32),
            ],
        ),
        compiler_params=pltpu.CompilerParams(vmem_limit_bytes=ROOM),
        cost_estimate=pl.CostEstimate(
            flops=pairs * HD * 4, bytes_accessed=count * width * 4, transcendentals=pairs
        ),
        name="decode",
    )(starts, q, mask, newk, newv, *kparts, *vparts)


def prepare_kernel(meta, k, v, send, keys, values):
    width = k.shape[1] // 2
    mine = pl.ds(pl.multiple_of(meta[0] * width, width), width)
    other = pl.ds(pl.multiple_of((1 - meta[0]) * width, width), width)
    send[:width] = k[:, other].astype(jnp.float32).T.astype(send.dtype)
    send[width:] = v[:, other]
    keys[:, mine] = k[:, mine].astype(jnp.float32).T.astype(keys.dtype)
    values[:, mine] = v[:, mine]


def prepare(k, v, core):
    tok, width = k.shape[0], k.shape[1] // 2
    assert tok == width
    block = jax.ShapeDtypeStruct((width, 2 * tok), k.dtype)
    return pl.pallas_call(
        prepare_kernel,
        out_shape=[jax.ShapeDtypeStruct((2 * tok, width), k.dtype), block, block],
        in_specs=[SMEM, VMEM, VMEM],
        out_specs=[VMEM] * 3,
        compiler_params=pltpu.CompilerParams(vmem_limit_bytes=LITTLE),
        name="prepare",
    )(core[None], k, v)


def join_kernel(meta, keys_in, values_in, theirs, q, keys, values, send_q, sem):
    columns = send_q.shape[1]
    where = pl.ds(pl.multiple_of((1 - meta[0]) * columns, columns), columns)
    copy = pltpu.make_async_copy(q.at[:, where], send_q, sem)
    copy.start()
    width = theirs.shape[1]
    other = pl.ds(pl.multiple_of((1 - meta[0]) * width, width), width)
    keys[...], values[...] = keys_in[...], values_in[...]
    keys[:, other] = theirs[:width]
    values[:, other] = theirs[width:]
    copy.wait()


def join(keys, values, theirs, q, core):
    return pl.pallas_call(
        join_kernel,
        out_shape=[
            jax.ShapeDtypeStruct(keys.shape, keys.dtype),
            jax.ShapeDtypeStruct(values.shape, values.dtype),
            jax.ShapeDtypeStruct((q.shape[0], q.shape[1] // 2), q.dtype),
        ],
        in_specs=[SMEM, VMEM, VMEM, VMEM, HBM],
        out_specs=[VMEM] * 3,
        scratch_shapes=[pltpu.SemaphoreType.DMA],
        compiler_params=pltpu.CompilerParams(vmem_limit_bytes=LITTLE),
        name="join",
    )(core[None], keys, values, theirs, q)


def take_kernel(meta, whole, out, sem):
    width = out.shape[1]
    where = pl.ds(pl.multiple_of((1 - meta[CORE]) * width, width), width)
    copy = pltpu.make_async_copy(whole.at[:, where], out, sem)
    copy.start()
    copy.wait()


def take_other_half(whole, meta):
    return pl.pallas_call(
        take_kernel,
        out_shape=jax.ShapeDtypeStruct((whole.shape[0], whole.shape[1] // 2), whole.dtype),
        in_specs=[SMEM, HBM],
        out_specs=VMEM,
        scratch_shapes=[pltpu.SemaphoreType.DMA],
        compiler_params=pltpu.CompilerParams(vmem_limit_bytes=LITTLE),
        name="take",
    )(meta, whole)


def project_kernel(meta, *refs):
    pieces, (whole, other), outs, (sorted_rows,) = refs[:-7], refs[-7:-5], refs[-5:-1], refs[-1:]
    parts = len(pieces)
    rows = pieces[0].shape[0]
    for i, piece in enumerate(pieces):
        at = pl.ds(pl.multiple_of(meta[LEVELS + i] * rows, rows), rows)
        sorted_rows[at] = piece[...]
    depth = other.shape[1]
    mine = whole[:, pl.ds(pl.multiple_of(meta[CORE] * depth, depth), depth)]
    half = parts * rows // 2
    here = pl.ds(pl.multiple_of(meta[ACROSS] * half, half), half)
    there = pl.ds(pl.multiple_of((1 - meta[ACROSS]) * half, half), half)
    kept, beside, across, corner = outs
    for at, near, far in ((here, kept, beside), (there, across, corner)):
        some = sorted_rows[at]
        near[...] = dot_nt(mine, some).astype(near.dtype)
        far[...] = dot_nt(other[...], some).astype(far.dtype)


def project(pieces, whole, other, meta):
    rows = len(pieces) * pieces[0].shape[0]
    width, depth = other.shape
    block = jax.ShapeDtypeStruct((width, rows // 2), jnp.bfloat16)
    return pl.pallas_call(
        project_kernel,
        out_shape=[jax.ShapeDtypeStruct(block.shape, jnp.float32)] + [block] * 3,
        in_specs=[SMEM] + [VMEM] * (len(pieces) + 2),
        out_specs=[VMEM] * 4,
        scratch_shapes=[pltpu.VMEM((rows, depth), jnp.bfloat16)],
        compiler_params=pltpu.CompilerParams(vmem_limit_bytes=2 * LITTLE),
        cost_estimate=pl.CostEstimate(
            flops=rows * width * depth * 4, bytes_accessed=width * depth * 4, transcendentals=0
        ),
        name="project",
    )(meta, *pieces, whole, other)


def index(z, y, c):
    return (z * 2 + y) * 2 + c


def on_ring(r, chips):
    return (r, 0) if r < chips // 2 else (chips - 1 - r, 1)


def ring_perm(chips, d):
    return [
        (index(*on_ring(r, chips), c), index(*on_ring((r + d) % chips, chips), c))
        for r in range(chips)
        for c in range(2)
    ]


def ring_place(r, chips):
    r = lax.rem(r + 2 * chips, chips)
    return jnp.where(r < chips // 2, r * 2, (chips - 1 - r) * 2 + 1)


def spread(x, n):
    place = lax.axis_index("seq")
    deep = n // 4
    everyone = [(z, y, c) for z in range(deep) for y in range(2) for c in range(2)]
    z, y, c = place // 4, (place // 2) % 2, place % 2
    held = [(x, z, y, c)]
    for d in range(1, deep):
        perm = [(index(*p), index((p[0] - d) % deep, p[1], p[2])) for p in everyone]
        held.append((lax.ppermute(x, "seq", perm), lax.rem(z + d, deep), y, c))
    perm = [(index(*p), index(p[0], 1 - p[1], p[2])) for p in everyone]
    held += [(lax.ppermute(b, "seq", perm), bz, 1 - by, bc) for b, bz, by, bc in held]
    perm = [(index(*p), index(p[0], p[1], 1 - p[2])) for p in everyone]
    held += [(lax.ppermute(b, "seq", perm), bz, by, 1 - bc) for b, bz, by, bc in held]
    return [b for b, *_ in held], jnp.stack([index(bz, by, bc) for _, bz, by, bc in held])


def open_blocks(table, steps, count):
    number = lax.broadcasted_iota(jnp.int32, (*table.shape, count), 2) // BLK
    mask = jnp.any(table[:, :, None] == number, axis=1).astype(jnp.float32)
    return jnp.repeat(mask, steps, axis=0)


def whole_heads(n, q_pre, k_cache, v_cache, lengths, q_dec, k_new, v_new, block_table, w_out):
    tok = q_pre.shape[0]
    place = lax.axis_index("seq").astype(jnp.int32)
    rows, steps = q_dec.shape[0], q_dec.shape[1]
    own = rows // n
    kparts, sources = spread(k_cache.T, n)
    vparts, _ = spread(v_cache, n)
    starts = sources.astype(jnp.int32) * tok

    def mine(x):
        y = lax.dynamic_slice_in_dim(x, place * own, own, 0)
        return y.reshape(own * steps, -1) if x.ndim == 3 else y

    mask = open_blocks(mine(block_table), steps, n * tok)
    attn_own, keys, values = decode(
        mine(q_dec), mask, mine(k_new), mine(v_new), kparts, vparts, starts, steps
    )
    attn = lax.all_gather(attn_own, "seq", axis=0, tiled=True)
    flat = jnp.dot(attn, w_out, preferred_element_type=jnp.float32).astype(jnp.bfloat16)
    dec_out = lax.psum_scatter(
        flat.reshape(rows, steps, -1), "tp", scatter_dimension=0, tiled=True
    )
    zero = jnp.zeros((), jnp.int32)
    meta = jnp.stack([place * tok, zero, zero, zero])
    groups = k_cache.shape[1] // HD
    pre_out = prefill(
        q_pre, keys, values, meta, lengths, groups, q_pre.shape[1], "prefill"
    )
    return (pre_out, dec_out)


def split_heads(n, q_pre, k_cache, v_cache, lengths, q_dec, k_new, v_new, block_table, w_out):
    tok = q_pre.shape[0]
    place = lax.axis_index("seq").astype(jnp.int32)
    across = lax.axis_index("tp").astype(jnp.int32)
    core, chip = lax.rem(place, 2), lax.div(place, 2)
    chips = n // 2
    far, deep = chips // 2, chips // 2
    z, y = lax.div(chip, 2), lax.rem(chip, 2)
    r = jnp.where(y == 0, z, chips - 1 - z)
    rows, steps = q_dec.shape[0], q_dec.shape[1]
    own = rows // deep
    sibling = [(i, i ^ 1) for i in range(n)]
    everyone = [(a, b, c) for a in range(deep) for b in range(2) for c in range(2)]

    order = [0] + [o for d in range(1, far) for o in (-d, d)] + [far]
    numbers = [ring_place(r + o, chips) for o in order]
    levels = [z] + [lax.rem(z + deep - d, deep) for d in range(1, deep)]
    assert len(numbers) == LEVELS - PARTS
    meta = jnp.stack([core, chip, across] + numbers + levels).astype(jnp.int32)

    send, keys, values = prepare(k_cache, v_cache, core)
    theirs = lax.ppermute(send, "seq", sibling)
    theirs, meta = lax.optimization_barrier((theirs, meta))
    held_k, held_v = {}, {}
    held_k[0], held_v[0], send_q = join(keys, values, theirs, q_pre, core)
    near_q = lax.ppermute(send_q, "seq", sibling)

    up, down = ring_perm(chips, 1), ring_perm(chips, -1)
    early, w_near = (), w_out
    for d in range(1, far + 1):
        held_k[-d] = lax.ppermute(held_k[1 - d], "seq", up)
        held_v[d] = lax.ppermute(held_v[d - 1], "seq", down)
        if d < far:
            held_k[d] = lax.ppermute(held_k[d - 1], "seq", down)
            held_v[-d] = lax.ppermute(held_v[1 - d], "seq", up)
            sides = (-d, d)
        else:
            held_k[d] = held_k[-d]
            sides = (d,)
        if d == 1:
            state = open_sums(q_pre, near_q, (held_k[0], held_v[0]), meta, lengths)
        elif d < far:
            pair = [(held_k[o], held_v[o]) for o in (1 - d, d - 1)]
            state = stage(state, pair, 2 * d - 3, meta, lengths)
        else:
            blocks = [(held_k[o], held_v[o]) for o in order[:-1]]
            early = early_decode(early, blocks)
        for x in (held_k, held_v):
            moved, state, early = lax.optimization_barrier(([x[o] for o in sides], state, early))
            x.update(zip(sides, moved))
            if d == 1 and x is held_k:
                state, block_table = lax.optimization_barrier((state, block_table))
                early = open_requests(
                    q_dec, k_new, v_new, block_table.T, 2 * tok, own, meta
                )
        if d == 3:
            w_near, state = lax.optimization_barrier((w_near, state))
            weights = w_near.T
            w_near = lax.ppermute(take_other_half(weights, meta), "seq", sibling)
    w_near, early = lax.optimization_barrier((w_near, early))
    blocks = [(held_k[o], held_v[o]) for o in order]
    attn_own = late_decode(early, blocks, len(blocks) - 1, own, steps, meta)

    pieces = [attn_own]
    for d in range(1, deep):
        perm = [(index(*p), index((p[0] + d) % deep, p[1], p[2])) for p in everyone]
        pieces.append(lax.ppermute(attn_own, "seq", perm))
    attn_own, state = lax.optimization_barrier((attn_own, state))
    near, pre_out = finish(state, blocks, 2 * far - 3, meta, lengths)
    pieces, near, pre_out = lax.optimization_barrier((pieces, near, pre_out))
    back = lax.ppermute(near, "seq", sibling)
    pre_out = settle(pre_out, back, meta)

    total, *sent = project(pieces, weights, w_near, meta)
    got = []
    for piece, (dc, dx) in zip(sent, ((1, 0), (0, 1), (1, 1))):
        perm = [
            (i * 2 + x, (i ^ dc) * 2 + (x ^ dx)) for i in range(n) for x in range(2)
        ]
        got.append(lax.ppermute(piece, ("seq", "tp"), perm))
    got[0], pre_out = lax.optimization_barrier((got[0], pre_out))
    for piece in got:
        total = total + piece.astype(jnp.float32)
    dec_out = total.astype(jnp.bfloat16).T.reshape(deep // 2, steps, own, -1)
    return (pre_out, dec_out.transpose(0, 2, 1, 3).reshape(rows // 2, steps, -1))


def per_device(n, tp, q_pre, k_cache, v_cache, prompt_lengths, *rest):
    groups = k_cache.shape[1] // HD
    square = groups % 2 == 0 and k_cache.shape[1] == 2 * k_cache.shape[0]
    small = n * k_cache.shape[0] // BLK <= 256 and n == 2 * (LEVELS - PARTS)
    form = split_heads if square and tp == 2 and small else whole_heads
    return form(n, q_pre, k_cache, v_cache, prompt_lengths.astype(jnp.int32), *rest)


def solution(mesh):
    placed = (
        P("seq", "tp"),
        P("seq", "tp"),
        P("seq", "tp"),
        P(),
        P(None, None, "tp"),
        P(None, None, "tp"),
        P(None, None, "tp"),
        P(),
        P("tp", "seq"),
    )
    return jax.shard_map(
        functools.partial(per_device, mesh.shape["seq"], mesh.shape["tp"]),
        mesh=mesh,
        in_specs=placed,
        out_specs=(P("seq", "tp"), P("tp", None, "seq")),
        check_vma=False,
    )
```

```python
import functools
import math

import jax
import jax.numpy as jnp
from jax import lax
from jax.experimental import pallas as pl
from jax.experimental.pallas import tpu as pltpu
from jax.sharding import PartitionSpec as P

H = 56
KVH = 8
HD = 128
BLK = 64
SPAN = 512
PAIR = 2
NEG = -1e30
LEAST, MOST = 2.0**-60, 2.0**100
FACTOR = math.log2(math.e) / math.sqrt(HD)
ROOM = 16 * 1024 * 1024
LITTLE = 4 * 1024 * 1024
CORE, CHIP, ACROSS, PARTS, LEVELS = 0, 1, 2, 3, 11
BRIEF = pl.CostEstimate(flops=1024, bytes_accessed=1024, transcendentals=0)
HBM = pl.BlockSpec(memory_space=pltpu.HBM)
VMEM = pl.BlockSpec(memory_space=pltpu.VMEM)
SMEM = pl.BlockSpec(memory_space=pltpu.SMEM)


def dot_nt(a, b):
    return lax.dot_general(a, b, (((1,), (1,)), ((), ())), preferred_element_type=jnp.float32)


def dot_nn(a, b):
    return lax.dot_general(a, b, (((1,), (0,)), ((), ())), preferred_element_type=jnp.float32)


def fold(x, op):
    out = x[:, :HD]
    for i in range(1, x.shape[1] // HD):
        out = op(out, x[:, i * HD : (i + 1) * HD])
    return out


def start_of(position, lengths):
    end = jnp.int32(0)
    out = jnp.zeros_like(position)
    for i in range(lengths.shape[0]):
        end = end + lengths[i]
        out = jnp.where(position >= end, end, out)
    return out


def sound(total):
    return (jnp.min(total) >= LEAST) & (jnp.max(total) <= MOST)


def prefill_kernel(tok, heads, meta, lengths, q, keys_all, values_all, *refs):
    out, qs, peak, total, acc = refs[-5:]
    for j in range(heads):
        qs[j * tok : (j + 1) * tok] = q[:, j * HD : (j + 1) * HD]
    total[...] = jnp.zeros_like(total)
    acc[...] = jnp.zeros_like(acc)

    begin = meta[0]
    finish = begin + tok
    low = start_of(begin, lengths)
    high = start_of(finish - 1, lengths)
    blocks = lax.div(finish - low + SPAN - 1, SPAN)
    clear = lax.div(finish - high, SPAN)

    def first_of(k):
        return jnp.maximum(finish - (k + 1) * SPAN, 0)

    def load(k):
        here = pl.ds(pl.multiple_of(first_of(k), HD), SPAN)
        return keys_all[:, here], values_all[here, :]

    def allowed_in(k):
        t = begin + lax.broadcasted_iota(jnp.int32, (tok, 1), 0)
        u = first_of(k) + lax.broadcasted_iota(jnp.int32, (tok, SPAN), 1)
        last = jnp.minimum(t, finish - k * SPAN - 1)
        return (u <= last) & (u >= start_of(t, lengths))

    def keep(allowed, x, other):
        some = x.shape[0] // tok
        return jnp.where(allowed[None], x.reshape(some, tok, SPAN), other).reshape(x.shape)

    def block(k, masked):
        keys, values = load(k)
        allowed = allowed_in(k) if masked else None
        for j in range(0, heads, PAIR):
            here = slice(j * tok, min(j + PAIR, heads) * tok)
            p = jnp.exp2(dot_nn(qs[here], keys) * FACTOR)
            if masked:
                p = keep(allowed, p, 0.0)
            total[here] += fold(p, jnp.add)
            acc[here] += dot_nn(p.astype(jnp.bfloat16), values)

    block(0, True)

    @pl.loop(1, jnp.maximum(clear, 1))
    def _(k):
        block(k, False)

    @pl.loop(jnp.maximum(clear, 1), blocks)
    def _(k):
        block(k, True)

    def write():
        whole = jnp.sum(total[...], axis=1, keepdims=True)
        result = (acc[...] / whole).astype(out.dtype)
        for j in range(heads):
            out[:, j * HD : (j + 1) * HD] = result[j * tok : (j + 1) * tok]
        return whole

    fine = sound(write())

    @pl.when(jnp.logical_not(fine))
    def _():
        peak[...] = jnp.full_like(peak, NEG)
        total[...] = jnp.zeros_like(total)
        acc[...] = jnp.zeros_like(acc)

        @pl.loop(0, blocks)
        def _(k):
            keys, values = load(k)
            allowed = allowed_in(k)

            @pl.loop(0, heads)
            def _(j):
                here = pl.ds(pl.multiple_of(j * tok, tok), tok)
                s = jnp.where(allowed, dot_nn(qs[here], keys) * FACTOR, NEG)
                top = jnp.maximum(peak[here], jnp.max(s, axis=1, keepdims=True))
                p = jnp.where(allowed, jnp.exp2(s - top[:, :1]), 0.0)
                shrink = jnp.exp2(peak[here] - top)
                total[here] = total[here] * shrink + fold(p, jnp.add)
                acc[here] = acc[here] * shrink + dot_nn(p.astype(jnp.bfloat16), values)
                peak[here] = top

        write()


def prefill(q, keys, values, meta, lengths, groups, columns, name, before=None):
    tok = q.shape[0]
    count = values.shape[0]
    heads = H // KVH
    rows = heads * tok
    pairs = rows * count // 2 * groups
    extra = [] if before is None else [before]
    return pl.pallas_call(
        functools.partial(prefill_kernel, tok, heads),
        out_shape=jax.ShapeDtypeStruct((tok, columns), jnp.bfloat16),
        grid_spec=pltpu.PrefetchScalarGridSpec(
            num_scalar_prefetch=2,
            grid=(groups,),
            in_specs=[
                pl.BlockSpec((tok, heads * HD), lambda g, meta, lengths: (0, meta[1] + g)),
                pl.BlockSpec((HD, count), lambda g, meta, lengths: (meta[2] + g, 0)),
                pl.BlockSpec((count, HD), lambda g, meta, lengths: (0, meta[2] + g)),
            ]
            + [HBM] * len(extra),
            out_specs=pl.BlockSpec((tok, heads * HD), lambda g, meta, lengths: (0, meta[3] + g)),
            scratch_shapes=[
                pltpu.VMEM((rows, HD), jnp.bfloat16),
                pltpu.VMEM((rows, HD), jnp.float32),
                pltpu.VMEM((rows, HD), jnp.float32),
                pltpu.VMEM((rows, HD), jnp.float32),
            ],
        ),
        compiler_params=pltpu.CompilerParams(vmem_limit_bytes=ROOM),
        cost_estimate=pl.CostEstimate(
            flops=pairs * HD * 8, bytes_accessed=count * HD * 4 * groups, transcendentals=pairs
        ),
        input_output_aliases={} if before is None else {5: 0},
        name=name,
    )(meta, lengths, q, keys, values, *extra)


def settle_kernel(meta, piece, whole, out, sem):
    width = piece.shape[1]
    where = pl.ds(pl.multiple_of((1 - meta[CORE]) * width, width), width)
    copy = pltpu.make_async_copy(piece, out.at[:, where], sem)
    copy.start()
    copy.wait()


def settle(whole, piece, meta):
    return pl.pallas_call(
        settle_kernel,
        out_shape=jax.ShapeDtypeStruct(whole.shape, whole.dtype),
        in_specs=[SMEM, VMEM, HBM],
        out_specs=HBM,
        scratch_shapes=[pltpu.SemaphoreType.DMA],
        input_output_aliases={2: 0},
        compiler_params=pltpu.CompilerParams(vmem_limit_bytes=LITTLE),
        cost_estimate=pl.CostEstimate(flops=0, bytes_accessed=piece.size * 4, transcendentals=0),
        name="settle",
    )(meta, piece, whole)


def allowed_at(first, base, tok, length, lengths):
    t = first + lax.broadcasted_iota(jnp.int32, (tok, 1), 0)
    u = base + lax.broadcasted_iota(jnp.int32, (tok, length), 1)
    return (u <= t) & (u >= start_of(t, lengths))


def column_block(at):
    return pl.ds(pl.multiple_of(at, HD), HD)


def keys_of(upper, g):
    return upper[column_block(g * HD), :]


def values_of(lower, g):
    half = lower.shape[1] // 2
    both = [lower[:, column_block(side * half + g * HD)] for side in range(2)]
    return jnp.concatenate(both, axis=0)


def block_bias(first, base, tok, length, lengths):
    start = start_of(first, lengths)
    t = first + lax.broadcasted_iota(jnp.int32, (tok, HD), 0)
    u = base + lax.broadcasted_iota(jnp.int32, (1, length), 1)
    row = jnp.where(start_of(t, lengths) == start, 0.0, -jnp.inf)
    return [jnp.concatenate([row] * (length // HD), axis=1), jnp.where(u >= start, 0.0, -jnp.inf)]


def add_block(tok, heads, q_at, keys, values, biases, sums, old):
    length = keys.shape[1]
    turns = [(j * tok, min(PAIR, heads - j)) for j in range(0, heads, PAIR)]

    def score(at, some):
        return dot_nn(q_at(at, some * tok), keys)

    coming = score(*turns[0])
    for number, (at, some) in enumerate(turns):
        s = coming * FACTOR
        if number + 1 < len(turns):
            coming = score(*turns[number + 1])
        for bias in biases:
            s = (s.reshape(some, tok, length) + bias[None]).reshape(some * tok, length)
        p = jnp.exp2(s)
        more = (fold(p, jnp.add), dot_nn(p.astype(jnp.bfloat16), values))
        here = slice(at, at + some * tok)
        for i in range(2):
            sums[i][here] = more[i] if old is None else old[i][here] + more[i]


def relation(meta, part, side, tok, lengths):
    first = (meta[CHIP] * 2 + side) * tok
    base = meta[PARTS + part] * 2 * tok
    relevant = (base < first) & (meta[PARTS + part] != meta[CHIP])
    relevant = relevant & (base + 2 * tok > start_of(first, lengths))
    return relevant, base >= start_of(first + tok - 1, lengths), first, base


def postponed(meta, tok, lengths, first, end, parts):
    def count(some):
        pairs = [relation(meta, part, side, tok, lengths)[0] for part in some for side in range(2)]
        return sum(pair.astype(jnp.int32) for pair in pairs)

    here, later = count(range(first, end)), count(range(end, parts))
    return (here == 2 * (end - first)) & (here + later <= 6)


def side_rows(side, heads, tok):
    return pl.ds(pl.multiple_of(side * (heads * tok), HD), heads * tok)


def open_kernel(tok, heads, groups, meta, lengths, q, q_near, upper, lower, qs, total, acc):
    core = meta[CORE]
    rows = heads * tok
    for source, side, skip in ((q, core, core * groups * heads), (q_near, 1 - core, 0)):
        for g in range(groups):
            for j in range(heads):
                at = pl.ds(pl.multiple_of(side * rows + j * tok, HD), tok)
                qs[g, at] = source[:, column_block((skip + g * heads + j) * HD)]

    @pl.loop(0, groups)
    def _(g):
        keys, values = keys_of(upper, g), values_of(lower, g)
        for side in range(2):
            length = (side + 1) * tok
            first = (meta[CHIP] * 2 + side) * tok
            allowed = allowed_at(first, meta[CHIP] * 2 * tok, tok, length, lengths)
            here = side_rows(side, heads, tok)
            q_at = lambda at, count: qs[g, pl.ds(side * rows + at, count)]
            bias = jnp.where(allowed, 0.0, -jnp.inf)
            add_block(tok, heads, q_at, keys[:, :length], values[:length], [bias],
                      (total.at[g, here], acc.at[g, here]), None)


def open_sums(q, q_near, block, meta, lengths):
    tok = q.shape[0]
    heads = H // KVH
    groups = q_near.shape[1] // (heads * HD)
    rows = 2 * heads * tok
    sums = jax.ShapeDtypeStruct((groups, rows, HD), jnp.float32)
    pairs = groups * rows * tok * 2
    return pl.pallas_call(
        functools.partial(open_kernel, tok, heads, groups),
        out_shape=[jax.ShapeDtypeStruct((groups, rows, HD), jnp.bfloat16), sums, sums],
        in_specs=[SMEM, SMEM, VMEM, VMEM, VMEM, VMEM],
        out_specs=[VMEM] * 3,
        compiler_params=pltpu.CompilerParams(vmem_limit_bytes=2 * LITTLE),
        cost_estimate=BRIEF,
        name="open",
    )(meta, lengths, q, q_near, *block)


def stage_body(tok, heads, groups, first_part, wait, meta, lengths, qs, before, pair, total, acc):
    later = False
    if wait:
        later = postponed(meta, tok, lengths, first_part, first_part + 2, LEVELS - PARTS)
    for which in range(2):
        upper, lower = pair[2 * which], pair[2 * which + 1]

        @pl.loop(0, 2 * groups)
        def _(step):
            g, side = lax.div(step, 2), lax.rem(step, 2)
            relevant, clear, first, base = relation(meta, first_part + which, side, tok, lengths)
            relevant = relevant & jnp.logical_not(later)
            here = side_rows(side, heads, tok)
            sums = (total.at[g, here], acc.at[g, here])
            old = sums if which else [ref.at[g, here] for ref in before]
            at = side * (heads * tok)
            q_at = lambda off, count: qs[g, pl.ds(pl.multiple_of(at + off, HD), count)]

            @pl.when(relevant & clear)
            def _():
                add_block(tok, heads, q_at, keys_of(upper, g), values_of(lower, g), [], sums, old)

            @pl.when(relevant & jnp.logical_not(clear))
            def _():
                biases = block_bias(first, base, tok, 2 * tok, lengths)
                add_block(
                    tok, heads, q_at, keys_of(upper, g), values_of(lower, g), biases, sums, old
                )

            if which == 0:

                @pl.when(jnp.logical_not(relevant))
                def _():
                    for i in range(2):
                        sums[i][...] = old[i][...]


def stage_kernel(tok, heads, groups, first_part, wait, meta, lengths, qs, total_in, acc_in, *refs):
    pair, (total, acc) = refs[:4], refs[4:]
    before = (total_in, acc_in)
    stage_body(
        tok, heads, groups, first_part, wait, meta, lengths, qs, before, pair, total, acc
    )


def stage(state, pair, first_part, wait, meta, lengths):
    qs, total, acc = state
    groups, rows, unused = qs.shape
    flat = [x for block in pair for x in block]
    tok = flat[0].shape[1] // 2
    new = pl.pallas_call(
        functools.partial(stage_kernel, tok, rows // (2 * tok), groups, first_part, wait),
        out_shape=[jax.ShapeDtypeStruct(x.shape, x.dtype) for x in (total, acc)],
        in_specs=[SMEM, SMEM] + [VMEM] * 7,
        out_specs=[VMEM] * 2,
        input_output_aliases={3: 0, 4: 1},
        compiler_params=pltpu.CompilerParams(vmem_limit_bytes=ROOM),
        cost_estimate=BRIEF,
        name=f"stage{first_part}",
    )(meta, lengths, qs, total, acc, *flat)
    return qs, *new


def finish_kernel(tok, heads, groups, done, meta, lengths, qs, total, acc, *refs):
    near, out, held_k, held_v, peak, total_now, acc_now, result, sem = refs[-9:]
    parts = held_k.shape[0]
    rows = heads * tok
    core = meta[CORE]

    def fill(first):
        for i in range(first, parts):
            held_k[i], held_v[i] = refs[2 * i][...], refs[2 * i + 1][...]

    def turn_of(step):
        turn, g = lax.div(step, groups), lax.rem(step, groups)
        side = jnp.where(turn == 0, 1 - core, core)
        at = side * rows
        q_at = lambda off, count: qs[g, pl.ds(pl.multiple_of(at + off, HD), count)]
        return turn, g, side, q_at

    def write(turn, g):
        whole = jnp.sum(total_now[...], axis=1, keepdims=True)
        value = (acc_now[...] / whole).astype(result.dtype)
        for j in range(heads):
            result[turn, :, column_block((g * heads + j) * HD)] = value[j * tok : (j + 1) * tok]
        return sound(whole)

    def one_turn(step, fine):
        turn, g, side, q_at = turn_of(step)
        here = side_rows(side, heads, tok)
        total_now[...] = total[g, here]
        acc_now[...] = acc[g, here]

        @pl.loop(done, parts)
        def _(i):
            relevant, clear, first, base = relation(meta, i, side, tok, lengths)
            relevant = relevant & ((i >= done + 2) | later)
            upper, lower = held_k.at[i], held_v.at[i]
            sums = (total_now, acc_now)

            @pl.when(relevant & clear)
            def _():
                add_block(tok, heads, q_at, keys_of(upper, g), values_of(lower, g), [], sums, sums)

            @pl.when(relevant & jnp.logical_not(clear))
            def _():
                biases = block_bias(first, base, tok, 2 * tok, lengths)
                add_block(
                    tok, heads, q_at, keys_of(upper, g), values_of(lower, g), biases, sums, sums
                )

        return fine & write(turn, g).astype(jnp.int32)

    later = postponed(meta, tok, lengths, done, done + 2, parts)
    fill(done)
    fine = lax.fori_loop(0, 2 * groups, one_turn, jnp.int32(1))

    @pl.when(fine == 0)
    def _():
        fill(0)

        @pl.loop(0, 2 * groups)
        def _(step):
            turn, g, side, q_at = turn_of(step)
            first = (meta[CHIP] * 2 + side) * tok
            peak[...] = jnp.full_like(peak, NEG)
            total_now[...] = jnp.zeros_like(total_now)
            acc_now[...] = jnp.zeros_like(acc_now)

            @pl.loop(0, parts * heads)
            def _(step):
                i, j = lax.div(step, heads), lax.rem(step, heads)
                keys, values = keys_of(held_k.at[i], g), values_of(held_v.at[i], g)
                allowed = allowed_at(first, meta[PARTS + i] * 2 * tok, tok, 2 * tok, lengths)
                mine = pl.ds(pl.multiple_of(j * tok, tok), tok)
                s = jnp.where(allowed, dot_nn(q_at(j * tok, tok), keys) * FACTOR, NEG)
                top = jnp.maximum(peak[mine], jnp.max(s, axis=1, keepdims=True))
                p = jnp.where(allowed, jnp.exp2(s - top[:, :1]), 0.0)
                shrink = jnp.exp2(peak[mine] - top)
                total_now[mine] = total_now[mine] * shrink + fold(p, jnp.add)
                acc_now[mine] = acc_now[mine] * shrink + dot_nn(p.astype(jnp.bfloat16), values)
                peak[mine] = top

            write(turn, g)

    width = near.shape[1]
    where = pl.ds(pl.multiple_of(core * width, width), width)
    copy = pltpu.make_async_copy(result.at[1], out.at[:, where], sem)
    copy.start()
    near[...] = result[0]
    copy.wait()


def finish(state, blocks, done, meta, lengths):
    qs, total, acc = state
    groups, rows, unused = qs.shape
    flat = [x for block in blocks for x in block]
    tok = flat[0].shape[1] // 2
    heads = rows // (2 * tok)
    width = groups * heads * HD
    sums = pltpu.VMEM((heads * tok, HD), jnp.float32)
    return pl.pallas_call(
        functools.partial(finish_kernel, tok, heads, groups, done),
        out_shape=[
            jax.ShapeDtypeStruct((tok, width), jnp.bfloat16),
            jax.ShapeDtypeStruct((tok, 2 * width), jnp.bfloat16),
        ],
        in_specs=[SMEM, SMEM] + [VMEM] * (3 + len(flat)),
        out_specs=[VMEM, HBM],
        scratch_shapes=[
            *[pltpu.VMEM((len(blocks), *x.shape), x.dtype) for x in blocks[0]],
            sums, sums, sums,
            pltpu.VMEM((2, tok, width), jnp.bfloat16),
            pltpu.SemaphoreType.DMA,
        ],
        compiler_params=pltpu.CompilerParams(vmem_limit_bytes=ROOM),
        cost_estimate=pl.CostEstimate(
            flops=groups * rows * tok * HD * 8, bytes_accessed=tok * width * 4,
            transcendentals=groups * rows * tok * 2,
        ),
        name="finish",
    )(meta, lengths, qs, total, acc, *flat)


def request_sums(query, keys, values, bias):
    s = dot_nn(query, keys) * FACTOR
    p = jnp.exp2((s.reshape(-1, *bias.shape) + bias[None]).reshape(s.shape))
    return fold(p, jnp.add), dot_nn(p.astype(jnp.bfloat16), values)


def fresh_scores(query, newk, own):
    s = dot_nt(query, newk) * FACTOR
    size = newk.shape[0]
    row = lax.broadcasted_iota(jnp.int32, (size, size), 0)
    col = lax.broadcasted_iota(jnp.int32, (size, size), 1)
    ok = (lax.rem(row, own) == lax.rem(col, own)) & (lax.div(col, own) <= lax.div(row, own))
    return s.reshape(-1, size, size), ok


def request_copies(own, meta, sources, held, sems):
    requests = pl.ds(lax.div(meta[CHIP], 2) * own, own)
    copies = []
    for i, (source, target) in enumerate(zip(sources, held)):
        width = target.shape[2]
        where = pl.ds(pl.multiple_of(meta[CORE] * width, width), width)
        copies.append(pltpu.make_async_copy(source.at[requests, :, where], target, sems.at[i]))
    return copies


def requests_body(own, heads, groups, length, meta, table, total, acc, query, newk, newv, mask, q3, k3, v3):
    steps = q3.shape[1]
    level = lax.div(meta[CHIP], 2)
    pick = lax.broadcasted_iota(jnp.int32, (own, table.shape[1]), 1) - level * own
    pick = (pick == lax.broadcasted_iota(jnp.int32, pick.shape, 0)).astype(jnp.float32)
    rows = dot_nt(pick.astype(jnp.bfloat16), table[...].astype(jnp.float32).astype(jnp.bfloat16))
    lane = lax.div(lax.broadcasted_iota(jnp.int32, (own, length), 1), BLK)
    for i in range(mask.shape[1] // length):
        number = (lane + meta[PARTS + i] * (length // BLK)).astype(jnp.float32)
        hit = rows[:, :1] == number
        for j in range(1, rows.shape[1]):
            hit = hit | (rows[:, j : j + 1] == number)
        mask[:, i * length : (i + 1) * length] = jnp.where(hit, 0.0, -jnp.inf)
    for s in range(steps):
        for g in range(groups):
            col = slice(g * HD, (g + 1) * HD)
            at = slice(s * own, (s + 1) * own)
            newk[at, col] = k3[:, s, col]
            newv[at, col] = v3[:, s, col]
            for j in range(heads):
                first = (g * heads + j) * HD
                row = (j * steps + s) * own
                query[g, row : row + own] = q3[:, s, first : first + HD]

    @pl.loop(0, groups)
    def _(g):
        col = column_block(g * HD)
        s, ok = fresh_scores(query[g], newk[:, col], own)
        p = jnp.where(ok[None], jnp.exp2(s), 0.0).reshape(-1, s.shape[2])
        first = jnp.sum(p, axis=1, keepdims=True)
        lead = lax.broadcasted_iota(jnp.int32, (p.shape[0], HD), 1) == 0
        total[g] = jnp.where(lead, first, 0.0)
        acc[g] = dot_nn(p.astype(jnp.bfloat16), newv[:, col])


def requests_kernel(own, heads, groups, length, meta, *refs):
    sources, table, state, (q3, k3, v3, sems) = refs[:3], refs[3], refs[4:10], refs[10:]
    copies = request_copies(own, meta, sources, (q3, k3, v3), sems)
    for copy in copies:
        copy.start()
    for copy in copies:
        copy.wait()
    requests_body(own, heads, groups, length, meta, table, *state, q3, k3, v3)


def open_requests(q_dec, k_new, v_new, table, length, own, meta):
    heads = H // KVH
    steps = q_dec.shape[1]
    width = k_new.shape[2] // 2
    groups = width // HD
    rows = heads * own * steps
    sums = jax.ShapeDtypeStruct((groups, rows, HD), jnp.float32)
    new = jax.ShapeDtypeStruct((own * steps, width), jnp.bfloat16)
    return pl.pallas_call(
        functools.partial(requests_kernel, own, heads, groups, length),
        out_shape=[
            sums, sums, jax.ShapeDtypeStruct((groups, rows, HD), jnp.bfloat16), new, new,
            jax.ShapeDtypeStruct((own, (LEVELS - PARTS) * length), jnp.float32),
        ],
        in_specs=[SMEM] + [HBM] * 3 + [VMEM],
        out_specs=[VMEM] * 6,
        scratch_shapes=[
            pltpu.VMEM((own, steps, groups * heads * HD), jnp.bfloat16),
            pltpu.VMEM((own, steps, width), jnp.bfloat16),
            pltpu.VMEM((own, steps, width), jnp.bfloat16),
            pltpu.SemaphoreType.DMA((3,)),
        ],
        compiler_params=pltpu.CompilerParams(vmem_limit_bytes=LITTLE),
        cost_estimate=BRIEF,
        name="requests",
    )(meta, q_dec, k_new, v_new, table)


def early_kernel(groups, total_in, acc_in, query, mask, *refs):
    total, acc = refs[-2:]
    length = refs[0].shape[1]

    @pl.loop(0, groups)
    def _(g):
        sums = [total_in[g], acc_in[g]]
        for i in range(len(refs) // 2 - 1):
            bias = mask[:, i * length : (i + 1) * length]
            keys, values = keys_of(refs[2 * i], g), values_of(refs[2 * i + 1], g)
            more = request_sums(query[g], keys, values, bias)
            sums = [x + y for x, y in zip(sums, more)]
        total[g], acc[g] = sums


def early_decode(state, blocks):
    total, acc, query, newk, newv, mask = state
    groups, rows, unused = query.shape
    flat = [x for block in blocks for x in block]
    sums = jax.ShapeDtypeStruct(total.shape, total.dtype)
    new = pl.pallas_call(
        functools.partial(early_kernel, groups),
        out_shape=[sums, sums],
        in_specs=[VMEM] * (4 + len(flat)),
        out_specs=[VMEM] * 2,
        input_output_aliases={0: 0, 1: 1},
        compiler_params=pltpu.CompilerParams(vmem_limit_bytes=2 * LITTLE),
        cost_estimate=BRIEF,
        name="early_decode",
    )(total, acc, query, mask, *flat)
    return [*new, query, newk, newv, mask]


def late_kernel(own, steps, heads, groups, done, meta, total, acc, query, newk, newv, mask, *refs):
    parts, out = len(refs) // 2, refs[-1]
    length = refs[0].shape[1]
    size = own * steps

    def write(g, sums, whole):
        result = (sums / whole).astype(out.dtype)
        for j in range(heads):
            out[:, column_block((g * heads + j) * HD)] = result[j * size : (j + 1) * size]

    def one_group(g, fine):
        sums = [total[g], acc[g]]
        for i in range(done, parts):
            bias = mask[:, i * length : (i + 1) * length]
            keys, values = keys_of(refs[2 * i], g), values_of(refs[2 * i + 1], g)
            more = request_sums(query[g], keys, values, bias)
            sums = [x + y for x, y in zip(sums, more)]
        whole = jnp.sum(sums[0], axis=1, keepdims=True)
        write(g, sums[1], whole)
        return fine & sound(whole).astype(jnp.int32)

    fine = lax.fori_loop(0, groups, one_group, jnp.int32(1))

    @pl.when(fine == 0)
    def _():
        @pl.loop(0, groups)
        def _(g):
            col = column_block(g * HD)
            fresh, ok = fresh_scores(query[g], newk[:, col], own)
            fresh = jnp.where(ok[None], fresh, NEG).reshape(-1, size)
            top = jnp.max(fresh, axis=1, keepdims=True)
            p = jnp.exp2(fresh - top)
            whole = jnp.sum(p, axis=1, keepdims=True)
            sums = dot_nn(p.astype(jnp.bfloat16), newv[:, col])
            for i in range(parts):
                s = dot_nn(query[g], keys_of(refs[2 * i], g)) * FACTOR
                open_to = mask[:, i * length : (i + 1) * length] >= 0
                s = jnp.where(open_to[None], s.reshape(-1, own, length), NEG).reshape(s.shape)
                higher = jnp.maximum(top, jnp.max(s, axis=1, keepdims=True))
                p = jnp.exp2(s - higher)
                shrink = jnp.exp2(top - higher)
                whole = whole * shrink + jnp.sum(p, axis=1, keepdims=True)
                sums = sums * shrink + dot_nn(p.astype(jnp.bfloat16), values_of(refs[2 * i + 1], g))
                top = higher
            write(g, sums, whole)


def late_decode(early, blocks, done, own, steps, meta):
    groups, rows, unused = early[0].shape
    heads = H // KVH
    flat = [x for block in blocks for x in block]
    parts, length = len(blocks), flat[0].shape[1]
    pairs = groups * rows * (parts - done) * length
    return pl.pallas_call(
        functools.partial(late_kernel, own, steps, heads, groups, done),
        out_shape=jax.ShapeDtypeStruct((own * steps, groups * heads * HD), jnp.bfloat16),
        in_specs=[SMEM] + [VMEM] * (len(early) + len(flat)),
        out_specs=VMEM,
        compiler_params=pltpu.CompilerParams(vmem_limit_bytes=ROOM),
        cost_estimate=pl.CostEstimate(
            flops=pairs * HD * 8, bytes_accessed=rows * HD, transcendentals=pairs
        ),
        name="late_decode",
    )(meta, *early, *flat)


def decode_kernel(parts, steps, heads, groups, starts, q, mask, newk, newv, *refs):
    kheld, vheld = refs[:parts], refs[parts : 2 * parts]
    out, kall, vall, sems, scores = refs[2 * parts :]
    own = q.shape[0]
    rows = heads * own
    length = kheld[0].shape[1]
    copies = []
    for i in range(parts):
        where = pl.ds(pl.multiple_of(starts[i], HD), length)
        copies.append(pltpu.make_async_copy(kheld[i], kall.at[:, where], sems.at[2 * i]))
        copies.append(pltpu.make_async_copy(vheld[i], vall.at[where], sems.at[2 * i + 1]))
    for copy in copies:
        copy.start()
    row = lax.broadcasted_iota(jnp.int32, (own, own), 0)
    col = lax.broadcasted_iota(jnp.int32, (own, own), 1)
    fresh_ok = (lax.div(row, steps) == lax.div(col, steps)) & (col <= row)

    def columns(g):
        return slice(g * HD, (g + 1) * HD)

    def stacked(g):
        first = g * heads
        slices = [q[:, (first + j) * HD : (first + j + 1) * HD] for j in range(heads)]
        return jnp.concatenate([x.astype(jnp.float32) for x in slices], 0).astype(jnp.bfloat16)

    def keep(allowed, x, other):
        y = x.reshape(heads, own, x.shape[1])
        return jnp.where(allowed[None], y, other).reshape(x.shape)

    def open_to(i):
        return mask[:, pl.ds(pl.multiple_of(starts[i], HD), length)] > 0

    def write(g, acc, whole):
        result = acc / whole
        for j in range(heads):
            out[:, (g * heads + j) * HD : (g * heads + j + 1) * HD] = result[
                j * own : (j + 1) * own
            ].astype(out.dtype)

    fine = None
    for g in range(groups):
        query = stacked(g)
        p = keep(fresh_ok, jnp.exp2(dot_nt(query, newk[:, columns(g)]) * FACTOR), 0.0)
        whole = jnp.sum(p, axis=1, keepdims=True)
        acc = dot_nn(p.astype(jnp.bfloat16), newv[:, columns(g)])
        total = jnp.zeros((rows, HD), jnp.float32)
        for i in range(parts):
            p = jnp.exp2(dot_nn(query, kheld[i][columns(g)]) * FACTOR)
            p = keep(open_to(i), p, 0.0)
            total = total + fold(p, jnp.add)
            acc = acc + dot_nn(p.astype(jnp.bfloat16), vheld[i][:, columns(g)])
        whole = whole + jnp.sum(total, axis=1, keepdims=True)
        write(g, acc, whole)
        fine = sound(whole) if fine is None else fine & sound(whole)

    @pl.when(jnp.logical_not(fine))
    def _():
        for g in range(groups):
            query = stacked(g)
            fresh = keep(fresh_ok, dot_nt(query, newk[:, columns(g)]) * FACTOR, NEG)
            top = jnp.max(fresh, axis=1, keepdims=True)
            for i in range(parts):
                s = keep(open_to(i), dot_nn(query, kheld[i][columns(g)]) * FACTOR, NEG)
                scores[:, i * length : (i + 1) * length] = s
                top = jnp.maximum(top, jnp.max(s, axis=1, keepdims=True))
            p = jnp.exp2(fresh - top)
            whole = jnp.sum(p, axis=1, keepdims=True)
            acc = dot_nn(p.astype(jnp.bfloat16), newv[:, columns(g)])
            for i in range(parts):
                p = jnp.exp2(scores[:, i * length : (i + 1) * length] - top)
                whole = whole + jnp.sum(p, axis=1, keepdims=True)
                acc = acc + dot_nn(p.astype(jnp.bfloat16), vheld[i][:, columns(g)])
            write(g, acc, whole)

    for copy in copies:
        copy.wait()


def decode(q, mask, newk, newv, kparts, vparts, starts, steps):
    own = q.shape[0]
    parts = len(kparts)
    length, width = vparts[0].shape
    count = parts * length
    heads = H // KVH
    groups = width // HD
    rows = heads * own
    pairs = groups * rows * count
    return pl.pallas_call(
        functools.partial(decode_kernel, parts, steps, heads, groups),
        out_shape=[
            jax.ShapeDtypeStruct(q.shape, jnp.bfloat16),
            jax.ShapeDtypeStruct((width, count), jnp.bfloat16),
            jax.ShapeDtypeStruct((count, width), jnp.bfloat16),
        ],
        grid_spec=pltpu.PrefetchScalarGridSpec(
            num_scalar_prefetch=1,
            grid=(),
            in_specs=[VMEM] * (4 + 2 * parts),
            out_specs=[VMEM, HBM, HBM],
            scratch_shapes=[
                pltpu.SemaphoreType.DMA((2 * parts,)),
                pltpu.VMEM((rows, count), jnp.float32),
            ],
        ),
        compiler_params=pltpu.CompilerParams(vmem_limit_bytes=ROOM),
        cost_estimate=pl.CostEstimate(
            flops=pairs * HD * 4, bytes_accessed=count * width * 4, transcendentals=pairs
        ),
        name="decode",
    )(starts, q, mask, newk, newv, *kparts, *vparts)


def prepare_kernel(meta, k, v, send, keys, values):
    width = k.shape[1] // 2
    mine = pl.ds(pl.multiple_of(meta[0] * width, width), width)
    other = pl.ds(pl.multiple_of((1 - meta[0]) * width, width), width)
    send[:width] = k[:, other].astype(jnp.float32).T.astype(send.dtype)
    send[width:] = v[:, other]
    keys[:, mine] = k[:, mine].astype(jnp.float32).T.astype(keys.dtype)
    values[:, mine] = v[:, mine]


def prepare(k, v, core):
    tok, width = k.shape[0], k.shape[1] // 2
    assert tok == width
    block = jax.ShapeDtypeStruct((width, 2 * tok), k.dtype)
    return pl.pallas_call(
        prepare_kernel,
        out_shape=[jax.ShapeDtypeStruct((2 * tok, width), k.dtype), block, block],
        in_specs=[SMEM, VMEM, VMEM],
        out_specs=[VMEM] * 3,
        compiler_params=pltpu.CompilerParams(vmem_limit_bytes=LITTLE),
        name="prepare",
    )(core[None], k, v)


def join_kernel(meta, keys_in, values_in, theirs, q, keys, values, send_q, sem):
    columns = send_q.shape[1]
    where = pl.ds(pl.multiple_of((1 - meta[0]) * columns, columns), columns)
    copy = pltpu.make_async_copy(q.at[:, where], send_q, sem)
    copy.start()
    width = theirs.shape[1]
    other = pl.ds(pl.multiple_of((1 - meta[0]) * width, width), width)
    keys[...], values[...] = keys_in[...], values_in[...]
    keys[:, other] = theirs[:width]
    values[:, other] = theirs[width:]
    copy.wait()


def join(keys, values, theirs, q, core):
    return pl.pallas_call(
        join_kernel,
        out_shape=[
            jax.ShapeDtypeStruct(keys.shape, keys.dtype),
            jax.ShapeDtypeStruct(values.shape, values.dtype),
            jax.ShapeDtypeStruct((q.shape[0], q.shape[1] // 2), q.dtype),
        ],
        in_specs=[SMEM, VMEM, VMEM, VMEM, HBM],
        out_specs=[VMEM] * 3,
        scratch_shapes=[pltpu.SemaphoreType.DMA],
        compiler_params=pltpu.CompilerParams(vmem_limit_bytes=LITTLE),
        name="join",
    )(core[None], keys, values, theirs, q)


def take_kernel(meta, whole, out, sem):
    width = out.shape[1]
    where = pl.ds(pl.multiple_of((1 - meta[CORE]) * width, width), width)
    copy = pltpu.make_async_copy(whole.at[:, where], out, sem)
    copy.start()
    copy.wait()


def take_other_half(whole, meta):
    return pl.pallas_call(
        take_kernel,
        out_shape=jax.ShapeDtypeStruct((whole.shape[0], whole.shape[1] // 2), whole.dtype),
        in_specs=[SMEM, HBM],
        out_specs=VMEM,
        scratch_shapes=[pltpu.SemaphoreType.DMA],
        compiler_params=pltpu.CompilerParams(vmem_limit_bytes=LITTLE),
        name="take",
    )(meta, whole)


def project_kernel(meta, *refs):
    pieces, (whole, other), outs, (sorted_rows,) = refs[:-7], refs[-7:-5], refs[-5:-1], refs[-1:]
    parts = len(pieces)
    rows = pieces[0].shape[0]
    for i, piece in enumerate(pieces):
        at = pl.ds(pl.multiple_of(meta[LEVELS + i] * rows, rows), rows)
        sorted_rows[at] = piece[...]
    depth = other.shape[1]
    mine = whole[:, pl.ds(pl.multiple_of(meta[CORE] * depth, depth), depth)]
    half = parts * rows // 2
    here = pl.ds(pl.multiple_of(meta[ACROSS] * half, half), half)
    there = pl.ds(pl.multiple_of((1 - meta[ACROSS]) * half, half), half)
    kept, beside, across, corner = outs
    for at, near, far in ((here, kept, beside), (there, across, corner)):
        some = sorted_rows[at]
        near[...] = dot_nt(mine, some).astype(near.dtype)
        far[...] = dot_nt(other[...], some).astype(far.dtype)


def project(pieces, whole, other, meta):
    rows = len(pieces) * pieces[0].shape[0]
    width, depth = other.shape
    block = jax.ShapeDtypeStruct((width, rows // 2), jnp.bfloat16)
    return pl.pallas_call(
        project_kernel,
        out_shape=[jax.ShapeDtypeStruct(block.shape, jnp.float32)] + [block] * 3,
        in_specs=[SMEM] + [VMEM] * (len(pieces) + 2),
        out_specs=[VMEM] * 4,
        scratch_shapes=[pltpu.VMEM((rows, depth), jnp.bfloat16)],
        compiler_params=pltpu.CompilerParams(vmem_limit_bytes=2 * LITTLE),
        cost_estimate=pl.CostEstimate(
            flops=rows * width * depth * 4, bytes_accessed=width * depth * 4, transcendentals=0
        ),
        name="project",
    )(meta, *pieces, whole, other)


def index(z, y, c):
    return (z * 2 + y) * 2 + c


def on_ring(r, chips):
    return (r, 0) if r < chips // 2 else (chips - 1 - r, 1)


def ring_perm(chips, d):
    return [
        (index(*on_ring(r, chips), c), index(*on_ring((r + d) % chips, chips), c))
        for r in range(chips)
        for c in range(2)
    ]


def ring_place(r, chips):
    r = lax.rem(r + 2 * chips, chips)
    return jnp.where(r < chips // 2, r * 2, (chips - 1 - r) * 2 + 1)


def spread(x, n):
    place = lax.axis_index("seq")
    deep = n // 4
    everyone = [(z, y, c) for z in range(deep) for y in range(2) for c in range(2)]
    z, y, c = place // 4, (place // 2) % 2, place % 2
    held = [(x, z, y, c)]
    for d in range(1, deep):
        perm = [(index(*p), index((p[0] - d) % deep, p[1], p[2])) for p in everyone]
        held.append((lax.ppermute(x, "seq", perm), lax.rem(z + d, deep), y, c))
    perm = [(index(*p), index(p[0], 1 - p[1], p[2])) for p in everyone]
    held += [(lax.ppermute(b, "seq", perm), bz, 1 - by, bc) for b, bz, by, bc in held]
    perm = [(index(*p), index(p[0], p[1], 1 - p[2])) for p in everyone]
    held += [(lax.ppermute(b, "seq", perm), bz, by, 1 - bc) for b, bz, by, bc in held]
    return [b for b, *_ in held], jnp.stack([index(bz, by, bc) for _, bz, by, bc in held])


def open_blocks(table, steps, count):
    number = lax.broadcasted_iota(jnp.int32, (*table.shape, count), 2) // BLK
    mask = jnp.any(table[:, :, None] == number, axis=1).astype(jnp.float32)
    return jnp.repeat(mask, steps, axis=0)


def whole_heads(n, q_pre, k_cache, v_cache, lengths, q_dec, k_new, v_new, block_table, w_out):
    tok = q_pre.shape[0]
    place = lax.axis_index("seq").astype(jnp.int32)
    rows, steps = q_dec.shape[0], q_dec.shape[1]
    own = rows // n
    kparts, sources = spread(k_cache.T, n)
    vparts, _ = spread(v_cache, n)
    starts = sources.astype(jnp.int32) * tok

    def mine(x):
        y = lax.dynamic_slice_in_dim(x, place * own, own, 0)
        return y.reshape(own * steps, -1) if x.ndim == 3 else y

    mask = open_blocks(mine(block_table), steps, n * tok)
    attn_own, keys, values = decode(
        mine(q_dec), mask, mine(k_new), mine(v_new), kparts, vparts, starts, steps
    )
    attn = lax.all_gather(attn_own, "seq", axis=0, tiled=True)
    flat = jnp.dot(attn, w_out, preferred_element_type=jnp.float32).astype(jnp.bfloat16)
    dec_out = lax.psum_scatter(
        flat.reshape(rows, steps, -1), "tp", scatter_dimension=0, tiled=True
    )
    zero = jnp.zeros((), jnp.int32)
    meta = jnp.stack([place * tok, zero, zero, zero])
    groups = k_cache.shape[1] // HD
    pre_out = prefill(
        q_pre, keys, values, meta, lengths, groups, q_pre.shape[1], "prefill"
    )
    return (pre_out, dec_out)


def split_heads(n, q_pre, k_cache, v_cache, lengths, q_dec, k_new, v_new, block_table, w_out):
    tok = q_pre.shape[0]
    place = lax.axis_index("seq").astype(jnp.int32)
    across = lax.axis_index("tp").astype(jnp.int32)
    core, chip = lax.rem(place, 2), lax.div(place, 2)
    chips = n // 2
    far, deep = chips // 2, chips // 2
    z, y = lax.div(chip, 2), lax.rem(chip, 2)
    r = jnp.where(y == 0, z, chips - 1 - z)
    rows, steps = q_dec.shape[0], q_dec.shape[1]
    own = rows // deep
    sibling = [(i, i ^ 1) for i in range(n)]
    everyone = [(a, b, c) for a in range(deep) for b in range(2) for c in range(2)]

    order = [0] + [o for d in range(1, far) for o in (-d, d)] + [far]
    numbers = [ring_place(r + o, chips) for o in order]
    levels = [z] + [lax.rem(z + deep - d, deep) for d in range(1, deep)]
    assert len(numbers) == LEVELS - PARTS
    meta = jnp.stack([core, chip, across] + numbers + levels).astype(jnp.int32)

    send, keys, values = prepare(k_cache, v_cache, core)
    theirs = lax.ppermute(send, "seq", sibling)
    theirs, meta = lax.optimization_barrier((theirs, meta))
    held_k, held_v = {}, {}
    held_k[0], held_v[0], send_q = join(keys, values, theirs, q_pre, core)
    near_q = lax.ppermute(send_q, "seq", sibling)

    up, down = ring_perm(chips, 1), ring_perm(chips, -1)
    early, w_near = (), w_out
    for d in range(1, far + 1):
        held_k[-d] = lax.ppermute(held_k[1 - d], "seq", up)
        held_v[d] = lax.ppermute(held_v[d - 1], "seq", down)
        if d < far:
            held_k[d] = lax.ppermute(held_k[d - 1], "seq", down)
            held_v[-d] = lax.ppermute(held_v[1 - d], "seq", up)
            sides = (-d, d)
        else:
            held_k[d] = held_k[-d]
            sides = (d,)
        if d == 1:
            state = open_sums(q_pre, near_q, (held_k[0], held_v[0]), meta, lengths)
        elif d < far:
            pair = [(held_k[o], held_v[o]) for o in (1 - d, d - 1)]
            state = stage(state, pair, 2 * d - 3, d == far - 1, meta, lengths)
        else:
            blocks = [(held_k[o], held_v[o]) for o in order[:-1]]
            early = early_decode(early, blocks)
        for x in (held_k, held_v):
            moved, state, early = lax.optimization_barrier(([x[o] for o in sides], state, early))
            x.update(zip(sides, moved))
            if d == 1 and x is held_k:
                state, block_table = lax.optimization_barrier((state, block_table))
                early = open_requests(
                    q_dec, k_new, v_new, block_table.T, 2 * tok, own, meta
                )
        if d == 3:
            w_near, state = lax.optimization_barrier((w_near, state))
            weights = w_near.T
            w_near = lax.ppermute(take_other_half(weights, meta), "seq", sibling)
    w_near, early = lax.optimization_barrier((w_near, early))
    blocks = [(held_k[o], held_v[o]) for o in order]
    attn_own = late_decode(early, blocks, len(blocks) - 1, own, steps, meta)

    pieces = [attn_own]
    for d in range(1, deep):
        perm = [(index(*p), index((p[0] + d) % deep, p[1], p[2])) for p in everyone]
        pieces.append(lax.ppermute(attn_own, "seq", perm))
    attn_own, state = lax.optimization_barrier((attn_own, state))
    near, pre_out = finish(state, blocks, 2 * far - 5, meta, lengths)
    pieces, near, pre_out = lax.optimization_barrier((pieces, near, pre_out))
    back = lax.ppermute(near, "seq", sibling)
    pre_out = settle(pre_out, back, meta)

    total, *sent = project(pieces, weights, w_near, meta)
    got = []
    for piece, (dc, dx) in zip(sent, ((1, 0), (0, 1), (1, 1))):
        perm = [
            (i * 2 + x, (i ^ dc) * 2 + (x ^ dx)) for i in range(n) for x in range(2)
        ]
        got.append(lax.ppermute(piece, ("seq", "tp"), perm))
    got[0], pre_out = lax.optimization_barrier((got[0], pre_out))
    for piece in got:
        total = total + piece.astype(jnp.float32)
    dec_out = total.astype(jnp.bfloat16).T.reshape(deep // 2, steps, own, -1)
    return (pre_out, dec_out.transpose(0, 2, 1, 3).reshape(rows // 2, steps, -1))


def per_device(n, tp, q_pre, k_cache, v_cache, prompt_lengths, *rest):
    groups = k_cache.shape[1] // HD
    square = groups % 2 == 0 and k_cache.shape[1] == 2 * k_cache.shape[0]
    small = n * k_cache.shape[0] // BLK <= 256 and n == 2 * (LEVELS - PARTS)
    form = split_heads if square and tp == 2 and small else whole_heads
    return form(n, q_pre, k_cache, v_cache, prompt_lengths.astype(jnp.int32), *rest)


def solution(mesh):
    placed = (
        P("seq", "tp"),
        P("seq", "tp"),
        P("seq", "tp"),
        P(),
        P(None, None, "tp"),
        P(None, None, "tp"),
        P(None, None, "tp"),
        P(),
        P("tp", "seq"),
    )
    return jax.shard_map(
        functools.partial(per_device, mesh.shape["seq"], mesh.shape["tp"]),
        mesh=mesh,
        in_specs=placed,
        out_specs=(P("seq", "tp"), P("tp", None, "seq")),
        check_vma=False,
    )
```

```python
import functools
import math

import jax
import jax.numpy as jnp
from jax import lax
from jax.experimental import pallas as pl
from jax.experimental.pallas import tpu as pltpu
from jax.sharding import PartitionSpec as P

H = 56
KVH = 8
HD = 128
BLK = 64
SPAN = 512
PAIR = 2
NEG = -1e30
LEAST, MOST = 2.0**-60, 2.0**100
FACTOR = math.log2(math.e) / math.sqrt(HD)
ROOM = 16 * 1024 * 1024
LITTLE = 4 * 1024 * 1024
CORE, CHIP, ACROSS, PARTS, LEVELS = 0, 1, 2, 3, 11
BRIEF = pl.CostEstimate(flops=1024, bytes_accessed=1024, transcendentals=0)
HBM = pl.BlockSpec(memory_space=pltpu.HBM)
VMEM = pl.BlockSpec(memory_space=pltpu.VMEM)
SMEM = pl.BlockSpec(memory_space=pltpu.SMEM)


def dot_nt(a, b):
    return lax.dot_general(a, b, (((1,), (1,)), ((), ())), preferred_element_type=jnp.float32)


def dot_nn(a, b):
    return lax.dot_general(a, b, (((1,), (0,)), ((), ())), preferred_element_type=jnp.float32)


def fold(x, op):
    out = x[:, :HD]
    for i in range(1, x.shape[1] // HD):
        out = op(out, x[:, i * HD : (i + 1) * HD])
    return out


def start_of(position, lengths):
    end = jnp.int32(0)
    out = jnp.zeros_like(position)
    for i in range(lengths.shape[0]):
        end = end + lengths[i]
        out = jnp.where(position >= end, end, out)
    return out


def sound(total):
    return (jnp.min(total) >= LEAST) & (jnp.max(total) <= MOST)


def prefill_kernel(tok, heads, meta, lengths, q, keys_all, values_all, *refs):
    out, qs, peak, total, acc = refs[-5:]
    for j in range(heads):
        qs[j * tok : (j + 1) * tok] = q[:, j * HD : (j + 1) * HD]
    total[...] = jnp.zeros_like(total)
    acc[...] = jnp.zeros_like(acc)

    begin = meta[0]
    finish = begin + tok
    low = start_of(begin, lengths)
    high = start_of(finish - 1, lengths)
    blocks = lax.div(finish - low + SPAN - 1, SPAN)
    clear = lax.div(finish - high, SPAN)

    def first_of(k):
        return jnp.maximum(finish - (k + 1) * SPAN, 0)

    def load(k):
        here = pl.ds(pl.multiple_of(first_of(k), HD), SPAN)
        return keys_all[:, here], values_all[here, :]

    def allowed_in(k):
        t = begin + lax.broadcasted_iota(jnp.int32, (tok, 1), 0)
        u = first_of(k) + lax.broadcasted_iota(jnp.int32, (tok, SPAN), 1)
        last = jnp.minimum(t, finish - k * SPAN - 1)
        return (u <= last) & (u >= start_of(t, lengths))

    def keep(allowed, x, other):
        some = x.shape[0] // tok
        return jnp.where(allowed[None], x.reshape(some, tok, SPAN), other).reshape(x.shape)

    def block(k, masked):
        keys, values = load(k)
        allowed = allowed_in(k) if masked else None
        for j in range(0, heads, PAIR):
            here = slice(j * tok, min(j + PAIR, heads) * tok)
            p = jnp.exp2(dot_nn(qs[here], keys) * FACTOR)
            if masked:
                p = keep(allowed, p, 0.0)
            total[here] += fold(p, jnp.add)
            acc[here] += dot_nn(p.astype(jnp.bfloat16), values)

    block(0, True)

    @pl.loop(1, jnp.maximum(clear, 1))
    def _(k):
        block(k, False)

    @pl.loop(jnp.maximum(clear, 1), blocks)
    def _(k):
        block(k, True)

    def write():
        whole = jnp.sum(total[...], axis=1, keepdims=True)
        result = (acc[...] / whole).astype(out.dtype)
        for j in range(heads):
            out[:, j * HD : (j + 1) * HD] = result[j * tok : (j + 1) * tok]
        return whole

    fine = sound(write())

    @pl.when(jnp.logical_not(fine))
    def _():
        peak[...] = jnp.full_like(peak, NEG)
        total[...] = jnp.zeros_like(total)
        acc[...] = jnp.zeros_like(acc)

        @pl.loop(0, blocks)
        def _(k):
            keys, values = load(k)
            allowed = allowed_in(k)

            @pl.loop(0, heads)
            def _(j):
                here = pl.ds(pl.multiple_of(j * tok, tok), tok)
                s = jnp.where(allowed, dot_nn(qs[here], keys) * FACTOR, NEG)
                top = jnp.maximum(peak[here], jnp.max(s, axis=1, keepdims=True))
                p = jnp.where(allowed, jnp.exp2(s - top[:, :1]), 0.0)
                shrink = jnp.exp2(peak[here] - top)
                total[here] = total[here] * shrink + fold(p, jnp.add)
                acc[here] = acc[here] * shrink + dot_nn(p.astype(jnp.bfloat16), values)
                peak[here] = top

        write()


def prefill(q, keys, values, meta, lengths, groups, columns, name, before=None):
    tok = q.shape[0]
    count = values.shape[0]
    heads = H // KVH
    rows = heads * tok
    pairs = rows * count // 2 * groups
    extra = [] if before is None else [before]
    return pl.pallas_call(
        functools.partial(prefill_kernel, tok, heads),
        out_shape=jax.ShapeDtypeStruct((tok, columns), jnp.bfloat16),
        grid_spec=pltpu.PrefetchScalarGridSpec(
            num_scalar_prefetch=2,
            grid=(groups,),
            in_specs=[
                pl.BlockSpec((tok, heads * HD), lambda g, meta, lengths: (0, meta[1] + g)),
                pl.BlockSpec((HD, count), lambda g, meta, lengths: (meta[2] + g, 0)),
                pl.BlockSpec((count, HD), lambda g, meta, lengths: (0, meta[2] + g)),
            ]
            + [HBM] * len(extra),
            out_specs=pl.BlockSpec((tok, heads * HD), lambda g, meta, lengths: (0, meta[3] + g)),
            scratch_shapes=[
                pltpu.VMEM((rows, HD), jnp.bfloat16),
                pltpu.VMEM((rows, HD), jnp.float32),
                pltpu.VMEM((rows, HD), jnp.float32),
                pltpu.VMEM((rows, HD), jnp.float32),
            ],
        ),
        compiler_params=pltpu.CompilerParams(vmem_limit_bytes=ROOM),
        cost_estimate=pl.CostEstimate(
            flops=pairs * HD * 8, bytes_accessed=count * HD * 4 * groups, transcendentals=pairs
        ),
        input_output_aliases={} if before is None else {5: 0},
        name=name,
    )(meta, lengths, q, keys, values, *extra)


def settle_kernel(meta, piece, whole, out, sem):
    width = piece.shape[1]
    where = pl.ds(pl.multiple_of((1 - meta[CORE]) * width, width), width)
    copy = pltpu.make_async_copy(piece, out.at[:, where], sem)
    copy.start()
    copy.wait()


def settle(whole, piece, meta):
    return pl.pallas_call(
        settle_kernel,
        out_shape=jax.ShapeDtypeStruct(whole.shape, whole.dtype),
        in_specs=[SMEM, VMEM, HBM],
        out_specs=HBM,
        scratch_shapes=[pltpu.SemaphoreType.DMA],
        input_output_aliases={2: 0},
        compiler_params=pltpu.CompilerParams(vmem_limit_bytes=LITTLE),
        cost_estimate=pl.CostEstimate(flops=0, bytes_accessed=piece.size * 4, transcendentals=0),
        name="settle",
    )(meta, piece, whole)


def allowed_at(first, base, tok, length, lengths):
    t = first + lax.broadcasted_iota(jnp.int32, (tok, 1), 0)
    u = base + lax.broadcasted_iota(jnp.int32, (tok, length), 1)
    return (u <= t) & (u >= start_of(t, lengths))


def column_block(at):
    return pl.ds(pl.multiple_of(at, HD), HD)


def keys_of(upper, g):
    return upper[column_block(g * HD), :]


def values_of(lower, g):
    half = lower.shape[1] // 2
    both = [lower[:, column_block(side * half + g * HD)] for side in range(2)]
    return jnp.concatenate(both, axis=0)


def block_bias(first, base, tok, length, lengths):
    start = start_of(first, lengths)
    t = first + lax.broadcasted_iota(jnp.int32, (tok, HD), 0)
    u = base + lax.broadcasted_iota(jnp.int32, (1, length), 1)
    row = jnp.where(start_of(t, lengths) == start, 0.0, -jnp.inf)
    return [jnp.concatenate([row] * (length // HD), axis=1), jnp.where(u >= start, 0.0, -jnp.inf)]


def add_block(tok, heads, q_at, keys, values, biases, sums, old):
    length = keys.shape[1]
    turns = [(j * tok, min(PAIR, heads - j)) for j in range(0, heads, PAIR)]

    def score(at, some):
        return dot_nn(q_at(at, some * tok), keys)

    coming = score(*turns[0])
    for number, (at, some) in enumerate(turns):
        s = coming * FACTOR
        if number + 1 < len(turns):
            coming = score(*turns[number + 1])
        for bias in biases:
            s = (s.reshape(some, tok, length) + bias[None]).reshape(some * tok, length)
        p = jnp.exp2(s)
        more = (fold(p, jnp.add), dot_nn(p.astype(jnp.bfloat16), values))
        here = slice(at, at + some * tok)
        for i in range(2):
            sums[i][here] = more[i] if old is None else old[i][here] + more[i]


def relation(meta, part, side, tok, lengths):
    first = (meta[CHIP] * 2 + side) * tok
    base = meta[PARTS + part] * 2 * tok
    relevant = (base < first) & (meta[PARTS + part] != meta[CHIP])
    relevant = relevant & (base + 2 * tok > start_of(first, lengths))
    return relevant, base >= start_of(first + tok - 1, lengths), first, base


def postponed(meta, tok, lengths, first, end, parts):
    def count(some):
        pairs = [relation(meta, part, side, tok, lengths)[0] for part in some for side in range(2)]
        return sum(pair.astype(jnp.int32) for pair in pairs)

    here, later = count(range(first, end)), count(range(end, parts))
    return (here == 2 * (end - first)) & (here + later <= 8)


def side_rows(side, heads, tok):
    return pl.ds(pl.multiple_of(side * (heads * tok), HD), heads * tok)


def open_kernel(tok, heads, groups, meta, lengths, q, q_near, upper, lower, qs, total, acc):
    core = meta[CORE]
    rows = heads * tok
    for source, side, skip in ((q, core, core * groups * heads), (q_near, 1 - core, 0)):
        for g in range(groups):
            for j in range(heads):
                at = pl.ds(pl.multiple_of(side * rows + j * tok, HD), tok)
                qs[g, at] = source[:, column_block((skip + g * heads + j) * HD)]

    @pl.loop(0, groups)
    def _(g):
        keys, values = keys_of(upper, g), values_of(lower, g)
        for side in range(2):
            length = (side + 1) * tok
            first = (meta[CHIP] * 2 + side) * tok
            allowed = allowed_at(first, meta[CHIP] * 2 * tok, tok, length, lengths)
            here = side_rows(side, heads, tok)
            q_at = lambda at, count: qs[g, pl.ds(side * rows + at, count)]
            bias = jnp.where(allowed, 0.0, -jnp.inf)
            add_block(tok, heads, q_at, keys[:, :length], values[:length], [bias],
                      (total.at[g, here], acc.at[g, here]), None)


def open_sums(q, q_near, block, meta, lengths):
    tok = q.shape[0]
    heads = H // KVH
    groups = q_near.shape[1] // (heads * HD)
    rows = 2 * heads * tok
    sums = jax.ShapeDtypeStruct((groups, rows, HD), jnp.float32)
    pairs = groups * rows * tok * 2
    return pl.pallas_call(
        functools.partial(open_kernel, tok, heads, groups),
        out_shape=[jax.ShapeDtypeStruct((groups, rows, HD), jnp.bfloat16), sums, sums],
        in_specs=[SMEM, SMEM, VMEM, VMEM, VMEM, VMEM],
        out_specs=[VMEM] * 3,
        compiler_params=pltpu.CompilerParams(vmem_limit_bytes=2 * LITTLE),
        cost_estimate=BRIEF,
        name="open",
    )(meta, lengths, q, q_near, *block)


def stage_body(tok, heads, groups, first_part, wait, meta, lengths, qs, before, pair, total, acc):
    later = False
    if wait:
        later = postponed(meta, tok, lengths, first_part, first_part + 2, LEVELS - PARTS)
    for which in range(2):
        upper, lower = pair[2 * which], pair[2 * which + 1]

        @pl.loop(0, 2 * groups)
        def _(step):
            g, side = lax.div(step, 2), lax.rem(step, 2)
            relevant, clear, first, base = relation(meta, first_part + which, side, tok, lengths)
            relevant = relevant & jnp.logical_not(later)
            here = side_rows(side, heads, tok)
            sums = (total.at[g, here], acc.at[g, here])
            old = sums if which else [ref.at[g, here] for ref in before]
            at = side * (heads * tok)
            q_at = lambda off, count: qs[g, pl.ds(pl.multiple_of(at + off, HD), count)]

            @pl.when(relevant & clear)
            def _():
                add_block(tok, heads, q_at, keys_of(upper, g), values_of(lower, g), [], sums, old)

            @pl.when(relevant & jnp.logical_not(clear))
            def _():
                biases = block_bias(first, base, tok, 2 * tok, lengths)
                add_block(
                    tok, heads, q_at, keys_of(upper, g), values_of(lower, g), biases, sums, old
                )

            if which == 0:

                @pl.when(jnp.logical_not(relevant))
                def _():
                    for i in range(2):
                        sums[i][...] = old[i][...]


def stage_kernel(tok, heads, groups, first_part, wait, meta, lengths, qs, total_in, acc_in, *refs):
    pair, (total, acc) = refs[:4], refs[4:]
    before = (total_in, acc_in)
    stage_body(
        tok, heads, groups, first_part, wait, meta, lengths, qs, before, pair, total, acc
    )


def stage(state, pair, first_part, wait, meta, lengths):
    qs, total, acc = state
    groups, rows, unused = qs.shape
    flat = [x for block in pair for x in block]
    tok = flat[0].shape[1] // 2
    new = pl.pallas_call(
        functools.partial(stage_kernel, tok, rows // (2 * tok), groups, first_part, wait),
        out_shape=[jax.ShapeDtypeStruct(x.shape, x.dtype) for x in (total, acc)],
        in_specs=[SMEM, SMEM] + [VMEM] * 7,
        out_specs=[VMEM] * 2,
        input_output_aliases={3: 0, 4: 1},
        compiler_params=pltpu.CompilerParams(vmem_limit_bytes=ROOM),
        cost_estimate=BRIEF,
        name=f"stage{first_part}",
    )(meta, lengths, qs, total, acc, *flat)
    return qs, *new


def finish_kernel(tok, heads, groups, done, meta, lengths, qs, total, acc, *refs):
    near, out, held_k, held_v, peak, total_now, acc_now, result, sem = refs[-9:]
    parts = held_k.shape[0]
    rows = heads * tok
    core = meta[CORE]

    def fill(first):
        for i in range(first, parts):
            held_k[i], held_v[i] = refs[2 * i][...], refs[2 * i + 1][...]

    def turn_of(step):
        turn, g = lax.div(step, groups), lax.rem(step, groups)
        side = jnp.where(turn == 0, 1 - core, core)
        at = side * rows
        q_at = lambda off, count: qs[g, pl.ds(pl.multiple_of(at + off, HD), count)]
        return turn, g, side, q_at

    def write(turn, g):
        whole = jnp.sum(total_now[...], axis=1, keepdims=True)
        value = (acc_now[...] / whole).astype(result.dtype)
        for j in range(heads):
            result[turn, :, column_block((g * heads + j) * HD)] = value[j * tok : (j + 1) * tok]
        return sound(whole)

    def one_turn(step, fine):
        turn, g, side, q_at = turn_of(step)
        here = side_rows(side, heads, tok)
        total_now[...] = total[g, here]
        acc_now[...] = acc[g, here]

        @pl.loop(done, parts)
        def _(i):
            relevant, clear, first, base = relation(meta, i, side, tok, lengths)
            relevant = relevant & ((i >= done + 2) | later)
            upper, lower = held_k.at[i], held_v.at[i]
            sums = (total_now, acc_now)

            @pl.when(relevant & clear)
            def _():
                add_block(tok, heads, q_at, keys_of(upper, g), values_of(lower, g), [], sums, sums)

            @pl.when(relevant & jnp.logical_not(clear))
            def _():
                biases = block_bias(first, base, tok, 2 * tok, lengths)
                add_block(
                    tok, heads, q_at, keys_of(upper, g), values_of(lower, g), biases, sums, sums
                )

        return fine & write(turn, g).astype(jnp.int32)

    later = postponed(meta, tok, lengths, done, done + 2, parts)
    fill(done)
    fine = lax.fori_loop(0, 2 * groups, one_turn, jnp.int32(1))

    @pl.when(fine == 0)
    def _():
        fill(0)

        @pl.loop(0, 2 * groups)
        def _(step):
            turn, g, side, q_at = turn_of(step)
            first = (meta[CHIP] * 2 + side) * tok
            peak[...] = jnp.full_like(peak, NEG)
            total_now[...] = jnp.zeros_like(total_now)
            acc_now[...] = jnp.zeros_like(acc_now)

            @pl.loop(0, parts * heads)
            def _(step):
                i, j = lax.div(step, heads), lax.rem(step, heads)
                keys, values = keys_of(held_k.at[i], g), values_of(held_v.at[i], g)
                allowed = allowed_at(first, meta[PARTS + i] * 2 * tok, tok, 2 * tok, lengths)
                mine = pl.ds(pl.multiple_of(j * tok, tok), tok)
                s = jnp.where(allowed, dot_nn(q_at(j * tok, tok), keys) * FACTOR, NEG)
                top = jnp.maximum(peak[mine], jnp.max(s, axis=1, keepdims=True))
                p = jnp.where(allowed, jnp.exp2(s - top[:, :1]), 0.0)
                shrink = jnp.exp2(peak[mine] - top)
                total_now[mine] = total_now[mine] * shrink + fold(p, jnp.add)
                acc_now[mine] = acc_now[mine] * shrink + dot_nn(p.astype(jnp.bfloat16), values)
                peak[mine] = top

            write(turn, g)

    width = near.shape[1]
    where = pl.ds(pl.multiple_of(core * width, width), width)
    copy = pltpu.make_async_copy(result.at[1], out.at[:, where], sem)
    copy.start()
    near[...] = result[0]
    copy.wait()


def finish(state, blocks, done, meta, lengths):
    qs, total, acc = state
    groups, rows, unused = qs.shape
    flat = [x for block in blocks for x in block]
    tok = flat[0].shape[1] // 2
    heads = rows // (2 * tok)
    width = groups * heads * HD
    sums = pltpu.VMEM((heads * tok, HD), jnp.float32)
    return pl.pallas_call(
        functools.partial(finish_kernel, tok, heads, groups, done),
        out_shape=[
            jax.ShapeDtypeStruct((tok, width), jnp.bfloat16),
            jax.ShapeDtypeStruct((tok, 2 * width), jnp.bfloat16),
        ],
        in_specs=[SMEM, SMEM] + [VMEM] * (3 + len(flat)),
        out_specs=[VMEM, HBM],
        scratch_shapes=[
            *[pltpu.VMEM((len(blocks), *x.shape), x.dtype) for x in blocks[0]],
            sums, sums, sums,
            pltpu.VMEM((2, tok, width), jnp.bfloat16),
            pltpu.SemaphoreType.DMA,
        ],
        compiler_params=pltpu.CompilerParams(vmem_limit_bytes=ROOM),
        cost_estimate=pl.CostEstimate(
            flops=groups * rows * tok * HD * 8, bytes_accessed=tok * width * 4,
            transcendentals=groups * rows * tok * 2,
        ),
        name="finish",
    )(meta, lengths, qs, total, acc, *flat)


def request_sums(query, keys, values, bias):
    s = dot_nn(query, keys) * FACTOR
    p = jnp.exp2((s.reshape(-1, *bias.shape) + bias[None]).reshape(s.shape))
    return fold(p, jnp.add), dot_nn(p.astype(jnp.bfloat16), values)


def fresh_scores(query, newk, own):
    s = dot_nt(query, newk) * FACTOR
    size = newk.shape[0]
    row = lax.broadcasted_iota(jnp.int32, (size, size), 0)
    col = lax.broadcasted_iota(jnp.int32, (size, size), 1)
    ok = (lax.rem(row, own) == lax.rem(col, own)) & (lax.div(col, own) <= lax.div(row, own))
    return s.reshape(-1, size, size), ok


def request_copies(own, meta, sources, held, sems):
    requests = pl.ds(lax.div(meta[CHIP], 2) * own, own)
    copies = []
    for i, (source, target) in enumerate(zip(sources, held)):
        width = target.shape[2]
        where = pl.ds(pl.multiple_of(meta[CORE] * width, width), width)
        copies.append(pltpu.make_async_copy(source.at[requests, :, where], target, sems.at[i]))
    return copies


def requests_body(own, heads, groups, length, meta, table, total, acc, query, newk, newv, mask, q3, k3, v3):
    steps = q3.shape[1]
    level = lax.div(meta[CHIP], 2)
    pick = lax.broadcasted_iota(jnp.int32, (own, table.shape[1]), 1) - level * own
    pick = (pick == lax.broadcasted_iota(jnp.int32, pick.shape, 0)).astype(jnp.float32)
    rows = dot_nt(pick.astype(jnp.bfloat16), table[...].astype(jnp.float32).astype(jnp.bfloat16))
    lane = lax.div(lax.broadcasted_iota(jnp.int32, (own, length), 1), BLK)
    for i in range(mask.shape[1] // length):
        number = (lane + meta[PARTS + i] * (length // BLK)).astype(jnp.float32)
        hit = rows[:, :1] == number
        for j in range(1, rows.shape[1]):
            hit = hit | (rows[:, j : j + 1] == number)
        mask[:, i * length : (i + 1) * length] = jnp.where(hit, 0.0, -jnp.inf)
    for s in range(steps):
        for g in range(groups):
            col = slice(g * HD, (g + 1) * HD)
            at = slice(s * own, (s + 1) * own)
            newk[at, col] = k3[:, s, col]
            newv[at, col] = v3[:, s, col]
            for j in range(heads):
                first = (g * heads + j) * HD
                row = (j * steps + s) * own
                query[g, row : row + own] = q3[:, s, first : first + HD]

    @pl.loop(0, groups)
    def _(g):
        col = column_block(g * HD)
        s, ok = fresh_scores(query[g], newk[:, col], own)
        p = jnp.where(ok[None], jnp.exp2(s), 0.0).reshape(-1, s.shape[2])
        first = jnp.sum(p, axis=1, keepdims=True)
        lead = lax.broadcasted_iota(jnp.int32, (p.shape[0], HD), 1) == 0
        total[g] = jnp.where(lead, first, 0.0)
        acc[g] = dot_nn(p.astype(jnp.bfloat16), newv[:, col])


def requests_kernel(own, heads, groups, length, meta, *refs):
    sources, table, state, (q3, k3, v3, sems) = refs[:3], refs[3], refs[4:10], refs[10:]
    copies = request_copies(own, meta, sources, (q3, k3, v3), sems)
    for copy in copies:
        copy.start()
    for copy in copies:
        copy.wait()
    requests_body(own, heads, groups, length, meta, table, *state, q3, k3, v3)


def open_requests(q_dec, k_new, v_new, table, length, own, meta):
    heads = H // KVH
    steps = q_dec.shape[1]
    width = k_new.shape[2] // 2
    groups = width // HD
    rows = heads * own * steps
    sums = jax.ShapeDtypeStruct((groups, rows, HD), jnp.float32)
    new = jax.ShapeDtypeStruct((own * steps, width), jnp.bfloat16)
    return pl.pallas_call(
        functools.partial(requests_kernel, own, heads, groups, length),
        out_shape=[
            sums, sums, jax.ShapeDtypeStruct((groups, rows, HD), jnp.bfloat16), new, new,
            jax.ShapeDtypeStruct((own, (LEVELS - PARTS) * length), jnp.float32),
        ],
        in_specs=[SMEM] + [HBM] * 3 + [VMEM],
        out_specs=[VMEM] * 6,
        scratch_shapes=[
            pltpu.VMEM((own, steps, groups * heads * HD), jnp.bfloat16),
            pltpu.VMEM((own, steps, width), jnp.bfloat16),
            pltpu.VMEM((own, steps, width), jnp.bfloat16),
            pltpu.SemaphoreType.DMA((3,)),
        ],
        compiler_params=pltpu.CompilerParams(vmem_limit_bytes=LITTLE),
        cost_estimate=BRIEF,
        name="requests",
    )(meta, q_dec, k_new, v_new, table)


def early_kernel(groups, total_in, acc_in, query, mask, *refs):
    total, acc = refs[-2:]
    length = refs[0].shape[1]

    @pl.loop(0, groups)
    def _(g):
        sums = [total_in[g], acc_in[g]]
        for i in range(len(refs) // 2 - 1):
            bias = mask[:, i * length : (i + 1) * length]
            keys, values = keys_of(refs[2 * i], g), values_of(refs[2 * i + 1], g)
            more = request_sums(query[g], keys, values, bias)
            sums = [x + y for x, y in zip(sums, more)]
        total[g], acc[g] = sums


def early_decode(state, blocks):
    total, acc, query, newk, newv, mask = state
    groups, rows, unused = query.shape
    flat = [x for block in blocks for x in block]
    sums = jax.ShapeDtypeStruct(total.shape, total.dtype)
    new = pl.pallas_call(
        functools.partial(early_kernel, groups),
        out_shape=[sums, sums],
        in_specs=[VMEM] * (4 + len(flat)),
        out_specs=[VMEM] * 2,
        input_output_aliases={0: 0, 1: 1},
        compiler_params=pltpu.CompilerParams(vmem_limit_bytes=2 * LITTLE),
        cost_estimate=BRIEF,
        name="early_decode",
    )(total, acc, query, mask, *flat)
    return [*new, query, newk, newv, mask]


def late_kernel(own, steps, heads, groups, done, meta, total, acc, query, newk, newv, mask, *refs):
    parts, out = len(refs) // 2, refs[-1]
    length = refs[0].shape[1]
    size = own * steps

    def write(g, sums, whole):
        result = (sums / whole).astype(out.dtype)
        for j in range(heads):
            out[:, column_block((g * heads + j) * HD)] = result[j * size : (j + 1) * size]

    def one_group(g, fine):
        sums = [total[g], acc[g]]
        for i in range(done, parts):
            bias = mask[:, i * length : (i + 1) * length]
            keys, values = keys_of(refs[2 * i], g), values_of(refs[2 * i + 1], g)
            more = request_sums(query[g], keys, values, bias)
            sums = [x + y for x, y in zip(sums, more)]
        whole = jnp.sum(sums[0], axis=1, keepdims=True)
        write(g, sums[1], whole)
        return fine & sound(whole).astype(jnp.int32)

    fine = lax.fori_loop(0, groups, one_group, jnp.int32(1))

    @pl.when(fine == 0)
    def _():
        @pl.loop(0, groups)
        def _(g):
            col = column_block(g * HD)
            fresh, ok = fresh_scores(query[g], newk[:, col], own)
            fresh = jnp.where(ok[None], fresh, NEG).reshape(-1, size)
            top = jnp.max(fresh, axis=1, keepdims=True)
            p = jnp.exp2(fresh - top)
            whole = jnp.sum(p, axis=1, keepdims=True)
            sums = dot_nn(p.astype(jnp.bfloat16), newv[:, col])
            for i in range(parts):
                s = dot_nn(query[g], keys_of(refs[2 * i], g)) * FACTOR
                open_to = mask[:, i * length : (i + 1) * length] >= 0
                s = jnp.where(open_to[None], s.reshape(-1, own, length), NEG).reshape(s.shape)
                higher = jnp.maximum(top, jnp.max(s, axis=1, keepdims=True))
                p = jnp.exp2(s - higher)
                shrink = jnp.exp2(top - higher)
                whole = whole * shrink + jnp.sum(p, axis=1, keepdims=True)
                sums = sums * shrink + dot_nn(p.astype(jnp.bfloat16), values_of(refs[2 * i + 1], g))
                top = higher
            write(g, sums, whole)


def late_decode(early, blocks, done, own, steps, meta):
    groups, rows, unused = early[0].shape
    heads = H // KVH
    flat = [x for block in blocks for x in block]
    parts, length = len(blocks), flat[0].shape[1]
    pairs = groups * rows * (parts - done) * length
    return pl.pallas_call(
        functools.partial(late_kernel, own, steps, heads, groups, done),
        out_shape=jax.ShapeDtypeStruct((own * steps, groups * heads * HD), jnp.bfloat16),
        in_specs=[SMEM] + [VMEM] * (len(early) + len(flat)),
        out_specs=VMEM,
        compiler_params=pltpu.CompilerParams(vmem_limit_bytes=ROOM),
        cost_estimate=pl.CostEstimate(
            flops=pairs * HD * 8, bytes_accessed=rows * HD, transcendentals=pairs
        ),
        name="late_decode",
    )(meta, *early, *flat)


def decode_kernel(parts, steps, heads, groups, starts, q, mask, newk, newv, *refs):
    kheld, vheld = refs[:parts], refs[parts : 2 * parts]
    out, kall, vall, sems, scores = refs[2 * parts :]
    own = q.shape[0]
    rows = heads * own
    length = kheld[0].shape[1]
    copies = []
    for i in range(parts):
        where = pl.ds(pl.multiple_of(starts[i], HD), length)
        copies.append(pltpu.make_async_copy(kheld[i], kall.at[:, where], sems.at[2 * i]))
        copies.append(pltpu.make_async_copy(vheld[i], vall.at[where], sems.at[2 * i + 1]))
    for copy in copies:
        copy.start()
    row = lax.broadcasted_iota(jnp.int32, (own, own), 0)
    col = lax.broadcasted_iota(jnp.int32, (own, own), 1)
    fresh_ok = (lax.div(row, steps) == lax.div(col, steps)) & (col <= row)

    def columns(g):
        return slice(g * HD, (g + 1) * HD)

    def stacked(g):
        first = g * heads
        slices = [q[:, (first + j) * HD : (first + j + 1) * HD] for j in range(heads)]
        return jnp.concatenate([x.astype(jnp.float32) for x in slices], 0).astype(jnp.bfloat16)

    def keep(allowed, x, other):
        y = x.reshape(heads, own, x.shape[1])
        return jnp.where(allowed[None], y, other).reshape(x.shape)

    def open_to(i):
        return mask[:, pl.ds(pl.multiple_of(starts[i], HD), length)] > 0

    def write(g, acc, whole):
        result = acc / whole
        for j in range(heads):
            out[:, (g * heads + j) * HD : (g * heads + j + 1) * HD] = result[
                j * own : (j + 1) * own
            ].astype(out.dtype)

    fine = None
    for g in range(groups):
        query = stacked(g)
        p = keep(fresh_ok, jnp.exp2(dot_nt(query, newk[:, columns(g)]) * FACTOR), 0.0)
        whole = jnp.sum(p, axis=1, keepdims=True)
        acc = dot_nn(p.astype(jnp.bfloat16), newv[:, columns(g)])
        total = jnp.zeros((rows, HD), jnp.float32)
        for i in range(parts):
            p = jnp.exp2(dot_nn(query, kheld[i][columns(g)]) * FACTOR)
            p = keep(open_to(i), p, 0.0)
            total = total + fold(p, jnp.add)
            acc = acc + dot_nn(p.astype(jnp.bfloat16), vheld[i][:, columns(g)])
        whole = whole + jnp.sum(total, axis=1, keepdims=True)
        write(g, acc, whole)
        fine = sound(whole) if fine is None else fine & sound(whole)

    @pl.when(jnp.logical_not(fine))
    def _():
        for g in range(groups):
            query = stacked(g)
            fresh = keep(fresh_ok, dot_nt(query, newk[:, columns(g)]) * FACTOR, NEG)
            top = jnp.max(fresh, axis=1, keepdims=True)
            for i in range(parts):
                s = keep(open_to(i), dot_nn(query, kheld[i][columns(g)]) * FACTOR, NEG)
                scores[:, i * length : (i + 1) * length] = s
                top = jnp.maximum(top, jnp.max(s, axis=1, keepdims=True))
            p = jnp.exp2(fresh - top)
            whole = jnp.sum(p, axis=1, keepdims=True)
            acc = dot_nn(p.astype(jnp.bfloat16), newv[:, columns(g)])
            for i in range(parts):
                p = jnp.exp2(scores[:, i * length : (i + 1) * length] - top)
                whole = whole + jnp.sum(p, axis=1, keepdims=True)
                acc = acc + dot_nn(p.astype(jnp.bfloat16), vheld[i][:, columns(g)])
            write(g, acc, whole)

    for copy in copies:
        copy.wait()


def decode(q, mask, newk, newv, kparts, vparts, starts, steps):
    own = q.shape[0]
    parts = len(kparts)
    length, width = vparts[0].shape
    count = parts * length
    heads = H // KVH
    groups = width // HD
    rows = heads * own
    pairs = groups * rows * count
    return pl.pallas_call(
        functools.partial(decode_kernel, parts, steps, heads, groups),
        out_shape=[
            jax.ShapeDtypeStruct(q.shape, jnp.bfloat16),
            jax.ShapeDtypeStruct((width, count), jnp.bfloat16),
            jax.ShapeDtypeStruct((count, width), jnp.bfloat16),
        ],
        grid_spec=pltpu.PrefetchScalarGridSpec(
            num_scalar_prefetch=1,
            grid=(),
            in_specs=[VMEM] * (4 + 2 * parts),
            out_specs=[VMEM, HBM, HBM],
            scratch_shapes=[
                pltpu.SemaphoreType.DMA((2 * parts,)),
                pltpu.VMEM((rows, count), jnp.float32),
            ],
        ),
        compiler_params=pltpu.CompilerParams(vmem_limit_bytes=ROOM),
        cost_estimate=pl.CostEstimate(
            flops=pairs * HD * 4, bytes_accessed=count * width * 4, transcendentals=pairs
        ),
        name="decode",
    )(starts, q, mask, newk, newv, *kparts, *vparts)


def prepare_kernel(meta, k, v, send, keys, values):
    width = k.shape[1] // 2
    mine = pl.ds(pl.multiple_of(meta[0] * width, width), width)
    other = pl.ds(pl.multiple_of((1 - meta[0]) * width, width), width)
    send[:width] = k[:, other].astype(jnp.float32).T.astype(send.dtype)
    send[width:] = v[:, other]
    keys[:, mine] = k[:, mine].astype(jnp.float32).T.astype(keys.dtype)
    values[:, mine] = v[:, mine]


def prepare(k, v, core):
    tok, width = k.shape[0], k.shape[1] // 2
    assert tok == width
    block = jax.ShapeDtypeStruct((width, 2 * tok), k.dtype)
    return pl.pallas_call(
        prepare_kernel,
        out_shape=[jax.ShapeDtypeStruct((2 * tok, width), k.dtype), block, block],
        in_specs=[SMEM, VMEM, VMEM],
        out_specs=[VMEM] * 3,
        compiler_params=pltpu.CompilerParams(vmem_limit_bytes=LITTLE),
        name="prepare",
    )(core[None], k, v)


def join_kernel(meta, keys_in, values_in, theirs, q, keys, values, send_q, sem):
    columns = send_q.shape[1]
    where = pl.ds(pl.multiple_of((1 - meta[0]) * columns, columns), columns)
    copy = pltpu.make_async_copy(q.at[:, where], send_q, sem)
    copy.start()
    width = theirs.shape[1]
    other = pl.ds(pl.multiple_of((1 - meta[0]) * width, width), width)
    keys[...], values[...] = keys_in[...], values_in[...]
    keys[:, other] = theirs[:width]
    values[:, other] = theirs[width:]
    copy.wait()


def join(keys, values, theirs, q, core):
    return pl.pallas_call(
        join_kernel,
        out_shape=[
            jax.ShapeDtypeStruct(keys.shape, keys.dtype),
            jax.ShapeDtypeStruct(values.shape, values.dtype),
            jax.ShapeDtypeStruct((q.shape[0], q.shape[1] // 2), q.dtype),
        ],
        in_specs=[SMEM, VMEM, VMEM, VMEM, HBM],
        out_specs=[VMEM] * 3,
        scratch_shapes=[pltpu.SemaphoreType.DMA],
        compiler_params=pltpu.CompilerParams(vmem_limit_bytes=LITTLE),
        name="join",
    )(core[None], keys, values, theirs, q)


def take_kernel(meta, whole, out, sem):
    width = out.shape[1]
    where = pl.ds(pl.multiple_of((1 - meta[CORE]) * width, width), width)
    copy = pltpu.make_async_copy(whole.at[:, where], out, sem)
    copy.start()
    copy.wait()


def take_other_half(whole, meta):
    return pl.pallas_call(
        take_kernel,
        out_shape=jax.ShapeDtypeStruct((whole.shape[0], whole.shape[1] // 2), whole.dtype),
        in_specs=[SMEM, HBM],
        out_specs=VMEM,
        scratch_shapes=[pltpu.SemaphoreType.DMA],
        compiler_params=pltpu.CompilerParams(vmem_limit_bytes=LITTLE),
        name="take",
    )(meta, whole)


def project_kernel(meta, *refs):
    pieces, (whole, other), outs, (sorted_rows,) = refs[:-7], refs[-7:-5], refs[-5:-1], refs[-1:]
    parts = len(pieces)
    rows = pieces[0].shape[0]
    for i, piece in enumerate(pieces):
        at = pl.ds(pl.multiple_of(meta[LEVELS + i] * rows, rows), rows)
        sorted_rows[at] = piece[...]
    depth = other.shape[1]
    mine = whole[:, pl.ds(pl.multiple_of(meta[CORE] * depth, depth), depth)]
    half = parts * rows // 2
    here = pl.ds(pl.multiple_of(meta[ACROSS] * half, half), half)
    there = pl.ds(pl.multiple_of((1 - meta[ACROSS]) * half, half), half)
    kept, beside, across, corner = outs
    for at, near, far in ((here, kept, beside), (there, across, corner)):
        some = sorted_rows[at]
        near[...] = dot_nt(mine, some).astype(near.dtype)
        far[...] = dot_nt(other[...], some).astype(far.dtype)


def project(pieces, whole, other, meta):
    rows = len(pieces) * pieces[0].shape[0]
    width, depth = other.shape
    block = jax.ShapeDtypeStruct((width, rows // 2), jnp.bfloat16)
    return pl.pallas_call(
        project_kernel,
        out_shape=[jax.ShapeDtypeStruct(block.shape, jnp.float32)] + [block] * 3,
        in_specs=[SMEM] + [VMEM] * (len(pieces) + 2),
        out_specs=[VMEM] * 4,
        scratch_shapes=[pltpu.VMEM((rows, depth), jnp.bfloat16)],
        compiler_params=pltpu.CompilerParams(vmem_limit_bytes=2 * LITTLE),
        cost_estimate=pl.CostEstimate(
            flops=rows * width * depth * 4, bytes_accessed=width * depth * 4, transcendentals=0
        ),
        name="project",
    )(meta, *pieces, whole, other)


def index(z, y, c):
    return (z * 2 + y) * 2 + c


def on_ring(r, chips):
    return (r, 0) if r < chips // 2 else (chips - 1 - r, 1)


def ring_perm(chips, d):
    return [
        (index(*on_ring(r, chips), c), index(*on_ring((r + d) % chips, chips), c))
        for r in range(chips)
        for c in range(2)
    ]


def ring_place(r, chips):
    r = lax.rem(r + 2 * chips, chips)
    return jnp.where(r < chips // 2, r * 2, (chips - 1 - r) * 2 + 1)


def spread(x, n):
    place = lax.axis_index("seq")
    deep = n // 4
    everyone = [(z, y, c) for z in range(deep) for y in range(2) for c in range(2)]
    z, y, c = place // 4, (place // 2) % 2, place % 2
    held = [(x, z, y, c)]
    for d in range(1, deep):
        perm = [(index(*p), index((p[0] - d) % deep, p[1], p[2])) for p in everyone]
        held.append((lax.ppermute(x, "seq", perm), lax.rem(z + d, deep), y, c))
    perm = [(index(*p), index(p[0], 1 - p[1], p[2])) for p in everyone]
    held += [(lax.ppermute(b, "seq", perm), bz, 1 - by, bc) for b, bz, by, bc in held]
    perm = [(index(*p), index(p[0], p[1], 1 - p[2])) for p in everyone]
    held += [(lax.ppermute(b, "seq", perm), bz, by, 1 - bc) for b, bz, by, bc in held]
    return [b for b, *_ in held], jnp.stack([index(bz, by, bc) for _, bz, by, bc in held])


def open_blocks(table, steps, count):
    number = lax.broadcasted_iota(jnp.int32, (*table.shape, count), 2) // BLK
    mask = jnp.any(table[:, :, None] == number, axis=1).astype(jnp.float32)
    return jnp.repeat(mask, steps, axis=0)


def whole_heads(n, q_pre, k_cache, v_cache, lengths, q_dec, k_new, v_new, block_table, w_out):
    tok = q_pre.shape[0]
    place = lax.axis_index("seq").astype(jnp.int32)
    rows, steps = q_dec.shape[0], q_dec.shape[1]
    own = rows // n
    kparts, sources = spread(k_cache.T, n)
    vparts, _ = spread(v_cache, n)
    starts = sources.astype(jnp.int32) * tok

    def mine(x):
        y = lax.dynamic_slice_in_dim(x, place * own, own, 0)
        return y.reshape(own * steps, -1) if x.ndim == 3 else y

    mask = open_blocks(mine(block_table), steps, n * tok)
    attn_own, keys, values = decode(
        mine(q_dec), mask, mine(k_new), mine(v_new), kparts, vparts, starts, steps
    )
    attn = lax.all_gather(attn_own, "seq", axis=0, tiled=True)
    flat = jnp.dot(attn, w_out, preferred_element_type=jnp.float32).astype(jnp.bfloat16)
    dec_out = lax.psum_scatter(
        flat.reshape(rows, steps, -1), "tp", scatter_dimension=0, tiled=True
    )
    zero = jnp.zeros((), jnp.int32)
    meta = jnp.stack([place * tok, zero, zero, zero])
    groups = k_cache.shape[1] // HD
    pre_out = prefill(
        q_pre, keys, values, meta, lengths, groups, q_pre.shape[1], "prefill"
    )
    return (pre_out, dec_out)


def split_heads(n, q_pre, k_cache, v_cache, lengths, q_dec, k_new, v_new, block_table, w_out):
    tok = q_pre.shape[0]
    place = lax.axis_index("seq").astype(jnp.int32)
    across = lax.axis_index("tp").astype(jnp.int32)
    core, chip = lax.rem(place, 2), lax.div(place, 2)
    chips = n // 2
    far, deep = chips // 2, chips // 2
    z, y = lax.div(chip, 2), lax.rem(chip, 2)
    r = jnp.where(y == 0, z, chips - 1 - z)
    rows, steps = q_dec.shape[0], q_dec.shape[1]
    own = rows // deep
    sibling = [(i, i ^ 1) for i in range(n)]
    everyone = [(a, b, c) for a in range(deep) for b in range(2) for c in range(2)]

    order = [0] + [o for d in range(1, far) for o in (-d, d)] + [far]
    numbers = [ring_place(r + o, chips) for o in order]
    levels = [z] + [lax.rem(z + deep - d, deep) for d in range(1, deep)]
    assert len(numbers) == LEVELS - PARTS
    meta = jnp.stack([core, chip, across] + numbers + levels).astype(jnp.int32)

    send, keys, values = prepare(k_cache, v_cache, core)
    theirs = lax.ppermute(send, "seq", sibling)
    theirs, meta = lax.optimization_barrier((theirs, meta))
    held_k, held_v = {}, {}
    held_k[0], held_v[0], send_q = join(keys, values, theirs, q_pre, core)
    near_q = lax.ppermute(send_q, "seq", sibling)

    up, down = ring_perm(chips, 1), ring_perm(chips, -1)
    early, w_near = (), w_out
    for d in range(1, far + 1):
        held_k[-d] = lax.ppermute(held_k[1 - d], "seq", up)
        held_v[d] = lax.ppermute(held_v[d - 1], "seq", down)
        if d < far:
            held_k[d] = lax.ppermute(held_k[d - 1], "seq", down)
            held_v[-d] = lax.ppermute(held_v[1 - d], "seq", up)
            sides = (-d, d)
        else:
            held_k[d] = held_k[-d]
            sides = (d,)
        if d == 1:
            state = open_sums(q_pre, near_q, (held_k[0], held_v[0]), meta, lengths)
        elif d < far:
            pair = [(held_k[o], held_v[o]) for o in (1 - d, d - 1)]
            state = stage(state, pair, 2 * d - 3, d == far - 1, meta, lengths)
        else:
            blocks = [(held_k[o], held_v[o]) for o in order[:-1]]
            early = early_decode(early, blocks)
        for x in (held_k, held_v):
            moved, state, early = lax.optimization_barrier(([x[o] for o in sides], state, early))
            x.update(zip(sides, moved))
            if d == 1 and x is held_k:
                state, block_table = lax.optimization_barrier((state, block_table))
                early = open_requests(
                    q_dec, k_new, v_new, block_table.T, 2 * tok, own, meta
                )
        if d == 3:
            w_near, state = lax.optimization_barrier((w_near, state))
            weights = w_near.T
            w_near = lax.ppermute(take_other_half(weights, meta), "seq", sibling)
    w_near, early = lax.optimization_barrier((w_near, early))
    blocks = [(held_k[o], held_v[o]) for o in order]
    attn_own = late_decode(early, blocks, len(blocks) - 1, own, steps, meta)

    pieces = [attn_own]
    for d in range(1, deep):
        perm = [(index(*p), index((p[0] + d) % deep, p[1], p[2])) for p in everyone]
        pieces.append(lax.ppermute(attn_own, "seq", perm))
    attn_own, state = lax.optimization_barrier((attn_own, state))
    near, pre_out = finish(state, blocks, 2 * far - 5, meta, lengths)
    pieces, near, pre_out = lax.optimization_barrier((pieces, near, pre_out))
    back = lax.ppermute(near, "seq", sibling)
    pre_out = settle(pre_out, back, meta)

    total, *sent = project(pieces, weights, w_near, meta)
    got = []
    for piece, (dc, dx) in zip(sent, ((1, 0), (0, 1), (1, 1))):
        perm = [
            (i * 2 + x, (i ^ dc) * 2 + (x ^ dx)) for i in range(n) for x in range(2)
        ]
        got.append(lax.ppermute(piece, ("seq", "tp"), perm))
    got[0], pre_out = lax.optimization_barrier((got[0], pre_out))
    for piece in got:
        total = total + piece.astype(jnp.float32)
    dec_out = total.astype(jnp.bfloat16).T.reshape(deep // 2, steps, own, -1)
    return (pre_out, dec_out.transpose(0, 2, 1, 3).reshape(rows // 2, steps, -1))


def per_device(n, tp, q_pre, k_cache, v_cache, prompt_lengths, *rest):
    groups = k_cache.shape[1] // HD
    square = groups % 2 == 0 and k_cache.shape[1] == 2 * k_cache.shape[0]
    small = n * k_cache.shape[0] // BLK <= 256 and n == 2 * (LEVELS - PARTS)
    form = split_heads if square and tp == 2 and small else whole_heads
    return form(n, q_pre, k_cache, v_cache, prompt_lengths.astype(jnp.int32), *rest)


def solution(mesh):
    placed = (
        P("seq", "tp"),
        P("seq", "tp"),
        P("seq", "tp"),
        P(),
        P(None, None, "tp"),
        P(None, None, "tp"),
        P(None, None, "tp"),
        P(),
        P("tp", "seq"),
    )
    return jax.shard_map(
        functools.partial(per_device, mesh.shape["seq"], mesh.shape["tp"]),
        mesh=mesh,
        in_specs=placed,
        out_specs=(P("seq", "tp"), P("tp", None, "seq")),
        check_vma=False,
    )
```
